32 devices in a mesh: dp: 8 (over y, x, core), ctx: 4 (over z).
Axes of the slice: x: 2, y: 2, z: 4, core: 2. Of those that a mesh axis runs over, the one named last changes fastest.
Arguments:
- tokens: bfloat16 [4096, 1536], P(('dp', 'ctx')), may hold values from -6 to 6
- cotangent: float32 [4096, 1536], P(('dp', 'ctx')), may hold values from -6 to 6
- w_qkv: bfloat16 [2, 1536, 3072], P(None, ('dp', 'ctx')), may hold values from -0.15625 to 0.15625
- w_out: bfloat16 [2, 1536, 1536], P(None, None, ('dp', 'ctx')), may hold values from -1.25 to 1.25
- w_gate_up: bfloat16 [2, 1536, 2, 4096], P(None, ('dp', 'ctx')), may hold values from -0.15625 to 0.15625
- w_down: bfloat16 [2, 4096, 1536], P(None, ('dp', 'ctx')), may hold values from -0.09375 to 0.09375
- gains: bfloat16 [2, 2, 1536], P(None, None, ('dp', 'ctx')), may hold values from 0.25 to 1.75
Outputs:
- out_act: float32 [4096, 1536], P(('dp', 'ctx'))
- grad_tokens: float32 [4096, 1536], P(('dp', 'ctx'))
- grad_qkv: float32 [2, 1536, 3072], P(None, ('dp', 'ctx'))
- grad_out: float32 [2, 1536, 1536], P(None, None, ('dp', 'ctx'))
- grad_gate_up: float32 [2, 1536, 2, 4096], P(None, ('dp', 'ctx'))
- grad_down: float32 [2, 4096, 1536], P(None, ('dp', 'ctx'))
- grad_gains: float32 [2, 2, 1536], P(None, None, ('dp', 'ctx'))
The draws below stay inside these ranges and needn't reach their ends.
All inputs are finite; a program needn't handle non-finite values.
Results may differ from the reference program's by a relative error of at most 0.025.
Values may be sent and summed in bfloat16 or wider, within the bound.
A program may use at most 640 MiB of HBM per device.

```python
import jax
import jax.numpy as jnp
from jax import lax

D = 1536
FF = 4096
HEADS = 16
KV_HEADS = 8
HEAD_DIM = 96
LAYERS = 2
LENGTH = 512
TOKENS = 4096
AW = 1536
QKV = 3072
N_DP = 8


def block_scale(own_key, dims, shards, smallest, top_value):
    gain = 1.0
    for position, parts in shards:
        steps = jax.random.uniform(jax.random.fold_in(jax.random.fold_in(own_key, 6), position), (parts,), jnp.float32, smallest / len(shards), top_value / len(shards))
        gain = gain * jnp.repeat(jnp.exp(steps), dims[position] // parts).reshape((-1,) + (1,) * (len(dims) - 1 - position))
    return gain


def centred(stream_key, extent, width, most, cuts=(), dtype=jnp.bfloat16):
    drawn = jax.random.normal(stream_key, extent, jnp.float32) * width
    if len(cuts) > 0:
        drawn = block_scale(stream_key, extent, cuts, -0.22, 0.18) * drawn
    return jnp.clip(drawn, min=-most, max=most).astype(dtype)


def setup_inputs(seed: int = 0) -> dict:
    key_of = jax.random.split(jax.random.key(seed), 8)
    tokens = centred(key_of[0], (TOKENS, D), 1.0, 6.0, ((0, 32),))
    cotangent = centred(key_of[1], (TOKENS, D), 1.0, 6.0, ((0, 32),), jnp.float32)
    w_qkv = centred(key_of[2], (LAYERS, D, QKV), D ** -0.5, 0.15625, ((1, 32),))
    w_out = centred(key_of[3], (LAYERS, AW, D), (AW * 8 // LENGTH) ** -0.5, 1.25, ((2, 32),))
    w_gate_up = centred(key_of[4], (LAYERS, D, 2, FF), D ** -0.5, 0.15625, ((1, 32),))
    w_down = centred(key_of[5], (LAYERS, FF, D), FF ** -0.5, 0.09375, ((1, 32),))
    gains = jnp.clip(1.0 + 0.15 * jax.random.normal(key_of[6], (LAYERS, 2, D), jnp.float32), 0.25, 1.75).astype(jnp.bfloat16)
    return dict(tokens=tokens, cotangent=cotangent, w_qkv=w_qkv, w_out=w_out, w_gate_up=w_gate_up, w_down=w_down, gains=gains)


NORM_EPS = 1e-05
ROPE_BASE = 100000.0
MASKED = -1e+30

def rotary_tables(positions, head_size):
    half_size = head_size // 2
    freq_index = jnp.arange(half_size).astype(jnp.float32)
    inverse = jnp.exp(freq_index * (-2.0 * jnp.log(ROPE_BASE) / head_size))
    angles = positions.astype(jnp.float32)[:, None] * inverse[None, :]
    return (jnp.cos(angles), jnp.sin(angles))

def rotate(values, cosine, sine_tab):
    half_size = values.shape[-1] // 2
    first_half = values[..., :half_size]
    second_half = values[..., half_size:]
    cos_wide = cosine[:, None, :]
    sin_wide = sine_tab[:, None, :]
    return jnp.concatenate([first_half * cos_wide - second_half * sin_wide, second_half * cos_wide + first_half * sin_wide], axis=-1)

def unrotate(grads, cosine, sine_tab):
    half_size = grads.shape[-1] // 2
    first_half = grads[..., :half_size]
    second_half = grads[..., half_size:]
    cos_wide = cosine[:, None, :]
    sin_wide = sine_tab[:, None, :]
    return jnp.concatenate([first_half * cos_wide + second_half * sin_wide, second_half * cos_wide - first_half * sin_wide], axis=-1)

def norm_forward(state, gain_row):
    factor = lax.rsqrt(lax.optimization_barrier(jnp.mean(state * state, axis=-1, keepdims=True)) + NORM_EPS)
    return (state * factor * gain_row.astype(jnp.float32), factor)

def norm_backward(state, factor, gain_row, grad_normed):
    weighted = grad_normed * gain_row.astype(jnp.float32)
    features = state.shape[-1]
    inner = lax.optimization_barrier(jnp.sum(weighted * state, axis=-1, keepdims=True))
    grad_state = factor * weighted - state * factor * factor * factor * inner / features
    grad_gain = lax.optimization_barrier(jnp.sum(grad_normed * state * factor, axis=0))
    return (grad_state, grad_gain)

def attend_forward(query_b, keys_all, values_all, causal):
    scale = HEAD_DIM ** (-0.5)
    scores = jnp.einsum('qkgd,skd->kgqs', query_b.astype(jnp.float32), keys_all.astype(jnp.float32)) * scale
    scores = jnp.where(causal[None, None], scores, MASKED)
    highest = lax.optimization_barrier(jnp.max(scores, axis=-1, keepdims=True))
    log_total = highest + jnp.log(lax.optimization_barrier(jnp.sum(jnp.exp(scores - highest), axis=-1, keepdims=True)))
    attend_b = jnp.exp(scores - log_total).astype(jnp.bfloat16)
    mixed = jnp.einsum('kgqs,skd->qkgd', attend_b.astype(jnp.float32), values_all.astype(jnp.float32)).astype(jnp.bfloat16)
    return (mixed, log_total)

def attend_backward(query_b, keys_all, values_all, mixed, log_total, grad_mixed, causal):
    scale = HEAD_DIM ** (-0.5)
    scores = jnp.einsum('qkgd,skd->kgqs', query_b.astype(jnp.float32), keys_all.astype(jnp.float32)) * scale
    scores = jnp.where(causal[None, None], scores, MASKED)
    attend_f = jnp.exp(scores - log_total)
    attend_b = attend_f.astype(jnp.bfloat16)
    grad_mixed_f = grad_mixed.astype(jnp.float32)
    grad_attend = jnp.einsum('qkgd,skd->kgqs', grad_mixed_f, values_all.astype(jnp.float32))
    delta = lax.optimization_barrier(jnp.sum(grad_mixed_f * mixed.astype(jnp.float32), axis=-1))
    delta = jnp.transpose(delta, (1, 2, 0))[..., None]
    grad_scores_b = (attend_f * (grad_attend - delta) * scale).astype(jnp.bfloat16)
    grad_scores_f = grad_scores_b.astype(jnp.float32)
    grad_query = jnp.einsum('kgqs,skd->qkgd', grad_scores_f, keys_all.astype(jnp.float32))
    grad_key = jnp.einsum('kgqs,qkgd->skd', grad_scores_f, query_b.astype(jnp.float32))
    grad_value = jnp.einsum('kgqs,qkgd->skd', attend_b.astype(jnp.float32), grad_mixed_f)
    return (grad_query, grad_key, grad_value)

def layer_forward(state, qkv_w, out_w, gu_w, down_w, gain_pair, cosine, sine_tab, causal):
    row_count = state.shape[0]
    attn_cols = HEADS * HEAD_DIM
    kv_cols = KV_HEADS * HEAD_DIM
    normed, factor_one = norm_forward(state, gain_pair[0])
    normed_b = normed.astype(jnp.bfloat16)
    project = jnp.dot(normed_b, qkv_w, preferred_element_type=jnp.float32)
    query = rotate(project[:, :attn_cols].reshape(row_count, HEADS, HEAD_DIM), cosine, sine_tab)
    query_b = query.astype(jnp.bfloat16).reshape(row_count, KV_HEADS, HEADS // KV_HEADS, HEAD_DIM)
    key_part = project[:, attn_cols:attn_cols + kv_cols].reshape(row_count, KV_HEADS, HEAD_DIM)
    key_b = rotate(key_part, cosine, sine_tab).astype(jnp.bfloat16)
    value_b = project[:, attn_cols + kv_cols:].astype(jnp.bfloat16).reshape(row_count, KV_HEADS, HEAD_DIM)
    mixed, log_total = attend_forward(query_b, key_b, value_b, causal)
    middle = state + jnp.dot(mixed.reshape(row_count, attn_cols), out_w, preferred_element_type=jnp.float32)
    normed_two, factor_two = norm_forward(middle, gain_pair[1])
    normed_two_b = normed_two.astype(jnp.bfloat16)
    ff_width = down_w.shape[0]
    gate_up = jnp.dot(normed_two_b, gu_w.reshape(gu_w.shape[0], 2 * ff_width), preferred_element_type=jnp.float32)
    gate = gate_up[:, :ff_width]
    up_part = gate_up[:, ff_width:]
    inner_b = (jax.nn.silu(gate) * up_part).astype(jnp.bfloat16)
    result = middle + jnp.dot(inner_b, down_w, preferred_element_type=jnp.float32)
    record = (state, normed_b, factor_one, query_b, key_b, value_b, mixed, log_total, middle, normed_two_b, factor_two, gate, up_part, inner_b)
    return (result, record)

def layer_backward(grad_next, record, qkv_w, out_w, gu_w, down_w, gain_pair, cosine, sine_tab, causal):
    state, normed_b, factor_one, query_b, key_b, value_b, mixed, log_total, middle, normed_two_b, factor_two, gate, up_part, inner_b = record
    row_count = state.shape[0]
    ff_width = down_w.shape[0]
    grad_b = grad_next.astype(jnp.bfloat16)
    grad_down = jnp.dot(inner_b.T, grad_b, preferred_element_type=jnp.float32)
    grad_inner = jnp.dot(grad_b, down_w.T, preferred_element_type=jnp.float32)
    sigmoid_gate = jax.nn.sigmoid(gate)
    grad_gate = grad_inner * up_part * sigmoid_gate * (1.0 + gate * (1.0 - sigmoid_gate))
    grad_up = grad_inner * gate * sigmoid_gate
    grad_gu_b = jnp.concatenate([grad_gate, grad_up], axis=1).astype(jnp.bfloat16)
    gu_flat = gu_w.reshape(gu_w.shape[0], 2 * ff_width)
    grad_gu = jnp.dot(normed_two_b.T, grad_gu_b, preferred_element_type=jnp.float32).reshape(gu_w.shape)
    grad_normed_two = jnp.dot(grad_gu_b, gu_flat.T, preferred_element_type=jnp.float32)
    grad_middle_part, grad_gain_two = norm_backward(middle, factor_two, gain_pair[1], grad_normed_two)
    grad_middle = grad_next + grad_middle_part
    grad_middle_b = grad_middle.astype(jnp.bfloat16)
    grad_out = jnp.dot(mixed.reshape(row_count, -1).T, grad_middle_b, preferred_element_type=jnp.float32)
    grad_mixed = jnp.dot(grad_middle_b, out_w.T, preferred_element_type=jnp.float32).astype(jnp.bfloat16).reshape(mixed.shape)
    grad_query, grad_key, grad_value = attend_backward(query_b, key_b, value_b, mixed, log_total, grad_mixed, causal)
    grad_query = unrotate(grad_query.reshape(row_count, HEADS, HEAD_DIM), cosine, sine_tab).reshape(row_count, -1)
    grad_key = unrotate(grad_key, cosine, sine_tab).reshape(row_count, -1)
    grad_qkv_b = jnp.concatenate([grad_query, grad_key, grad_value.reshape(row_count, -1)], axis=1).astype(jnp.bfloat16)
    grad_qkv = jnp.dot(normed_b.T, grad_qkv_b, preferred_element_type=jnp.float32)
    grad_normed = jnp.dot(grad_qkv_b, qkv_w.T, preferred_element_type=jnp.float32)
    grad_state_part, grad_gain_one = norm_backward(state, factor_one, gain_pair[0], grad_normed)
    grads = (grad_qkv, grad_out, grad_gu, grad_down, jnp.stack([grad_gain_one, grad_gain_two]))
    return (grad_middle + grad_state_part, grads)

def reference(tokens, cotangent, w_qkv, w_out, w_gate_up, w_down, gains):
    sequences = tokens.reshape(N_DP, LENGTH, D)
    upstream = cotangent.reshape(N_DP, LENGTH, D)
    positions = jnp.arange(LENGTH).astype(jnp.int32)
    cosine, sine_tab = rotary_tables(positions, HEAD_DIM)
    causal = positions[None, :] <= positions[:, None]
    starting = (jnp.zeros(w_qkv.shape, jnp.float32), jnp.zeros(w_out.shape, jnp.float32), jnp.zeros(w_gate_up.shape, jnp.float32), jnp.zeros(w_down.shape, jnp.float32), jnp.zeros(gains.shape, jnp.float32))

    def one_sequence(totals, inputs):
        seq_tokens, seq_grad = inputs
        state = seq_tokens.astype(jnp.float32)
        records = []
        for layer_index in range(LAYERS):
            state, record = layer_forward(state, w_qkv[layer_index], w_out[layer_index], w_gate_up[layer_index], w_down[layer_index], gains[layer_index], cosine, sine_tab, causal)
            records.append(record)
        grad_state = seq_grad
        totals = list(totals)
        for layer_index in reversed(range(LAYERS)):
            grad_state, grads = layer_backward(grad_state, records[layer_index], w_qkv[layer_index], w_out[layer_index], w_gate_up[layer_index], w_down[layer_index], gains[layer_index], cosine, sine_tab, causal)
            for which in range(5):
                totals[which] = totals[which].at[layer_index].add(grads[which])
        return (tuple(totals), (state, grad_state))
    totals, outputs = lax.scan(one_sequence, starting, (sequences, upstream))
    out_act = outputs[0].reshape(TOKENS, D)
    grad_tokens = outputs[1].reshape(TOKENS, D)
    return (out_act, grad_tokens, totals[0], totals[1], totals[2], totals[3], totals[4])
```

```python
import functools

import jax
import jax.numpy as jnp
from jax import lax
from jax.experimental import pallas as pl
from jax.experimental.pallas import tpu as pltpu
from jax.sharding import PartitionSpec as P

HEADS = 16
KV_HEADS = 8
HEAD_DIM = 96
LAYERS = 2
RANKS = 4
GAIN_COLS = 128

NORM_EPS = 1e-05
ROPE_BASE = 100000.0
MASKED = -1e30
MESH = pl.DeviceIdType.MESH
BF16 = jnp.bfloat16
F32 = jnp.float32
VMEM_BYTES = 60 * 1024 * 1024


class Place:
    def __init__(self):
        self.dp = lax.axis_index("dp")
        self.ctx = lax.axis_index("ctx")
        self.core = lax.rem(self.dp, 2)
        self.x = lax.rem(lax.div(self.dp, 2), 2)
        self.a = lax.div(self.dp, 4)
        self.zh = lax.div(self.ctx, 2)
        self.zl = lax.rem(self.ctx, 2)
        self.rank = self.x * 2 + self.zl

    def rank_peers(self):
        dpx = self.dp + 2 - 4 * self.x
        ctz = self.ctx + 1 - 2 * self.zl
        x2, z2 = 1 - self.x, 1 - self.zl
        return (
            ((dpx, self.ctx), x2 * 2 + self.zl),
            ((self.dp, ctz), self.x * 2 + z2),
            ((dpx, ctz), x2 * 2 + z2),
        )

    def core_peer(self):
        return (self.dp + 1 - 2 * self.core, self.ctx)

    def zh_peer(self):
        return (self.dp, self.ctx + 2 - 4 * self.zh)

    def a_peer(self, k, count):
        ahead = lax.rem(self.a + k, count)
        behind = lax.rem(self.a + count - k, count)
        return (self.dp + (ahead - self.a) * 4, self.ctx), ahead, behind


def greet(devices):
    barrier = pltpu.get_barrier_semaphore()
    for device in devices:
        pl.semaphore_signal(barrier, inc=1, device_id=device, device_id_type=MESH)
    pl.semaphore_wait(barrier, len(devices))


def remote(src, dst, send, recv, device):
    return pltpu.make_async_remote_copy(
        src_ref=src, dst_ref=dst, send_sem=send, recv_sem=recv, device_id=device, device_id_type=MESH
    )


def products(x, w_ref, count, tile, transposed, use):
    @pl.loop(0, count // tile)
    def _(j):
        cols = pl.ds(pl.multiple_of(j * tile, tile), tile)
        if transposed:
            w, dims = w_ref[cols, :], (((1,), (1,)), ((), ()))
        else:
            w, dims = w_ref[:, cols], (((1,), (0,)), ((), ()))
        use(cols, lax.dot_general(x(), w, dims, preferred_element_type=F32))


def norm_rows(h, gain):
    factor = lax.rsqrt(jnp.mean(h * h, axis=-1, keepdims=True) + NORM_EPS)
    return (h * factor * gain).astype(BF16)


def norm_rows_back(h, gain, grad):
    factor = lax.rsqrt(jnp.mean(h * h, axis=-1, keepdims=True) + NORM_EPS)
    z = grad * gain
    inner = jnp.sum(z * h, axis=-1, keepdims=True)
    back = factor * z - h * (factor * factor * factor * inner / h.shape[-1])
    return back, jnp.sum(grad * h * factor, axis=0, keepdims=True)


class Exchange:
    def __init__(self, place, land, send, recv, base):
        self.place, self.land, self.send, self.recv, self.base = place, land, send, recv, base
        self.started = []

    def spread(self):
        me = self.place.rank
        for i, (device, _) in enumerate(self.place.rank_peers()):
            copy = remote(
                self.land.at[me], self.land.at[me],
                self.send.at[self.base + i], self.recv.at[self.base + i], device,
            )
            copy.start()
            self.started.append(copy)

    def push(self, i, out):
        copy = remote(
            out.at[i], self.land.at[i],
            self.send.at[self.base + i], self.recv.at[self.base + i],
            self.place.rank_peers()[i][0],
        )
        copy.start()
        self.started.append(copy)


def head_kernel(rows, h_ref, gain_ref, wq_hbm, proj_ref, ng_hbm, wq, land, send, recv, local):
    load = pltpu.make_async_copy(wq_hbm.at[:, pl.ds(0, wq.shape[1])], wq, local.at[0])
    load.start()
    place = Place()
    greet([d for d, _ in place.rank_peers()])
    land[place.rank] = norm_rows(h_ref[...], gain_ref[...])
    gather = Exchange(place, land, send, recv, 0)
    gather.spread()
    load.wait()
    project_blocks(place, rows, gather, wq, proj_ref)
    keep = pltpu.make_async_copy(land, ng_hbm, local.at[0])
    keep.start()
    for copy in gather.started:
        copy.wait_send()
    keep.wait()


def project_blocks(place, rows, gather, wq, proj_ref):
    land = gather.land
    count = wq.shape[1]

    def block(rank):
        span = pl.ds(pl.multiple_of(rank * rows, rows), rows)

        def use(cols, y):
            proj_ref[span, cols] = y

        products(lambda: land[rank], wq, count, 256, False, use)

    block(place.rank)
    for i, (_, rank) in enumerate(place.rank_peers()):
        gather.started[i].wait_recv()
        block(rank)


def body_kernel(rows, more, *refs):
    refs = list(refs)
    take = lambda n: [refs.pop(0) for _ in range(n)]
    o_ref, h_ref, gain_ref, wo_hbm, wgu_hbm, wd_hbm = take(6)
    if more:
        gain_next, wq_hbm = take(2)
    h1_ref, hn_ref, gate_ref, up_ref, u_ref, ng_hbm = take(6)
    if more:
        proj_ref, nn_hbm = take(2)
    wo, wgu, wd = take(3)
    if more:
        (wq,) = take(1)
    out_a, land_a, land_n, out_b, land_b = take(5)
    if more:
        (land_q,) = take(1)
    send, recv, local = take(3)

    loads = [
        pltpu.make_async_copy(wo_hbm, wo, local.at[0]),
        pltpu.make_async_copy(wgu_hbm, wgu, local.at[1]),
        pltpu.make_async_copy(wd_hbm, wd, local.at[2]),
    ]
    if more:
        loads.append(pltpu.make_async_copy(wq_hbm.at[:, pl.ds(0, wq.shape[1])], wq, local.at[3]))
    for load in loads:
        load.start()
    place = Place()
    peers = place.rank_peers()
    greet([d for d, _ in peers])
    width = h_ref.shape[1]
    hidden = wd.shape[0]
    loads[0].wait()

    total = Exchange(place, land_a, send, recv, 0)
    for i in (2, 0, 1):
        span = pl.ds(pl.multiple_of(peers[i][1] * rows, rows), rows)

        def use(cols, y, i=i):
            out_a[i, :, cols] = y.astype(BF16)

        products(lambda: o_ref[span, :], wo, width, 512, True, use)
        total.push(i, out_a)
    span = pl.ds(pl.multiple_of(place.rank * rows, rows), rows)

    def use_own(cols, y):
        h1_ref[:, cols] = h_ref[:, cols] + y

    products(lambda: o_ref[span, :], wo, width, 512, True, use_own)
    for copy in total.started:
        copy.wait_recv()
    h1 = h1_ref[...] + land_a[0].astype(F32) + land_a[1].astype(F32) + land_a[2].astype(F32)
    h1_ref[...] = h1
    land_n[place.rank] = norm_rows(h1, gain_ref[...])
    gather = Exchange(place, land_n, send, recv, 3)
    gather.spread()
    loads[1].wait()
    loads[2].wait()

    def inner_block(rank):
        span = pl.ds(pl.multiple_of(rank * rows, rows), rows)

        @pl.loop(0, hidden // 256)
        def _(j):
            cols = pl.ds(pl.multiple_of(j * 256, 256), 256)
            ups = pl.ds(pl.multiple_of(j * 256 + hidden, 256), 256)
            gate = jnp.dot(land_n[rank], wgu[:, cols], preferred_element_type=F32)
            up = jnp.dot(land_n[rank], wgu[:, ups], preferred_element_type=F32)
            gate_ref[span, cols] = gate
            up_ref[span, cols] = up
            u_ref[span, cols] = (gate / (1.0 + jnp.exp(-gate)) * up).astype(BF16)

        return span

    span = inner_block(place.rank)

    def use_down(cols, y):
        hn_ref[:, cols] = h1_ref[:, cols] + y

    products(lambda: u_ref[span, :], wd, width, 512, False, use_down)
    second = Exchange(place, land_b, send, recv, 6)
    for i, (_, rank) in enumerate(peers):
        gather.started[i].wait_recv()
        span = inner_block(rank)

        def use(cols, y, i=i):
            out_b[i, :, cols] = y.astype(BF16)

        products(lambda: u_ref[span, :], wd, width, 512, False, use)
        second.push(i, out_b)
    keep = pltpu.make_async_copy(land_n, ng_hbm, local.at[0])
    keep.start()
    for copy in second.started:
        copy.wait_recv()
    hn = hn_ref[...] + land_b[0].astype(F32) + land_b[1].astype(F32) + land_b[2].astype(F32)
    hn_ref[...] = hn
    every = [total, gather, second]
    if more:
        land_q[place.rank] = norm_rows(hn, gain_next[...])
        third = Exchange(place, land_q, send, recv, 9)
        third.spread()
        loads[3].wait()
        project_blocks(place, rows, third, wq, proj_ref)
        keep_next = pltpu.make_async_copy(land_q, nn_hbm, local.at[1])
        keep_next.start()
        keep_next.wait()
        every.append(third)
    keep.wait()
    for exchange in every:
        for copy in exchange.started:
            copy.wait_send()


def back_kernel(rows, first, last, *refs):
    refs = list(refs)
    take = lambda n: [refs.pop(0) for _ in range(n)]
    if first:
        (g_ref,) = take(1)
    else:
        dqkv_ref, wq_hbm, ghin_ref, hin_ref, gainin_ref = take(5)
    if not last:
        wd_hbm, wgu_hbm, wo_hbm, gate_ref, up_ref, h1_ref, gain_ref = take(7)
    if not first:
        gnew_ref, ggin_ref = take(2)
    if not last:
        gbg_hbm, dgu_ref, gh_ref, gg_ref, ghg_hbm, do_ref = take(6)
    if not first:
        wq, out_a, land_a = take(3)
    if not last:
        wd, wgu, wo, land_g, out_b, land_b, land_h = take(7)
    send, recv, local = take(3)

    loads = []
    if not first:
        loads.append(pltpu.make_async_copy(wq_hbm.at[:, pl.ds(0, wq.shape[1])], wq, local.at[0]))
    if not last:
        loads.append(pltpu.make_async_copy(wd_hbm, wd, local.at[1]))
        loads.append(pltpu.make_async_copy(wgu_hbm, wgu, local.at[2]))
        loads.append(pltpu.make_async_copy(wo_hbm, wo, local.at[3]))
    for load in loads:
        load.start()
    place = Place()
    peers = place.rank_peers()
    greet([d for d, _ in peers])
    own = pl.ds(pl.multiple_of(place.rank * rows, rows), rows)
    every = []
    if not first:
        loads.pop(0).wait()
        width = ghin_ref.shape[1]
        total = Exchange(place, land_a, send, recv, 0)
        every.append(total)
        for i in (2, 0, 1):
            span = pl.ds(pl.multiple_of(peers[i][1] * rows, rows), rows)

            def use(cols, y, i=i):
                out_a[i, :, cols] = y.astype(BF16)

            products(lambda: dqkv_ref[span, :], wq, width, 512, True, use)
            total.push(i, out_a)

        def use_own(cols, y):
            gnew_ref[:, cols] = y

        products(lambda: dqkv_ref[own, :], wq, width, 512, True, use_own)
        for copy in total.started:
            copy.wait_recv()
        dn = gnew_ref[...] + land_a[0].astype(F32) + land_a[1].astype(F32) + land_a[2].astype(F32)
        back, ggain = norm_rows_back(hin_ref[...], gainin_ref[...], dn)
        gnew_ref[...] = ghin_ref[...] + back
        ggin_ref[...] = ggain
        g_ref = gnew_ref
    if not last:
        width = g_ref.shape[1]
        hidden = wd.shape[0]
        land_g[place.rank] = g_ref[...].astype(BF16)
        gather = Exchange(place, land_g, send, recv, 3)
        gather.spread()
        every.append(gather)
        loads[0].wait()
        loads[1].wait()

        def inner_block(rank):
            span = pl.ds(pl.multiple_of(rank * rows, rows), rows)

            @pl.loop(0, hidden // 256)
            def _(j):
                cols = pl.ds(pl.multiple_of(j * 256, 256), 256)
                ups = pl.ds(pl.multiple_of(j * 256 + hidden, 256), 256)
                du = lax.dot_general(
                    land_g[rank], wd[cols, :], (((1,), (1,)), ((), ())), preferred_element_type=F32
                )
                gate, up = gate_ref[span, cols], up_ref[span, cols]
                sg = 1.0 / (1.0 + jnp.exp(-gate))
                dgu_ref[span, cols] = (du * up * sg * (1.0 + gate * (1.0 - sg))).astype(BF16)
                dgu_ref[span, ups] = (du * gate * sg).astype(BF16)

            return span

        span = inner_block(place.rank)

        def use_mid(cols, y):
            gh_ref[:, cols] = y

        products(lambda: dgu_ref[span, :], wgu, width, 512, True, use_mid)
        second = Exchange(place, land_b, send, recv, 6)
        every.append(second)
        for i, (_, rank) in enumerate(peers):
            gather.started[i].wait_recv()
            span = inner_block(rank)

            def use(cols, y, i=i):
                out_b[i, :, cols] = y.astype(BF16)

            products(lambda: dgu_ref[span, :], wgu, width, 512, True, use)
            second.push(i, out_b)
        keep = pltpu.make_async_copy(land_g, gbg_hbm, local.at[0])
        keep.start()
        for copy in second.started:
            copy.wait_recv()
        dn = gh_ref[...] + land_b[0].astype(F32) + land_b[1].astype(F32) + land_b[2].astype(F32)
        back, ggain = norm_rows_back(h1_ref[...], gain_ref[...], dn)
        gh = g_ref[...] + back
        gh_ref[...] = gh
        gg_ref[...] = ggain
        land_h[place.rank] = gh.astype(BF16)
        third = Exchange(place, land_h, send, recv, 9)
        third.spread()
        every.append(third)
        loads[2].wait()

        def out_block(rank):
            span = pl.ds(pl.multiple_of(rank * rows, rows), rows)

            def use(cols, y):
                do_ref[span, cols] = y.astype(BF16)

            products(lambda: land_h[rank], wo, wo.shape[1], wo.shape[1], False, use)

        out_block(place.rank)
        for i, (_, rank) in enumerate(peers):
            third.started[i].wait_recv()
            out_block(rank)
        keep_h = pltpu.make_async_copy(land_h, ghg_hbm, local.at[1])
        keep_h.start()
        keep_h.wait()
        keep.wait()
    for exchange in every:
        for copy in exchange.started:
            copy.wait_send()


def gather_kernel(count, n_cols, *refs):
    pieces, down = refs[:n_cols], refs[n_cols]
    outs, down_out = refs[n_cols + 1 : 2 * n_cols + 1], refs[2 * n_cols + 1]
    send, recv, local = refs[2 * n_cols + 2 :]
    place = Place()
    peers = place.rank_peers()
    others = [place.a_peer(k, count) for k in range(1, count)]
    a, x, core, zh, zl = place.a, place.x, place.core, place.zh, place.zl
    greet([d for d, _ in peers] + [place.zh_peer(), place.core_peer()] + [o[0] for o in others])
    sends = []

    def go(src, dst, i, slot, device):
        copy = remote(src, dst, send.at[i, slot], recv.at[i, slot], device)
        copy.start()
        sends.append(copy)
        return copy

    first, locals_ = [], []
    down_local = pltpu.make_async_copy(down, down_out.at[a, core, zh], local.at[n_cols])
    down_local.start()
    for i in range(n_cols):
        mine = outs[i].at[a, x, core, zh, zl]
        first.append([go(pieces[i].at[rank], mine, i, j, device) for j, (device, rank) in enumerate(peers)])
        own = pltpu.make_async_copy(pieces[i].at[place.rank], mine, local.at[i])
        own.start()
        locals_.append(own)
    down_local.wait()

    def block(i, aa, zz):
        if i == n_cols:
            return down_out.at[aa, core, zz]
        return outs[i].at[aa, :, core, zz, :]

    def column(i, aa):
        if i == n_cols:
            return down_out.at[aa, core]
        return outs[i].at[aa, :, core, :, :]

    base_y = 8
    base_c = base_y + 2 * (count - 1)
    across, near, far, cores = {}, {}, {}, {}
    order = [n_cols] + list(range(n_cols))
    for i in order:
        if i < n_cols:
            for copy in first[i]:
                copy.wait_recv()
            locals_[i].wait()
        across[i] = go(block(i, a, zh), block(i, a, zh), i, 3, place.zh_peer())
        near[i] = [
            go(block(i, a, zh), block(i, a, zh), i, base_y + k, others[k][0]) for k in range(count - 1)
        ]
    for i in order:
        across[i].wait_recv()
        far[i] = [
            go(block(i, a, 1 - zh), block(i, a, 1 - zh), i, base_y + count - 1 + k, others[k][0])
            for k in range(count - 1)
        ]
        cores[i] = [go(column(i, a), column(i, a), i, base_c, place.core_peer())]
    for i in order:
        for k in range(count - 1):
            near[i][k].wait_recv()
            far[i][k].wait_recv()
            behind = others[k][2]
            cores[i].append(
                go(column(i, behind), column(i, behind), i, base_c + 1 + k, place.core_peer())
            )
    for i in order:
        for copy in cores[i]:
            copy.wait_recv()
    for copy in sends:
        copy.wait_send()


def gather_layer(pieces, down, count):
    n = len(pieces)
    slots = 8 + 2 * (count - 1) + count
    outs = [
        jax.ShapeDtypeStruct((count, 2, 2, 2, 2) + p.shape[1:], BF16) for p in pieces
    ] + [jax.ShapeDtypeStruct((count, 2, 2) + down.shape, BF16)]
    any_space = pl.BlockSpec(memory_space=pl.ANY)
    full = pl.pallas_call(
        functools.partial(gather_kernel, count, n),
        out_shape=outs,
        in_specs=[any_space] * (n + 1),
        out_specs=[any_space] * (n + 1),
        scratch_shapes=[
            pltpu.SemaphoreType.DMA((n + 1, slots)),
            pltpu.SemaphoreType.DMA((n + 1, slots)),
            pltpu.SemaphoreType.DMA((n + 1,)),
        ],
        compiler_params=pltpu.CompilerParams(
            collective_id=1, has_side_effects=True, vmem_limit_bytes=VMEM_BYTES
        ),
        name="gather_layer",
    )(*pieces, down)
    return [f.reshape(-1, f.shape[-1]) for f in full]


def reduce_kernel(count, n_cols, *refs):
    n = n_cols + 1
    parts, outs = refs[:n], refs[n : 2 * n]
    rest = list(refs[2 * n :])
    held = [rest.pop(0) for _ in range(n)]
    from_core = [rest.pop(0) for _ in range(n)]
    from_a = [rest.pop(0) for _ in range(n)]
    from_zh = [rest.pop(0) for _ in range(n)]
    from_rank = [rest.pop(0) for _ in range(n_cols)]
    send, recv, local = rest
    place = Place()
    peers = place.rank_peers()
    others = [place.a_peer(k, count) for k in range(1, count)]
    a, core, zh = place.a, place.core, place.zh
    sends = []

    def go(src, dst, i, slot, device):
        copy = remote(src, dst, send.at[i, slot], recv.at[i, slot], device)
        copy.start()
        sends.append(copy)
        return copy

    def half(i, c):
        if i == n_cols:
            return parts[i].at[:, c]
        return parts[i].at[:, :, c]

    order = [n_cols] + list(range(n_cols))
    loads = {}
    for i in order:
        loads[i] = pltpu.make_async_copy(half(i, core), held[i], local.at[i])
        loads[i].start()
    greet([d for d, _ in peers] + [place.zh_peer(), place.core_peer()] + [o[0] for o in others])
    by_core, by_a, by_zh, by_rank = {}, {}, {}, {}
    for i in order:
        by_core[i] = go(half(i, 1 - core), from_core[i], i, 0, place.core_peer())

    for i in order:
        loads[i].wait()
        by_core[i].wait_recv()
        h, s = held[i], from_core[i]
        for aa in range(count):
            add_into(h.at[aa], s.at[aa])
        by_a[i] = []
        for k in range(count - 1):
            device, ahead, _ = others[k]
            by_a[i].append(go(h.at[ahead], from_a[i].at[k], i, 1 + k, device))
    for i in order:
        h = held[i].at[a]
        for k in range(count - 1):
            by_a[i][k].wait_recv()
            add_into(h, from_a[i].at[k])
        if i == n_cols:
            by_zh[i] = go(h.at[1 - zh], from_zh[i], i, count, place.zh_peer())
        else:
            by_zh[i] = go(h.at[:, 1 - zh], from_zh[i], i, count, place.zh_peer())
    stores = []
    for i in order:
        by_zh[i].wait_recv()
        if i == n_cols:
            outs[i][...] = held[i][a, zh].astype(F32) + from_zh[i][...].astype(F32)
            continue
        for xx in range(2):
            for ll in range(2):
                h = held[i]
                h[a, xx, zh, ll] = (
                    h[a, xx, zh, ll].astype(F32) + from_zh[i][xx, ll].astype(F32)
                ).astype(BF16)
        by_rank[i] = []
        for j, (device, rank) in enumerate(peers):
            xx, ll = lax.div(rank, 2), lax.rem(rank, 2)
            by_rank[i].append(
                go(held[i].at[a, xx, zh, ll], from_rank[i].at[j], i, count + 1 + j, device)
            )
    for i in range(n_cols):
        outs[i][place.rank] = held[i][a, place.x, zh, place.zl].astype(F32)
        for j, (_, rank) in enumerate(peers):
            by_rank[i][j].wait_recv()
            outs[i][rank] = from_rank[i][j].astype(F32)
    for copy in sends:
        copy.wait_send()


def add_into(target, source):
    lead = target.shape[:-2]
    total = 1
    for size in lead:
        total *= size

    @pl.loop(0, total)
    def _(j):
        index, left = [], j
        for size in reversed(lead):
            index.append(lax.rem(left, size))
            left = lax.div(left, size)
        index = tuple(reversed(index))
        target[index] = (target[index].astype(F32) + source[index].astype(F32)).astype(BF16)


def reduce_layer(parts, down, count):
    n_cols = len(parts)
    shaped = [p.reshape(count, 2, 2, 2, 2, -1, p.shape[-1]) for p in parts]
    shaped.append(down.reshape(count, 2, 2, -1, down.shape[-1]))
    n = n_cols + 1
    tails = [s.shape[-2:] for s in shaped]
    held = [(count, 2, 2, 2) + t for t in tails[:-1]] + [(count, 2) + tails[-1]]
    from_a = [(max(count - 1, 1), 2, 2, 2) + t for t in tails[:-1]] + [(max(count - 1, 1), 2) + tails[-1]]
    from_zh = [(2, 2) + t for t in tails[:-1]] + [tails[-1]]
    from_rank = [(3,) + t for t in tails[:-1]]
    vmem = pl.BlockSpec(memory_space=pltpu.VMEM)
    scratch = [pltpu.VMEM(s, BF16) for s in held + held + from_a + from_zh + from_rank]
    slots = count + 4
    return pl.pallas_call(
        functools.partial(reduce_kernel, count, n_cols),
        out_shape=[jax.ShapeDtypeStruct((RANKS,) + t, F32) for t in tails[:-1]]
        + [jax.ShapeDtypeStruct(tails[-1], F32)],
        in_specs=[pl.BlockSpec(memory_space=pl.ANY)] * n,
        out_specs=[vmem] * n,
        scratch_shapes=scratch
        + [
            pltpu.SemaphoreType.DMA((n, slots)),
            pltpu.SemaphoreType.DMA((n, slots)),
            pltpu.SemaphoreType.DMA((n,)),
        ],
        compiler_params=pltpu.CompilerParams(
            collective_id=2, has_side_effects=True, vmem_limit_bytes=VMEM_BYTES
        ),
        name="reduce_layer",
    )(*shaped)


def pack_weights(w_qkv, w_out, w_gate_up, gains, count, layer):
    rows = w_qkv.shape[1]
    attn_cols = HEADS * HEAD_DIM
    kv_cols = KV_HEADS * HEAD_DIM
    qkv = w_qkv[layer]
    q = qkv[:, :attn_cols].reshape(rows, RANKS, -1)
    k = qkv[:, attn_cols : attn_cols + kv_cols].reshape(rows, RANKS, -1)
    v = qkv[:, attn_cols + kv_cols :].reshape(rows, RANKS, -1)
    scales = jnp.pad(gains[layer].T, ((0, 0), (0, GAIN_COLS - 2)))
    scales = jnp.broadcast_to(scales[:, None], (rows, RANKS, GAIN_COLS))
    head = jnp.concatenate([q, k, v, scales], axis=2).transpose(1, 0, 2)
    out = w_out[layer].T.reshape(rows, RANKS, -1).transpose(1, 0, 2)
    gu = w_gate_up[layer].reshape(rows, 2, count, 2, 2, 2, 2, -1)
    gu = gu.transpose(3, 6, 0, 1, 2, 4, 5, 7).reshape(RANKS, rows, -1)
    return head, out, gu


def unpack_grads(head, out, gu, count):
    rows = head.shape[1]
    q_cols = HEADS * HEAD_DIM // RANKS
    kv_cols = KV_HEADS * HEAD_DIM // RANKS
    wide = lambda part: part.transpose(1, 0, 2).reshape(rows, -1)
    qkv = jnp.concatenate(
        [
            wide(head[:, :, :q_cols]),
            wide(head[:, :, q_cols : q_cols + kv_cols]),
            wide(head[:, :, q_cols + kv_cols : q_cols + 2 * kv_cols]),
        ],
        axis=1,
    )
    gains = jnp.sum(head[:, :, q_cols + 2 * kv_cols :][:, :, :2], axis=0).T
    w_out = wide(out).T
    w_gu = gu.reshape(2, 2, rows, 2, count, 2, 2, -1).transpose(2, 3, 4, 0, 5, 6, 1, 7)
    return qkv, w_out, w_gu.reshape(rows, 2, -1), gains


def rotary_tables(positions, head_size):
    half_size = head_size // 2
    freq_index = jnp.arange(half_size).astype(F32)
    inverse = jnp.exp(freq_index * (-2.0 * jnp.log(ROPE_BASE) / head_size))
    angles = positions.astype(F32)[:, None] * inverse[None, :]
    return (jnp.cos(angles), jnp.sin(angles))


def rotate(values, cosine, sine_tab):
    half_size = values.shape[-1] // 2
    first, second = values[..., :half_size], values[..., half_size:]
    c, s = cosine[:, None, :], sine_tab[:, None, :]
    return jnp.concatenate([first * c - second * s, second * c + first * s], axis=-1)


def unrotate(grads, cosine, sine_tab):
    return rotate(grads, cosine, -sine_tab)


def attend(proj, cosine, sine_tab, causal):
    length = proj.shape[0]
    kv = KV_HEADS // RANKS
    groups = HEADS // KV_HEADS
    q_cols = kv * groups * HEAD_DIM
    kv_cols = kv * HEAD_DIM
    query = rotate(proj[:, :q_cols].reshape(length, kv * groups, HEAD_DIM), cosine, sine_tab)
    query = query.astype(BF16).reshape(length, kv, groups, HEAD_DIM)
    key = rotate(proj[:, q_cols : q_cols + kv_cols].reshape(length, kv, HEAD_DIM), cosine, sine_tab)
    key = key.astype(BF16)
    value = proj[:, q_cols + kv_cols :].astype(BF16).reshape(length, kv, HEAD_DIM)
    scale = HEAD_DIM ** (-0.5)
    scores = jnp.einsum("qkgd,skd->kgqs", query, key, preferred_element_type=F32) * scale
    scores = jnp.where(causal[None, None], scores, MASKED)
    highest = jnp.max(scores, axis=-1, keepdims=True)
    lse = highest + jnp.log(jnp.sum(jnp.exp(scores - highest), axis=-1, keepdims=True))
    weights = jnp.exp(scores - lse).astype(BF16)
    mixed = jnp.einsum("kgqs,skd->qkgd", weights, value, preferred_element_type=F32).astype(BF16)
    return mixed.reshape(length, q_cols), (query, key, value, lse)


def attend_back(saved, mixed, grad_mixed, cosine, sine_tab, causal):
    query, key, value, lse = saved
    length = query.shape[0]
    grad_mixed = grad_mixed.reshape(query.shape)
    mixed = mixed.reshape(query.shape)
    scale = HEAD_DIM ** (-0.5)
    scores = jnp.einsum("qkgd,skd->kgqs", query, key, preferred_element_type=F32) * scale
    scores = jnp.where(causal[None, None], scores, MASKED)
    weights = jnp.exp(scores - lse)
    grad_weights = jnp.einsum("qkgd,skd->kgqs", grad_mixed, value, preferred_element_type=F32)
    delta = jnp.sum(grad_mixed.astype(F32) * mixed.astype(F32), axis=-1)
    delta = jnp.transpose(delta, (1, 2, 0))[..., None]
    grad_scores = (weights * (grad_weights - delta) * scale).astype(BF16)
    grad_query = jnp.einsum("kgqs,skd->qkgd", grad_scores, key, preferred_element_type=F32)
    grad_key = jnp.einsum("kgqs,qkgd->skd", grad_scores, query, preferred_element_type=F32)
    grad_value = jnp.einsum(
        "kgqs,qkgd->skd", weights.astype(BF16), grad_mixed, preferred_element_type=F32
    )
    grad_query = unrotate(grad_query.reshape(length, -1, HEAD_DIM), cosine, sine_tab)
    grad_key = unrotate(grad_key, cosine, sine_tab)
    return jnp.concatenate(
        [g.reshape(length, -1) for g in (grad_query, grad_key, grad_value)], axis=1
    ).astype(BF16)


VM = pl.BlockSpec(memory_space=pltpu.VMEM)
AN = pl.BlockSpec(memory_space=pl.ANY)


def params(collective_id):
    return pltpu.CompilerParams(
        collective_id=collective_id, has_side_effects=True, vmem_limit_bytes=VMEM_BYTES
    )


def sems(n):
    return [
        pltpu.SemaphoreType.DMA((n,)),
        pltpu.SemaphoreType.DMA((n,)),
        pltpu.SemaphoreType.DMA((4,)),
    ]


def call_head(h, gain, wq):
    rows, width = h.shape
    cols = wq.shape[1] - GAIN_COLS
    return pl.pallas_call(
        functools.partial(head_kernel, rows),
        out_shape=[
            jax.ShapeDtypeStruct((RANKS * rows, cols), F32),
            jax.ShapeDtypeStruct((RANKS, rows, width), BF16),
        ],
        in_specs=[VM, VM, AN],
        out_specs=[VM, AN],
        scratch_shapes=[pltpu.VMEM((width, cols), BF16), pltpu.VMEM((RANKS, rows, width), BF16)] + sems(3),
        compiler_params=params(3),
        name="head",
    )(h, gain, wq)


def call_body(o, h, gain, wo, wgu, wd, gain_next=None, wq=None):
    rows, width = h.shape
    tall = RANKS * rows
    hidden = wd.shape[0]
    more = wq is not None
    cols = wq.shape[1] - GAIN_COLS if more else 0
    three = pltpu.VMEM((3, rows, width), BF16)
    four = pltpu.VMEM((RANKS, rows, width), BF16)
    return pl.pallas_call(
        functools.partial(body_kernel, rows, more),
        out_shape=[
            jax.ShapeDtypeStruct((rows, width), F32),
            jax.ShapeDtypeStruct((rows, width), F32),
            jax.ShapeDtypeStruct((tall, hidden), F32),
            jax.ShapeDtypeStruct((tall, hidden), F32),
            jax.ShapeDtypeStruct((tall, hidden), BF16),
            jax.ShapeDtypeStruct((RANKS, rows, width), BF16),
        ]
        + (
            [
                jax.ShapeDtypeStruct((tall, cols), F32),
                jax.ShapeDtypeStruct((RANKS, rows, width), BF16),
            ]
            if more
            else []
        ),
        in_specs=[VM, VM, VM, AN, AN, AN] + ([VM, AN] if more else []),
        out_specs=[VM] * 5 + [AN] + ([VM, AN] if more else []),
        scratch_shapes=[
            pltpu.VMEM(wo.shape, BF16),
            pltpu.VMEM(wgu.shape, BF16),
            pltpu.VMEM(wd.shape, BF16),
        ]
        + ([pltpu.VMEM((width, cols), BF16)] if more else [])
        + [three, three, four, three, three]
        + ([four] if more else [])
        + sems(12),
        compiler_params=params(4 if more else 5),
        name="body_more" if more else "body",
    )(o, h, gain, wo, wgu, wd, *((gain_next, wq) if more else ()))


def call_back(start, rest):
    first, last = len(start) == 1, rest is None
    rows, width = start[0].shape if first else start[2].shape
    tall = RANKS * rows
    outs, out_specs, scratch = [], [], []
    three = pltpu.VMEM((3, rows, width), BF16)
    four = pltpu.VMEM((RANKS, rows, width), BF16)
    in_specs = [VM] if first else [VM, AN, VM, VM, VM]
    if not first:
        outs += [jax.ShapeDtypeStruct((rows, width), F32), jax.ShapeDtypeStruct((1, width), F32)]
        out_specs += [VM, VM]
        scratch += [pltpu.VMEM((width, start[0].shape[1]), BF16), three, three]
    if not last:
        wd, wgu, wo = rest[:3]
        in_specs += [AN, AN, AN, VM, VM, VM, VM]
        outs += [
            jax.ShapeDtypeStruct((RANKS, rows, width), BF16),
            jax.ShapeDtypeStruct((tall, wgu.shape[1]), BF16),
            jax.ShapeDtypeStruct((rows, width), F32),
            jax.ShapeDtypeStruct((1, width), F32),
            jax.ShapeDtypeStruct((RANKS, rows, width), BF16),
            jax.ShapeDtypeStruct((tall, wo.shape[1]), BF16),
        ]
        out_specs += [AN, VM, VM, VM, AN, VM]
        scratch += [pltpu.VMEM(w.shape, BF16) for w in (wd, wgu, wo)] + [four, three, three, four]
    return pl.pallas_call(
        functools.partial(back_kernel, rows, first, last),
        out_shape=outs,
        in_specs=in_specs,
        out_specs=out_specs,
        scratch_shapes=scratch + sems(12),
        compiler_params=params(6 if first else (7 if not last else 8)),
        name="back_first" if first else ("back_last" if last else "back_mid"),
    )(*start, *(rest or ()))


def dot_t(a, b):
    return lax.dot_general(a, b, (((0,), (0,)), ((), ())), preferred_element_type=F32).astype(BF16)


def swap_pairs(dp_size, ctx_size):
    pairs = []
    for dp in range(dp_size):
        for ctx in range(ctx_size):
            a, x, core = dp // 4, dp // 2 % 2, dp % 2
            zh, zl = ctx // 2, ctx % 2
            pairs.append((dp * ctx_size + ctx, (a * 4 + zh * 2 + core) * ctx_size + x * 2 + zl))
    return pairs


def shards(dp_size, ctx_size, tokens, cotangent, w_qkv, w_out, w_gate_up, w_down, gains):
    count = dp_size // 4
    pairs = swap_pairs(dp_size, ctx_size)
    swap = lambda value: lax.ppermute(value, ("dp", "ctx"), pairs)
    rows, width = tokens.shape
    length = RANKS * rows
    positions = jnp.arange(length, dtype=jnp.int32)
    cosine, sine_tab = rotary_tables(positions, HEAD_DIM)
    causal = positions[None, :] <= positions[:, None]

    full, gain_rows = [], []
    for layer in range(LAYERS):
        head, out, gu = pack_weights(w_qkv, w_out, w_gate_up, gains, count, layer)
        wq, wo, wgu, wd = gather_layer([head, out, gu], w_down[layer], count)
        full.append((wq, wo, wgu, wd))
        gain_rows.append(wq[:, -GAIN_COLS:][:, :2].astype(F32).T)
    h = swap(tokens).astype(F32)
    g = swap(cotangent.astype(BF16)).astype(F32)

    gain = lambda layer, which: gain_rows[layer][which : which + 1]
    records = []
    proj, n1 = call_head(h, gain(0, 0), full[0][0])
    for layer in range(LAYERS):
        mixed, saved = attend(proj, cosine, sine_tab, causal)
        wq, wo, wgu, wd = full[layer]
        more = (gain(layer + 1, 0), full[layer + 1][0]) if layer + 1 < LAYERS else ()
        h1, h_next, gate, up, u, n2, *ahead = call_body(mixed, h, gain(layer, 1), wo, wgu, wd, *more)
        records.append((h, n1, saved, mixed, h1, n2, gate, up, u))
        h = h_next
        if more:
            proj, n1 = ahead

    start = (g,)
    grads = [None] * LAYERS
    late = None
    tall = lambda value: value.reshape(length, width)
    for layer in reversed(range(LAYERS)):
        h_in, n1, saved, mixed, h1, n2, gate, up, u = records[layer]
        wq, wo, wgu, wd = full[layer]
        got = call_back(start, (wd, wgu, wo, gate, up, h1, gain(layer, 1)))
        if layer + 1 < LAYERS:
            _, gg_in, *got = got
            late(gg_in)
        gbg, dgu, gh, gg2, ghg, do = got
        g_down = dot_t(u, tall(gbg))
        g_gu = dot_t(tall(n2), dgu)
        g_out = dot_t(tall(ghg), mixed)
        dqkv = attend_back(saved, mixed, do, cosine, sine_tab, causal)
        g_qkv = dot_t(tall(n1), dqkv)

        def late(gg1, layer=layer, g_qkv=g_qkv, g_out=g_out, g_gu=g_gu, g_down=g_down, gg2=gg2):
            scales = jnp.concatenate([gg1, gg2], axis=0).astype(BF16).T
            scales = jnp.pad(scales, ((0, 0), (0, GAIN_COLS - 2)))
            head = jnp.concatenate([g_qkv, scales], axis=1)
            r_head, r_out, r_gu, r_down = reduce_layer([head, g_out, g_gu], g_down, count)
            grads[layer] = unpack_grads(r_head, r_out, r_gu, count) + (r_down,)

        start = (dqkv, wq, gh, h_in, gain(layer, 0))
    g, gg_in = call_back(start, None)
    late(gg_in)
    stacked = [jnp.stack([grads[layer][which] for layer in range(LAYERS)]) for which in range(5)]
    s_qkv, s_out, s_gu, s_gains, s_down = stacked
    return (swap(h), swap(g), s_qkv, s_out, s_gu, s_down, s_gains)


def solution(mesh):
    both = ("dp", "ctx")
    return jax.shard_map(
        functools.partial(shards, mesh.shape["dp"], mesh.shape["ctx"]),
        mesh=mesh,
        in_specs=(
            P(both, None),
            P(both, None),
            P(None, both, None),
            P(None, None, both),
            P(None, both, None, None),
            P(None, both, None),
            P(None, None, both),
        ),
        out_specs=(
            P(both, None),
            P(both, None),
            P(None, both, None),
            P(None, None, both),
            P(None, both, None, None),
            P(None, both, None),
            P(None, None, both),
        ),
        check_vma=False,
    )
```

```python
import functools

import jax
import jax.numpy as jnp
from jax import lax
from jax.experimental import pallas as pl
from jax.experimental.pallas import tpu as pltpu
from jax.sharding import PartitionSpec as P

HEADS = 16
KV_HEADS = 8
HEAD_DIM = 96
LAYERS = 2
RANKS = 4
GAIN_COLS = 128

NORM_EPS = 1e-05
ROPE_BASE = 100000.0
MASKED = -1e30
MESH = pl.DeviceIdType.MESH
BF16 = jnp.bfloat16
F32 = jnp.float32
VMEM_BYTES = 62 * 1024 * 1024


class Place:
    def __init__(self, count):
        self.count = count
        self.dp = lax.axis_index("dp")
        self.ctx = lax.axis_index("ctx")
        self.core = lax.rem(self.dp, 2)
        self.x = lax.rem(lax.div(self.dp, 2), 2)
        self.a = lax.div(self.dp, 4)
        self.zh = lax.div(self.ctx, 2)
        self.zl = lax.rem(self.ctx, 2)
        self.rank = self.x * 2 + self.zl
        dpx = self.dp + 2 - 4 * self.x
        ctz = self.ctx + 1 - 2 * self.zl
        x2, z2 = 1 - self.x, 1 - self.zl
        self.peers = (
            ((dpx, self.ctx), x2 * 2 + self.zl),
            ((self.dp, ctz), self.x * 2 + z2),
            ((dpx, ctz), x2 * 2 + z2),
        )
        self.core_peer = (self.dp + 1 - 2 * self.core, self.ctx)
        self.zh_peer = (self.dp, self.ctx + 2 - 4 * self.zh)
        self.others = []
        for k in range(1, count):
            ahead = lax.rem(self.a + k, count)
            behind = lax.rem(self.a + count - k, count)
            self.others.append(((self.dp + (ahead - self.a) * 4, self.ctx), ahead, behind))
        self.moves = self.x != self.zh
        self.swap_peer = (self.dp + (self.zh - self.x) * 2, self.ctx + (self.x - self.zh) * 2)

    def greet(self, weights, swap):
        devices = [d for d, _ in self.peers]
        if weights:
            devices += [self.core_peer, self.zh_peer] + [o[0] for o in self.others]
        barrier = pltpu.get_barrier_semaphore()
        for device in devices:
            pl.semaphore_signal(barrier, inc=1, device_id=device, device_id_type=MESH)
        if swap:

            @pl.when(self.moves)
            def _():
                pl.semaphore_signal(barrier, inc=1, device_id=self.swap_peer, device_id_type=MESH)

        expected = len(devices)
        if swap:
            expected = expected + self.x + self.zh - 2 * self.x * self.zh
        pl.semaphore_wait(barrier, expected)


class Net:
    def __init__(self, place, send, recv, local):
        self.place, self.send, self.recv, self.local = place, send, recv, local
        self.n, self.m = 0, 0
        self.sends = []

    def remote(self, src, dst, device):
        copy = self.prepare(src, dst, device)
        copy.start()
        self.sends.append(copy)
        return copy

    def prepare(self, src, dst, device):
        i = self.n
        self.n += 1
        return pltpu.make_async_remote_copy(
            src_ref=src, dst_ref=dst, send_sem=self.send.at[i], recv_sem=self.recv.at[i],
            device_id=device, device_id_type=MESH,
        )

    def here(self, src, dst):
        i = self.m
        self.m += 1
        copy = pltpu.make_async_copy(src, dst, self.local.at[i])
        copy.start()
        return copy

    def finish(self):
        for copy in self.sends:
            copy.wait_send()


REMOTE_SEMS, LOCAL_SEMS = 128, 32


def sems(count=2):
    n = REMOTE_SEMS * max(1, count // 2)
    return [
        pltpu.SemaphoreType.DMA((n,)),
        pltpu.SemaphoreType.DMA((n,)),
        pltpu.SemaphoreType.DMA((LOCAL_SEMS,)),
    ]


class Swap:
    def __init__(self, net, src, dst):
        self.net, self.src, self.dst = net, src, dst

    def start(self):
        net, place = self.net, self.net.place
        self.copy = net.prepare(self.src, self.dst, place.swap_peer)
        self.stay = pltpu.make_async_copy(self.src, self.dst, net.local.at[net.m])
        net.m += 1

        @pl.when(place.moves)
        def _():
            self.copy.start()

        @pl.when(jnp.logical_not(place.moves))
        def _():
            self.stay.start()

    def wait(self):
        @pl.when(self.net.place.moves)
        def _():
            self.copy.wait_recv()
            self.copy.wait_send()

        @pl.when(jnp.logical_not(self.net.place.moves))
        def _():
            self.stay.wait()


class Share:
    def __init__(self, net, piece, block):
        self.net, self.piece, self.block = net, piece, block

    def start(self):
        net, place = self.net, self.net.place
        mine = self.block.at[place.x, place.zl]
        self.copies = [net.remote(self.piece.at[rank], mine, device) for device, rank in place.peers]
        self.own = net.here(self.piece.at[place.rank], mine)

    def wait(self):
        for copy in self.copies:
            copy.wait_recv()
        self.own.wait()


class Gather:
    def __init__(self, net, block, full, ranks=True):
        self.net, self.block, self.full, self.ranks = net, block, full, ranks

    def slot(self, a, core, zh):
        if self.ranks:
            return self.full.at[a, :, core, zh, :]
        return self.full.at[a, core, zh]

    def column(self, a, core):
        if self.ranks:
            return self.full.at[a, :, core, :, :]
        return self.full.at[a, core]

    def begin(self):
        net, p = self.net, self.net.place
        mine = self.slot(p.a, p.core, p.zh)
        self.across = net.remote(self.block, mine, p.zh_peer)
        self.near = [net.remote(self.block, mine, o[0]) for o in p.others]
        self.cores = [net.remote(self.block, mine, p.core_peer)]
        self.own = net.here(self.block, mine)

    def middle(self):
        net, p = self.net, self.net.place
        self.across.wait_recv()
        got = self.slot(p.a, p.core, 1 - p.zh)
        self.far = [net.remote(got, got, o[0]) for o in p.others]
        self.cores.append(net.remote(got, got, p.core_peer))

    def final(self):
        net, p = self.net, self.net.place
        for k, other in enumerate(p.others):
            self.near[k].wait_recv()
            self.far[k].wait_recv()
            got = self.column(other[2], p.core)
            self.cores.append(net.remote(got, got, p.core_peer))

    def done(self):
        self.own.wait()
        for copy in self.cores:
            copy.wait_recv()


class Reduce:
    def __init__(self, net, part, out, held, from_core, from_a, from_zh, from_rank, ranks=True, added=False):
        self.net, self.part, self.out = net, part, out
        self.held, self.from_core, self.from_a = held, from_core, from_a
        self.from_zh, self.from_rank = from_zh, from_rank
        self.ranks, self.added = ranks, added

    def half(self, core):
        return self.part.at[:, :, core] if self.ranks else self.part.at[:, core]

    def begin(self):
        net, p = self.net, self.net.place
        self.load = net.here(self.half(p.core), self.held)
        self.by_core = net.remote(self.half(1 - p.core), self.from_core, p.core_peer)

    def along_a(self):
        net, p = self.net, self.net.place
        self.load.wait()
        self.by_core.wait_recv()
        add_into(self.held, self.from_core)
        self.by_a = [
            net.remote(self.held.at[other[1]], self.from_a.at[k], other[0])
            for k, other in enumerate(p.others)
        ]

    def along_zh(self):
        net, p = self.net, self.net.place
        mine = self.held.at[p.a]
        for k, copy in enumerate(self.by_a):
            copy.wait_recv()
            add_into(mine, self.from_a.at[k])
        there = mine.at[:, 1 - p.zh] if self.ranks else mine.at[1 - p.zh]
        self.by_zh = net.remote(there, self.from_zh, p.zh_peer)

    def among_ranks(self):
        net, p = self.net, self.net.place
        self.by_zh.wait_recv()
        if not self.ranks:
            self.out[...] = self.held[p.a, p.zh].astype(F32) + self.from_zh[...].astype(F32)
            return
        for x in range(2):
            for zl in range(2):
                add_into(self.held.at[p.a, x, p.zh, zl], self.from_zh.at[x, zl])
        self.by_rank = []
        for device, rank in p.peers:
            rank_x, rank_zl = lax.div(rank, 2), lax.rem(rank, 2)
            self.by_rank.append(
                net.remote(
                    self.held.at[p.a, rank_x, p.zh, rank_zl], self.from_rank.at[len(self.by_rank)], device
                )
            )

    def done(self):
        if not self.ranks:
            return
        p = self.net.place
        own = self.held[p.a, p.x, p.zh, p.zl].astype(F32)
        for copy in self.by_rank:
            copy.wait_recv()
        if self.added:
            for j in range(3):
                own = own + self.from_rank[j].astype(F32)
            self.out[...] = own
            return
        self.out[p.rank] = own
        for j, (_, rank) in enumerate(p.peers):
            self.out[rank] = self.from_rank[j].astype(F32)

    @staticmethod
    def scratch(shape, ranks=True):
        tail = shape[-2:]
        count = shape[0]
        inner = ((2, 2, 2) if ranks else (2,)) + tail
        fewer = ((2, 2) if ranks else ()) + tail
        shapes = [(count,) + inner, (count,) + inner, (max(count - 1, 1),) + inner, fewer]
        if ranks:
            shapes.append((3,) + tail)
        return [pltpu.VMEM(s, BF16) for s in shapes]


def add_into(target, source):
    lead = target.shape[:-2]
    total = 1
    for size in lead:
        total *= size
    if total == 1 and not lead:
        target[...] = (target[...].astype(F32) + source[...].astype(F32)).astype(BF16)
        return

    @pl.loop(0, total)
    def _(j):
        index, left = [], j
        for size in reversed(lead):
            index.append(lax.rem(left, size))
            left = lax.div(left, size)
        index = tuple(reversed(index))
        target[index] = (target[index].astype(F32) + source[index].astype(F32)).astype(BF16)


def spread(net, land):
    mine = land.at[net.place.rank]
    return [net.remote(mine, mine, device) for device, _ in net.place.peers]


def push(net, out, land, i):
    return net.remote(out.at[i], land.at[i], net.place.peers[i][0])


def products(x, w_ref, count, tile, transposed, use):
    @pl.loop(0, count // tile)
    def _(j):
        cols = pl.ds(pl.multiple_of(j * tile, tile), tile)
        if transposed:
            w, dims = w_ref[cols, :], (((1,), (1,)), ((), ()))
        else:
            w, dims = w_ref[:, cols], (((1,), (0,)), ((), ()))
        use(cols, lax.dot_general(x(), w, dims, preferred_element_type=F32))


def norm_rows(h, gain):
    factor = lax.rsqrt(jnp.mean(h * h, axis=-1, keepdims=True) + NORM_EPS)
    return (h * factor * gain).astype(BF16)


def norm_rows_back(h, gain, grad):
    factor = lax.rsqrt(jnp.mean(h * h, axis=-1, keepdims=True) + NORM_EPS)
    z = grad * gain
    inner = jnp.sum(z * h, axis=-1, keepdims=True)
    back = factor * z - h * (factor * factor * factor * inner / h.shape[-1])
    return back, jnp.sum(grad * h * factor, axis=0, keepdims=True)


def landed_sum(first, land):
    return first + land[0].astype(F32) + land[1].astype(F32) + land[2].astype(F32)


def rows_of(rank, rows):
    return pl.ds(pl.multiple_of(rank * rows, rows), rows)


class Refs:
    def __init__(self, refs):
        self.refs = list(refs)

    def take(self, n):
        got, self.refs = self.refs[:n], self.refs[n:]
        return got


class Ticks:
    def __init__(self, plan):
        self.plan = list(plan)

    def __call__(self):
        if self.plan:
            for step in self.plan.pop(0):
                step()

    def rest(self):
        while self.plan:
            self()


def start_kernel(count, n, ahead, *refs):
    refs = Refs(refs)
    (tokens,) = refs.take(1)
    pieces, later = refs.take(n), refs.take(ahead)
    (all_tokens,) = refs.take(1)
    full, blocks_later = refs.take(n), refs.take(ahead)
    (land,) = refs.take(1)
    blocks = refs.take(n)
    send, recv, local = refs.take(3)
    place = Place(count)
    net = Net(place, send, recv, local)
    shares = [Share(net, pieces[i], blocks[i]) for i in range(n)]
    gathers = [Gather(net, blocks[i], full[i]) for i in range(n)]
    shares_later = [Share(net, later[i], blocks_later[i]) for i in range(ahead)]
    swap = Swap(net, tokens, land.at[place.zh * 2 + place.zl])
    place.greet(True, True)
    shares[0].start()
    swap.start()
    shares[1].start()
    shares[0].wait()
    gathers[0].begin()
    swap.wait()
    spreads = spread(net, land)
    shares[1].wait()
    gathers[1].begin()
    for share in shares[2:]:
        share.start()
    gathers[0].middle()
    for i in range(2, n):
        shares[i].wait()
        gathers[i].begin()
        gathers[i - 1].middle()
        gathers[i - 2].final()
        if i == 2:
            for copy in spreads:
                copy.wait_recv()
            keep = net.here(land, all_tokens)
            for share in shares_later:
                share.start()
    gathers[n - 1].middle()
    gathers[n - 2].final()
    gathers[n - 1].final()
    for gather in gathers:
        gather.done()
    for share in shares_later:
        share.wait()
    keep.wait()
    net.finish()


def body_kernel(count, rows, more, *refs):
    refs = Refs(refs)
    o_ref, h_ref, gain_ref, wo_hbm, wgate_hbm, wup_hbm, down_hbm = refs.take(7)
    if more:
        (gain_next,) = refs.take(1)
        blocks = refs.take(more)
    else:
        (swap_src,) = refs.take(1)
    h1_ref, hn_ref, gate_ref, up_ref, u_ref, ng_hbm, wd_out = refs.take(7)
    if more:
        (nn_hbm,) = refs.take(1)
        full = refs.take(more)
    else:
        (swap_dst,) = refs.take(1)
    wo, wgu, wd_blocks, out_a, land_a, land_n, out_b, land_b = refs.take(8)
    if more:
        (land_q,) = refs.take(1)
    send, recv, local = refs.take(3)

    place = Place(count)
    net = Net(place, send, recv, local)
    width = h_ref.shape[1]
    hidden = wgate_hbm.shape[1]
    load_out = net.here(wo_hbm, wo)
    load_gate = net.here(wgate_hbm, wgu.at[:, pl.ds(0, hidden)])
    load_up = net.here(wup_hbm, wgu.at[:, pl.ds(hidden, hidden)])
    peers = place.peers
    place.greet(True, not more)
    down = Gather(net, down_hbm, wd_blocks, ranks=False)
    wd = wd_blocks.reshape(hidden, width)
    jobs = [Gather(net, blocks[i], full[i]) for i in range(more)]
    if more:
        j = jobs
        tick = Ticks(
            [
                [down.begin],
                [j[0].begin],
                [down.middle],
                [j[1].begin, down.final],
                [j[0].middle, j[2].begin],
                [j[0].final, j[1].middle],
                [j[1].final],
                [j[2].middle, j[3].begin],
                [j[2].final],
                [j[3].middle],
                [j[3].final],
            ]
        )
    else:
        swap = Swap(net, swap_src, swap_dst)
        tick = Ticks([[down.begin], [], [down.middle], [swap.start, down.final]])
    tick()
    load_out.wait()

    sums = [None] * 3
    for i in (2, 0, 1):
        span = rows_of(peers[i][1], rows)

        def use(cols, y, i=i):
            out_a[i, :, cols] = y.astype(BF16)

        products(lambda: o_ref[span, :], wo, width, 512, True, use)
        sums[i] = push(net, out_a, land_a, i)
    span = rows_of(place.rank, rows)

    def use_own(cols, y):
        h1_ref[:, cols] = h_ref[:, cols].astype(F32) + y

    products(lambda: o_ref[span, :], wo, width, 512, True, use_own)
    tick()
    for copy in sums:
        copy.wait_recv()
    h1 = landed_sum(h1_ref[...], land_a)
    h1_ref[...] = h1
    land_n[place.rank] = norm_rows(h1, gain_ref[...])
    gather = spread(net, land_n)
    tick()
    load_gate.wait()
    load_up.wait()

    def inner_block(rank):
        span = rows_of(rank, rows)

        @pl.loop(0, hidden // 256)
        def _(j):
            cols = pl.ds(pl.multiple_of(j * 256, 256), 256)
            ups = pl.ds(pl.multiple_of(j * 256 + hidden, 256), 256)
            gate = jnp.dot(land_n[rank], wgu[:, cols], preferred_element_type=F32)
            up = jnp.dot(land_n[rank], wgu[:, ups], preferred_element_type=F32)
            gate_ref[span, cols] = gate
            up_ref[span, cols] = up
            u_ref[span, cols] = (gate / (1.0 + jnp.exp(-gate)) * up).astype(BF16)

        return span

    span = inner_block(place.rank)
    tick()
    second = []
    for i, (_, rank) in enumerate(peers):
        gather[i].wait_recv()
        span = inner_block(rank)
        if i == 0:
            down.done()
            keep_down = net.here(wd_blocks, wd_out)

        def use(cols, y, i=i):
            out_b[i, :, cols] = y.astype(BF16)

        products(lambda: u_ref[span, :], wd, width, 512, False, use)
        second.append(push(net, out_b, land_b, i))
        tick()
    keep = net.here(land_n, ng_hbm)
    span = rows_of(place.rank, rows)

    def use_down(cols, y):
        hn_ref[:, cols] = h1_ref[:, cols] + y

    products(lambda: u_ref[span, :], wd, width, 512, False, use_down)
    for copy in second:
        copy.wait_recv()
    hn = landed_sum(hn_ref[...], land_b)
    hn_ref[...] = hn
    if more:
        land_q[place.rank] = norm_rows(hn, gain_next[...])
        third = spread(net, land_q)
        tick()
        for copy in third:
            copy.wait_recv()
            tick()
        keep_next = net.here(land_q, nn_hbm)
        keep_next.wait()
    tick.rest()
    if more:
        for job in jobs:
            job.done()
    else:
        swap.wait()
    keep.wait()
    keep_down.wait()
    net.finish()


def back_kernel(count, rows, first, last, n_red, *refs):
    refs = Refs(refs)
    if first:
        g_ref, swap_src = refs.take(2)
    else:
        dqkv_ref, wq_hbm, ghin_ref, hin_ref, gainin_ref = refs.take(5)
    if not last:
        wd_hbm, wgate_hbm, wup_hbm, wo_hbm, gate_ref, up_ref, h1_ref, gain_ref = refs.take(8)
    else:
        (other_gains,) = refs.take(1)
    parts = refs.take(n_red)
    if first:
        (swap_dst,) = refs.take(1)
    elif not last:
        gnew_ref, ggin_ref = refs.take(2)
    else:
        swap_dst, gains_out = refs.take(2)
    if not last:
        gbg_hbm, dgu_ref, gh_ref, gg_ref, ghg_hbm, do_ref = refs.take(6)
    red_out = refs.take(n_red)
    if not first:
        wq, out_a, land_a = refs.take(3)
    if last:
        gnew_ref, gains_all, gains_part = refs.take(3)
        gains_scratch = refs.take(5)
    if not last:
        wd, wgu, wo, land_g, out_b, land_b, land_h = refs.take(7)
    red_scratch = [refs.take(4 if i == 0 else 5) for i in range(n_red)]
    send, recv, local = refs.take(3)

    place = Place(count)
    net = Net(place, send, recv, local)
    jobs = []
    for i in range(n_red):
        scratch = red_scratch[i] + ([None] if i == 0 else [])
        jobs.append(Reduce(net, parts[i], red_out[i], *scratch, ranks=i > 0))
    peers = place.peers
    if not first:
        load_q = net.here(wq_hbm.at[:, pl.ds(0, wq.shape[1])], wq)
    if not last:
        hidden = wd.shape[0]
        load_down = net.here(wd_hbm, wd)
        load_gate = net.here(wgate_hbm, wgu.at[:, pl.ds(0, hidden)])
        load_up = net.here(wup_hbm, wgu.at[:, pl.ds(hidden, hidden)])
        load_out = net.here(wo_hbm, wo)
    place.greet(n_red > 0, first or last)
    if first:
        swap = Swap(net, swap_src, swap_dst)
        tick = Ticks([[swap.start]])
    elif not last:
        j = jobs
        tick = Ticks(
            [
                [j[0].begin, j[1].begin],
                [j[0].along_a, j[2].begin],
                [j[1].along_a, j[3].begin],
                [j[0].along_zh, j[4].begin],
                [],
                [j[2].along_a],
                [j[1].along_zh],
                [j[0].among_ranks, j[3].along_a],
                [j[2].along_zh],
                [j[1].among_ranks, j[4].along_a],
                [j[3].along_zh],
                [j[2].among_ranks, j[4].along_zh],
                [j[1].done, j[2].done, j[3].among_ranks, j[4].among_ranks],
                [j[3].done, j[4].done],
            ]
        )
    else:
        j = jobs
        tick = Ticks(
            [
                [j[0].begin, j[1].begin, j[2].begin],
                [j[0].along_a, j[3].begin, j[4].begin],
            ]
        )
    tick()
    own = rows_of(place.rank, rows)
    if not first:
        load_q.wait()
        width = ghin_ref.shape[1]
        total = [None] * 3
        for i in (2, 0, 1):
            span = rows_of(peers[i][1], rows)

            def use(cols, y, i=i):
                out_a[i, :, cols] = y.astype(BF16)

            products(lambda: dqkv_ref[span, :], wq, width, 512, True, use)
            total[i] = push(net, out_a, land_a, i)

        def use_own(cols, y):
            gnew_ref[:, cols] = y

        products(lambda: dqkv_ref[own, :], wq, width, 512, True, use_own)
        tick()
        for copy in total:
            copy.wait_recv()
        dn = landed_sum(gnew_ref[...], land_a)
        back, ggain = norm_rows_back(hin_ref[...].astype(F32), gainin_ref[...], dn)
        gnew_ref[...] = ghin_ref[...] + back
        if last:
            finish_last(
                place, net, jobs, gnew_ref, ggain, other_gains, gains_all, gains_part, gains_scratch,
                gains_out, swap_dst,
            )
            return
        ggin_ref[...] = ggain
        g_ref = gnew_ref
    width = g_ref.shape[1]
    land_g[place.rank] = g_ref[...].astype(BF16)
    gather = spread(net, land_g)
    tick()
    load_down.wait()
    load_gate.wait()
    load_up.wait()

    def inner_block(rank):
        span = rows_of(rank, rows)

        @pl.loop(0, hidden // 256)
        def _(j):
            cols = pl.ds(pl.multiple_of(j * 256, 256), 256)
            ups = pl.ds(pl.multiple_of(j * 256 + hidden, 256), 256)
            du = lax.dot_general(
                land_g[rank], wd[cols, :], (((1,), (1,)), ((), ())), preferred_element_type=F32
            )
            gate, up = gate_ref[span, cols], up_ref[span, cols]
            sg = 1.0 / (1.0 + jnp.exp(-gate))
            dgu_ref[span, cols] = (du * up * sg * (1.0 + gate * (1.0 - sg))).astype(BF16)
            dgu_ref[span, ups] = (du * gate * sg).astype(BF16)

        return span

    span = inner_block(place.rank)

    def use_mid(cols, y):
        gh_ref[:, cols] = y

    products(lambda: dgu_ref[span, :], wgu, width, 512, True, use_mid)
    tick()
    second = []
    for i, (_, rank) in enumerate(peers):
        gather[i].wait_recv()
        span = inner_block(rank)

        def use(cols, y, i=i):
            out_b[i, :, cols] = y.astype(BF16)

        products(lambda: dgu_ref[span, :], wgu, width, 512, True, use)
        second.append(push(net, out_b, land_b, i))
        tick()
    keep = net.here(land_g, gbg_hbm)
    for copy in second:
        copy.wait_recv()
    dn = landed_sum(gh_ref[...], land_b)
    back, ggain = norm_rows_back(h1_ref[...], gain_ref[...], dn)
    gh = g_ref[...].astype(F32) + back
    gh_ref[...] = gh
    gg_ref[...] = ggain
    land_h[place.rank] = gh.astype(BF16)
    third = spread(net, land_h)
    tick()
    load_out.wait()

    def out_block(rank):
        span = rows_of(rank, rows)

        def use(cols, y):
            do_ref[span, cols] = y.astype(BF16)

        products(lambda: land_h[rank], wo, wo.shape[1], wo.shape[1], False, use)

    out_block(place.rank)
    for i, (_, rank) in enumerate(peers):
        tick()
        third[i].wait_recv()
        out_block(rank)
    keep_h = net.here(land_h, ghg_hbm)
    tick.rest()
    keep_h.wait()
    keep.wait()
    if first:
        swap.wait()
    net.finish()


def finish_last(place, net, jobs, gnew_ref, ggain, other_gains, gains_all, gains_part, scratch, gains_out, swap_dst):
    swap = Swap(net, gnew_ref, swap_dst)
    swap.start()
    gains_all[...] = other_gains[...]
    gains_all[0:1, :] = ggain
    gains_part[...] = jnp.zeros(gains_part.shape, BF16)
    count = gains_part.shape[0]
    piece = gains_all.shape[1] // (16 * count)
    for block in range(16 * count):
        index = (block // 16, block // 8 % 2, block // 4 % 2, block // 2 % 2, block % 2)
        gains_part[index + (slice(None), slice(0, piece))] = gains_all[
            :, block * piece : (block + 1) * piece
        ].astype(BF16)
    small = Reduce(net, gains_part, gains_out, *scratch, added=True)
    small.begin()
    j = jobs
    j[1].along_a()
    j[0].along_zh()
    small.along_a()
    j[2].along_a()
    j[1].along_zh()
    small.along_zh()
    j[0].among_ranks()
    j[3].along_a()
    j[2].along_zh()
    small.among_ranks()
    j[1].among_ranks()
    j[4].along_a()
    j[3].along_zh()
    j[2].among_ranks()
    j[1].done()
    j[4].along_zh()
    j[3].among_ranks()
    j[2].done()
    small.done()
    j[4].among_ranks()
    j[3].done()
    j[4].done()
    swap.wait()
    net.finish()


def pack_weights(w_qkv, w_out, w_gate_up, gains, count, layer):
    rows = w_qkv.shape[1]
    attn_cols = HEADS * HEAD_DIM
    kv_cols = KV_HEADS * HEAD_DIM
    qkv = w_qkv[layer]
    q = qkv[:, :attn_cols].reshape(rows, RANKS, -1)
    k = qkv[:, attn_cols : attn_cols + kv_cols].reshape(rows, RANKS, -1)
    v = qkv[:, attn_cols + kv_cols :].reshape(rows, RANKS, -1)
    columns = [q, k, v]
    if layer == 0:
        scales = jnp.pad(gains.reshape(2 * LAYERS, rows).T, ((0, 0), (0, GAIN_COLS - 2 * LAYERS)))
        columns.append(jnp.broadcast_to(scales[:, None], (rows, RANKS, GAIN_COLS)))
    head = jnp.concatenate(columns, axis=2).transpose(1, 0, 2)
    out = w_out[layer].T.reshape(rows, RANKS, -1).transpose(1, 0, 2)
    gu = w_gate_up[layer].reshape(rows, 2, count, 2, 2, 2, 2, -1)
    gu = gu.transpose(1, 3, 6, 0, 2, 4, 5, 7).reshape(2, RANKS, rows, -1)
    return head, out, gu[0], gu[1]


def unpack_grads(head, out, gate, up, count):
    rows = head.shape[1]
    q_cols = HEADS * HEAD_DIM // RANKS
    kv_cols = KV_HEADS * HEAD_DIM // RANKS
    wide = lambda part: part.transpose(1, 0, 2).reshape(rows, -1)
    qkv = jnp.concatenate(
        [
            wide(head[:, :, :q_cols]),
            wide(head[:, :, q_cols : q_cols + kv_cols]),
            wide(head[:, :, q_cols + kv_cols : q_cols + 2 * kv_cols]),
        ],
        axis=1,
    )
    order = lambda part: (
        part.reshape(2, 2, rows, count, 2, 2, -1).transpose(2, 3, 0, 4, 5, 1, 6).reshape(rows, -1)
    )
    return qkv, wide(out).T, jnp.stack([order(gate), order(up)], axis=1)


def rotary_tables(positions, head_size):
    half_size = head_size // 2
    freq_index = jnp.arange(half_size).astype(F32)
    inverse = jnp.exp(freq_index * (-2.0 * jnp.log(ROPE_BASE) / head_size))
    angles = positions.astype(F32)[:, None] * inverse[None, :]
    return (jnp.cos(angles), jnp.sin(angles))


def rotate(values, cosine, sine_tab):
    half_size = values.shape[-1] // 2
    first, second = values[..., :half_size], values[..., half_size:]
    c, s = cosine[:, None, :], sine_tab[:, None, :]
    return jnp.concatenate([first * c - second * s, second * c + first * s], axis=-1)


def unrotate(grads, cosine, sine_tab):
    return rotate(grads, cosine, -sine_tab)


def attend(proj, cosine, sine_tab, causal):
    length = proj.shape[0]
    kv = KV_HEADS // RANKS
    groups = HEADS // KV_HEADS
    q_cols = kv * groups * HEAD_DIM
    kv_cols = kv * HEAD_DIM
    query = rotate(proj[:, :q_cols].reshape(length, kv * groups, HEAD_DIM), cosine, sine_tab)
    query = query.astype(BF16).reshape(length, kv, groups, HEAD_DIM)
    key = rotate(proj[:, q_cols : q_cols + kv_cols].reshape(length, kv, HEAD_DIM), cosine, sine_tab)
    key = key.astype(BF16)
    value = proj[:, q_cols + kv_cols :].astype(BF16).reshape(length, kv, HEAD_DIM)
    scale = HEAD_DIM ** (-0.5)
    scores = jnp.einsum("qkgd,skd->kgqs", query, key, preferred_element_type=F32) * scale
    scores = jnp.where(causal[None, None], scores, MASKED)
    highest = jnp.max(scores, axis=-1, keepdims=True)
    lse = highest + jnp.log(jnp.sum(jnp.exp(scores - highest), axis=-1, keepdims=True))
    weights = jnp.exp(scores - lse).astype(BF16)
    mixed = jnp.einsum("kgqs,skd->qkgd", weights, value, preferred_element_type=F32).astype(BF16)
    return mixed.reshape(length, q_cols), (query, key, value, lse)


def attend_back(saved, mixed, grad_mixed, cosine, sine_tab, causal):
    query, key, value, lse = saved
    length = query.shape[0]
    grad_mixed = grad_mixed.reshape(query.shape)
    mixed = mixed.reshape(query.shape)
    scale = HEAD_DIM ** (-0.5)
    scores = jnp.einsum("qkgd,skd->kgqs", query, key, preferred_element_type=F32) * scale
    scores = jnp.where(causal[None, None], scores, MASKED)
    weights = jnp.exp(scores - lse)
    grad_weights = jnp.einsum("qkgd,skd->kgqs", grad_mixed, value, preferred_element_type=F32)
    delta = jnp.sum(grad_mixed.astype(F32) * mixed.astype(F32), axis=-1)
    delta = jnp.transpose(delta, (1, 2, 0))[..., None]
    grad_scores = (weights * (grad_weights - delta) * scale).astype(BF16)
    grad_query = jnp.einsum("kgqs,skd->qkgd", grad_scores, key, preferred_element_type=F32)
    grad_key = jnp.einsum("kgqs,qkgd->skd", grad_scores, query, preferred_element_type=F32)
    grad_value = jnp.einsum(
        "kgqs,qkgd->skd", weights.astype(BF16), grad_mixed, preferred_element_type=F32
    )
    grad_query = unrotate(grad_query.reshape(length, -1, HEAD_DIM), cosine, sine_tab)
    grad_key = unrotate(grad_key, cosine, sine_tab)
    return jnp.concatenate(
        [g.reshape(length, -1) for g in (grad_query, grad_key, grad_value)], axis=1
    ).astype(BF16)


VM = pl.BlockSpec(memory_space=pltpu.VMEM)
AN = pl.BlockSpec(memory_space=pl.ANY)


def params(collective_id):
    return pltpu.CompilerParams(
        collective_id=collective_id, has_side_effects=True, vmem_limit_bytes=VMEM_BYTES
    )


def like(shape, dtype=BF16):
    return jax.ShapeDtypeStruct(tuple(shape), dtype)


def full_shape(count, tail):
    return (count, 2, 2, 2, 2) + tuple(tail)


def call_start(count, tokens, pieces, later):
    rows, width = tokens.shape
    n, ahead = len(pieces), len(later)
    got = pl.pallas_call(
        functools.partial(start_kernel, count, n, ahead),
        out_shape=[like((RANKS, rows, width))]
        + [like(full_shape(count, p.shape[1:])) for p in pieces]
        + [like((2, 2) + p.shape[1:]) for p in later],
        in_specs=[AN] * (1 + n + ahead),
        out_specs=[AN] * (1 + n + ahead),
        scratch_shapes=[pltpu.VMEM((RANKS, rows, width), BF16)]
        + [pltpu.VMEM((2, 2) + p.shape[1:], BF16) for p in pieces]
        + sems(count),
        compiler_params=params(1),
        name="start",
    )(tokens, *pieces, *later)
    return got[0], [f.reshape(-1, f.shape[-1]) for f in got[1 : n + 1]], got[n + 1 :]


def call_body(count, o, h, gain, weights, down, extra):
    rows, width = h.shape
    tall = RANKS * rows
    wo, wgate, wup = weights
    hidden = wgate.shape[1]
    more = len(extra) - 1
    blocks = extra[1:]
    three = pltpu.VMEM((3, rows, width), BF16)
    four = pltpu.VMEM((RANKS, rows, width), BF16)
    wd_shape = (count, 2, 2) + down.shape
    got = pl.pallas_call(
        functools.partial(body_kernel, count, rows, more),
        out_shape=[
            like((rows, width), F32),
            like((rows, width), F32),
            like((tall, hidden), F32),
            like((tall, hidden), F32),
            like((tall, hidden)),
            like((RANKS, rows, width)),
            like(wd_shape),
        ]
        + (
            [like((RANKS, rows, width))] + [like(full_shape(count, b.shape[2:])) for b in blocks]
            if more
            else [like(extra[0].shape)]
        ),
        in_specs=[VM, VM, VM, AN, AN, AN, AN] + ([VM] + [AN] * more if more else [AN]),
        out_specs=[VM] * 5 + [AN] * 2 + [AN] * (1 + more),
        scratch_shapes=[
            pltpu.VMEM(wo.shape, BF16),
            pltpu.VMEM((width, 2 * hidden), BF16),
            pltpu.VMEM(wd_shape, BF16),
            three,
            three,
            four,
            three,
            three,
        ]
        + ([four] if more else [])
        + sems(count),
        compiler_params=params(2 if more else 3),
        name="body_more" if more else "body",
    )(o, h, gain, wo, wgate, wup, down, *extra)
    got = list(got)
    got[6] = got[6].reshape(-1, width)
    return got[:7], got[7], [f.reshape(-1, f.shape[-1]) for f in got[8:]]


def call_back(count, start, rest, parts):
    first, last = len(start) == 2, len(rest) == 1
    rows, width = start[0].shape if first else start[2].shape
    tall = RANKS * rows
    three = pltpu.VMEM((3, rows, width), BF16)
    four = pltpu.VMEM((RANKS, rows, width), BF16)
    in_specs = [VM, AN] if first else [VM, AN, VM, VM, VM]
    in_specs += [VM] if last else [AN, AN, AN, AN, VM, VM, VM, VM]
    n_red = len(parts)
    in_specs += [AN] * n_red
    outs, out_specs, scratch = [], [], []
    if first:
        outs, out_specs = [like(start[1].shape, start[1].dtype)], [AN]
    elif not last:
        outs, out_specs = [like((rows, width), F32), like((1, width), F32)], [VM, VM]
    else:
        outs, out_specs = [like((rows, width), F32), like((16, GAIN_COLS), F32)], [AN, VM]
    if not first:
        scratch += [pltpu.VMEM((width, start[0].shape[1]), BF16), three, three]
    if last:
        gains_shape = full_shape(count, (16, GAIN_COLS))
        scratch += [
            pltpu.VMEM((rows, width), F32),
            pltpu.VMEM((16, width), F32),
            pltpu.VMEM(gains_shape, BF16),
        ]
        scratch += Reduce.scratch(gains_shape)
    else:
        wd, wgate, wup, wo = rest[:4]
        hidden = wgate.shape[1]
        outs += [
            like((RANKS, rows, width)),
            like((tall, 2 * hidden)),
            like((rows, width), F32),
            like((1, width), F32),
            like((RANKS, rows, width)),
            like((tall, wo.shape[1])),
        ]
        out_specs += [AN, VM, VM, VM, AN, VM]
        scratch += [pltpu.VMEM(s, BF16) for s in (wd.shape, (width, 2 * hidden), wo.shape)]
        scratch += [four, three, three, four]
    for i, part in enumerate(parts):
        scratch += Reduce.scratch(part.shape, ranks=i > 0)
        tail = part.shape[-2:]
        outs.append(like(tail if i == 0 else (RANKS,) + tail, F32))
        out_specs.append(VM)
    return pl.pallas_call(
        functools.partial(back_kernel, count, rows, first, last, n_red),
        out_shape=outs,
        in_specs=in_specs,
        out_specs=out_specs,
        scratch_shapes=scratch + sems(count),
        compiler_params=params(4 if first else (6 if last else 5)),
        name="back_first" if first else ("back_last" if last else "back_mid"),
    )(*start, *rest, *parts)


def dot_t(a, b):
    return lax.dot_general(a, b, (((0,), (0,)), ((), ())), preferred_element_type=F32).astype(BF16)


def shards(dp_size, ctx_size, tokens, cotangent, w_qkv, w_out, w_gate_up, w_down, gains):
    count = dp_size // 4
    rows, width = tokens.shape
    length = RANKS * rows
    hidden = w_gate_up.shape[-1] // RANKS
    positions = jnp.arange(length, dtype=jnp.int32)
    cosine, sine_tab = rotary_tables(positions, HEAD_DIM)
    causal = positions[None, :] <= positions[:, None]
    tall = lambda value: value.reshape(length, width)
    rank = lax.rem(lax.div(lax.axis_index("dp"), 2), 2) * 2 + lax.rem(lax.axis_index("ctx"), 2)

    packed = [pack_weights(w_qkv, w_out, w_gate_up, gains, count, layer) for layer in range(LAYERS)]
    all_tokens, full, blocks = call_start(count, tokens, packed[0], packed[1])
    gain_rows = full[0][:, -GAIN_COLS:][:, : 2 * LAYERS].astype(F32).T
    gain = lambda layer, which: gain_rows[2 * layer + which][None]
    h = lax.dynamic_index_in_dim(all_tokens, rank, 0, keepdims=False)
    states = tall(all_tokens).astype(F32)
    n1 = norm_rows(states, gain(0, 0))

    records = []
    swapped = None
    for layer in range(LAYERS):
        wq, wo, wgate, wup = full
        wq_now = wq[:, : wq.shape[1] - GAIN_COLS] if layer == 0 else wq
        proj = jnp.dot(tall(n1), wq_now, preferred_element_type=F32)
        mixed, saved = attend(proj, cosine, sine_tab, causal)
        if layer + 1 < LAYERS:
            extra = (gain(layer + 1, 0), *blocks)
        else:
            extra = (cotangent.astype(BF16),)
        got, ahead, full = call_body(
            count, mixed, h, gain(layer, 1), (wo, wgate, wup), w_down[layer], extra
        )
        h1, h_next, gate, up, u, n2, wd = got
        records.append((h, n1, saved, mixed, h1, n2, gate, up, u, (wq, wo, wgate, wup, wd)))
        h = h_next
        if layer + 1 < LAYERS:
            n1 = ahead
        else:
            g = ahead

    shape7 = lambda value: value.reshape(count, 2, 2, 2, 2, -1, value.shape[-1])
    start, parts = (g, h), []
    grads = [None] * LAYERS
    gain_grads = [None] * (2 * LAYERS)
    for layer in reversed(range(LAYERS)):
        h_in, n1, saved, mixed, h1, n2, gate, up, u, (wq, wo, wgate, wup, wd) = records[layer]
        got = call_back(count, start, (wd, wgate, wup, wo, gate, up, h1, gain(layer, 1)), parts)
        if layer == LAYERS - 1:
            out_act, *got = got
        else:
            _, gain_grads[2 * layer + 2], *got = got
            grads[layer + 1] = got[6:]
        gbg, dgu, gh, gain_grads[2 * layer + 1], ghg, do = got[:6]
        dqkv = attend_back(saved, mixed, do, cosine, sine_tab, causal)
        parts = [
            dot_t(u, tall(gbg)).reshape(count, 2, 2, -1, width),
            shape7(dot_t(tall(n2), dgu[:, :hidden])),
            shape7(dot_t(tall(n2), dgu[:, hidden:])),
            shape7(dot_t(tall(ghg), mixed)),
            shape7(dot_t(tall(n1), dqkv)),
        ]
        start = (dqkv, wq, gh, h_in, gain(layer, 0))
    others = jnp.concatenate([jnp.zeros((1, width), F32)] + gain_grads[1:], axis=0)
    others = jnp.pad(others, ((0, 16 - 2 * LAYERS), (0, 0)))
    grad_tokens, gains_sum, *last = call_back(count, start, (others,), parts)
    grads[0] = last
    piece = gains.shape[-1]
    grad_gains = gains_sum[: 2 * LAYERS, :piece].reshape(LAYERS, 2, piece)
    stacked = [unpack_grads(q, o, gate, up, count) for _, gate, up, o, q in grads]
    s_qkv, s_out, s_gu = (jnp.stack([s[i] for s in stacked]) for i in range(3))
    s_down = jnp.stack([g[0] for g in grads])
    return (out_act, grad_tokens, s_qkv, s_out, s_gu, s_down, grad_gains)


def solution(mesh):
    both = ("dp", "ctx")
    return jax.shard_map(
        functools.partial(shards, mesh.shape["dp"], mesh.shape["ctx"]),
        mesh=mesh,
        in_specs=(
            P(both, None),
            P(both, None),
            P(None, both, None),
            P(None, None, both),
            P(None, both, None, None),
            P(None, both, None),
            P(None, None, both),
        ),
        out_specs=(
            P(both, None),
            P(both, None),
            P(None, both, None),
            P(None, None, both),
            P(None, both, None, None),
            P(None, both, None),
            P(None, None, both),
        ),
        check_vma=False,
    )
```

```python
import functools

import jax
import jax.numpy as jnp
from jax import lax
from jax.experimental import pallas as pl
from jax.experimental.pallas import tpu as pltpu
from jax.sharding import PartitionSpec as P

HEADS = 16
KV_HEADS = 8
HEAD_DIM = 96
LAYERS = 2
RANKS = 4
GAIN_COLS = 128

NORM_EPS = 1e-05
ROPE_BASE = 100000.0
MASKED = -1e30
MESH = pl.DeviceIdType.MESH
BF16 = jnp.bfloat16
F32 = jnp.float32
VMEM_BYTES = 62 * 1024 * 1024


class Place:
    def __init__(self, count):
        self.count = count
        self.dp = lax.axis_index("dp")
        self.ctx = lax.axis_index("ctx")
        self.core = lax.rem(self.dp, 2)
        self.x = lax.rem(lax.div(self.dp, 2), 2)
        self.a = lax.div(self.dp, 4)
        self.zh = lax.div(self.ctx, 2)
        self.zl = lax.rem(self.ctx, 2)
        self.rank = self.x * 2 + self.zl
        dpx = self.dp + 2 - 4 * self.x
        ctz = self.ctx + 1 - 2 * self.zl
        x2, z2 = 1 - self.x, 1 - self.zl
        self.peers = (
            ((dpx, self.ctx), x2 * 2 + self.zl),
            ((self.dp, ctz), self.x * 2 + z2),
            ((dpx, ctz), x2 * 2 + z2),
        )
        self.core_peer = (self.dp + 1 - 2 * self.core, self.ctx)
        self.zh_peer = (self.dp, self.ctx + 2 - 4 * self.zh)
        self.others = []
        for k in range(1, count):
            ahead = lax.rem(self.a + k, count)
            behind = lax.rem(self.a + count - k, count)
            self.others.append(((self.dp + (ahead - self.a) * 4, self.ctx), ahead, behind))
        self.moves = self.x != self.zh
        self.swap_peer = (self.dp + (self.zh - self.x) * 2, self.ctx + (self.x - self.zh) * 2)

    def greet(self, weights, swap):
        devices = [d for d, _ in self.peers]
        if weights:
            devices += [self.core_peer, self.zh_peer] + [o[0] for o in self.others]
        barrier = pltpu.get_barrier_semaphore()
        for device in devices:
            pl.semaphore_signal(barrier, inc=1, device_id=device, device_id_type=MESH)
        if swap:

            @pl.when(self.moves)
            def _():
                pl.semaphore_signal(barrier, inc=1, device_id=self.swap_peer, device_id_type=MESH)

        expected = len(devices)
        if swap:
            expected = expected + self.x + self.zh - 2 * self.x * self.zh
        pl.semaphore_wait(barrier, expected)


class Net:
    def __init__(self, place, send, recv, local):
        self.place, self.send, self.recv, self.local = place, send, recv, local
        self.n, self.m = 0, 0
        self.sends = []

    def remote(self, src, dst, device):
        copy = self.prepare(src, dst, device)
        copy.start()
        self.sends.append(copy)
        return copy

    def prepare(self, src, dst, device):
        i = self.n
        self.n += 1
        return pltpu.make_async_remote_copy(
            src_ref=src, dst_ref=dst, send_sem=self.send.at[i], recv_sem=self.recv.at[i],
            device_id=device, device_id_type=MESH,
        )

    def here(self, src, dst):
        i = self.m
        self.m += 1
        copy = pltpu.make_async_copy(src, dst, self.local.at[i])
        copy.start()
        return copy

    def finish(self):
        for copy in self.sends:
            copy.wait_send()


REMOTE_SEMS, LOCAL_SEMS = 128, 32


def sems(count=2):
    n = REMOTE_SEMS * max(1, count // 2)
    return [
        pltpu.SemaphoreType.DMA((n,)),
        pltpu.SemaphoreType.DMA((n,)),
        pltpu.SemaphoreType.DMA((LOCAL_SEMS,)),
    ]


class Swap:
    def __init__(self, net, src, dst):
        self.net, self.src, self.dst = net, src, dst

    def start(self):
        net, place = self.net, self.net.place
        self.copy = net.prepare(self.src, self.dst, place.swap_peer)
        self.stay = pltpu.make_async_copy(self.src, self.dst, net.local.at[net.m])
        net.m += 1

        @pl.when(place.moves)
        def _():
            self.copy.start()

        @pl.when(jnp.logical_not(place.moves))
        def _():
            self.stay.start()

    def wait(self):
        @pl.when(self.net.place.moves)
        def _():
            self.copy.wait_recv()
            self.copy.wait_send()

        @pl.when(jnp.logical_not(self.net.place.moves))
        def _():
            self.stay.wait()


class Share:
    def __init__(self, net, piece, block):
        self.net, self.piece, self.block = net, piece, block

    def start(self):
        net, place = self.net, self.net.place
        mine = self.block.at[place.x, place.zl]
        self.copies = [net.remote(self.piece.at[rank], mine, device) for device, rank in place.peers]
        self.own = net.here(self.piece.at[place.rank], mine)

    def wait(self):
        for copy in self.copies:
            copy.wait_recv()
        self.own.wait()


class Gather:
    def __init__(self, net, block, full, ranks=True):
        self.net, self.block, self.full, self.ranks = net, block, full, ranks

    def slot(self, a, core, zh):
        if self.ranks:
            return self.full.at[a, :, core, zh, :]
        return self.full.at[a, core, zh]

    def column(self, a, core):
        if self.ranks:
            return self.full.at[a, :, core, :, :]
        return self.full.at[a, core]

    def begin(self):
        net, p = self.net, self.net.place
        mine = self.slot(p.a, p.core, p.zh)
        self.across = net.remote(self.block, mine, p.zh_peer)
        self.near = [net.remote(self.block, mine, o[0]) for o in p.others]
        self.cores = [net.remote(self.block, mine, p.core_peer)]
        self.own = net.here(self.block, mine)

    def middle(self):
        net, p = self.net, self.net.place
        self.across.wait_recv()
        got = self.slot(p.a, p.core, 1 - p.zh)
        self.far = [net.remote(got, got, o[0]) for o in p.others]
        self.cores.append(net.remote(got, got, p.core_peer))

    def final(self):
        net, p = self.net, self.net.place
        for k, other in enumerate(p.others):
            self.near[k].wait_recv()
            self.far[k].wait_recv()
            got = self.column(other[2], p.core)
            self.cores.append(net.remote(got, got, p.core_peer))

    def done(self):
        self.own.wait()
        for copy in self.cores:
            copy.wait_recv()


class Reduce:
    def __init__(self, net, part, out, held, from_core, from_a, from_zh, from_rank, ranks=True, added=False):
        self.net, self.part, self.out = net, part, out
        self.held, self.from_core, self.from_a = held, from_core, from_a
        self.from_zh, self.from_rank = from_zh, from_rank
        self.ranks, self.added = ranks, added

    def half(self, core):
        return self.part.at[:, :, core] if self.ranks else self.part.at[:, core]

    def begin(self):
        net, p = self.net, self.net.place
        self.load = net.here(self.half(p.core), self.held)
        self.by_core = net.remote(self.half(1 - p.core), self.from_core, p.core_peer)

    def along_a(self):
        net, p = self.net, self.net.place
        self.load.wait()
        self.by_core.wait_recv()
        add_into(self.held, self.from_core)
        self.by_a = [
            net.remote(self.held.at[other[1]], self.from_a.at[k], other[0])
            for k, other in enumerate(p.others)
        ]

    def along_zh(self):
        net, p = self.net, self.net.place
        mine = self.held.at[p.a]
        for k, copy in enumerate(self.by_a):
            copy.wait_recv()
            add_into(mine, self.from_a.at[k])
        there = mine.at[:, 1 - p.zh] if self.ranks else mine.at[1 - p.zh]
        self.by_zh = net.remote(there, self.from_zh, p.zh_peer)

    def among_ranks(self):
        net, p = self.net, self.net.place
        self.by_zh.wait_recv()
        if not self.ranks:
            self.out[...] = self.held[p.a, p.zh].astype(F32) + self.from_zh[...].astype(F32)
            return
        for x in range(2):
            for zl in range(2):
                add_into(self.held.at[p.a, x, p.zh, zl], self.from_zh.at[x, zl])
        self.by_rank = []
        for device, rank in p.peers:
            rank_x, rank_zl = lax.div(rank, 2), lax.rem(rank, 2)
            self.by_rank.append(
                net.remote(
                    self.held.at[p.a, rank_x, p.zh, rank_zl], self.from_rank.at[len(self.by_rank)], device
                )
            )

    def done(self):
        if not self.ranks:
            return
        p = self.net.place
        own = self.held[p.a, p.x, p.zh, p.zl].astype(F32)
        for copy in self.by_rank:
            copy.wait_recv()
        if self.added:
            for j in range(3):
                own = own + self.from_rank[j].astype(F32)
            self.out[...] = own
            return
        self.out[p.rank] = own
        for j, (_, rank) in enumerate(p.peers):
            self.out[rank] = self.from_rank[j].astype(F32)

    @staticmethod
    def scratch(shape, ranks=True):
        tail = shape[-2:]
        count = shape[0]
        inner = ((2, 2, 2) if ranks else (2,)) + tail
        fewer = ((2, 2) if ranks else ()) + tail
        shapes = [(count,) + inner, (count,) + inner, (max(count - 1, 1),) + inner, fewer]
        if ranks:
            shapes.append((3,) + tail)
        return [pltpu.VMEM(s, BF16) for s in shapes]


def add_into(target, source):
    lead = target.shape[:-2]
    total = 1
    for size in lead:
        total *= size
    if total == 1 and not lead:
        target[...] = (target[...].astype(F32) + source[...].astype(F32)).astype(BF16)
        return

    @pl.loop(0, total)
    def _(j):
        index, left = [], j
        for size in reversed(lead):
            index.append(lax.rem(left, size))
            left = lax.div(left, size)
        index = tuple(reversed(index))
        target[index] = (target[index].astype(F32) + source[index].astype(F32)).astype(BF16)


class Spread:
    def __init__(self, net, land):
        self.net, self.land = net, land
        self.peers = net.place.peers
        mine = land.at[net.place.rank]
        self.along_x = net.remote(mine, mine, self.peers[0][0])
        self.along_zl = net.remote(mine, mine, self.peers[1][0])

    def arrivals(self):
        self.along_zl.wait_recv()
        got = self.land.at[self.peers[1][1]]
        relay = self.net.remote(got, got, self.peers[0][0])
        yield 1, self.peers[1][1]
        self.along_x.wait_recv()
        yield 0, self.peers[0][1]
        relay.wait_recv()
        yield 2, self.peers[2][1]

    def wait(self):
        for _ in self.arrivals():
            pass


class Sum:
    def __init__(self, net, out, land):
        self.net, self.out, self.land = net, out, land
        self.peers = net.place.peers

    def ready(self, i):
        if i == 2:
            self.diagonal = self.net.remote(self.out.at[2], self.land.at[0], self.peers[0][0])
        elif i == 0:
            self.along_x = self.net.remote(self.out.at[0], self.land.at[1], self.peers[0][0])

    def forward(self):
        self.diagonal.wait_recv()
        add_into(self.out.at[1], self.land.at[0])
        self.along_zl = self.net.remote(self.out.at[1], self.land.at[2], self.peers[1][0])

    def result(self, own):
        self.along_x.wait_recv()
        self.along_zl.wait_recv()
        return own + self.land[1].astype(F32) + self.land[2].astype(F32)


def products(x, w_ref, count, tile, transposed, use):
    @pl.loop(0, count // tile)
    def _(j):
        cols = pl.ds(pl.multiple_of(j * tile, tile), tile)
        if transposed:
            w, dims = w_ref[cols, :], (((1,), (1,)), ((), ()))
        else:
            w, dims = w_ref[:, cols], (((1,), (0,)), ((), ()))
        use(cols, lax.dot_general(x(), w, dims, preferred_element_type=F32))


def norm_rows(h, gain):
    factor = lax.rsqrt(jnp.mean(h * h, axis=-1, keepdims=True) + NORM_EPS)
    return (h * factor * gain).astype(BF16)


def norm_rows_back(h, gain, grad):
    factor = lax.rsqrt(jnp.mean(h * h, axis=-1, keepdims=True) + NORM_EPS)
    z = grad * gain
    inner = jnp.sum(z * h, axis=-1, keepdims=True)
    back = factor * z - h * (factor * factor * factor * inner / h.shape[-1])
    return back, jnp.sum(grad * h * factor, axis=0, keepdims=True)


def rows_of(rank, rows):
    return pl.ds(pl.multiple_of(rank * rows, rows), rows)


class Refs:
    def __init__(self, refs):
        self.refs = list(refs)

    def take(self, n):
        got, self.refs = self.refs[:n], self.refs[n:]
        return got


class Ticks:
    def __init__(self, plan):
        self.plan = list(plan)

    def __call__(self):
        if self.plan:
            for step in self.plan.pop(0):
                step()

    def rest(self):
        while self.plan:
            self()


def start_kernel(count, n, ahead, *refs):
    refs = Refs(refs)
    (tokens,) = refs.take(1)
    pieces, later = refs.take(n), refs.take(ahead)
    (all_tokens,) = refs.take(1)
    full, blocks_later = refs.take(n), refs.take(ahead)
    (land,) = refs.take(1)
    blocks = refs.take(n)
    send, recv, local = refs.take(3)
    place = Place(count)
    net = Net(place, send, recv, local)
    shares = [Share(net, pieces[i], blocks[i]) for i in range(n)]
    gathers = [Gather(net, blocks[i], full[i]) for i in range(n)]
    shares_later = [Share(net, later[i], blocks_later[i]) for i in range(ahead)]
    swap = Swap(net, tokens, land.at[place.zh * 2 + place.zl])
    place.greet(True, True)
    shares[0].start()
    swap.start()
    shares[1].start()
    shares[0].wait()
    gathers[0].begin()
    swap.wait()
    spreads = Spread(net, land)
    shares[1].wait()
    gathers[1].begin()
    for share in shares[2:]:
        share.start()
    gathers[0].middle()
    for i in range(2, n):
        shares[i].wait()
        gathers[i].begin()
        gathers[i - 1].middle()
        gathers[i - 2].final()
        if i == 2:
            spreads.wait()
            keep = net.here(land, all_tokens)
            for share in shares_later:
                share.start()
    gathers[n - 1].middle()
    gathers[n - 2].final()
    gathers[n - 1].final()
    for gather in gathers:
        gather.done()
    for share in shares_later:
        share.wait()
    keep.wait()
    net.finish()


def body_kernel(count, rows, more, *refs):
    refs = Refs(refs)
    o_ref, h_ref, gain_ref, wo_hbm, wgate_hbm, wup_hbm, down_hbm = refs.take(7)
    if more:
        (gain_next,) = refs.take(1)
        blocks = refs.take(more)
    else:
        (swap_src,) = refs.take(1)
    h1_ref, hn_ref, gate_ref, up_ref, u_ref, ng_hbm, wd_out = refs.take(7)
    if more:
        (nn_hbm,) = refs.take(1)
        full = refs.take(more)
    else:
        (swap_dst,) = refs.take(1)
    wo, wgu, wd_blocks, out_a, land_a, land_n, out_b, land_b = refs.take(8)
    if more:
        (land_q,) = refs.take(1)
    send, recv, local = refs.take(3)

    place = Place(count)
    net = Net(place, send, recv, local)
    width = h_ref.shape[1]
    hidden = wgate_hbm.shape[1]
    load_out = net.here(wo_hbm, wo)
    load_gate = net.here(wgate_hbm, wgu.at[:, pl.ds(0, hidden)])
    load_up = net.here(wup_hbm, wgu.at[:, pl.ds(hidden, hidden)])
    peers = place.peers
    place.greet(True, not more)
    down = Gather(net, down_hbm, wd_blocks, ranks=False)
    wd = wd_blocks.reshape(hidden, width)
    jobs = [Gather(net, blocks[i], full[i]) for i in range(more)]
    if more:
        j = jobs
        tick = Ticks(
            [
                [down.begin],
                [j[0].begin],
                [down.middle],
                [j[1].begin, down.final],
                [j[0].middle, j[2].begin],
                [j[0].final, j[1].middle],
                [j[1].final],
                [j[2].middle, j[3].begin],
                [j[2].final],
                [j[3].middle],
                [j[3].final],
            ]
        )
    else:
        swap = Swap(net, swap_src, swap_dst)
        tick = Ticks([[down.begin], [], [down.middle], [swap.start, down.final]])
    tick()
    load_out.wait()

    sums = Sum(net, out_a, land_a)
    for i in (2, 0, 1):
        span = rows_of(peers[i][1], rows)

        def use(cols, y, i=i):
            out_a[i, :, cols] = y.astype(BF16)

        products(lambda: o_ref[span, :], wo, width, 512, True, use)
        sums.ready(i)
    span = rows_of(place.rank, rows)

    def use_own(cols, y):
        h1_ref[:, cols] = h_ref[:, cols].astype(F32) + y

    products(lambda: o_ref[span, :], wo, width, 512, True, use_own)
    sums.forward()
    tick()
    h1 = sums.result(h1_ref[...])
    h1_ref[...] = h1
    land_n[place.rank] = norm_rows(h1, gain_ref[...])
    gather = Spread(net, land_n)
    tick()
    load_gate.wait()
    load_up.wait()

    def inner_block(rank):
        span = rows_of(rank, rows)

        @pl.loop(0, hidden // 256)
        def _(j):
            cols = pl.ds(pl.multiple_of(j * 256, 256), 256)
            ups = pl.ds(pl.multiple_of(j * 256 + hidden, 256), 256)
            gate = jnp.dot(land_n[rank], wgu[:, cols], preferred_element_type=F32)
            up = jnp.dot(land_n[rank], wgu[:, ups], preferred_element_type=F32)
            gate_ref[span, cols] = gate
            up_ref[span, cols] = up
            u_ref[span, cols] = (gate / (1.0 + jnp.exp(-gate)) * up).astype(BF16)

        return span

    span = inner_block(place.rank)
    tick()
    second = Sum(net, out_b, land_b)
    for i, rank in gather.arrivals():
        span = inner_block(rank)
        if i == 1:
            down.done()
            keep_down = net.here(wd_blocks, wd_out)

        def use(cols, y, i=i):
            out_b[i, :, cols] = y.astype(BF16)

        products(lambda: u_ref[span, :], wd, width, 512, False, use)
        second.ready(i)
        tick()
    keep = net.here(land_n, ng_hbm)
    span = rows_of(place.rank, rows)

    def use_down(cols, y):
        hn_ref[:, cols] = h1_ref[:, cols] + y

    products(lambda: u_ref[span, :], wd, width, 512, False, use_down)
    second.forward()
    hn = second.result(hn_ref[...])
    hn_ref[...] = hn
    if more:
        land_q[place.rank] = norm_rows(hn, gain_next[...])
        third = Spread(net, land_q)
        tick()
        for _ in third.arrivals():
            tick()
        keep_next = net.here(land_q, nn_hbm)
        keep_next.wait()
    tick.rest()
    if more:
        for job in jobs:
            job.done()
    else:
        swap.wait()
    keep.wait()
    keep_down.wait()
    net.finish()


def back_kernel(count, rows, first, last, n_red, *refs):
    refs = Refs(refs)
    if first:
        g_ref, swap_src = refs.take(2)
    else:
        dqkv_ref, wq_hbm, ghin_ref, hin_ref, gainin_ref = refs.take(5)
    if not last:
        wd_hbm, wgate_hbm, wup_hbm, wo_hbm, gate_ref, up_ref, h1_ref, gain_ref = refs.take(8)
    else:
        (other_gains,) = refs.take(1)
    parts = refs.take(n_red)
    if first:
        (swap_dst,) = refs.take(1)
    elif not last:
        gnew_ref, ggin_ref = refs.take(2)
    else:
        swap_dst, gains_out = refs.take(2)
    if not last:
        gbg_hbm, dgu_ref, gh_ref, gg_ref, ghg_hbm, do_ref = refs.take(6)
    red_out = refs.take(n_red)
    if not first:
        wq, out_a, land_a = refs.take(3)
    if last:
        gnew_ref, gsend_ref, gains_all, gains_part = refs.take(4)
        gains_scratch = refs.take(5)
    if not last:
        wd, wgu, wo, land_g, out_b, land_b, land_h = refs.take(7)
    red_scratch = [refs.take(4 if i == 0 else 5) for i in range(n_red)]
    send, recv, local = refs.take(3)

    place = Place(count)
    net = Net(place, send, recv, local)
    jobs = []
    for i in range(n_red):
        scratch = red_scratch[i] + ([None] if i == 0 else [])
        jobs.append(Reduce(net, parts[i], red_out[i], *scratch, ranks=i > 0))
    peers = place.peers
    if not first:
        load_q = net.here(wq_hbm.at[:, pl.ds(0, wq.shape[1])], wq)
    if not last:
        hidden = wd.shape[0]
        load_down = net.here(wd_hbm, wd)
        load_gate = net.here(wgate_hbm, wgu.at[:, pl.ds(0, hidden)])
        load_up = net.here(wup_hbm, wgu.at[:, pl.ds(hidden, hidden)])
        load_out = net.here(wo_hbm, wo)
    place.greet(n_red > 0, first or last)
    if first:
        swap = Swap(net, swap_src, swap_dst)
        tick = Ticks([[swap.start]])
    elif not last:
        j = jobs
        tick = Ticks(
            [
                [j[0].begin, j[1].begin],
                [j[0].along_a, j[2].begin],
                [j[1].along_a, j[3].begin],
                [j[0].along_zh, j[4].begin],
                [],
                [j[2].along_a],
                [j[1].along_zh],
                [j[0].among_ranks, j[3].along_a],
                [j[2].along_zh],
                [j[1].among_ranks, j[4].along_a],
                [j[3].along_zh],
                [j[2].among_ranks, j[4].along_zh],
                [j[1].done, j[2].done, j[3].among_ranks, j[4].among_ranks],
                [j[3].done, j[4].done],
            ]
        )
    else:
        j = jobs
        tick = Ticks(
            [
                [j[0].begin, j[1].begin, j[2].begin],
                [j[0].along_a, j[3].begin, j[4].begin],
            ]
        )
    tick()
    own = rows_of(place.rank, rows)
    if not first:
        load_q.wait()
        width = ghin_ref.shape[1]
        total = Sum(net, out_a, land_a)
        for i in (2, 0, 1):
            span = rows_of(peers[i][1], rows)

            def use(cols, y, i=i):
                out_a[i, :, cols] = y.astype(BF16)

            products(lambda: dqkv_ref[span, :], wq, width, 512, True, use)
            total.ready(i)

        def use_own(cols, y):
            gnew_ref[:, cols] = y

        products(lambda: dqkv_ref[own, :], wq, width, 512, True, use_own)
        total.forward()
        tick()
        dn = total.result(gnew_ref[...])
        back, ggain = norm_rows_back(hin_ref[...].astype(F32), gainin_ref[...], dn)
        gnew_ref[...] = ghin_ref[...] + back
        if last:
            finish_last(
                place, net, jobs, gnew_ref, gsend_ref, ggain, other_gains, gains_all, gains_part, gains_scratch,
                gains_out, swap_dst,
            )
            return
        ggin_ref[...] = ggain
        g_ref = gnew_ref
    width = g_ref.shape[1]
    land_g[place.rank] = g_ref[...].astype(BF16)
    gather = Spread(net, land_g)
    tick()
    load_down.wait()
    load_gate.wait()
    load_up.wait()

    def inner_block(rank):
        span = rows_of(rank, rows)

        @pl.loop(0, hidden // 256)
        def _(j):
            cols = pl.ds(pl.multiple_of(j * 256, 256), 256)
            ups = pl.ds(pl.multiple_of(j * 256 + hidden, 256), 256)
            du = lax.dot_general(
                land_g[rank], wd[cols, :], (((1,), (1,)), ((), ())), preferred_element_type=F32
            )
            gate, up = gate_ref[span, cols], up_ref[span, cols]
            sg = 1.0 / (1.0 + jnp.exp(-gate))
            dgu_ref[span, cols] = (du * up * sg * (1.0 + gate * (1.0 - sg))).astype(BF16)
            dgu_ref[span, ups] = (du * gate * sg).astype(BF16)

        return span

    span = inner_block(place.rank)

    def use_mid(cols, y):
        gh_ref[:, cols] = y

    products(lambda: dgu_ref[span, :], wgu, width, 512, True, use_mid)
    tick()
    second = Sum(net, out_b, land_b)
    for i, rank in gather.arrivals():
        span = inner_block(rank)

        def use(cols, y, i=i):
            out_b[i, :, cols] = y.astype(BF16)

        products(lambda: dgu_ref[span, :], wgu, width, 512, True, use)
        second.ready(i)
        tick()
    keep = net.here(land_g, gbg_hbm)
    second.forward()
    dn = second.result(gh_ref[...])
    back, ggain = norm_rows_back(h1_ref[...], gain_ref[...], dn)
    gh = g_ref[...].astype(F32) + back
    gh_ref[...] = gh
    gg_ref[...] = ggain
    land_h[place.rank] = gh.astype(BF16)
    third = Spread(net, land_h)
    tick()
    load_out.wait()

    def out_block(rank):
        span = rows_of(rank, rows)

        def use(cols, y):
            do_ref[span, cols] = y.astype(BF16)

        products(lambda: land_h[rank], wo, wo.shape[1], wo.shape[1], False, use)

    out_block(place.rank)
    for _, rank in third.arrivals():
        tick()
        out_block(rank)
    keep_h = net.here(land_h, ghg_hbm)
    tick.rest()
    keep_h.wait()
    keep.wait()
    if first:
        swap.wait()
    net.finish()


def finish_last(place, net, jobs, gnew_ref, gsend_ref, ggain, other_gains, gains_all, gains_part, scratch, gains_out, swap_dst):
    gsend_ref[...] = gnew_ref[...].astype(BF16)
    swap = Swap(net, gsend_ref, swap_dst)
    swap.start()
    gains_all[...] = other_gains[...]
    gains_all[0:1, :] = ggain
    gains_part[...] = jnp.zeros(gains_part.shape, BF16)
    count = gains_part.shape[0]
    piece = gains_all.shape[1] // (16 * count)
    for block in range(16 * count):
        index = (block // 16, block // 8 % 2, block // 4 % 2, block // 2 % 2, block % 2)
        gains_part[index + (slice(None), slice(0, piece))] = gains_all[
            :, block * piece : (block + 1) * piece
        ].astype(BF16)
    small = Reduce(net, gains_part, gains_out, *scratch, added=True)
    small.begin()
    j = jobs
    j[1].along_a()
    j[0].along_zh()
    small.along_a()
    j[2].along_a()
    j[1].along_zh()
    small.along_zh()
    j[0].among_ranks()
    j[3].along_a()
    j[2].along_zh()
    small.among_ranks()
    j[1].among_ranks()
    j[4].along_a()
    j[3].along_zh()
    j[2].among_ranks()
    j[1].done()
    j[4].along_zh()
    j[3].among_ranks()
    j[2].done()
    small.done()
    j[4].among_ranks()
    j[3].done()
    j[4].done()
    swap.wait()
    net.finish()


def pack_weights(w_qkv, w_out, w_gate_up, gains, count, layer):
    rows = w_qkv.shape[1]
    attn_cols = HEADS * HEAD_DIM
    kv_cols = KV_HEADS * HEAD_DIM
    qkv = w_qkv[layer]
    q = qkv[:, :attn_cols].reshape(rows, RANKS, -1)
    k = qkv[:, attn_cols : attn_cols + kv_cols].reshape(rows, RANKS, -1)
    v = qkv[:, attn_cols + kv_cols :].reshape(rows, RANKS, -1)
    columns = [q, k, v]
    if layer == 0:
        scales = jnp.pad(gains.reshape(2 * LAYERS, rows).T, ((0, 0), (0, GAIN_COLS - 2 * LAYERS)))
        columns.append(jnp.broadcast_to(scales[:, None], (rows, RANKS, GAIN_COLS)))
    head = jnp.concatenate(columns, axis=2).transpose(1, 0, 2)
    out = w_out[layer].T.reshape(rows, RANKS, -1).transpose(1, 0, 2)
    gu = w_gate_up[layer].reshape(rows, 2, count, 2, 2, 2, 2, -1)
    gu = gu.transpose(1, 3, 6, 0, 2, 4, 5, 7).reshape(2, RANKS, rows, -1)
    return head, out, gu[0], gu[1]


def unpack_grads(head, out, gate, up, count):
    rows = head.shape[1]
    q_cols = HEADS * HEAD_DIM // RANKS
    kv_cols = KV_HEADS * HEAD_DIM // RANKS
    wide = lambda part: part.transpose(1, 0, 2).reshape(rows, -1)
    qkv = jnp.concatenate(
        [
            wide(head[:, :, :q_cols]),
            wide(head[:, :, q_cols : q_cols + kv_cols]),
            wide(head[:, :, q_cols + kv_cols : q_cols + 2 * kv_cols]),
        ],
        axis=1,
    )
    order = lambda part: (
        part.reshape(2, 2, rows, count, 2, 2, -1).transpose(2, 3, 0, 4, 5, 1, 6).reshape(rows, -1)
    )
    return qkv, wide(out).T, jnp.stack([order(gate), order(up)], axis=1)


def rotary_tables(positions, head_size):
    half_size = head_size // 2
    freq_index = jnp.arange(half_size).astype(F32)
    inverse = jnp.exp(freq_index * (-2.0 * jnp.log(ROPE_BASE) / head_size))
    angles = positions.astype(F32)[:, None] * inverse[None, :]
    return (jnp.cos(angles), jnp.sin(angles))


def rotate(values, cosine, sine_tab):
    half_size = values.shape[-1] // 2
    first, second = values[..., :half_size], values[..., half_size:]
    c, s = cosine[:, None, :], sine_tab[:, None, :]
    return jnp.concatenate([first * c - second * s, second * c + first * s], axis=-1)


def unrotate(grads, cosine, sine_tab):
    return rotate(grads, cosine, -sine_tab)


def attend(proj, cosine, sine_tab, causal):
    length = proj.shape[0]
    kv = KV_HEADS // RANKS
    groups = HEADS // KV_HEADS
    q_cols = kv * groups * HEAD_DIM
    kv_cols = kv * HEAD_DIM
    query = rotate(proj[:, :q_cols].reshape(length, kv * groups, HEAD_DIM), cosine, sine_tab)
    query = query.astype(BF16).reshape(length, kv, groups, HEAD_DIM)
    key = rotate(proj[:, q_cols : q_cols + kv_cols].reshape(length, kv, HEAD_DIM), cosine, sine_tab)
    key = key.astype(BF16)
    value = proj[:, q_cols + kv_cols :].astype(BF16).reshape(length, kv, HEAD_DIM)
    scale = HEAD_DIM ** (-0.5)
    scores = jnp.einsum("qkgd,skd->kgqs", query, key, preferred_element_type=F32) * scale
    scores = jnp.where(causal[None, None], scores, MASKED)
    highest = jnp.max(scores, axis=-1, keepdims=True)
    lse = highest + jnp.log(jnp.sum(jnp.exp(scores - highest), axis=-1, keepdims=True))
    weights = jnp.exp(scores - lse).astype(BF16)
    mixed = jnp.einsum("kgqs,skd->qkgd", weights, value, preferred_element_type=F32).astype(BF16)
    return mixed.reshape(length, q_cols), (query, key, value, lse)


def attend_back(saved, mixed, grad_mixed, cosine, sine_tab, causal):
    query, key, value, lse = saved
    length = query.shape[0]
    grad_mixed = grad_mixed.reshape(query.shape)
    mixed = mixed.reshape(query.shape)
    scale = HEAD_DIM ** (-0.5)
    scores = jnp.einsum("qkgd,skd->kgqs", query, key, preferred_element_type=F32) * scale
    scores = jnp.where(causal[None, None], scores, MASKED)
    weights = jnp.exp(scores - lse)
    grad_weights = jnp.einsum("qkgd,skd->kgqs", grad_mixed, value, preferred_element_type=F32)
    delta = jnp.sum(grad_mixed.astype(F32) * mixed.astype(F32), axis=-1)
    delta = jnp.transpose(delta, (1, 2, 0))[..., None]
    grad_scores = (weights * (grad_weights - delta) * scale).astype(BF16)
    grad_query = jnp.einsum("kgqs,skd->qkgd", grad_scores, key, preferred_element_type=F32)
    grad_key = jnp.einsum("kgqs,qkgd->skd", grad_scores, query, preferred_element_type=F32)
    grad_value = jnp.einsum(
        "kgqs,qkgd->skd", weights.astype(BF16), grad_mixed, preferred_element_type=F32
    )
    grad_query = unrotate(grad_query.reshape(length, -1, HEAD_DIM), cosine, sine_tab)
    grad_key = unrotate(grad_key, cosine, sine_tab)
    return jnp.concatenate(
        [g.reshape(length, -1) for g in (grad_query, grad_key, grad_value)], axis=1
    ).astype(BF16)


VM = pl.BlockSpec(memory_space=pltpu.VMEM)
AN = pl.BlockSpec(memory_space=pl.ANY)


def params(collective_id):
    return pltpu.CompilerParams(
        collective_id=collective_id, has_side_effects=True, vmem_limit_bytes=VMEM_BYTES
    )


def like(shape, dtype=BF16):
    return jax.ShapeDtypeStruct(tuple(shape), dtype)


def full_shape(count, tail):
    return (count, 2, 2, 2, 2) + tuple(tail)


def call_start(count, tokens, pieces, later):
    rows, width = tokens.shape
    n, ahead = len(pieces), len(later)
    got = pl.pallas_call(
        functools.partial(start_kernel, count, n, ahead),
        out_shape=[like((RANKS, rows, width))]
        + [like(full_shape(count, p.shape[1:])) for p in pieces]
        + [like((2, 2) + p.shape[1:]) for p in later],
        in_specs=[AN] * (1 + n + ahead),
        out_specs=[AN] * (1 + n + ahead),
        scratch_shapes=[pltpu.VMEM((RANKS, rows, width), BF16)]
        + [pltpu.VMEM((2, 2) + p.shape[1:], BF16) for p in pieces]
        + sems(count),
        compiler_params=params(1),
        name="start",
    )(tokens, *pieces, *later)
    return got[0], [f.reshape(-1, f.shape[-1]) for f in got[1 : n + 1]], got[n + 1 :]


def call_body(count, o, h, gain, weights, down, extra):
    rows, width = h.shape
    tall = RANKS * rows
    wo, wgate, wup = weights
    hidden = wgate.shape[1]
    more = len(extra) - 1
    blocks = extra[1:]
    three = pltpu.VMEM((3, rows, width), BF16)
    four = pltpu.VMEM((RANKS, rows, width), BF16)
    wd_shape = (count, 2, 2) + down.shape
    got = pl.pallas_call(
        functools.partial(body_kernel, count, rows, more),
        out_shape=[
            like((rows, width), F32),
            like((rows, width), F32),
            like((tall, hidden), F32),
            like((tall, hidden), F32),
            like((tall, hidden)),
            like((RANKS, rows, width)),
            like(wd_shape),
        ]
        + (
            [like((RANKS, rows, width))] + [like(full_shape(count, b.shape[2:])) for b in blocks]
            if more
            else [like(extra[0].shape)]
        ),
        in_specs=[VM, VM, VM, AN, AN, AN, AN] + ([VM] + [AN] * more if more else [AN]),
        out_specs=[VM] * 5 + [AN] * 2 + [AN] * (1 + more),
        scratch_shapes=[
            pltpu.VMEM(wo.shape, BF16),
            pltpu.VMEM((width, 2 * hidden), BF16),
            pltpu.VMEM(wd_shape, BF16),
            three,
            three,
            four,
            three,
            three,
        ]
        + ([four] if more else [])
        + sems(count),
        compiler_params=params(2 if more else 3),
        name="body_more" if more else "body",
    )(o, h, gain, wo, wgate, wup, down, *extra)
    got = list(got)
    got[6] = got[6].reshape(-1, width)
    return got[:7], got[7], [f.reshape(-1, f.shape[-1]) for f in got[8:]]


def call_back(count, start, rest, parts):
    first, last = len(start) == 2, len(rest) == 1
    rows, width = start[0].shape if first else start[2].shape
    tall = RANKS * rows
    three = pltpu.VMEM((3, rows, width), BF16)
    four = pltpu.VMEM((RANKS, rows, width), BF16)
    in_specs = [VM, AN] if first else [VM, AN, VM, VM, VM]
    in_specs += [VM] if last else [AN, AN, AN, AN, VM, VM, VM, VM]
    n_red = len(parts)
    in_specs += [AN] * n_red
    outs, out_specs, scratch = [], [], []
    if first:
        outs, out_specs = [like(start[1].shape, start[1].dtype)], [AN]
    elif not last:
        outs, out_specs = [like((rows, width), F32), like((1, width), F32)], [VM, VM]
    else:
        outs, out_specs = [like((rows, width)), like((16, GAIN_COLS), F32)], [AN, VM]
    if not first:
        scratch += [pltpu.VMEM((width, start[0].shape[1]), BF16), three, three]
    if last:
        gains_shape = full_shape(count, (16, GAIN_COLS))
        scratch += [
            pltpu.VMEM((rows, width), F32),
            pltpu.VMEM((rows, width), BF16),
            pltpu.VMEM((16, width), F32),
            pltpu.VMEM(gains_shape, BF16),
        ]
        scratch += Reduce.scratch(gains_shape)
    else:
        wd, wgate, wup, wo = rest[:4]
        hidden = wgate.shape[1]
        outs += [
            like((RANKS, rows, width)),
            like((tall, 2 * hidden)),
            like((rows, width), F32),
            like((1, width), F32),
            like((RANKS, rows, width)),
            like((tall, wo.shape[1])),
        ]
        out_specs += [AN, VM, VM, VM, AN, VM]
        scratch += [pltpu.VMEM(s, BF16) for s in (wd.shape, (width, 2 * hidden), wo.shape)]
        scratch += [four, three, three, four]
    for i, part in enumerate(parts):
        scratch += Reduce.scratch(part.shape, ranks=i > 0)
        tail = part.shape[-2:]
        outs.append(like(tail if i == 0 else (RANKS,) + tail, F32))
        out_specs.append(VM)
    return pl.pallas_call(
        functools.partial(back_kernel, count, rows, first, last, n_red),
        out_shape=outs,
        in_specs=in_specs,
        out_specs=out_specs,
        scratch_shapes=scratch + sems(count),
        compiler_params=params(4 if first else (6 if last else 5)),
        name="back_first" if first else ("back_last" if last else "back_mid"),
    )(*start, *rest, *parts)


def dot_t(a, b):
    return lax.dot_general(a, b, (((0,), (0,)), ((), ())), preferred_element_type=F32).astype(BF16)


def shards(dp_size, ctx_size, tokens, cotangent, w_qkv, w_out, w_gate_up, w_down, gains):
    count = dp_size // 4
    rows, width = tokens.shape
    length = RANKS * rows
    hidden = w_gate_up.shape[-1] // RANKS
    positions = jnp.arange(length, dtype=jnp.int32)
    cosine, sine_tab = rotary_tables(positions, HEAD_DIM)
    causal = positions[None, :] <= positions[:, None]
    tall = lambda value: value.reshape(length, width)
    rank = lax.rem(lax.div(lax.axis_index("dp"), 2), 2) * 2 + lax.rem(lax.axis_index("ctx"), 2)

    packed = [pack_weights(w_qkv, w_out, w_gate_up, gains, count, layer) for layer in range(LAYERS)]
    all_tokens, full, blocks = call_start(count, tokens, packed[0], packed[1])
    gain_rows = full[0][:, -GAIN_COLS:][:, : 2 * LAYERS].astype(F32).T
    gain = lambda layer, which: gain_rows[2 * layer + which][None]
    h = lax.dynamic_index_in_dim(all_tokens, rank, 0, keepdims=False)
    states = tall(all_tokens).astype(F32)
    n1 = norm_rows(states, gain(0, 0))

    records = []
    swapped = None
    for layer in range(LAYERS):
        wq, wo, wgate, wup = full
        wq_now = wq[:, : wq.shape[1] - GAIN_COLS] if layer == 0 else wq
        proj = jnp.dot(tall(n1), wq_now, preferred_element_type=F32)
        mixed, saved = attend(proj, cosine, sine_tab, causal)
        if layer + 1 < LAYERS:
            extra = (gain(layer + 1, 0), *blocks)
        else:
            extra = (cotangent.astype(BF16),)
        got, ahead, full = call_body(
            count, mixed, h, gain(layer, 1), (wo, wgate, wup), w_down[layer], extra
        )
        h1, h_next, gate, up, u, n2, wd = got
        records.append((h, n1, saved, mixed, h1, n2, gate, up, u, (wq, wo, wgate, wup, wd)))
        h = h_next
        if layer + 1 < LAYERS:
            n1 = ahead
        else:
            g = ahead

    shape7 = lambda value: value.reshape(count, 2, 2, 2, 2, -1, value.shape[-1])
    start, parts = (g, h.astype(BF16)), []
    grads = [None] * LAYERS
    gain_grads = [None] * (2 * LAYERS)
    for layer in reversed(range(LAYERS)):
        h_in, n1, saved, mixed, h1, n2, gate, up, u, (wq, wo, wgate, wup, wd) = records[layer]
        got = call_back(count, start, (wd, wgate, wup, wo, gate, up, h1, gain(layer, 1)), parts)
        if layer == LAYERS - 1:
            out_act, *got = got
        else:
            _, gain_grads[2 * layer + 2], *got = got
            grads[layer + 1] = got[6:]
        gbg, dgu, gh, gain_grads[2 * layer + 1], ghg, do = got[:6]
        dqkv = attend_back(saved, mixed, do, cosine, sine_tab, causal)
        parts = [
            dot_t(u, tall(gbg)).reshape(count, 2, 2, -1, width),
            shape7(dot_t(tall(n2), dgu[:, :hidden])),
            shape7(dot_t(tall(n2), dgu[:, hidden:])),
            shape7(dot_t(tall(ghg), mixed)),
            shape7(dot_t(tall(n1), dqkv)),
        ]
        start = (dqkv, wq, gh, h_in, gain(layer, 0))
    others = jnp.concatenate([jnp.zeros((1, width), F32)] + gain_grads[1:], axis=0)
    others = jnp.pad(others, ((0, 16 - 2 * LAYERS), (0, 0)))
    grad_tokens, gains_sum, *last = call_back(count, start, (others,), parts)
    grads[0] = last
    piece = gains.shape[-1]
    grad_gains = gains_sum[: 2 * LAYERS, :piece].reshape(LAYERS, 2, piece)
    stacked = [unpack_grads(q, o, gate, up, count) for _, gate, up, o, q in grads]
    s_qkv, s_out, s_gu = (jnp.stack([s[i] for s in stacked]) for i in range(3))
    s_down = jnp.stack([g[0] for g in grads])
    return (out_act.astype(F32), grad_tokens.astype(F32), s_qkv, s_out, s_gu, s_down, grad_gains)


def solution(mesh):
    both = ("dp", "ctx")
    return jax.shard_map(
        functools.partial(shards, mesh.shape["dp"], mesh.shape["ctx"]),
        mesh=mesh,
        in_specs=(
            P(both, None),
            P(both, None),
            P(None, both, None),
            P(None, None, both),
            P(None, both, None, None),
            P(None, both, None),
            P(None, None, both),
        ),
        out_specs=(
            P(both, None),
            P(both, None),
            P(None, both, None),
            P(None, None, both),
            P(None, both, None, None),
            P(None, both, None),
            P(None, None, both),
        ),
        check_vma=False,
    )
```

```python
import functools

import jax
import jax.numpy as jnp
import numpy as np
from jax import lax
from jax.experimental import pallas as pl
from jax.experimental.pallas import tpu as pltpu
from jax.sharding import PartitionSpec as P

HEADS = 16
KV_HEADS = 8
HEAD_DIM = 96
LAYERS = 2
RANKS = 4
GAIN_COLS = 128

NORM_EPS = 1e-05
ROPE_BASE = 100000.0
MASKED = -1e30
MESH = pl.DeviceIdType.MESH
BF16 = jnp.bfloat16
F32 = jnp.float32
VMEM_BYTES = 62 * 1024 * 1024


class Place:
    def __init__(self, count):
        self.count = count
        self.dp = lax.axis_index("dp")
        self.ctx = lax.axis_index("ctx")
        self.core = lax.rem(self.dp, 2)
        self.x = lax.rem(lax.div(self.dp, 2), 2)
        self.a = lax.div(self.dp, 4)
        self.zh = lax.div(self.ctx, 2)
        self.zl = lax.rem(self.ctx, 2)
        self.rank = self.x * 2 + self.zl
        dpx = self.dp + 2 - 4 * self.x
        ctz = self.ctx + 1 - 2 * self.zl
        x2, z2 = 1 - self.x, 1 - self.zl
        self.peers = (
            ((dpx, self.ctx), x2 * 2 + self.zl),
            ((self.dp, ctz), self.x * 2 + z2),
            ((dpx, ctz), x2 * 2 + z2),
        )
        self.core_peer = (self.dp + 1 - 2 * self.core, self.ctx)
        self.zh_peer = (self.dp, self.ctx + 2 - 4 * self.zh)
        self.others = []
        for k in range(1, count):
            ahead = lax.rem(self.a + k, count)
            behind = lax.rem(self.a + count - k, count)
            self.others.append(((self.dp + (ahead - self.a) * 4, self.ctx), ahead, behind))
        self.moves = self.x != self.zh
        self.swap_peer = (self.dp + (self.zh - self.x) * 2, self.ctx + (self.x - self.zh) * 2)

    def greet(self, weights, swap):
        devices = [d for d, _ in self.peers]
        if weights:
            devices += [self.core_peer, self.zh_peer] + [o[0] for o in self.others]
        barrier = pltpu.get_barrier_semaphore()
        for device in devices:
            pl.semaphore_signal(barrier, inc=1, device_id=device, device_id_type=MESH)
        if swap:

            @pl.when(self.moves)
            def _():
                pl.semaphore_signal(barrier, inc=1, device_id=self.swap_peer, device_id_type=MESH)

        expected = len(devices)
        if swap:
            expected = expected + self.x + self.zh - 2 * self.x * self.zh
        pl.semaphore_wait(barrier, expected)


class Net:
    def __init__(self, place, send, recv, local):
        self.place, self.send, self.recv, self.local = place, send, recv, local
        self.n, self.m = 0, 0
        self.sends = []

    def remote(self, src, dst, device):
        copy = self.prepare(src, dst, device)
        copy.start()
        self.sends.append(copy)
        return copy

    def prepare(self, src, dst, device):
        i = self.n
        self.n += 1
        return pltpu.make_async_remote_copy(
            src_ref=src, dst_ref=dst, send_sem=self.send.at[i], recv_sem=self.recv.at[i],
            device_id=device, device_id_type=MESH,
        )

    def here(self, src, dst):
        i = self.m
        self.m += 1
        copy = pltpu.make_async_copy(src, dst, self.local.at[i])
        copy.start()
        return copy

    def finish(self):
        for copy in self.sends:
            copy.wait_send()


REMOTE_SEMS, LOCAL_SEMS = 128, 32


def sems(count=2):
    n = REMOTE_SEMS * max(1, count // 2)
    return [
        pltpu.SemaphoreType.DMA((n,)),
        pltpu.SemaphoreType.DMA((n,)),
        pltpu.SemaphoreType.DMA((LOCAL_SEMS,)),
    ]


class Swap:
    def __init__(self, net, src, dst):
        self.net, self.src, self.dst = net, src, dst

    def start(self):
        net, place = self.net, self.net.place
        self.copy = net.prepare(self.src, self.dst, place.swap_peer)
        self.stay = pltpu.make_async_copy(self.src, self.dst, net.local.at[net.m])
        net.m += 1

        @pl.when(place.moves)
        def _():
            self.copy.start()

        @pl.when(jnp.logical_not(place.moves))
        def _():
            self.stay.start()

    def wait(self):
        @pl.when(self.net.place.moves)
        def _():
            self.copy.wait_recv()
            self.copy.wait_send()

        @pl.when(jnp.logical_not(self.net.place.moves))
        def _():
            self.stay.wait()


class Share:
    def __init__(self, net, piece, block):
        self.net, self.piece, self.block = net, piece, block

    def start(self):
        net, place = self.net, self.net.place
        mine = self.block.at[place.x, place.zl]
        self.copies = [net.remote(self.piece.at[rank], mine, device) for device, rank in place.peers]
        self.own = net.here(self.piece.at[place.rank], mine)

    def wait(self):
        for copy in self.copies:
            copy.wait_recv()
        self.own.wait()


class Gather:
    def __init__(self, net, block, full, ranks=True):
        self.net, self.block, self.full, self.ranks = net, block, full, ranks

    def slot(self, a, core, zh):
        if self.ranks:
            return self.full.at[a, :, core, zh, :]
        return self.full.at[a, core, zh]

    def column(self, a, core):
        if self.ranks:
            return self.full.at[a, :, core, :, :]
        return self.full.at[a, core]

    def begin(self):
        net, p = self.net, self.net.place
        mine = self.slot(p.a, p.core, p.zh)
        self.across = net.remote(self.block, mine, p.zh_peer)
        self.near = [net.remote(self.block, mine, o[0]) for o in p.others]
        self.cores = [net.remote(self.block, mine, p.core_peer)]
        self.own = net.here(self.block, mine)

    def middle(self):
        net, p = self.net, self.net.place
        self.across.wait_recv()
        got = self.slot(p.a, p.core, 1 - p.zh)
        self.far = [net.remote(got, got, o[0]) for o in p.others]
        self.cores.append(net.remote(got, got, p.core_peer))

    def final(self):
        net, p = self.net, self.net.place
        for k, other in enumerate(p.others):
            self.near[k].wait_recv()
            self.far[k].wait_recv()
            got = self.column(other[2], p.core)
            self.cores.append(net.remote(got, got, p.core_peer))

    def done(self):
        self.own.wait()
        for copy in self.cores:
            copy.wait_recv()


class Reduce:
    def __init__(self, net, part, out, held, from_core, from_a, from_zh, from_rank, ranks=True, added=False):
        self.net, self.part, self.out = net, part, out
        self.held, self.from_core, self.from_a = held, from_core, from_a
        self.from_zh, self.from_rank = from_zh, from_rank
        self.ranks, self.added = ranks, added

    def half(self, core):
        return self.part.at[:, :, core] if self.ranks else self.part.at[:, core]

    def begin(self):
        net, p = self.net, self.net.place
        self.load = net.here(self.half(p.core), self.held)
        self.by_core = net.remote(self.half(1 - p.core), self.from_core, p.core_peer)

    def along_a(self):
        net, p = self.net, self.net.place
        self.load.wait()
        self.by_core.wait_recv()
        add_into(self.held, self.from_core)
        self.by_a = [
            net.remote(self.held.at[other[1]], self.from_a.at[k], other[0])
            for k, other in enumerate(p.others)
        ]

    def along_zh(self):
        net, p = self.net, self.net.place
        mine = self.held.at[p.a]
        for k, copy in enumerate(self.by_a):
            copy.wait_recv()
            add_into(mine, self.from_a.at[k])
        there = mine.at[:, 1 - p.zh] if self.ranks else mine.at[1 - p.zh]
        self.by_zh = net.remote(there, self.from_zh, p.zh_peer)

    def among_ranks(self):
        net, p = self.net, self.net.place
        self.by_zh.wait_recv()
        if not self.ranks:
            self.out[...] = self.held[p.a, p.zh].astype(F32) + self.from_zh[...].astype(F32)
            return
        for x in range(2):
            for zl in range(2):
                add_into(self.held.at[p.a, x, p.zh, zl], self.from_zh.at[x, zl])
        self.by_rank = []
        for device, rank in p.peers:
            rank_x, rank_zl = lax.div(rank, 2), lax.rem(rank, 2)
            self.by_rank.append(
                net.remote(
                    self.held.at[p.a, rank_x, p.zh, rank_zl], self.from_rank.at[len(self.by_rank)], device
                )
            )

    def done(self):
        if not self.ranks:
            return
        p = self.net.place
        own = self.held[p.a, p.x, p.zh, p.zl].astype(F32)
        for copy in self.by_rank:
            copy.wait_recv()
        if self.added:
            for j in range(3):
                own = own + self.from_rank[j].astype(F32)
            self.out[...] = own
            return
        self.out[p.rank] = own
        for j, (_, rank) in enumerate(p.peers):
            self.out[rank] = self.from_rank[j].astype(F32)

    @staticmethod
    def scratch(shape, ranks=True):
        tail = shape[-2:]
        count = shape[0]
        inner = ((2, 2, 2) if ranks else (2,)) + tail
        fewer = ((2, 2) if ranks else ()) + tail
        shapes = [(count,) + inner, (count,) + inner, (max(count - 1, 1),) + inner, fewer]
        if ranks:
            shapes.append((3,) + tail)
        return [pltpu.VMEM(s, BF16) for s in shapes]


def add_into(target, source):
    lead = target.shape[:-2]
    total = 1
    for size in lead:
        total *= size
    if total == 1 and not lead:
        target[...] = (target[...].astype(F32) + source[...].astype(F32)).astype(BF16)
        return

    @pl.loop(0, total)
    def _(j):
        index, left = [], j
        for size in reversed(lead):
            index.append(lax.rem(left, size))
            left = lax.div(left, size)
        index = tuple(reversed(index))
        target[index] = (target[index].astype(F32) + source[index].astype(F32)).astype(BF16)


class Spread:
    def __init__(self, net, land):
        self.net, self.land = net, land
        self.peers = net.place.peers
        mine = land.at[net.place.rank]
        self.along_x = net.remote(mine, mine, self.peers[0][0])
        self.along_zl = net.remote(mine, mine, self.peers[1][0])

    def arrivals(self):
        self.along_zl.wait_recv()
        got = self.land.at[self.peers[1][1]]
        relay = self.net.remote(got, got, self.peers[0][0])
        yield 1, self.peers[1][1]
        self.along_x.wait_recv()
        yield 0, self.peers[0][1]
        relay.wait_recv()
        yield 2, self.peers[2][1]

    def wait(self):
        for _ in self.arrivals():
            pass


class Sum:
    def __init__(self, net, out, land):
        self.net, self.out, self.land = net, out, land
        self.peers = net.place.peers

    def ready(self, i):
        if i == 2:
            self.diagonal = self.net.remote(self.out.at[2], self.land.at[0], self.peers[0][0])
        elif i == 0:
            self.along_x = self.net.remote(self.out.at[0], self.land.at[1], self.peers[0][0])

    def forward(self):
        self.diagonal.wait_recv()
        add_into(self.out.at[1], self.land.at[0])
        self.along_zl = self.net.remote(self.out.at[1], self.land.at[2], self.peers[1][0])

    def result(self, own):
        self.along_x.wait_recv()
        self.along_zl.wait_recv()
        return own + self.land[1].astype(F32) + self.land[2].astype(F32)


def products(x, w_ref, count, tile, transposed, use):
    def part(cols):
        if transposed:
            w, dims = w_ref[cols, :], (((1,), (1,)), ((), ()))
        else:
            w, dims = w_ref[:, cols], (((1,), (0,)), ((), ()))
        use(cols, lax.dot_general(x(), w, dims, preferred_element_type=F32))

    for j in range(count // tile):
        part(pl.ds(j * tile, tile))


def norm_rows(h, gain):
    factor = lax.rsqrt(jnp.mean(h * h, axis=-1, keepdims=True) + NORM_EPS)
    return (h * factor * gain).astype(BF16)


def norm_rows_back(h, gain, grad):
    factor = lax.rsqrt(jnp.mean(h * h, axis=-1, keepdims=True) + NORM_EPS)
    z = grad * gain
    inner = jnp.sum(z * h, axis=-1, keepdims=True)
    back = factor * z - h * (factor * factor * factor * inner / h.shape[-1])
    return back, jnp.sum(grad * h * factor, axis=0, keepdims=True)


def rows_of(rank, rows):
    return pl.ds(pl.multiple_of(rank * rows, rows), rows)


class Refs:
    def __init__(self, refs):
        self.refs = list(refs)

    def take(self, n):
        got, self.refs = self.refs[:n], self.refs[n:]
        return got


class Ticks:
    def __init__(self, plan):
        self.plan = list(plan)

    def __call__(self):
        if self.plan:
            for step in self.plan.pop(0):
                step()

    def rest(self):
        while self.plan:
            self()


def wide_tables(length):
    steps = np.arange(HEAD_DIM // 2, dtype=np.float32)
    inverse = np.exp(steps * np.float32(-2.0 * np.log(ROPE_BASE) / HEAD_DIM)).astype(np.float32)
    angles = np.arange(length, dtype=np.float32)[:, None] * inverse[None, :]
    cosine, sine = np.cos(angles), np.sin(angles)
    turned = (HEADS + KV_HEADS) // RANKS
    still = KV_HEADS // RANKS * HEAD_DIM
    cos_all = np.concatenate([cosine] * (2 * turned) + [np.ones((length, still))], axis=1)
    sin_all = np.concatenate([-sine, sine] * turned + [np.zeros((length, still))], axis=1)
    return jnp.asarray(cos_all, F32), jnp.asarray(sin_all, F32)


def turn(values, cosine, sine):
    cols = values.shape[1]
    half = HEAD_DIM // 2
    lane = lax.broadcasted_iota(jnp.int32, values.shape, 1)
    other = jnp.where(
        lax.rem(lane, HEAD_DIM) < half,
        pltpu.roll(values, cols - half, 1),
        pltpu.roll(values, half, 1),
    )
    return values * cosine + other * sine


def head_window(values, h):
    offset = HEAD_DIM * h
    start = offset // 128 * 128
    size = 128 if offset - start + HEAD_DIM <= 128 else 256
    window = values[:, start : start + size]
    if offset > start:
        window = pltpu.roll(window, size - (offset - start), 1)
    window = window[:, :128]
    lane = lax.broadcasted_iota(jnp.int32, window.shape, 1)
    return jnp.where(lane < HEAD_DIM, window, 0.0)


def heads_joined(parts):
    rows = parts[0].shape[0]
    columns = [jnp.zeros((rows, 128), F32) for _ in range(len(parts) * HEAD_DIM // 128 + 1)]
    for h, part in enumerate(parts):
        offset = HEAD_DIM * h
        first = offset // 128
        shift = offset - first * 128
        if shift == 0:
            columns[first] = columns[first] + part
            continue
        double = jnp.concatenate([part, jnp.zeros((rows, 128), F32)], axis=1)
        double = pltpu.roll(double, shift, 1)
        columns[first] = columns[first] + double[:, :128]
        columns[first + 1] = columns[first + 1] + double[:, 128:]
    return jnp.concatenate(columns[:-1], axis=1)


def project_heads(rows, n1, wq, cos_ref, sin_ref, qkv_ref, heads):
    count = heads.shape[0]

    @pl.loop(0, RANKS)
    def _(b):
        span = rows_of(b, rows)
        y = jnp.dot(n1[b], wq[...], preferred_element_type=F32)
        y = turn(y, cos_ref[span, :], sin_ref[span, :])
        qkv_ref[span, :] = y.astype(BF16)
        for h in range(count):
            heads[h, span, :] = head_window(y, h).astype(BF16)


def causal_scores(rows, rank, query, key):
    scores = lax.dot_general(query, key, (((1,), (1,)), ((), ())), preferred_element_type=F32)
    row = lax.broadcasted_iota(jnp.int32, scores.shape, 0) + rank * rows
    col = lax.broadcasted_iota(jnp.int32, scores.shape, 1)
    return jnp.where(col <= row, scores * HEAD_DIM ** (-0.5), MASKED)


def attend_rows(rows, rank, heads, o_ref, lse_ref):
    span = rows_of(rank, rows)
    queries = HEADS // RANKS
    pairs = KV_HEADS // RANKS
    groups = HEADS // KV_HEADS
    mixed = []
    lane = lax.broadcasted_iota(jnp.int32, (rows, 128), 1)
    lse_all = jnp.zeros((rows, 128), F32)
    for h in range(queries):
        kv = h // groups
        scores = causal_scores(rows, rank, heads[h, span, :], heads[queries + kv])
        highest = jnp.max(scores, axis=-1, keepdims=True)
        weights = jnp.exp(scores - highest)
        total = jnp.sum(weights, axis=-1, keepdims=True)
        lse = highest + jnp.log(total)
        lse_all = jnp.where(lane == h, lse, lse_all)
        weights = (weights * (1.0 / total)).astype(BF16)
        mixed.append(
            jnp.dot(weights, heads[queries + pairs + kv], preferred_element_type=F32)
        )
    lse_ref[span, :] = lse_all
    o_ref[span, :] = heads_joined(mixed).astype(BF16)


def start_kernel(count, n, ahead, n_down, *refs):
    refs = Refs(refs)
    (tokens,) = refs.take(1)
    pieces, later, downs = refs.take(n), refs.take(ahead), refs.take(n_down)
    (all_tokens,) = refs.take(1)
    full, blocks_later, downs_full = refs.take(n), refs.take(ahead), refs.take(n_down)
    (land,) = refs.take(1)
    blocks = refs.take(n)
    send, recv, local = refs.take(3)
    place = Place(count)
    net = Net(place, send, recv, local)
    shares = [Share(net, pieces[i], blocks[i]) for i in range(n)]
    shares_later = [Share(net, later[i], blocks_later[i]) for i in range(ahead)]
    gathers = [Gather(net, blocks[i], full[i]) for i in range(n)]
    gathers += [Gather(net, downs[i], downs_full[i], ranks=False) for i in range(n_down)]
    swap = Swap(net, tokens, land.at[place.zh * 2 + place.zl])
    place.greet(True, True)
    shares[0].start()
    swap.start()
    for share in shares[1:]:
        share.start()
    for i in range(2):
        shares[i].wait()
        gathers[i].begin()
    swap.wait()
    spreads = Spread(net, land)
    for i in range(2, len(gathers)):
        if i < n:
            shares[i].wait()
        gathers[i].begin()
    arrivals = spreads.arrivals()
    next(arrivals)
    for share in shares_later:
        share.start()
    gathers[0].middle()
    gathers[1].middle()
    for _ in arrivals:
        pass
    keep = net.here(land, all_tokens)
    gathers[0].final()
    for i in range(2, len(gathers)):
        gathers[i].middle()
        gathers[i - 1].final()
    gathers[-1].final()
    for gather in gathers:
        gather.done()
    for share in shares_later:
        share.wait()
    keep.wait()
    net.finish()


def body_kernel(count, rows, late, n_next, plan, *refs):
    refs = Refs(refs)
    n1_hbm, wq_hbm, cos_ref, sin_ref, h_ref, gain_ref, wo_hbm = refs.take(7)
    inner_hbm = refs.take(3)
    if n_next:
        (gain_next,) = refs.take(1)
        blocks = refs.take(n_next)
    else:
        (swap_src,) = refs.take(1)
    qkv_ref, o_ref, lse_ref, h1_ref, hn_ref, gate_ref, up_ref, u_ref, ng_hbm = refs.take(9)
    late_out = [refs.take(1)[0] if late[i] else None for i in range(3)]
    if n_next:
        (nn_hbm,) = refs.take(1)
        full = refs.take(n_next)
    else:
        (swap_dst,) = refs.take(1)
    n1, wq, heads, wo = refs.take(4)
    inner = refs.take(3)
    out_a, land_a, land_n, out_b, land_b = refs.take(5)
    if n_next:
        (land_q,) = refs.take(1)
    send, recv, local = refs.take(3)

    place = Place(count)
    net = Net(place, send, recv, local)
    width = h_ref.shape[1]
    hidden = u_ref.shape[1]
    load_q = net.here(wq_hbm.at[:, pl.ds(0, wq.shape[1])], wq)
    load_n = net.here(n1_hbm, n1)
    load_out = net.here(wo_hbm, wo)
    jobs = {}
    loads, weights = [], []
    for i in range(3):
        if late[i]:
            jobs[("gate", "up", "down")[i]] = Gather(net, inner_hbm[i], inner[i], ranks=i < 2)
            loads.append(None)
        else:
            loads.append(net.here(inner_hbm[i], inner[i]))
        weights.append(inner[i].reshape((hidden, width) if i == 2 else (width, hidden)) if late[i] else inner[i])
    wg, wu, wd = weights
    for i in range(n_next):
        jobs[i] = Gather(net, blocks[i], full[i])
    if not n_next:
        jobs["swap"] = Swap(net, swap_src, swap_dst)
    peers = place.peers
    place.greet(True, not n_next)
    keeps = []

    def ready(i):
        if late[i]:
            jobs[("gate", "up", "down")[i]].done()
            keeps.append(net.here(inner[i], late_out[i]))
        else:
            loads[i].wait()

    tick = Ticks(plan(jobs))
    tick()

    load_q.wait()
    load_n.wait()
    project_heads(rows, n1, wq, cos_ref, sin_ref, qkv_ref, heads)
    load_out.wait()
    sums = Sum(net, out_a, land_a)
    for i in (2, 0, 1):
        attend_rows(rows, peers[i][1], heads, o_ref, lse_ref)
        span = rows_of(peers[i][1], rows)

        def use(cols, y, i=i):
            out_a[i, :, cols] = y.astype(BF16)

        products(lambda: o_ref[span, :], wo, width, width, True, use)
        sums.ready(i)
    attend_rows(rows, place.rank, heads, o_ref, lse_ref)
    span = rows_of(place.rank, rows)

    def use_own(cols, y):
        h1_ref[:, cols] = h_ref[:, cols].astype(F32) + y

    products(lambda: o_ref[span, :], wo, width, width, True, use_own)
    sums.forward()
    tick()
    h1 = sums.result(h1_ref[...])
    h1_ref[...] = h1
    land_n[place.rank] = norm_rows(h1, gain_ref[...])
    gather = Spread(net, land_n)
    tick()
    ready(0)
    ready(1)

    def inner_block(rank):
        span = rows_of(rank, rows)

        gate = jnp.dot(land_n[rank], wg[...], preferred_element_type=F32)
        up = jnp.dot(land_n[rank], wu[...], preferred_element_type=F32)
        gate_ref[span, :] = gate
        up_ref[span, :] = up
        u_ref[span, :] = (gate / (1.0 + jnp.exp(-gate)) * up).astype(BF16)

        return span

    inner_block(place.rank)
    tick()
    second = Sum(net, out_b, land_b)
    for i, rank in gather.arrivals():
        span = inner_block(rank)
        if i == 1:
            tick()
            ready(2)

        def use(cols, y, i=i):
            out_b[i, :, cols] = y.astype(BF16)

        products(lambda: u_ref[span, :], wd, width, width, False, use)
        second.ready(i)
        tick()
    keep = net.here(land_n, ng_hbm)
    span = rows_of(place.rank, rows)

    def use_down(cols, y):
        hn_ref[:, cols] = h1_ref[:, cols] + y

    products(lambda: u_ref[span, :], wd, width, width, False, use_down)
    second.forward()
    tick()
    hn = second.result(hn_ref[...])
    hn_ref[...] = hn
    if n_next:
        land_q[place.rank] = norm_rows(hn, gain_next[...])
        third = Spread(net, land_q)
        tick()
        for _ in third.arrivals():
            tick()
        keep_next = net.here(land_q, nn_hbm)
        keep_next.wait()
    tick.rest()
    for i in range(n_next):
        jobs[i].done()
    if not n_next:
        jobs["swap"].wait()
    keep.wait()
    for copy in keeps:
        copy.wait()
    net.finish()


def plan_late(j):
    gate, down = j["gate"], j["down"]
    return [
        [gate.begin],
        [gate.middle, down.begin],
        [gate.final],
        [down.middle, j[0].begin, j[1].begin],
        [down.final],
        [],
        [],
        [j[0].middle],
        [j[0].final, j[1].middle],
        [j[2].begin, j[1].final],
        [],
        [],
        [j[2].middle],
        [j[2].final],
    ]


def plan_late_end(j):
    up, down = j["up"], j["down"]
    return [
        [up.begin],
        [up.middle, down.begin],
        [up.final],
        [down.middle],
        [down.final],
        [],
        [],
        [j["swap"].start],
    ]


def plan_early(j):
    return [
        [j[0].begin],
        [j[1].begin],
        [j[0].middle, j[1].middle, j[2].begin],
        [],
        [j[0].final],
        [j[1].final],
        [j[2].middle],
        [],
        [j[3].begin, j[2].final],
        [],
        [],
        [],
        [j[3].middle],
        [j[3].final],
    ]


def plan_end(j):
    down = j["down"]
    return [
        [down.begin],
        [],
        [down.middle],
        [],
        [down.final],
        [],
        [],
        [j["swap"].start],
    ]


def back_kernel(count, rows, first, last, n_red, *refs):
    refs = Refs(refs)
    if first:
        (g_ref,) = refs.take(1)
    else:
        dqkv_ref, wq_hbm, ghin_ref, hin_ref, gainin_ref = refs.take(5)
    if not last:
        wd_hbm, wgate_hbm, wup_hbm, wo_hbm, gate_ref, up_ref, h1_ref, gain_ref = refs.take(8)
    else:
        (other_gains,) = refs.take(1)
    parts = refs.take(n_red)
    if last:
        swap_dst, gains_out = refs.take(2)
    elif not first:
        gnew_ref, ggin_ref = refs.take(2)
    if not last:
        gbg_hbm, dgu_ref, gh_ref, gg_ref, ghg_hbm, do_ref = refs.take(6)
    red_out = refs.take(n_red)
    if not first:
        wq, out_a, land_a = refs.take(3)
    if last:
        gnew_ref, gsend_ref, gains_all, gains_part = refs.take(4)
        gains_scratch = refs.take(5)
    if not last:
        wd, wgu, wo, land_g, out_b, land_b, land_h = refs.take(7)
    red_scratch = [refs.take(4 if i == 0 else 5) for i in range(n_red)]
    send, recv, local = refs.take(3)

    place = Place(count)
    net = Net(place, send, recv, local)
    jobs = []
    for i in range(n_red):
        scratch = red_scratch[i] + ([None] if i == 0 else [])
        jobs.append(Reduce(net, parts[i], red_out[i], *scratch, ranks=i > 0))
    peers = place.peers
    if not first:
        load_q = net.here(wq_hbm.at[:, pl.ds(0, wq.shape[1])], wq)
    if not last:
        hidden = wd.shape[0]
        load_down = net.here(wd_hbm, wd)
        load_gate = net.here(wgate_hbm, wgu.at[:, pl.ds(0, hidden)])
        load_up = net.here(wup_hbm, wgu.at[:, pl.ds(hidden, hidden)])
        load_out = net.here(wo_hbm, wo)
    place.greet(n_red > 0, last)
    if first:
        tick = Ticks([])
    elif not last:
        j = jobs
        tick = Ticks(
            [
                [j[0].begin, j[1].begin],
                [j[0].along_a, j[2].begin],
                [j[1].along_a, j[3].begin],
                [j[0].along_zh, j[4].begin],
                [],
                [j[2].along_a],
                [j[1].along_zh],
                [j[0].among_ranks, j[3].along_a],
                [j[2].along_zh],
                [j[1].among_ranks, j[4].along_a],
                [j[3].along_zh],
                [j[2].among_ranks, j[4].along_zh],
                [j[1].done, j[2].done, j[3].among_ranks, j[4].among_ranks],
                [j[3].done, j[4].done],
            ]
        )
    else:
        j = jobs
        tick = Ticks(
            [
                [j[0].begin, j[1].begin, j[2].begin],
                [j[0].along_a, j[3].begin, j[4].begin],
            ]
        )
    tick()
    own = rows_of(place.rank, rows)
    if not first:
        load_q.wait()
        width = ghin_ref.shape[1]
        total = Sum(net, out_a, land_a)
        for i in (2, 0, 1):
            span = rows_of(peers[i][1], rows)

            def use(cols, y, i=i):
                out_a[i, :, cols] = y.astype(BF16)

            products(lambda: dqkv_ref[span, :], wq, width, width, True, use)
            total.ready(i)

        def use_own(cols, y):
            gnew_ref[:, cols] = y

        products(lambda: dqkv_ref[own, :], wq, width, width, True, use_own)
        total.forward()
        tick()
        dn = total.result(gnew_ref[...])
        back, ggain = norm_rows_back(hin_ref[...].astype(F32), gainin_ref[...], dn)
        gnew_ref[...] = ghin_ref[...] + back
        if last:
            finish_last(
                place, net, jobs, gnew_ref, gsend_ref, ggain, other_gains, gains_all, gains_part, gains_scratch,
                gains_out, swap_dst,
            )
            return
        ggin_ref[...] = ggain
        g_ref = gnew_ref
    width = g_ref.shape[1]
    land_g[place.rank] = g_ref[...].astype(BF16)
    gather = Spread(net, land_g)
    tick()
    load_down.wait()
    load_gate.wait()
    load_up.wait()

    def inner_block(rank):
        span = rows_of(rank, rows)

        du = lax.dot_general(land_g[rank], wd[...], (((1,), (1,)), ((), ())), preferred_element_type=F32)
        gate, up = gate_ref[span, :], up_ref[span, :]
        sg = 1.0 / (1.0 + jnp.exp(-gate))
        dgu_ref[span, pl.ds(0, hidden)] = (du * up * sg * (1.0 + gate * (1.0 - sg))).astype(BF16)
        dgu_ref[span, pl.ds(hidden, hidden)] = (du * gate * sg).astype(BF16)

        return span

    span = inner_block(place.rank)

    def use_mid(cols, y):
        gh_ref[:, cols] = y

    products(lambda: dgu_ref[span, :], wgu, width, width, True, use_mid)
    tick()
    second = Sum(net, out_b, land_b)
    for i, rank in gather.arrivals():
        span = inner_block(rank)

        def use(cols, y, i=i):
            out_b[i, :, cols] = y.astype(BF16)

        products(lambda: dgu_ref[span, :], wgu, width, width, True, use)
        second.ready(i)
        tick()
    keep = net.here(land_g, gbg_hbm)
    second.forward()
    dn = second.result(gh_ref[...])
    back, ggain = norm_rows_back(h1_ref[...], gain_ref[...], dn)
    gh = g_ref[...].astype(F32) + back
    gh_ref[...] = gh
    gg_ref[...] = ggain
    land_h[place.rank] = gh.astype(BF16)
    third = Spread(net, land_h)
    tick()
    load_out.wait()

    def out_block(rank):
        span = rows_of(rank, rows)

        def use(cols, y):
            do_ref[span, cols] = y.astype(BF16)

        products(lambda: land_h[rank], wo, wo.shape[1], wo.shape[1], False, use)

    out_block(place.rank)
    for _, rank in third.arrivals():
        tick()
        out_block(rank)
    keep_h = net.here(land_h, ghg_hbm)
    tick.rest()
    keep_h.wait()
    keep.wait()
    net.finish()


def finish_last(place, net, jobs, gnew_ref, gsend_ref, ggain, other_gains, gains_all, gains_part, scratch, gains_out, swap_dst):
    gsend_ref[...] = gnew_ref[...].astype(BF16)
    swap = Swap(net, gsend_ref, swap_dst)
    swap.start()
    gains_all[...] = other_gains[...]
    gains_all[0:1, :] = ggain
    gains_part[...] = jnp.zeros(gains_part.shape, BF16)
    count = gains_part.shape[0]
    piece = gains_all.shape[1] // (16 * count)
    for block in range(16 * count):
        index = (block // 16, block // 8 % 2, block // 4 % 2, block // 2 % 2, block % 2)
        gains_part[index + (slice(None), slice(0, piece))] = gains_all[
            :, block * piece : (block + 1) * piece
        ].astype(BF16)
    small = Reduce(net, gains_part, gains_out, *scratch, added=True)
    small.begin()
    j = jobs
    j[1].along_a()
    j[0].along_zh()
    small.along_a()
    j[2].along_a()
    j[1].along_zh()
    small.along_zh()
    j[0].among_ranks()
    j[3].along_a()
    j[2].along_zh()
    small.among_ranks()
    j[1].among_ranks()
    j[4].along_a()
    j[3].along_zh()
    j[2].among_ranks()
    j[1].done()
    j[4].along_zh()
    j[3].among_ranks()
    j[2].done()
    small.done()
    j[4].among_ranks()
    j[3].done()
    j[4].done()
    swap.wait()
    net.finish()


def pack_weights(w_qkv, w_out, w_gate_up, gains, count, layer):
    rows = w_qkv.shape[1]
    attn_cols = HEADS * HEAD_DIM
    kv_cols = KV_HEADS * HEAD_DIM
    qkv = w_qkv[layer]
    q = qkv[:, :attn_cols].reshape(rows, RANKS, -1)
    k = qkv[:, attn_cols : attn_cols + kv_cols].reshape(rows, RANKS, -1)
    v = qkv[:, attn_cols + kv_cols :].reshape(rows, RANKS, -1)
    columns = [q, k, v]
    if layer == 0:
        scales = jnp.pad(gains.reshape(2 * LAYERS, rows).T, ((0, 0), (0, GAIN_COLS - 2 * LAYERS)))
        columns.append(jnp.broadcast_to(scales[:, None], (rows, RANKS, GAIN_COLS)))
    head = jnp.concatenate(columns, axis=2).transpose(1, 0, 2)
    out = w_out[layer].T.reshape(rows, RANKS, -1).transpose(1, 0, 2)
    gu = w_gate_up[layer].reshape(rows, 2, count, 2, 2, 2, 2, -1)
    gu = gu.transpose(1, 3, 6, 0, 2, 4, 5, 7).reshape(2, RANKS, rows, -1)
    return head, out, gu[0], gu[1]


def unpack_grads(head, out, gate, up, count):
    rows = head.shape[1]
    q_cols = HEADS * HEAD_DIM // RANKS
    kv_cols = KV_HEADS * HEAD_DIM // RANKS
    wide = lambda part: part.transpose(1, 0, 2).reshape(rows, -1)
    qkv = jnp.concatenate(
        [
            wide(head[:, :, :q_cols]),
            wide(head[:, :, q_cols : q_cols + kv_cols]),
            wide(head[:, :, q_cols + kv_cols : q_cols + 2 * kv_cols]),
        ],
        axis=1,
    )
    order = lambda part: (
        part.reshape(2, 2, rows, count, 2, 2, -1).transpose(2, 3, 0, 4, 5, 1, 6).reshape(rows, -1)
    )
    return qkv, wide(out).T, jnp.stack([order(gate), order(up)], axis=1)


def rotary_tables(positions, head_size):
    half_size = head_size // 2
    freq_index = jnp.arange(half_size).astype(F32)
    inverse = jnp.exp(freq_index * (-2.0 * jnp.log(ROPE_BASE) / head_size))
    angles = positions.astype(F32)[:, None] * inverse[None, :]
    return (jnp.cos(angles), jnp.sin(angles))


def rotate(values, cosine, sine_tab):
    half_size = values.shape[-1] // 2
    first, second = values[..., :half_size], values[..., half_size:]
    c, s = cosine[:, None, :], sine_tab[:, None, :]
    return jnp.concatenate([first * c - second * s, second * c + first * s], axis=-1)


def unrotate(grads, cosine, sine_tab):
    return rotate(grads, cosine, -sine_tab)


def saved_heads(qkv, lse):
    length = qkv.shape[0]
    kv = KV_HEADS // RANKS
    groups = HEADS // KV_HEADS
    q_cols = kv * groups * HEAD_DIM
    kv_cols = kv * HEAD_DIM
    query = qkv[:, :q_cols].reshape(length, kv, groups, HEAD_DIM)
    key = qkv[:, q_cols : q_cols + kv_cols].reshape(length, kv, HEAD_DIM)
    value = qkv[:, q_cols + kv_cols :].reshape(length, kv, HEAD_DIM)
    return query, key, value, lse[:, : kv * groups].T.reshape(kv, groups, length, 1)


def attend_back(saved, mixed, grad_mixed, cosine, sine_tab, causal):
    query, key, value, lse = saved
    length = query.shape[0]
    grad_mixed = grad_mixed.reshape(query.shape)
    mixed = mixed.reshape(query.shape)
    scale = HEAD_DIM ** (-0.5)
    scores = jnp.einsum("qkgd,skd->kgqs", query, key, preferred_element_type=F32) * scale
    scores = jnp.where(causal[None, None], scores, MASKED)
    weights = jnp.exp(scores - lse)
    grad_weights = jnp.einsum("qkgd,skd->kgqs", grad_mixed, value, preferred_element_type=F32)
    delta = jnp.sum(grad_mixed.astype(F32) * mixed.astype(F32), axis=-1)
    delta = jnp.transpose(delta, (1, 2, 0))[..., None]
    grad_scores = (weights * (grad_weights - delta) * scale).astype(BF16)
    grad_query = jnp.einsum("kgqs,skd->qkgd", grad_scores, key, preferred_element_type=F32)
    grad_key = jnp.einsum("kgqs,qkgd->skd", grad_scores, query, preferred_element_type=F32)
    grad_value = jnp.einsum(
        "kgqs,qkgd->skd", weights.astype(BF16), grad_mixed, preferred_element_type=F32
    )
    grad_query = unrotate(grad_query.reshape(length, -1, HEAD_DIM), cosine, sine_tab)
    grad_key = unrotate(grad_key, cosine, sine_tab)
    return jnp.concatenate(
        [g.reshape(length, -1) for g in (grad_query, grad_key, grad_value)], axis=1
    ).astype(BF16)


VM = pl.BlockSpec(memory_space=pltpu.VMEM)
AN = pl.BlockSpec(memory_space=pl.ANY)


def params(collective_id):
    return pltpu.CompilerParams(
        collective_id=collective_id, has_side_effects=True, vmem_limit_bytes=VMEM_BYTES
    )


def like(shape, dtype=BF16):
    return jax.ShapeDtypeStruct(tuple(shape), dtype)


def full_shape(count, tail):
    return (count, 2, 2, 2, 2) + tuple(tail)


def call_start(count, tokens, pieces, later, downs):
    rows, width = tokens.shape
    n, ahead, n_down = len(pieces), len(later), len(downs)
    outs = [like((RANKS, rows, width))]
    outs += [like(full_shape(count, p.shape[1:])) for p in pieces]
    outs += [like((2, 2) + p.shape[1:]) for p in later]
    outs += [like((count, 2, 2) + d.shape) for d in downs]
    got = pl.pallas_call(
        functools.partial(start_kernel, count, n, ahead, n_down),
        out_shape=outs,
        in_specs=[AN] * len(outs),
        out_specs=[AN] * len(outs),
        scratch_shapes=[pltpu.VMEM((RANKS, rows, width), BF16)]
        + [pltpu.VMEM((2, 2) + p.shape[1:], BF16) for p in pieces]
        + sems(count),
        compiler_params=params(1),
        name="start",
    )(tokens, *pieces, *later, *downs)
    cut = n + 1 + ahead
    return got[0], [flat(f) for f in got[1 : n + 1]], got[n + 1 : cut], [flat(d) for d in got[cut:]]


def flat(value):
    return value.reshape(-1, value.shape[-1])


def call_body(count, n1, wq, tables, h, gain, wo, inner, late, plan, gain_next=None, blocks=(), swap=None):
    rows, width = h.shape
    tall = RANKS * rows
    hidden = inner[0].shape[-1]
    n_next = len(blocks)
    heads = (HEADS + 2 * KV_HEADS) // RANKS
    cols = heads * HEAD_DIM
    o_cols = HEADS // RANKS * HEAD_DIM
    three = pltpu.VMEM((3, rows, width), BF16)
    four = pltpu.VMEM((RANKS, rows, width), BF16)
    shapes = []
    for i in range(3):
        shape = inner[i].shape
        if late[i]:
            shape = full_shape(count, shape[2:]) if i < 2 else (count, 2, 2) + shape
        shapes.append(shape)
    outs = [
        like((tall, cols)),
        like((tall, o_cols)),
        like((tall, 128), F32),
        like((rows, width), F32),
        like((rows, width), F32),
        like((tall, hidden), F32),
        like((tall, hidden), F32),
        like((tall, hidden)),
        like((RANKS, rows, width)),
    ]
    n_state = len(outs)
    outs += [like(shapes[i]) for i in range(3) if late[i]]
    if n_next:
        outs += [like((RANKS, rows, width))] + [like(full_shape(count, b.shape[2:])) for b in blocks]
        extra = (gain_next, *blocks)
    else:
        outs += [like(swap.shape)]
        extra = (swap,)
    got = pl.pallas_call(
        functools.partial(body_kernel, count, rows, late, n_next, plan),
        out_shape=outs,
        in_specs=[AN, AN, VM, VM, VM, VM, AN, AN, AN, AN] + ([VM] + [AN] * n_next if n_next else [AN]),
        out_specs=[VM] * (n_state - 1) + [AN] * (len(outs) - n_state + 1),
        scratch_shapes=[
            four,
            pltpu.VMEM((width, cols), BF16),
            pltpu.VMEM((heads, tall, 128), BF16),
            pltpu.VMEM(wo.shape, BF16),
        ]
        + [pltpu.VMEM(shape, BF16) for shape in shapes]
        + [three, three, four, three, three]
        + ([four] if n_next else [])
        + sems(count),
        compiler_params=params(2 if n_next else 3),
        name="body_more" if n_next else "body",
    )(n1, wq, *tables, h, gain, wo, *inner, *extra)
    got = list(got)
    state, rest = got[:n_state], got[n_state:]
    inner = [flat(rest.pop(0)) if late[i] else inner[i] for i in range(3)]
    return state, inner, rest[0], [flat(f) for f in rest[1:]]


def call_back(count, start, rest, parts):
    first, last = len(start) == 1, len(rest) == 1
    rows, width = start[0].shape if first else start[2].shape
    tall = RANKS * rows
    three = pltpu.VMEM((3, rows, width), BF16)
    four = pltpu.VMEM((RANKS, rows, width), BF16)
    in_specs = [VM] if first else [VM, AN, VM, VM, VM]
    in_specs += [VM] if last else [AN, AN, AN, AN, VM, VM, VM, VM]
    n_red = len(parts)
    in_specs += [AN] * n_red
    outs, out_specs, scratch = [], [], []
    if last:
        outs, out_specs = [like((rows, width)), like((16, GAIN_COLS), F32)], [AN, VM]
    elif not first:
        outs, out_specs = [like((rows, width), F32), like((1, width), F32)], [VM, VM]
    if not first:
        scratch += [pltpu.VMEM((width, start[0].shape[1]), BF16), three, three]
    if last:
        gains_shape = full_shape(count, (16, GAIN_COLS))
        scratch += [
            pltpu.VMEM((rows, width), F32),
            pltpu.VMEM((rows, width), BF16),
            pltpu.VMEM((16, width), F32),
            pltpu.VMEM(gains_shape, BF16),
        ]
        scratch += Reduce.scratch(gains_shape)
    else:
        wd, wgate, wup, wo = rest[:4]
        hidden = wgate.shape[1]
        outs += [
            like((RANKS, rows, width)),
            like((tall, 2 * hidden)),
            like((rows, width), F32),
            like((1, width), F32),
            like((RANKS, rows, width)),
            like((tall, wo.shape[1])),
        ]
        out_specs += [AN, VM, VM, VM, AN, VM]
        scratch += [pltpu.VMEM(s, BF16) for s in (wd.shape, (width, 2 * hidden), wo.shape)]
        scratch += [four, three, three, four]
    for i, part in enumerate(parts):
        scratch += Reduce.scratch(part.shape, ranks=i > 0)
        tail = part.shape[-2:]
        outs.append(like(tail if i == 0 else (RANKS,) + tail, F32))
        out_specs.append(VM)
    return pl.pallas_call(
        functools.partial(back_kernel, count, rows, first, last, n_red),
        out_shape=outs,
        in_specs=in_specs,
        out_specs=out_specs,
        scratch_shapes=scratch + sems(count),
        compiler_params=params(4 if first else (6 if last else 5)),
        name="back_first" if first else ("back_last" if last else "back_mid"),
    )(*start, *rest, *parts)


def dot_t(a, b):
    return lax.dot_general(a, b, (((0,), (0,)), ((), ())), preferred_element_type=F32).astype(BF16)


def swap_pairs(dp_size, ctx_size):
    pairs = []
    for dp in range(dp_size):
        for ctx in range(ctx_size):
            a, x, core = dp // 4, dp // 2 % 2, dp % 2
            zh, zl = ctx // 2, ctx % 2
            pairs.append((dp * ctx_size + ctx, (a * 4 + zh * 2 + core) * ctx_size + x * 2 + zl))
    return pairs


def shards(dp_size, ctx_size, tokens, cotangent, w_qkv, w_out, w_gate_up, w_down, gains):
    count = dp_size // 4
    rows, width = tokens.shape
    length = RANKS * rows
    hidden = w_gate_up.shape[-1] // RANKS
    positions = jnp.arange(length, dtype=jnp.int32)
    cosine, sine_tab = rotary_tables(positions, HEAD_DIM)
    causal = positions[None, :] <= positions[:, None]
    tall = lambda value: value.reshape(length, width)
    rank = lax.rem(lax.div(lax.axis_index("dp"), 2), 2) * 2 + lax.rem(lax.axis_index("ctx"), 2)

    swap = lambda value: lax.ppermute(value, ("dp", "ctx"), swap_pairs(dp_size, ctx_size))
    tie = lax.optimization_barrier

    swap = lambda value: lax.ppermute(value, ("dp", "ctx"), swap_pairs(dp_size, ctx_size))
    tie = lax.optimization_barrier
    tables = wide_tables(length)

    packed = [pack_weights(w_qkv, w_out, w_gate_up, gains, count, layer) for layer in range(LAYERS)]
    whole_rows = w_qkv.shape[1] % 16 == 0
    if whole_rows:
        head, out, gate, up = packed[0]
        now, later, downs = (head, out, up), (gate, *packed[1]), ()
    else:
        now, later, downs = packed[0], packed[1], (w_down[0],)
    all_tokens, full, blocks, downs = call_start(count, tokens, now, later, downs)
    gain_rows = full[0][:, -GAIN_COLS:][:, : 2 * LAYERS].astype(F32).T
    gain = lambda layer, which: gain_rows[2 * layer + which][None]
    h = lax.dynamic_index_in_dim(all_tokens, rank, 0, keepdims=False)
    n1 = norm_rows(all_tokens.astype(F32), gain(0, 0))
    if whole_rows:
        inner, late, plan = (blocks[0], full[2], w_down[0]), (True, False, True), plan_late
        *blocks, last_up = blocks[1:]
    else:
        inner, late, plan = (*full[2:], *downs), (False, False, False), plan_early

    records = []
    for layer in range(LAYERS):
        wq, wo = full[:2]
        if layer + 1 < LAYERS:
            state, inner, n1_next, full = call_body(
                count, n1, wq, tables, h, gain(layer, 1), wo, inner, late, plan, gain(layer + 1, 0), blocks
            )
            if whole_rows:
                late, plan = (False, True, True), plan_late_end
                next_inner = (full[2], last_up, w_down[layer + 1])
            else:
                late, plan = (False, False, True), plan_end
                next_inner = (*full[2:], w_down[layer + 1])
        else:
            state, inner, g, _ = call_body(
                count, n1, wq, tables, h, gain(layer, 1), wo, inner, late, plan,
                swap=cotangent.astype(BF16),
            )
            n1_next = None
        qkv, mixed, lse, h1, h_next, gate, up, u, n2 = state
        saved = saved_heads(qkv, lse)
        records.append((h, n1, saved, mixed, h1, n2, gate, up, u, (wq, wo, *inner)))
        h, n1, inner = h_next, n1_next, next_inner

    shape7 = lambda value: value.reshape(count, 2, 2, 2, 2, -1, value.shape[-1])
    start, parts = (g,), []
    grads = [None] * LAYERS
    gain_grads = [None] * (2 * LAYERS)
    for layer in reversed(range(LAYERS)):
        h_in, n1, saved, mixed, h1, n2, gate, up, u, (wq, wo, wgate, wup, wd) = records[layer]
        got = call_back(count, start, (wd, wgate, wup, wo, gate, up, h1, gain(layer, 1)), parts)
        if layer < LAYERS - 1:
            _, gain_grads[2 * layer + 2], *got = got
            grads[layer + 1] = got[6:]
        gbg, dgu, gh, gain_grads[2 * layer + 1], ghg, do = got[:6]
        if layer == LAYERS - 1:
            do, send = tie((do, h.astype(BF16)))
            out_act = swap(send)
        dqkv = attend_back(saved, mixed, do, cosine, sine_tab, causal)
        if layer == LAYERS - 1:
            dqkv, out_act = tie((dqkv, out_act))
        parts = [
            dot_t(u, tall(gbg)).reshape(count, 2, 2, -1, width),
            shape7(dot_t(tall(n2), dgu[:, :hidden])),
            shape7(dot_t(tall(n2), dgu[:, hidden:])),
            shape7(dot_t(tall(ghg), mixed)),
            shape7(dot_t(tall(n1), dqkv)),
        ]
        start = (dqkv, wq, gh, h_in, gain(layer, 0))
    others = jnp.concatenate([jnp.zeros((1, width), F32)] + gain_grads[1:], axis=0)
    others = jnp.pad(others, ((0, 16 - 2 * LAYERS), (0, 0)))
    grad_tokens, gains_sum, *last = call_back(count, start, (others,), parts)
    grads[0] = last
    piece = gains.shape[-1]
    grad_gains = gains_sum[: 2 * LAYERS, :piece].reshape(LAYERS, 2, piece)
    stacked = [unpack_grads(q, o, gate, up, count) for _, gate, up, o, q in grads]
    s_qkv, s_out, s_gu = (jnp.stack([s[i] for s in stacked]) for i in range(3))
    s_down = jnp.stack([g[0] for g in grads])
    return (out_act.astype(F32), grad_tokens.astype(F32), s_qkv, s_out, s_gu, s_down, grad_gains)


def solution(mesh):
    both = ("dp", "ctx")
    return jax.shard_map(
        functools.partial(shards, mesh.shape["dp"], mesh.shape["ctx"]),
        mesh=mesh,
        in_specs=(
            P(both, None),
            P(both, None),
            P(None, both, None),
            P(None, None, both),
            P(None, both, None, None),
            P(None, both, None),
            P(None, None, both),
        ),
        out_specs=(
            P(both, None),
            P(both, None),
            P(None, both, None),
            P(None, None, both),
            P(None, both, None, None),
            P(None, both, None),
            P(None, None, both),
        ),
        check_vma=False,
    )
```

```python
import functools

import jax
import jax.numpy as jnp
import numpy as np
from jax import lax
from jax.experimental import pallas as pl
from jax.experimental.pallas import tpu as pltpu
from jax.sharding import PartitionSpec as P

HEADS = 16
KV_HEADS = 8
HEAD_DIM = 96
LAYERS = 2
RANKS = 4
GAIN_COLS = 128

NORM_EPS = 1e-05
ROPE_BASE = 100000.0
MASKED = -1e30
MESH = pl.DeviceIdType.MESH
BF16 = jnp.bfloat16
F32 = jnp.float32
VMEM_BYTES = 62 * 1024 * 1024


class Place:
    def __init__(self, count):
        self.count = count
        self.dp = lax.axis_index("dp")
        self.ctx = lax.axis_index("ctx")
        self.core = lax.rem(self.dp, 2)
        self.x = lax.rem(lax.div(self.dp, 2), 2)
        self.a = lax.div(self.dp, 4)
        self.zh = lax.div(self.ctx, 2)
        self.zl = lax.rem(self.ctx, 2)
        self.rank = self.x * 2 + self.zl
        dpx = self.dp + 2 - 4 * self.x
        ctz = self.ctx + 1 - 2 * self.zl
        x2, z2 = 1 - self.x, 1 - self.zl
        self.peers = (
            ((dpx, self.ctx), x2 * 2 + self.zl),
            ((self.dp, ctz), self.x * 2 + z2),
            ((dpx, ctz), x2 * 2 + z2),
        )
        self.core_peer = (self.dp + 1 - 2 * self.core, self.ctx)
        self.zh_peer = (self.dp, self.ctx + 2 - 4 * self.zh)
        self.others = []
        for k in range(1, count):
            ahead = lax.rem(self.a + k, count)
            behind = lax.rem(self.a + count - k, count)
            self.others.append(((self.dp + (ahead - self.a) * 4, self.ctx), ahead, behind))
        self.moves = self.x != self.zh
        self.swap_peer = (self.dp + (self.zh - self.x) * 2, self.ctx + (self.x - self.zh) * 2)

    def greet(self, weights, swap):
        devices = [d for d, _ in self.peers]
        if weights:
            devices += [self.core_peer, self.zh_peer] + [o[0] for o in self.others]
        barrier = pltpu.get_barrier_semaphore()
        for device in devices:
            pl.semaphore_signal(barrier, inc=1, device_id=device, device_id_type=MESH)
        if swap:

            @pl.when(self.moves)
            def _():
                pl.semaphore_signal(barrier, inc=1, device_id=self.swap_peer, device_id_type=MESH)

        expected = len(devices)
        if swap:
            expected = expected + self.x + self.zh - 2 * self.x * self.zh
        pl.semaphore_wait(barrier, expected)


class Net:
    def __init__(self, place, send, recv, local):
        self.place, self.send, self.recv, self.local = place, send, recv, local
        self.n, self.m = 0, 0
        self.sends = []

    def remote(self, src, dst, device):
        copy = self.prepare(src, dst, device)
        copy.start()
        self.sends.append(copy)
        return copy

    def prepare(self, src, dst, device):
        i = self.n
        self.n += 1
        return pltpu.make_async_remote_copy(
            src_ref=src, dst_ref=dst, send_sem=self.send.at[i], recv_sem=self.recv.at[i],
            device_id=device, device_id_type=MESH,
        )

    def here(self, src, dst):
        i = self.m
        self.m += 1
        copy = pltpu.make_async_copy(src, dst, self.local.at[i])
        copy.start()
        return copy

    def finish(self):
        for copy in self.sends:
            copy.wait_send()


REMOTE_SEMS, LOCAL_SEMS = 128, 48


def sems(count=2):
    n = REMOTE_SEMS * max(1, count // 2)
    return [
        pltpu.SemaphoreType.DMA((n,)),
        pltpu.SemaphoreType.DMA((n,)),
        pltpu.SemaphoreType.DMA((LOCAL_SEMS,)),
    ]


class Swap:
    def __init__(self, net, src, dst):
        self.net, self.src, self.dst = net, src, dst

    def start(self):
        net, place = self.net, self.net.place
        self.copy = net.prepare(self.src, self.dst, place.swap_peer)
        self.stay = pltpu.make_async_copy(self.src, self.dst, net.local.at[net.m])
        net.m += 1

        @pl.when(place.moves)
        def _():
            self.copy.start()

        @pl.when(jnp.logical_not(place.moves))
        def _():
            self.stay.start()

    def wait(self):
        @pl.when(self.net.place.moves)
        def _():
            self.copy.wait_recv()
            self.copy.wait_send()

        @pl.when(jnp.logical_not(self.net.place.moves))
        def _():
            self.stay.wait()


class Share:
    def __init__(self, net, piece, block):
        self.net, self.piece, self.block = net, piece, block

    def start(self):
        net, place = self.net, self.net.place
        mine = self.block.at[place.x, place.zl]
        self.copies = [net.remote(self.piece.at[rank], mine, device) for device, rank in place.peers]
        self.own = net.here(self.piece.at[place.rank], mine)

    def wait(self):
        for copy in self.copies:
            copy.wait_recv()
        self.own.wait()


class Gather:
    def __init__(self, net, block, full, ranks=True):
        self.net, self.block, self.full, self.ranks = net, block, full, ranks

    def slot(self, a, core, zh):
        if self.ranks:
            return self.full.at[a, :, core, zh, :]
        return self.full.at[a, core, zh]

    def column(self, a, core):
        if self.ranks:
            return self.full.at[a, :, core, :, :]
        return self.full.at[a, core]

    def begin(self):
        net, p = self.net, self.net.place
        mine = self.slot(p.a, p.core, p.zh)
        self.across = net.remote(self.block, mine, p.zh_peer)
        self.near = [net.remote(self.block, mine, o[0]) for o in p.others]
        self.cores = [net.remote(self.block, mine, p.core_peer)]
        self.own = net.here(self.block, mine)

    def middle(self):
        net, p = self.net, self.net.place
        self.across.wait_recv()
        got = self.slot(p.a, p.core, 1 - p.zh)
        self.far = [net.remote(got, got, o[0]) for o in p.others]
        self.cores.append(net.remote(got, got, p.core_peer))

    def final(self):
        net, p = self.net, self.net.place
        for k, other in enumerate(p.others):
            self.near[k].wait_recv()
            self.far[k].wait_recv()
            got = self.column(other[2], p.core)
            self.cores.append(net.remote(got, got, p.core_peer))

    def done(self):
        self.own.wait()
        for copy in self.cores:
            copy.wait_recv()


class Reduce:
    def __init__(self, net, part, out, held, from_core, from_a, from_zh, from_rank, ranks=True, added=False):
        self.net, self.part, self.out = net, part, out
        self.held, self.from_core, self.from_a = held, from_core, from_a
        self.from_zh, self.from_rank = from_zh, from_rank
        self.ranks, self.added = ranks, added

    def half(self, core):
        return self.part.at[:, :, core] if self.ranks else self.part.at[:, core]

    def begin(self):
        net, p = self.net, self.net.place
        self.load = net.here(self.half(p.core), self.held)
        self.by_core = net.remote(self.half(1 - p.core), self.from_core, p.core_peer)

    def along_a(self):
        net, p = self.net, self.net.place
        self.load.wait()
        self.by_core.wait_recv()
        add_into(self.held, self.from_core)
        self.by_a = [
            net.remote(self.held.at[other[1]], self.from_a.at[k], other[0])
            for k, other in enumerate(p.others)
        ]

    def along_zh(self):
        net, p = self.net, self.net.place
        mine = self.held.at[p.a]
        for k, copy in enumerate(self.by_a):
            copy.wait_recv()
            add_into(mine, self.from_a.at[k])
        there = mine.at[:, 1 - p.zh] if self.ranks else mine.at[1 - p.zh]
        self.by_zh = net.remote(there, self.from_zh, p.zh_peer)

    def among_ranks(self):
        net, p = self.net, self.net.place
        self.by_zh.wait_recv()
        if not self.ranks:
            self.out[...] = self.held[p.a, p.zh].astype(F32) + self.from_zh[...].astype(F32)
            return
        for x in range(2):
            for zl in range(2):
                add_into(self.held.at[p.a, x, p.zh, zl], self.from_zh.at[x, zl])
        self.by_rank = []
        for device, rank in p.peers:
            rank_x, rank_zl = lax.div(rank, 2), lax.rem(rank, 2)
            self.by_rank.append(
                net.remote(
                    self.held.at[p.a, rank_x, p.zh, rank_zl], self.from_rank.at[len(self.by_rank)], device
                )
            )

    def done(self):
        if not self.ranks:
            return
        p = self.net.place
        own = self.held[p.a, p.x, p.zh, p.zl].astype(F32)
        for copy in self.by_rank:
            copy.wait_recv()
        if self.added:
            for j in range(3):
                own = own + self.from_rank[j].astype(F32)
            self.out[...] = own
            return
        self.out[p.rank] = own
        for j, (_, rank) in enumerate(p.peers):
            self.out[rank] = self.from_rank[j].astype(F32)

    @staticmethod
    def scratch(shape, ranks=True):
        tail = shape[-2:]
        count = shape[0]
        inner = ((2, 2, 2) if ranks else (2,)) + tail
        fewer = ((2, 2) if ranks else ()) + tail
        shapes = [(count,) + inner, (count,) + inner, (max(count - 1, 1),) + inner, fewer]
        if ranks:
            shapes.append((3,) + tail)
        return [pltpu.VMEM(s, BF16) for s in shapes]


def add_into(target, source):
    lead = target.shape[:-2]
    total = 1
    for size in lead:
        total *= size
    if total == 1 and not lead:
        target[...] = (target[...].astype(F32) + source[...].astype(F32)).astype(BF16)
        return

    @pl.loop(0, total)
    def _(j):
        index, left = [], j
        for size in reversed(lead):
            index.append(lax.rem(left, size))
            left = lax.div(left, size)
        index = tuple(reversed(index))
        target[index] = (target[index].astype(F32) + source[index].astype(F32)).astype(BF16)


class Spread:
    def __init__(self, net, land):
        self.net, self.land = net, land
        self.peers = net.place.peers
        mine = land.at[net.place.rank]
        self.along_x = net.remote(mine, mine, self.peers[0][0])
        self.along_zl = net.remote(mine, mine, self.peers[1][0])

    def arrivals(self):
        self.along_zl.wait_recv()
        got = self.land.at[self.peers[1][1]]
        relay = self.net.remote(got, got, self.peers[0][0])
        yield 1, self.peers[1][1]
        self.along_x.wait_recv()
        yield 0, self.peers[0][1]
        relay.wait_recv()
        yield 2, self.peers[2][1]

    def wait(self):
        for _ in self.arrivals():
            pass


class Sum:
    def __init__(self, net, out, land):
        self.net, self.out, self.land = net, out, land
        self.peers = net.place.peers

    def ready(self, i):
        if i == 2:
            self.diagonal = self.net.remote(self.out.at[2], self.land.at[0], self.peers[0][0])
        elif i == 0:
            self.along_x = self.net.remote(self.out.at[0], self.land.at[1], self.peers[0][0])

    def forward(self):
        self.diagonal.wait_recv()
        add_into(self.out.at[1], self.land.at[0])
        self.along_zl = self.net.remote(self.out.at[1], self.land.at[2], self.peers[1][0])

    def result(self, own):
        self.along_x.wait_recv()
        self.along_zl.wait_recv()
        return own + self.land[1].astype(F32) + self.land[2].astype(F32)


def products(x, w_ref, count, tile, transposed, use):
    def part(cols):
        if transposed:
            w, dims = w_ref[cols, :], (((1,), (1,)), ((), ()))
        else:
            w, dims = w_ref[:, cols], (((1,), (0,)), ((), ()))
        use(cols, lax.dot_general(x(), w, dims, preferred_element_type=F32))

    for j in range(count // tile):
        part(pl.ds(j * tile, tile))


def norm_rows(h, gain):
    factor = lax.rsqrt(jnp.mean(h * h, axis=-1, keepdims=True) + NORM_EPS)
    return (h * factor * gain).astype(BF16)


def norm_rows_back(h, gain, grad):
    factor = lax.rsqrt(jnp.mean(h * h, axis=-1, keepdims=True) + NORM_EPS)
    z = grad * gain
    inner = jnp.sum(z * h, axis=-1, keepdims=True)
    back = factor * z - h * (factor * factor * factor * inner / h.shape[-1])
    return back, jnp.sum(grad * h * factor, axis=0, keepdims=True)


def rows_of(rank, rows):
    return pl.ds(pl.multiple_of(rank * rows, rows), rows)


class Refs:
    def __init__(self, refs):
        self.refs = list(refs)

    def take(self, n):
        got, self.refs = self.refs[:n], self.refs[n:]
        return got


class Ticks:
    def __init__(self, plan):
        self.plan = list(plan)

    def __call__(self):
        if self.plan:
            for step in self.plan.pop(0):
                step()

    def rest(self):
        while self.plan:
            self()


def np_tables(length):
    steps = np.arange(HEAD_DIM // 2, dtype=np.float32)
    inverse = np.exp(steps * np.float32(-2.0 * np.log(ROPE_BASE) / HEAD_DIM)).astype(np.float32)
    angles = np.arange(length, dtype=np.float32)[:, None] * inverse[None, :]
    return np.cos(angles), np.sin(angles)


def wide_tables(length):
    cosine, sine = np_tables(length)
    turned = (HEADS + KV_HEADS) // RANKS
    still = KV_HEADS // RANKS * HEAD_DIM
    cos_all = np.concatenate([cosine] * (2 * turned) + [np.ones((length, still))], axis=1)
    sin_all = np.concatenate([-sine, sine] * turned + [np.zeros((length, still))], axis=1)
    return jnp.asarray(cos_all, F32), jnp.asarray(sin_all, F32)


def turn(values, cosine, sine):
    cols = values.shape[1]
    half = HEAD_DIM // 2
    lane = lax.broadcasted_iota(jnp.int32, values.shape, 1)
    other = jnp.where(
        lax.rem(lane, HEAD_DIM) < half,
        pltpu.roll(values, cols - half, 1),
        pltpu.roll(values, half, 1),
    )
    return values * cosine + other * sine


def head_window(values, h):
    offset = HEAD_DIM * h
    start = offset // 128 * 128
    size = 128 if offset - start + HEAD_DIM <= 128 else 256
    window = values[:, start : start + size]
    if offset > start:
        window = pltpu.roll(window, size - (offset - start), 1)
    window = window[:, :128]
    lane = lax.broadcasted_iota(jnp.int32, window.shape, 1)
    return jnp.where(lane < HEAD_DIM, window, 0.0)


def heads_joined(parts):
    rows = parts[0].shape[0]
    columns = [jnp.zeros((rows, 128), F32) for _ in range(len(parts) * HEAD_DIM // 128 + 1)]
    for h, part in enumerate(parts):
        offset = HEAD_DIM * h
        first = offset // 128
        shift = offset - first * 128
        if shift == 0:
            columns[first] = columns[first] + part
            continue
        double = jnp.concatenate([part, jnp.zeros((rows, 128), F32)], axis=1)
        double = pltpu.roll(double, shift, 1)
        columns[first] = columns[first] + double[:, :128]
        columns[first + 1] = columns[first + 1] + double[:, 128:]
    return jnp.concatenate(columns[:-1], axis=1)


def project_heads(rows, n1, wq, cos_ref, sin_ref, heads):
    count = heads.shape[0]

    @pl.loop(0, RANKS)
    def _(b):
        span = rows_of(b, rows)
        y = jnp.dot(n1[b], wq[...], preferred_element_type=F32)
        y = turn(y, cos_ref[span, :], sin_ref[span, :])
        for h in range(count):
            heads[h, span, :] = head_window(y, h).astype(BF16)


def causal_scores(rows, rank, query, key):
    scores = lax.dot_general(query, key, (((1,), (1,)), ((), ())), preferred_element_type=F32)
    row = lax.broadcasted_iota(jnp.int32, scores.shape, 0) + rank * rows
    col = lax.broadcasted_iota(jnp.int32, scores.shape, 1)
    return jnp.where(col <= row, scores * HEAD_DIM ** (-0.5), MASKED)


def attend_rows(rows, rank, heads, o_ref, lse_ref):
    span = rows_of(rank, rows)
    queries = HEADS // RANKS
    pairs = KV_HEADS // RANKS
    groups = HEADS // KV_HEADS
    mixed = []
    lane = lax.broadcasted_iota(jnp.int32, (rows, 128), 1)
    lse_all = jnp.zeros((rows, 128), F32)
    for h in range(queries):
        kv = h // groups
        scores = causal_scores(rows, rank, heads[h, span, :], heads[queries + kv])
        highest = jnp.max(scores, axis=-1, keepdims=True)
        weights = jnp.exp(scores - highest)
        total = jnp.sum(weights, axis=-1, keepdims=True)
        lse = highest + jnp.log(total)
        lse_all = jnp.where(lane == h, lse, lse_all)
        weights = (weights * (1.0 / total)).astype(BF16)
        mixed.append(
            jnp.dot(weights, heads[queries + pairs + kv], preferred_element_type=F32)
        )
    lse_ref[span, :] = lse_all
    o_ref[span, :] = heads_joined(mixed).astype(BF16)


def window_tables(length):
    cosine, sine = np_tables(length)
    none = np.zeros((length, 128 - HEAD_DIM))
    cos_one = np.concatenate([cosine, cosine, none], axis=1)
    sin_one = np.concatenate([-sine, sine, none], axis=1)
    return jnp.asarray(cos_one, F32), jnp.asarray(sin_one, F32)


def turn_window(values, cosine, sine):
    half = HEAD_DIM // 2
    lane = lax.broadcasted_iota(jnp.int32, values.shape, 1)
    other = jnp.where(lane < half, pltpu.roll(values, 128 - half, 1), pltpu.roll(values, half, 1))
    return values * cosine + other * sine


def dot_tn(a, b):
    return lax.dot_general(a, b, (((0,), (0,)), ((), ())), preferred_element_type=F32)


def attend_rows_back(rows, rank, do_rows, heads, o_ref, lse_ref, cos_ref, sin_ref, dq_ref, dkv):
    span = rows_of(rank, rows)
    queries = HEADS // RANKS
    pairs = KV_HEADS // RANKS
    groups = HEADS // KV_HEADS
    o_rows = o_ref[span, :].astype(F32)
    parts = []
    for h in range(queries):
        kv = h // groups
        do_h = head_window(do_rows, h)
        delta = jnp.sum(do_h * head_window(o_rows, h), axis=-1, keepdims=True)
        do_b = do_h.astype(BF16)
        query, key, value = heads[h, span, :], heads[queries + kv], heads[queries + pairs + kv]
        weights = jnp.exp(causal_scores(rows, rank, query, key) - lse_ref[span, h : h + 1])
        grad_w = lax.dot_general(do_b, value, (((1,), (1,)), ((), ())), preferred_element_type=F32)
        ds = (weights * (grad_w - delta) * HEAD_DIM ** (-0.5)).astype(BF16)
        dq = jnp.dot(ds, key, preferred_element_type=F32)
        parts.append(turn_window(dq, cos_ref[span, :], -sin_ref[span, :]))
        dkv[kv] += dot_tn(ds, query)
        dkv[pairs + kv] += dot_tn(weights.astype(BF16), do_b)
    joined = heads_joined(parts)
    dq_ref[span, pl.ds(0, joined.shape[1])] = joined.astype(BF16)


def close_keys(rows, dkv, cos_ref, sin_ref, dqkv_ref):
    pairs = KV_HEADS // RANKS
    first = HEADS // RANKS * HEAD_DIM

    @pl.loop(0, RANKS)
    def _(b):
        span = rows_of(b, rows)
        parts = [turn_window(dkv[i, span, :], cos_ref[span, :], -sin_ref[span, :]) for i in range(pairs)]
        parts += [dkv[pairs + i, span, :] for i in range(pairs)]
        joined = heads_joined(parts)
        dqkv_ref[span, pl.ds(first, joined.shape[1])] = joined.astype(BF16)


def put_blocks(target, value):
    *lead, rows, cols = target.shape
    if rows % 16 == 0:
        target.reshape(value.shape[0], cols)[...] = value.astype(BF16)
        return
    for block in range(value.shape[0] // rows):
        index, left = [], block
        for size in reversed(lead):
            index.append(left % size)
            left //= size
        target[tuple(reversed(index))] = value[block * rows : (block + 1) * rows].astype(BF16)


def start_kernel(count, n, ahead, n_down, *refs):
    refs = Refs(refs)
    (tokens,) = refs.take(1)
    pieces, later, downs = refs.take(n), refs.take(ahead), refs.take(n_down)
    (all_tokens,) = refs.take(1)
    full, blocks_later, downs_full = refs.take(n), refs.take(ahead), refs.take(n_down)
    (land,) = refs.take(1)
    blocks = refs.take(n)
    send, recv, local = refs.take(3)
    place = Place(count)
    net = Net(place, send, recv, local)
    shares = [Share(net, pieces[i], blocks[i]) for i in range(n)]
    shares_later = [Share(net, later[i], blocks_later[i]) for i in range(ahead)]
    gathers = [Gather(net, blocks[i], full[i]) for i in range(n)]
    gathers += [Gather(net, downs[i], downs_full[i], ranks=False) for i in range(n_down)]
    swap = Swap(net, tokens, land.at[place.zh * 2 + place.zl])
    place.greet(True, True)
    shares[0].start()
    swap.start()
    for share in shares[1:]:
        share.start()
    for i in range(2):
        shares[i].wait()
        gathers[i].begin()
    swap.wait()
    spreads = Spread(net, land)
    for i in range(2, len(gathers)):
        if i < n:
            shares[i].wait()
        gathers[i].begin()
    arrivals = spreads.arrivals()
    next(arrivals)
    for share in shares_later:
        share.start()
    gathers[0].middle()
    gathers[1].middle()
    for _ in arrivals:
        pass
    keep = net.here(land, all_tokens)
    gathers[0].final()
    for i in range(2, len(gathers)):
        gathers[i].middle()
        gathers[i - 1].final()
    gathers[-1].final()
    for gather in gathers:
        gather.done()
    for share in shares_later:
        share.wait()
    keep.wait()
    net.finish()


def body_kernel(count, rows, late, n_next, plan, *refs):
    refs = Refs(refs)
    n1_hbm, wq_hbm, cos_ref, sin_ref, h_ref, gain_ref, wo_hbm = refs.take(7)
    inner_hbm = refs.take(3)
    if n_next:
        (gain_next,) = refs.take(1)
        blocks = refs.take(n_next)
    else:
        (swap_src,) = refs.take(1)
    heads, o_ref, lse_ref, h1_ref, hn_ref, gate_ref, up_ref, u_ref, ng_hbm = refs.take(9)
    late_out = [refs.take(1)[0] if late[i] else None for i in range(3)]
    if n_next:
        (nn_hbm,) = refs.take(1)
        full = refs.take(n_next)
    else:
        (swap_dst,) = refs.take(1)
    n1, wq, wo = refs.take(3)
    inner = refs.take(3)
    out_a, land_a, land_n, out_b, land_b = refs.take(5)
    if n_next:
        (land_q,) = refs.take(1)
    send, recv, local = refs.take(3)

    place = Place(count)
    net = Net(place, send, recv, local)
    width = h_ref.shape[1]
    hidden = u_ref.shape[1]
    load_q = net.here(wq_hbm.at[:, pl.ds(0, wq.shape[1])], wq)
    load_n = net.here(n1_hbm, n1)
    load_out = net.here(wo_hbm, wo)
    jobs = {}
    loads, weights = [], []
    for i in range(3):
        if late[i]:
            jobs[("gate", "up", "down")[i]] = Gather(net, inner_hbm[i], inner[i], ranks=i < 2)
            loads.append(None)
        else:
            loads.append(net.here(inner_hbm[i], inner[i]))
        weights.append(inner[i].reshape((hidden, width) if i == 2 else (width, hidden)) if late[i] else inner[i])
    wg, wu, wd = weights
    for i in range(n_next):
        jobs[i] = Gather(net, blocks[i], full[i])
    if not n_next:
        jobs["swap"] = Swap(net, swap_src, swap_dst)
    peers = place.peers
    place.greet(True, not n_next)
    keeps = []

    def ready(i):
        if late[i]:
            jobs[("gate", "up", "down")[i]].done()
            keeps.append(net.here(inner[i], late_out[i]))
        else:
            loads[i].wait()

    tick = Ticks(plan(jobs))
    tick()

    load_q.wait()
    load_n.wait()
    project_heads(rows, n1, wq, cos_ref, sin_ref, heads)
    load_out.wait()
    sums = Sum(net, out_a, land_a)
    for i in (2, 0, 1):
        attend_rows(rows, peers[i][1], heads, o_ref, lse_ref)
        span = rows_of(peers[i][1], rows)

        def use(cols, y, i=i):
            out_a[i, :, cols] = y.astype(BF16)

        products(lambda: o_ref[span, :], wo, width, width, True, use)
        sums.ready(i)
    attend_rows(rows, place.rank, heads, o_ref, lse_ref)
    span = rows_of(place.rank, rows)

    def use_own(cols, y):
        h1_ref[:, cols] = h_ref[:, cols].astype(F32) + y

    products(lambda: o_ref[span, :], wo, width, width, True, use_own)
    sums.forward()
    tick()
    h1 = sums.result(h1_ref[...])
    h1_ref[...] = h1
    land_n[place.rank] = norm_rows(h1, gain_ref[...])
    gather = Spread(net, land_n)
    tick()
    ready(0)
    ready(1)

    def inner_block(rank):
        span = rows_of(rank, rows)

        gate = jnp.dot(land_n[rank], wg[...], preferred_element_type=F32)
        up = jnp.dot(land_n[rank], wu[...], preferred_element_type=F32)
        gate_ref[span, :] = gate
        up_ref[span, :] = up
        u_ref[span, :] = (gate / (1.0 + jnp.exp(-gate)) * up).astype(BF16)

        return span

    inner_block(place.rank)
    tick()
    second = Sum(net, out_b, land_b)
    for i, rank in gather.arrivals():
        span = inner_block(rank)
        if i == 1:
            tick()
            ready(2)

        def use(cols, y, i=i):
            out_b[i, :, cols] = y.astype(BF16)

        products(lambda: u_ref[span, :], wd, width, width, False, use)
        second.ready(i)
        tick()
    keep = net.here(land_n, ng_hbm)
    span = rows_of(place.rank, rows)

    def use_down(cols, y):
        hn_ref[:, cols] = h1_ref[:, cols] + y

    products(lambda: u_ref[span, :], wd, width, width, False, use_down)
    second.forward()
    tick()
    hn = second.result(hn_ref[...])
    hn_ref[...] = hn
    if n_next:
        land_q[place.rank] = norm_rows(hn, gain_next[...])
        third = Spread(net, land_q)
        tick()
        for _ in third.arrivals():
            tick()
        keep_next = net.here(land_q, nn_hbm)
        keep_next.wait()
    tick.rest()
    for i in range(n_next):
        jobs[i].done()
    if not n_next:
        jobs["swap"].wait()
    keep.wait()
    for copy in keeps:
        copy.wait()
    net.finish()


def plan_late(j):
    gate, down = j["gate"], j["down"]
    return [
        [gate.begin],
        [gate.middle, down.begin],
        [gate.final],
        [down.middle, j[0].begin, j[1].begin],
        [down.final],
        [],
        [],
        [j[0].middle],
        [j[0].final, j[1].middle],
        [j[2].begin, j[1].final],
        [],
        [],
        [j[2].middle],
        [j[2].final],
    ]


def plan_late_end(j):
    up, down = j["up"], j["down"]
    return [
        [up.begin],
        [up.middle, down.begin],
        [up.final],
        [down.middle],
        [down.final],
        [],
        [],
        [j["swap"].start],
    ]


def plan_early(j):
    return [
        [j[0].begin],
        [j[1].begin],
        [j[0].middle, j[1].middle, j[2].begin],
        [],
        [j[0].final],
        [j[1].final],
        [j[2].middle],
        [],
        [j[3].begin, j[2].final],
        [],
        [],
        [],
        [j[3].middle],
        [j[3].final],
    ]


def plan_end(j):
    down = j["down"]
    return [
        [down.begin],
        [],
        [down.middle],
        [],
        [down.final],
        [],
        [],
        [j["swap"].start],
    ]


class Back:
    def __init__(self, net, rows):
        self.net, self.place, self.rows = net, net.place, rows
        self.peers = net.place.peers

    def enter(self, r, tick):
        rows, place = self.rows, self.place
        width = r["gnew"].shape[1]
        total = Sum(self.net, r["out_a"], r["land_a"])
        for i in (2, 0, 1):
            span = rows_of(self.peers[i][1], rows)

            def use(cols, y, i=i):
                r["out_a"][i, :, cols] = y.astype(BF16)

            products(lambda: r["dqkv"][span, :], r["wq"], width, width, True, use)
            total.ready(i)
        own = rows_of(place.rank, rows)

        def use_own(cols, y):
            r["gnew"][:, cols] = y

        products(lambda: r["dqkv"][own, :], r["wq"], width, width, True, use_own)
        total.forward()
        tick()
        dn = total.result(r["gnew"][...])
        back, ggain = norm_rows_back(r["hin"][...].astype(F32), r["gain_in"][...], dn)
        r["gnew"][...] = r["ghin"][...] + back
        return ggain

    def feed_forward(self, r, tick, ready, between):
        net, rows, place = self.net, self.rows, self.place
        land_g, dgu, out_b = r["land_g"], r["dgu"], r["out_b"]
        width = land_g.shape[2]
        hidden = r["gate"].shape[1]
        land_g[place.rank] = r["g"][...].astype(BF16)
        gather = Spread(net, land_g)
        tick()
        ready()

        def inner_block(rank):
            span = rows_of(rank, rows)
            du = lax.dot_general(
                land_g[rank], r["wd"][...], (((1,), (1,)), ((), ())), preferred_element_type=F32
            )
            gate, up = r["gate"][span, :], r["up"][span, :]
            sg = 1.0 / (1.0 + jnp.exp(-gate))
            dgu[span, pl.ds(0, hidden)] = (du * up * sg * (1.0 + gate * (1.0 - sg))).astype(BF16)
            dgu[span, pl.ds(hidden, hidden)] = (du * gate * sg).astype(BF16)
            return span

        span = inner_block(place.rank)

        def use_mid(cols, y):
            r["gh"][:, cols] = y

        products(lambda: dgu[span, :], r["wgu"], width, width, True, use_mid)
        tick()
        second = Sum(net, out_b, r["land_b"])
        for i, rank in gather.arrivals():
            span = inner_block(rank)

            def use(cols, y, i=i):
                out_b[i, :, cols] = y.astype(BF16)

            products(lambda: dgu[span, :], r["wgu"], width, width, True, use)
            second.ready(i)
            tick()
        second.forward()
        tick()
        between()
        tick()
        dn = second.result(r["gh"][...])
        back, ggain = norm_rows_back(r["h1"][...], r["gain"][...], dn)
        r["gh"][...] = r["g"][...].astype(F32) + back
        r["gg"][...] = ggain

    def weight_grads(self, r):
        net = self.net
        buffers, copies = r["buffers"], []
        tile = buffers.shape[1]
        tall, hidden = r["u"].shape
        width = r["land_g"].shape[2]
        g_all = r["land_g"][...].reshape(tall, width)

        def emit(lhs, rhs, outs, m):
            slot = len(copies) % 2
            if len(copies) >= 2:
                for copy in copies[-2]:
                    copy.wait()
            buffers[slot, :, pl.ds(0, rhs.shape[1])] = dot_tn(lhs, rhs).astype(BF16)
            cols = rhs.shape[1] // len(outs)
            copies.append([
                net.here(buffers.at[slot, :, pl.ds(k * cols, cols)], out.at[pl.ds(m * tile, tile)])
                for k, out in enumerate(outs)
            ])

        for m in range(hidden // tile):
            emit(r["u"][:, m * tile : (m + 1) * tile], g_all, [r["g_down"]], m)
        for m in range(width // tile):
            emit(r["n2"][:, m * tile : (m + 1) * tile], r["dgu"][...], [r["g_gate"], r["g_up"]], m)
        return copies[-2] + copies[-1]

    def attention(self, r, tick, ready):
        net, rows, place = self.net, self.rows, self.place
        land_h = r["land_h"]
        land_h[place.rank] = r["gh"][...].astype(BF16)
        gather = Spread(net, land_h)
        tick()
        ready()
        r["dkv"][...] = jnp.zeros(r["dkv"].shape, F32)

        def block(rank):
            do_rows = jnp.dot(land_h[rank], r["wo"][...], preferred_element_type=F32)
            do_rows = do_rows.astype(BF16).astype(F32)
            attend_rows_back(
                rows, rank, do_rows, r["heads"], r["o"], r["lse"], r["cos"], r["sin"], r["dqkv"], r["dkv"]
            )

        block(place.rank)
        tick()
        for _, rank in gather.arrivals():
            block(rank)
            tick()
        close_keys(rows, r["dkv"], r["cos"], r["sin"], r["dqkv"])


ATTEND = ("wo", "heads", "o", "lse", "cos", "sin")


def back_kernel(count, rows, names, out_names, scratch_names, n_parts, n_red, plan, *refs):
    refs = Refs(refs)
    r = dict(zip(names, refs.take(len(names))))
    parts = refs.take(n_parts)
    r.update(zip(out_names, refs.take(len(out_names))))
    red_out = refs.take(n_red)
    r.update(zip(scratch_names, refs.take(len(scratch_names))))
    red_scratch = [refs.take(4 if i == 0 else 5) for i in range(n_red)]
    gains_scratch = refs.take(5) if "gains_out" in r else None
    send, recv, local = refs.take(3)

    place = Place(count)
    net = Net(place, send, recv, local)
    back = Back(net, rows)
    entering, inner, attention = "hin" in r, "h1" in r, "heads_hbm" in r
    last = "gains_out" in r
    waits = {}

    def load(name, source, target):
        waits[name] = net.here(source, target)

    if last:
        parts = parts + [r["part_o"], r["part_q"]]
    jobs = []
    for i, part in enumerate(parts):
        scratch = red_scratch[i] + ([None] if i == 0 else [])
        jobs.append(Reduce(net, part, red_out[i], *scratch, ranks=i > 0))
    if entering:
        load("wq", r["wq_hbm"].at[:, pl.ds(0, r["wq"].shape[1])], r["wq"])
    if inner:
        hidden = r["wd"].shape[0]
        load("wd", r["wd_hbm"], r["wd"])
        load("wg", r["wgate_hbm"], r["wgu"].at[:, pl.ds(0, hidden)])
        load("wu", r["wup_hbm"], r["wgu"].at[:, pl.ds(hidden, hidden)])
        load("u", r["u_hbm"], r["u"])
        load("n2", r["n2_hbm"], r["n2"])
    if attention:
        for name in ("wo", "heads", "o", "lse", "n1"):
            load(name, r[name + "_hbm"], r[name])
    place.greet(len(jobs) > 0, "swap_src" in r or last)
    if "swap_src" in r:
        jobs.append(Swap(net, r["swap_src"], r["swap_dst"]))
    tick = Ticks(plan(jobs))
    tick()
    ends = []

    def ready_inner():
        for name in ("wd", "wg", "wu"):
            waits[name].wait()

    def between():
        waits["u"].wait()
        waits["n2"].wait()
        ends.extend(back.weight_grads(r))

    def ready_attention():
        for name in ("wo", "heads", "o", "lse"):
            waits[name].wait()

    if entering and inner:
        waits["wq"].wait()
        r["ggin"][...] = back.enter(r, tick)
        r["g"] = r["gnew"]
    if inner:
        back.feed_forward(r, tick, ready_inner, between)
    if attention:
        back.attention(r, tick, ready_attention)
        waits["n1"].wait()
        width = r["land_h"].shape[2]
        tall = r["o"].shape[0]

        def grad_out():
            return dot_tn(r["land_h"][...].reshape(tall, width), r["o"][...])

        def grad_qkv():
            return dot_tn(r["n1"][...].reshape(tall, width), r["dqkv"][...])

        if not last:
            r["g_out"][...] = grad_out().astype(BF16)
            r["g_qkv"][...] = grad_qkv().astype(BF16)
        else:
            waits["wq"].wait()
            made = Ticks([[lambda: put_blocks(r["part_q"], grad_qkv()), lambda: put_blocks(r["part_o"], grad_out())]])

            def both():
                made()
                tick()

            ggain = back.enter(r, both)
            finish_last(net, r, jobs, ggain, gains_scratch)
            for copy in ends:
                copy.wait()
            net.finish()
            return
    tick.rest()
    if "swap_src" in r:
        jobs[-1].wait()
    for copy in ends:
        copy.wait()
    net.finish()


def finish_last(net, r, jobs, ggain, scratch):
    r["gsend"][...] = r["gnew"][...].astype(BF16)
    swap = Swap(net, r["gsend"], r["swap_dst"])
    swap.start()
    gains_all, gains_part = r["gains_all"], r["gains_part"]
    gains_all[...] = r["other_gains"][...]
    gains_all[0:1, :] = ggain
    gains_part[...] = jnp.zeros(gains_part.shape, BF16)
    count = gains_part.shape[0]
    piece = gains_all.shape[1] // (16 * count)
    for block in range(16 * count):
        index = (block // 16, block // 8 % 2, block // 4 % 2, block // 2 % 2, block % 2)
        gains_part[index + (slice(None), slice(0, piece))] = gains_all[
            :, block * piece : (block + 1) * piece
        ].astype(BF16)
    small = Reduce(net, gains_part, r["gains_out"], *scratch, added=True)
    small.begin()
    for step in plan_finish(jobs, small):
        step()
    swap.wait()


def plan_finish(j, s):
    return [
        s.along_a, j[1].along_zh, j[3].along_a, j[0].among_ranks, s.along_zh, j[4].along_a, j[2].along_zh,
        j[1].among_ranks, s.among_ranks, j[3].along_zh, j[2].among_ranks, j[0].done, j[4].along_zh,
        j[3].among_ranks, j[1].done, s.done, j[4].among_ranks, j[2].done, j[3].done, j[4].done,
    ]


def plan_first(j):
    return [[], [], [], [], [], [], [j[-1].start]]


def plan_middle(j):
    return [
        [j[0].begin, j[1].begin],
        [j[0].along_a, j[2].begin],
        [j[1].along_a, j[3].begin],
        [j[0].along_zh, j[4].begin],
        [],
        [j[2].along_a],
        [j[1].along_zh],
        [j[0].among_ranks, j[3].along_a],
        [j[2].along_zh],
        [j[1].among_ranks, j[4].along_a],
        [j[3].along_zh],
        [j[2].among_ranks, j[4].along_zh],
        [j[1].done, j[2].done, j[3].among_ranks, j[4].among_ranks],
        [j[0].done, j[3].done, j[4].done],
    ]


def plan_last(j):
    return [
        [j[0].begin, j[1].begin, j[2].begin],
        [j[0].along_a],
        [j[1].along_a],
        [],
        [j[0].along_zh],
        [j[2].along_a],
        [j[3].begin, j[4].begin],
    ]


def pack_weights(w_qkv, w_out, w_gate_up, gains, count, layer):
    rows = w_qkv.shape[1]
    attn_cols = HEADS * HEAD_DIM
    kv_cols = KV_HEADS * HEAD_DIM
    qkv = w_qkv[layer]
    q = qkv[:, :attn_cols].reshape(rows, RANKS, -1)
    k = qkv[:, attn_cols : attn_cols + kv_cols].reshape(rows, RANKS, -1)
    v = qkv[:, attn_cols + kv_cols :].reshape(rows, RANKS, -1)
    columns = [q, k, v]
    if layer == 0:
        scales = jnp.pad(gains.reshape(2 * LAYERS, rows).T, ((0, 0), (0, GAIN_COLS - 2 * LAYERS)))
        columns.append(jnp.broadcast_to(scales[:, None], (rows, RANKS, GAIN_COLS)))
    head = jnp.concatenate(columns, axis=2).transpose(1, 0, 2)
    out = w_out[layer].T.reshape(rows, RANKS, -1).transpose(1, 0, 2)
    gu = w_gate_up[layer].reshape(rows, 2, count, 2, 2, 2, 2, -1)
    gu = gu.transpose(1, 3, 6, 0, 2, 4, 5, 7).reshape(2, RANKS, rows, -1)
    return head, out, gu[0], gu[1]


def unpack_grads(head, out, gate, up, count):
    rows = head.shape[1]
    q_cols = HEADS * HEAD_DIM // RANKS
    kv_cols = KV_HEADS * HEAD_DIM // RANKS
    wide = lambda part: part.transpose(1, 0, 2).reshape(rows, -1)
    qkv = jnp.concatenate(
        [
            wide(head[:, :, :q_cols]),
            wide(head[:, :, q_cols : q_cols + kv_cols]),
            wide(head[:, :, q_cols + kv_cols : q_cols + 2 * kv_cols]),
        ],
        axis=1,
    )
    order = lambda part: (
        part.reshape(2, 2, rows, count, 2, 2, -1).transpose(2, 3, 0, 4, 5, 1, 6).reshape(rows, -1)
    )
    return qkv, wide(out).T, jnp.stack([order(gate), order(up)], axis=1)


VM = pl.BlockSpec(memory_space=pltpu.VMEM)
AN = pl.BlockSpec(memory_space=pl.ANY)


def params(collective_id):
    return pltpu.CompilerParams(
        collective_id=collective_id, has_side_effects=True, vmem_limit_bytes=VMEM_BYTES
    )


def like(shape, dtype=BF16):
    return jax.ShapeDtypeStruct(tuple(shape), dtype)


def full_shape(count, tail):
    return (count, 2, 2, 2, 2) + tuple(tail)


def call_start(count, tokens, pieces, later, downs):
    rows, width = tokens.shape
    n, ahead, n_down = len(pieces), len(later), len(downs)
    outs = [like((RANKS, rows, width))]
    outs += [like(full_shape(count, p.shape[1:])) for p in pieces]
    outs += [like((2, 2) + p.shape[1:]) for p in later]
    outs += [like((count, 2, 2) + d.shape) for d in downs]
    got = pl.pallas_call(
        functools.partial(start_kernel, count, n, ahead, n_down),
        out_shape=outs,
        in_specs=[AN] * len(outs),
        out_specs=[AN] * len(outs),
        scratch_shapes=[pltpu.VMEM((RANKS, rows, width), BF16)]
        + [pltpu.VMEM((2, 2) + p.shape[1:], BF16) for p in pieces]
        + sems(count),
        compiler_params=params(1),
        name="start",
    )(tokens, *pieces, *later, *downs)
    cut = n + 1 + ahead
    return got[0], [flat(f) for f in got[1 : n + 1]], got[n + 1 : cut], [flat(d) for d in got[cut:]]


def flat(value):
    return value.reshape(-1, value.shape[-1])


def call_body(count, n1, wq, tables, h, gain, wo, inner, late, plan, gain_next=None, blocks=(), swap=None):
    rows, width = h.shape
    tall = RANKS * rows
    hidden = inner[0].shape[-1]
    n_next = len(blocks)
    heads = (HEADS + 2 * KV_HEADS) // RANKS
    cols = heads * HEAD_DIM
    o_cols = HEADS // RANKS * HEAD_DIM
    three = pltpu.VMEM((3, rows, width), BF16)
    four = pltpu.VMEM((RANKS, rows, width), BF16)
    shapes = []
    for i in range(3):
        shape = inner[i].shape
        if late[i]:
            shape = full_shape(count, shape[2:]) if i < 2 else (count, 2, 2) + shape
        shapes.append(shape)
    outs = [
        like((heads, tall, 128)),
        like((tall, o_cols)),
        like((tall, 128), F32),
        like((rows, width), F32),
        like((rows, width), F32),
        like((tall, hidden), F32),
        like((tall, hidden), F32),
        like((tall, hidden)),
        like((RANKS, rows, width)),
    ]
    n_state = len(outs)
    outs += [like(shapes[i]) for i in range(3) if late[i]]
    if n_next:
        outs += [like((RANKS, rows, width))] + [like(full_shape(count, b.shape[2:])) for b in blocks]
        extra = (gain_next, *blocks)
    else:
        outs += [like(swap.shape)]
        extra = (swap,)
    got = pl.pallas_call(
        functools.partial(body_kernel, count, rows, late, n_next, plan),
        out_shape=outs,
        in_specs=[AN, AN, VM, VM, VM, VM, AN, AN, AN, AN] + ([VM] + [AN] * n_next if n_next else [AN]),
        out_specs=[VM] * (n_state - 1) + [AN] * (len(outs) - n_state + 1),
        scratch_shapes=[
            four,
            pltpu.VMEM((width, cols), BF16),
            pltpu.VMEM(wo.shape, BF16),
        ]
        + [pltpu.VMEM(shape, BF16) for shape in shapes]
        + [three, three, four, three, three]
        + ([four] if n_next else [])
        + sems(count),
        compiler_params=params(2 if n_next else 3),
        name="body_more" if n_next else "body",
    )(n1, wq, *tables, h, gain, wo, *inner, *extra)
    got = list(got)
    state, rest = got[:n_state], got[n_state:]
    inner = [flat(rest.pop(0)) if late[i] else inner[i] for i in range(3)]
    return state, inner, rest[0], [flat(f) for f in rest[1:]]


def call_back(name, count, rows, inputs, outputs, scratch, parts, made, plan, collective_id):
    shapes = [p.shape for p in parts] + list(made)
    red_out = [like(shape[-2:] if i == 0 else (RANKS,) + shape[-2:], F32) for i, shape in enumerate(shapes)]
    scratch_shapes = [pltpu.VMEM(shape, dtype) for shape, dtype in scratch.values()]
    for i, shape in enumerate(shapes):
        scratch_shapes += Reduce.scratch(shape, ranks=i > 0)
    if "gains_out" in outputs:
        scratch_shapes += Reduce.scratch(scratch["gains_part"][0])
    got = pl.pallas_call(
        functools.partial(
            back_kernel, count, rows, tuple(inputs), tuple(outputs), tuple(scratch), len(parts), len(shapes), plan
        ),
        out_shape=[shape for shape, _ in outputs.values()] + red_out,
        in_specs=[spec for _, spec in inputs.values()] + [AN] * len(parts),
        out_specs=[spec for _, spec in outputs.values()] + [VM] * len(red_out),
        scratch_shapes=scratch_shapes + sems(count),
        compiler_params=params(collective_id),
        name=name,
    )(*[value for value, _ in inputs.values()], *parts)
    return dict(zip(outputs, got)), got[len(outputs) :]


def shards(dp_size, ctx_size, tokens, cotangent, w_qkv, w_out, w_gate_up, w_down, gains):
    count = dp_size // 4
    rows, width = tokens.shape
    length = RANKS * rows
    hidden = w_gate_up.shape[-1] // RANKS
    tall = lambda value: value.reshape(length, width)
    rank = lax.rem(lax.div(lax.axis_index("dp"), 2), 2) * 2 + lax.rem(lax.axis_index("ctx"), 2)

    swap = lambda value: lax.ppermute(value, ("dp", "ctx"), swap_pairs(dp_size, ctx_size))
    tie = lax.optimization_barrier

    tables = wide_tables(length)
    windows = window_tables(length)

    packed = [pack_weights(w_qkv, w_out, w_gate_up, gains, count, layer) for layer in range(LAYERS)]
    whole_rows = w_qkv.shape[1] % 16 == 0
    if whole_rows:
        head, out, gate, up = packed[0]
        now, later, downs = (head, out, up), (gate, *packed[1]), ()
    else:
        now, later, downs = packed[0], packed[1], (w_down[0],)
    all_tokens, full, blocks, downs = call_start(count, tokens, now, later, downs)
    gain_rows = full[0][:, -GAIN_COLS:][:, : 2 * LAYERS].astype(F32).T
    gain = lambda layer, which: gain_rows[2 * layer + which][None]
    h = lax.dynamic_index_in_dim(all_tokens, rank, 0, keepdims=False)
    n1 = norm_rows(all_tokens.astype(F32), gain(0, 0))
    if whole_rows:
        inner, late, plan = (blocks[0], full[2], w_down[0]), (True, False, True), plan_late
        *blocks, last_up = blocks[1:]
    else:
        inner, late, plan = (*full[2:], *downs), (False, False, False), plan_early

    records = []
    for layer in range(LAYERS):
        wq, wo = full[:2]
        if layer + 1 < LAYERS:
            state, inner, n1_next, full = call_body(
                count, n1, wq, tables, h, gain(layer, 1), wo, inner, late, plan, gain(layer + 1, 0), blocks
            )
            if whole_rows:
                late, plan = (False, True, True), plan_late_end
                next_inner = (full[2], last_up, w_down[layer + 1])
            else:
                late, plan = (False, False, True), plan_end
                next_inner = (*full[2:], w_down[layer + 1])
        else:
            state, inner, g, _ = call_body(
                count, n1, wq, tables, h, gain(layer, 1), wo, inner, late, plan,
                swap=cotangent.astype(BF16),
            )
            n1_next = None
        heads, mixed, lse, h1, h_next, gate, up, u, n2 = state
        records.append(dict(
            hin=h, n1=n1, heads=heads, o=mixed, lse=lse, h1=h1, n2=tall(n2), gate=gate, up=up, u=u,
            wq=wq, wo=wo, wgate=inner[0], wup=inner[1], wd=inner[2],
        ))
        h, n1, inner = h_next, n1_next, next_inner

    hidden = records[0]["u"].shape[1]
    heads = (HEADS + 2 * KV_HEADS) // RANKS
    cols = heads * HEAD_DIM
    o_cols = HEADS // RANKS * HEAD_DIM
    shape7 = lambda value: value.reshape(count, 2, 2, 2, 2, -1, value.shape[-1])
    three, four = ((3, rows, width), BF16), ((RANKS, rows, width), BF16)
    row_f32 = ((rows, width), F32)

    def inner_in(layer):
        rec = records[layer]
        names = dict(wd="wd", wgate="wgate", wup="wup", u="u", n2="n2")
        values = {key + "_hbm": (rec[name], AN) for key, name in names.items()}
        return dict(
            values, gate=(rec["gate"], VM), up=(rec["up"], VM), h1=(rec["h1"], VM), gain=(gain(layer, 1), VM)
        )

    inner_out = dict(
        gh=(like((rows, width), F32), VM),
        gg=(like((1, width), F32), VM),
        g_down=(like((hidden, width)), AN),
        g_gate=(like((width, hidden)), AN),
        g_up=(like((width, hidden)), AN),
    )
    inner_scratch = dict(
        wd=((hidden, width), BF16),
        wgu=((width, 2 * hidden), BF16),
        u=((length, hidden), BF16),
        n2=((length, width), BF16),
        dgu=((length, 2 * hidden), BF16),
        buffers=((2, 256, 2 * hidden), BF16),
        land_g=four,
        out_b=three,
        land_b=three,
    )

    def attention_in(layer):
        rec = records[layer]
        values = {name + "_hbm": (rec[name], AN) for name in ("wo", "heads", "o", "lse", "n1")}
        return dict(values, cos=(windows[0], VM), sin=(windows[1], VM))

    attention_scratch = dict(
        wo=((width, o_cols), BF16),
        heads=((heads, length, 128), BF16),
        o=((length, o_cols), BF16),
        lse=((length, 128), F32),
        n1=four,
        dkv=((2 * KV_HEADS // RANKS, length, 128), F32),
        land_h=four,
    )

    def enter_in(layer):
        rec = records[layer]
        return dict(wq_hbm=(rec["wq"], AN), hin=(rec["hin"], VM), gain_in=(gain(layer, 0), VM))

    enter_scratch = dict(wq=((width, cols), BF16), out_a=three, land_a=three)

    first, _ = call_back(
        "back_first", count, rows,
        dict(g=(g, VM), swap_src=(h.astype(BF16), AN), **inner_in(1), **attention_in(1)),
        dict(
            inner_out,
            dqkv=(like((length, cols)), VM),
            g_out=(like((width, o_cols)), VM),
            g_qkv=(like((width, cols)), VM),
            swap_dst=(like((rows, width)), AN),
        ),
        dict(**inner_scratch, **attention_scratch), [], [], plan_first, 4,
    )
    parts_of = lambda got: [
        got["g_down"].reshape(count, 2, 2, -1, width),
        shape7(got["g_gate"]),
        shape7(got["g_up"]),
    ]
    middle, grads_1 = call_back(
        "back_mid", count, rows,
        dict(dqkv=(first["dqkv"], VM), ghin=(first["gh"], VM), **enter_in(1), **inner_in(0)),
        dict(ggin=(like((1, width), F32), VM), **inner_out),
        dict(gnew=row_f32, **enter_scratch, **inner_scratch),
        parts_of(first) + [shape7(first["g_out"]), shape7(first["g_qkv"])], [], plan_middle, 5,
    )
    others = jnp.concatenate([jnp.zeros((1, width), F32), middle["gg"], middle["ggin"], first["gg"]], axis=0)
    others = jnp.pad(others, ((0, 16 - 2 * LAYERS), (0, 0)))
    shard_rows = w_qkv.shape[1]
    shape_o, shape_q = (full_shape(count, (shard_rows, c)) for c in (o_cols, cols))
    final, grads_0 = call_back(
        "back_last", count, rows,
        dict(gh=(middle["gh"], VM), ghin=(middle["gh"], VM), other_gains=(others, VM), **enter_in(0), **attention_in(0)),
        dict(swap_dst=(like((rows, width)), AN), gains_out=(like((16, GAIN_COLS), F32), VM)),
        dict(
            gnew=row_f32,
            gsend=((rows, width), BF16),
            gains_all=((16, width), F32),
            gains_part=(full_shape(count, (16, GAIN_COLS)), BF16),
            part_o=(shape_o, BF16),
            part_q=(shape_q, BF16),
            dqkv=((length, cols), BF16),
            **enter_scratch,
            **attention_scratch,
        ),
        parts_of(middle), [shape_o, shape_q], plan_last, 6,
    )
    out_act, grad_tokens, gains_sum = first["swap_dst"], final["swap_dst"], final["gains_out"]
    grads = (grads_0, grads_1)
    piece = gains.shape[-1]
    grad_gains = gains_sum[: 2 * LAYERS, :piece].reshape(LAYERS, 2, piece)
    stacked = [unpack_grads(q, o, gate, up, count) for _, gate, up, o, q in grads]
    s_qkv, s_out, s_gu = (jnp.stack([s[i] for s in stacked]) for i in range(3))
    s_down = jnp.stack([g[0] for g in grads])
    return (out_act.astype(F32), grad_tokens.astype(F32), s_qkv, s_out, s_gu, s_down, grad_gains)


def solution(mesh):
    both = ("dp", "ctx")
    return jax.shard_map(
        functools.partial(shards, mesh.shape["dp"], mesh.shape["ctx"]),
        mesh=mesh,
        in_specs=(
            P(both, None),
            P(both, None),
            P(None, both, None),
            P(None, None, both),
            P(None, both, None, None),
            P(None, both, None),
            P(None, None, both),
        ),
        out_specs=(
            P(both, None),
            P(both, None),
            P(None, both, None),
            P(None, None, both),
            P(None, both, None, None),
            P(None, both, None),
            P(None, None, both),
        ),
        check_vma=False,
    )
```

```python
import functools

import jax
import jax.numpy as jnp
import numpy as np
from jax import lax
from jax.experimental import pallas as pl
from jax.experimental.pallas import tpu as pltpu
from jax.sharding import PartitionSpec as P

HEADS = 16
KV_HEADS = 8
HEAD_DIM = 96
LAYERS = 2
RANKS = 4
GAIN_COLS = 128

NORM_EPS = 1e-05
ROPE_BASE = 100000.0
MASKED = -1e30
MESH = pl.DeviceIdType.MESH
BF16 = jnp.bfloat16
F32 = jnp.float32
VMEM_BYTES = 62 * 1024 * 1024


class Place:
    def __init__(self, count):
        self.count = count
        self.dp = lax.axis_index("dp")
        self.ctx = lax.axis_index("ctx")
        self.core = lax.rem(self.dp, 2)
        self.x = lax.rem(lax.div(self.dp, 2), 2)
        self.a = lax.div(self.dp, 4)
        self.zh = lax.div(self.ctx, 2)
        self.zl = lax.rem(self.ctx, 2)
        self.rank = self.x * 2 + self.zl
        dpx = self.dp + 2 - 4 * self.x
        ctz = self.ctx + 1 - 2 * self.zl
        x2, z2 = 1 - self.x, 1 - self.zl
        self.peers = (
            ((dpx, self.ctx), x2 * 2 + self.zl),
            ((self.dp, ctz), self.x * 2 + z2),
            ((dpx, ctz), x2 * 2 + z2),
        )
        self.core_peer = (self.dp + 1 - 2 * self.core, self.ctx)
        self.zh_peer = (self.dp, self.ctx + 2 - 4 * self.zh)
        self.others = []
        for k in range(1, count):
            ahead = lax.rem(self.a + k, count)
            behind = lax.rem(self.a + count - k, count)
            self.others.append(((self.dp + (ahead - self.a) * 4, self.ctx), ahead, behind))
        self.moves = self.x != self.zh
        self.swap_peer = (self.dp + (self.zh - self.x) * 2, self.ctx + (self.x - self.zh) * 2)

    def greet(self, weights, swap):
        devices = [d for d, _ in self.peers]
        if weights:
            devices += [self.core_peer, self.zh_peer] + [o[0] for o in self.others]
        barrier = pltpu.get_barrier_semaphore()
        for device in devices:
            pl.semaphore_signal(barrier, inc=1, device_id=device, device_id_type=MESH)
        if swap:

            @pl.when(self.moves)
            def _():
                pl.semaphore_signal(barrier, inc=1, device_id=self.swap_peer, device_id_type=MESH)

        expected = len(devices)
        if swap:
            expected = expected + self.x + self.zh - 2 * self.x * self.zh
        pl.semaphore_wait(barrier, expected)


class Net:
    def __init__(self, place, send, recv, local):
        self.place, self.send, self.recv, self.local = place, send, recv, local
        self.n, self.m = 0, 0
        self.sends = []

    def remote(self, src, dst, device):
        copy = self.prepare(src, dst, device)
        copy.start()
        self.sends.append(copy)
        return copy

    def prepare(self, src, dst, device):
        i = self.n
        self.n += 1
        return pltpu.make_async_remote_copy(
            src_ref=src, dst_ref=dst, send_sem=self.send.at[i], recv_sem=self.recv.at[i],
            device_id=device, device_id_type=MESH,
        )

    def here(self, src, dst):
        i = self.m
        self.m += 1
        copy = pltpu.make_async_copy(src, dst, self.local.at[i])
        copy.start()
        return copy

    def finish(self):
        for copy in self.sends:
            copy.wait_send()


REMOTE_SEMS, LOCAL_SEMS = 128, 48


def sems(count=2):
    n = REMOTE_SEMS * max(1, count // 2)
    return [
        pltpu.SemaphoreType.DMA((n,)),
        pltpu.SemaphoreType.DMA((n,)),
        pltpu.SemaphoreType.DMA((LOCAL_SEMS,)),
    ]


class Swap:
    def __init__(self, net, src, dst):
        self.net, self.src, self.dst = net, src, dst

    def start(self):
        net, place = self.net, self.net.place
        self.copy = net.prepare(self.src, self.dst, place.swap_peer)
        self.stay = pltpu.make_async_copy(self.src, self.dst, net.local.at[net.m])
        net.m += 1

        @pl.when(place.moves)
        def _():
            self.copy.start()

        @pl.when(jnp.logical_not(place.moves))
        def _():
            self.stay.start()

    def wait(self):
        @pl.when(self.net.place.moves)
        def _():
            self.copy.wait_recv()
            self.copy.wait_send()

        @pl.when(jnp.logical_not(self.net.place.moves))
        def _():
            self.stay.wait()


class Share:
    def __init__(self, net, piece, block):
        self.net, self.piece, self.block = net, piece, block

    def start(self):
        net, place = self.net, self.net.place
        mine = self.block.at[place.x, place.zl]
        self.copies = [net.remote(self.piece.at[rank], mine, device) for device, rank in place.peers]
        self.own = net.here(self.piece.at[place.rank], mine)

    def wait(self):
        for copy in self.copies:
            copy.wait_recv()
        self.own.wait()


class Gather:
    def __init__(self, net, block, full, ranks=True):
        self.net, self.block, self.full, self.ranks = net, block, full, ranks

    def slot(self, a, core, zh):
        if self.ranks:
            return self.full.at[a, :, core, zh, :]
        return self.full.at[a, core, zh]

    def column(self, a, core):
        if self.ranks:
            return self.full.at[a, :, core, :, :]
        return self.full.at[a, core]

    def begin(self):
        net, p = self.net, self.net.place
        mine = self.slot(p.a, p.core, p.zh)
        self.across = net.remote(self.block, mine, p.zh_peer)
        self.near = [net.remote(self.block, mine, o[0]) for o in p.others]
        self.cores = [net.remote(self.block, mine, p.core_peer)]
        self.own = net.here(self.block, mine)

    def middle(self):
        net, p = self.net, self.net.place
        self.across.wait_recv()
        got = self.slot(p.a, p.core, 1 - p.zh)
        self.far = [net.remote(got, got, o[0]) for o in p.others]
        self.cores.append(net.remote(got, got, p.core_peer))

    def final(self):
        net, p = self.net, self.net.place
        for k, other in enumerate(p.others):
            self.near[k].wait_recv()
            self.far[k].wait_recv()
            got = self.column(other[2], p.core)
            self.cores.append(net.remote(got, got, p.core_peer))

    def done(self):
        self.own.wait()
        for copy in self.cores:
            copy.wait_recv()


class Reduce:
    def __init__(self, net, part, out, held, from_core, from_a, from_zh, from_rank, ranks=True, added=False):
        self.net, self.part, self.out = net, part, out
        self.held, self.from_core, self.from_a = held, from_core, from_a
        self.from_zh, self.from_rank = from_zh, from_rank
        self.ranks, self.added = ranks, added

    def half(self, core):
        return self.part.at[:, :, core] if self.ranks else self.part.at[:, core]

    def begin(self):
        net, p = self.net, self.net.place
        self.load = net.here(self.half(p.core), self.held)
        self.by_core = net.remote(self.half(1 - p.core), self.from_core, p.core_peer)

    def along_a(self):
        net, p = self.net, self.net.place
        self.load.wait()
        self.by_core.wait_recv()
        add_into(self.held, self.from_core)
        self.by_a = [
            net.remote(self.held.at[other[1]], self.from_a.at[k], other[0])
            for k, other in enumerate(p.others)
        ]

    def along_zh(self):
        net, p = self.net, self.net.place
        mine = self.held.at[p.a]
        for k, copy in enumerate(self.by_a):
            copy.wait_recv()
            add_into(mine, self.from_a.at[k])
        there = mine.at[:, 1 - p.zh] if self.ranks else mine.at[1 - p.zh]
        self.by_zh = net.remote(there, self.from_zh, p.zh_peer)

    def among_ranks(self):
        net, p = self.net, self.net.place
        self.by_zh.wait_recv()
        if not self.ranks:
            total = self.held[p.a, p.zh].astype(F32) + self.from_zh[...].astype(F32)
            self.out[...] = total.astype(self.out.dtype)
            return
        for x in range(2):
            for zl in range(2):
                add_into(self.held.at[p.a, x, p.zh, zl], self.from_zh.at[x, zl])
        self.by_rank = []
        for device, rank in p.peers:
            rank_x, rank_zl = lax.div(rank, 2), lax.rem(rank, 2)
            self.by_rank.append(
                net.remote(
                    self.held.at[p.a, rank_x, p.zh, rank_zl], self.from_rank.at[len(self.by_rank)], device
                )
            )

    def done(self):
        if not self.ranks:
            return
        p = self.net.place
        own = self.held[p.a, p.x, p.zh, p.zl].astype(F32)
        for copy in self.by_rank:
            copy.wait_recv()
        if self.added:
            for j in range(3):
                own = own + self.from_rank[j].astype(F32)
            self.out[...] = own
            return
        self.out[p.rank] = own.astype(self.out.dtype)
        for j, (_, rank) in enumerate(p.peers):
            self.out[rank] = self.from_rank[j].astype(self.out.dtype)

    @staticmethod
    def scratch(shape, ranks=True):
        tail = shape[-2:]
        count = shape[0]
        inner = ((2, 2, 2) if ranks else (2,)) + tail
        fewer = ((2, 2) if ranks else ()) + tail
        shapes = [(count,) + inner, (count,) + inner, (max(count - 1, 1),) + inner, fewer]
        if ranks:
            shapes.append((3,) + tail)
        return [pltpu.VMEM(s, BF16) for s in shapes]


def add_into(target, source):
    lead = target.shape[:-2]
    total = 1
    for size in lead:
        total *= size
    if total == 1 and not lead:
        target[...] = (target[...].astype(F32) + source[...].astype(F32)).astype(BF16)
        return

    @pl.loop(0, total)
    def _(j):
        index, left = [], j
        for size in reversed(lead):
            index.append(lax.rem(left, size))
            left = lax.div(left, size)
        index = tuple(reversed(index))
        target[index] = (target[index].astype(F32) + source[index].astype(F32)).astype(BF16)


class Spread:
    def __init__(self, net, land):
        self.net, self.land = net, land
        self.peers = net.place.peers
        mine = land.at[net.place.rank]
        self.along_x = net.remote(mine, mine, self.peers[0][0])
        self.along_zl = net.remote(mine, mine, self.peers[1][0])

    def arrivals(self):
        self.along_zl.wait_recv()
        got = self.land.at[self.peers[1][1]]
        relay = self.net.remote(got, got, self.peers[0][0])
        yield 1, self.peers[1][1]
        self.along_x.wait_recv()
        yield 0, self.peers[0][1]
        relay.wait_recv()
        yield 2, self.peers[2][1]

    def wait(self):
        for _ in self.arrivals():
            pass


class Sum:
    def __init__(self, net, out, land):
        self.net, self.out, self.land = net, out, land
        self.peers = net.place.peers

    def ready(self, i):
        if i == 2:
            self.diagonal = self.net.remote(self.out.at[2], self.land.at[0], self.peers[0][0])
        elif i == 0:
            self.along_x = self.net.remote(self.out.at[0], self.land.at[1], self.peers[0][0])

    def forward(self):
        self.diagonal.wait_recv()
        add_into(self.out.at[1], self.land.at[0])
        self.along_zl = self.net.remote(self.out.at[1], self.land.at[2], self.peers[1][0])

    def result(self, own):
        self.along_x.wait_recv()
        self.along_zl.wait_recv()
        return own + self.land[1].astype(F32) + self.land[2].astype(F32)


class EvenSpread:
    def __init__(self, net, land):
        self.net, self.land = net, land
        self.peers = net.place.peers
        self.half = land.shape[1] // 2
        me = net.place.rank
        self.x_high = self.go(me, 1, 0)
        self.z_low = self.go(me, 0, 1)
        self.x_low = self.go(me, 0, 0)
        self.z_high = self.go(me, 1, 1)

    def go(self, rank, part, i):
        rows = self.land.at[rank, pl.ds(part * self.half, self.half)]
        return self.net.remote(rows, rows, self.peers[i][0])

    def arrivals(self):
        self.x_high.wait_recv()
        on_z = self.go(self.peers[0][1], 1, 1)
        self.z_low.wait_recv()
        on_x = self.go(self.peers[1][1], 0, 0)
        self.x_low.wait_recv()
        yield 0, self.peers[0][1]
        self.z_high.wait_recv()
        yield 1, self.peers[1][1]
        on_z.wait_recv()
        on_x.wait_recv()
        yield 2, self.peers[2][1]

    def wait(self):
        for _ in self.arrivals():
            pass


class EvenSum:
    def __init__(self, net, out, land):
        self.net, self.out, self.land = net, out, land
        self.peers = net.place.peers
        self.half = out.shape[1] // 2

    def go(self, i, part, slot, peer):
        rows = pl.ds(part * self.half, self.half)
        return self.net.remote(self.out.at[i, rows], self.land.at[slot, rows], self.peers[peer][0])

    def ready(self, i):
        if i == 2:
            self.low, self.high = self.go(2, 0, 0, 0), self.go(2, 1, 0, 1)
        elif i == 0:
            self.x_low = self.go(0, 0, 1, 0)
        else:
            self.z_high = self.go(1, 1, 2, 1)

    def forward(self):
        low, high = pl.ds(0, self.half), pl.ds(self.half, self.half)
        self.high.wait_recv()
        add_into(self.out.at[0, high], self.land.at[0, high])
        self.x_high = self.go(0, 1, 1, 0)
        self.low.wait_recv()
        add_into(self.out.at[1, low], self.land.at[0, low])
        self.z_low = self.go(1, 0, 2, 1)

    def result(self, own):
        for copy in (self.x_low, self.x_high, self.z_low, self.z_high):
            copy.wait_recv()
        return own + self.land[1].astype(F32) + self.land[2].astype(F32)


def products(x, w_ref, count, tile, transposed, use):
    def part(cols):
        if transposed:
            w, dims = w_ref[cols, :], (((1,), (1,)), ((), ()))
        else:
            w, dims = w_ref[:, cols], (((1,), (0,)), ((), ()))
        use(cols, lax.dot_general(x(), w, dims, preferred_element_type=F32))

    for j in range(count // tile):
        part(pl.ds(j * tile, tile))


def norm_rows(h, gain):
    factor = lax.rsqrt(jnp.mean(h * h, axis=-1, keepdims=True) + NORM_EPS)
    return (h * factor * gain).astype(BF16)


def norm_rows_back(h, gain, grad):
    factor = lax.rsqrt(jnp.mean(h * h, axis=-1, keepdims=True) + NORM_EPS)
    z = grad * gain
    inner = jnp.sum(z * h, axis=-1, keepdims=True)
    back = factor * z - h * (factor * factor * factor * inner / h.shape[-1])
    return back, jnp.sum(grad * h * factor, axis=0, keepdims=True)


def rows_of(rank, rows):
    return pl.ds(pl.multiple_of(rank * rows, rows), rows)


class Refs:
    def __init__(self, refs):
        self.refs = list(refs)

    def take(self, n):
        got, self.refs = self.refs[:n], self.refs[n:]
        return got


class Ticks:
    def __init__(self, plan):
        self.plan = list(plan)

    def __call__(self):
        if self.plan:
            for step in self.plan.pop(0):
                step()

    def rest(self):
        while self.plan:
            self()


def np_tables(length):
    steps = np.arange(HEAD_DIM // 2, dtype=np.float32)
    inverse = np.exp(steps * np.float32(-2.0 * np.log(ROPE_BASE) / HEAD_DIM)).astype(np.float32)
    angles = np.arange(length, dtype=np.float32)[:, None] * inverse[None, :]
    return np.cos(angles), np.sin(angles)


def wide_tables(length):
    cosine, sine = np_tables(length)
    turned = (HEADS + KV_HEADS) // RANKS
    still = KV_HEADS // RANKS * HEAD_DIM
    cos_all = np.concatenate([cosine] * (2 * turned) + [np.ones((length, still))], axis=1)
    sin_all = np.concatenate([-sine, sine] * turned + [np.zeros((length, still))], axis=1)
    return jnp.asarray(cos_all, F32), jnp.asarray(sin_all, F32)


def turn(values, cosine, sine):
    cols = values.shape[1]
    half = HEAD_DIM // 2
    lane = lax.broadcasted_iota(jnp.int32, values.shape, 1)
    other = jnp.where(
        lax.rem(lane, HEAD_DIM) < half,
        pltpu.roll(values, cols - half, 1),
        pltpu.roll(values, half, 1),
    )
    return values * cosine + other * sine


def head_window(values, h):
    offset = HEAD_DIM * h
    start = offset // 128 * 128
    size = 128 if offset - start + HEAD_DIM <= 128 else 256
    window = values[:, start : start + size]
    if offset > start:
        window = pltpu.roll(window, size - (offset - start), 1)
    window = window[:, :128]
    lane = lax.broadcasted_iota(jnp.int32, window.shape, 1)
    return jnp.where(lane < HEAD_DIM, window, 0.0)


def heads_joined(parts):
    rows = parts[0].shape[0]
    columns = [jnp.zeros((rows, 128), F32) for _ in range(len(parts) * HEAD_DIM // 128 + 1)]
    for h, part in enumerate(parts):
        offset = HEAD_DIM * h
        first = offset // 128
        shift = offset - first * 128
        if shift == 0:
            columns[first] = columns[first] + part
            continue
        double = jnp.concatenate([part, jnp.zeros((rows, 128), F32)], axis=1)
        double = pltpu.roll(double, shift, 1)
        columns[first] = columns[first] + double[:, :128]
        columns[first + 1] = columns[first + 1] + double[:, 128:]
    return jnp.concatenate(columns[:-1], axis=1)


def project_heads(rows, n1, wq, cos_ref, sin_ref, heads):
    count = heads.shape[0]

    @pl.loop(0, RANKS)
    def _(b):
        span = rows_of(b, rows)
        y = jnp.dot(n1[b], wq[...], preferred_element_type=F32)
        y = turn(y, cos_ref[span, :], sin_ref[span, :])
        for h in range(count):
            heads[h, span, :] = head_window(y, h).astype(BF16)


def causal_scores(rows, rank, query, key):
    scores = lax.dot_general(query, key, (((1,), (1,)), ((), ())), preferred_element_type=F32)
    row = lax.broadcasted_iota(jnp.int32, scores.shape, 0) + rank * rows
    col = lax.broadcasted_iota(jnp.int32, scores.shape, 1)
    return jnp.where(col <= row, scores * HEAD_DIM ** (-0.5), MASKED)


def attend_rows(rows, rank, heads, o_ref, lse_ref):
    span = rows_of(rank, rows)
    queries = HEADS // RANKS
    pairs = KV_HEADS // RANKS
    groups = HEADS // KV_HEADS
    mixed = []
    lane = lax.broadcasted_iota(jnp.int32, (rows, 128), 1)
    lse_all = jnp.zeros((rows, 128), F32)
    for h in range(queries):
        kv = h // groups
        scores = causal_scores(rows, rank, heads[h, span, :], heads[queries + kv])
        highest = jnp.max(scores, axis=-1, keepdims=True)
        weights = jnp.exp(scores - highest)
        total = jnp.sum(weights, axis=-1, keepdims=True)
        lse = highest + jnp.log(total)
        lse_all = jnp.where(lane == h, lse, lse_all)
        weights = (weights * (1.0 / total)).astype(BF16)
        mixed.append(
            jnp.dot(weights, heads[queries + pairs + kv], preferred_element_type=F32)
        )
    lse_ref[span, :] = lse_all
    o_ref[span, :] = heads_joined(mixed).astype(BF16)


def window_tables(length):
    cosine, sine = np_tables(length)
    none = np.zeros((length, 128 - HEAD_DIM))
    cos_one = np.concatenate([cosine, cosine, none], axis=1)
    sin_one = np.concatenate([-sine, sine, none], axis=1)
    return jnp.asarray(cos_one, F32), jnp.asarray(sin_one, F32)


def turn_window(values, cosine, sine):
    half = HEAD_DIM // 2
    lane = lax.broadcasted_iota(jnp.int32, values.shape, 1)
    other = jnp.where(lane < half, pltpu.roll(values, 128 - half, 1), pltpu.roll(values, half, 1))
    return values * cosine + other * sine


def dot_tn(a, b):
    return lax.dot_general(a, b, (((0,), (0,)), ((), ())), preferred_element_type=F32)


def attend_rows_back(rows, rank, do_rows, heads, o_ref, lse_ref, cos_ref, sin_ref, dq_ref, dkv):
    span = rows_of(rank, rows)
    queries = HEADS // RANKS
    pairs = KV_HEADS // RANKS
    groups = HEADS // KV_HEADS
    o_rows = o_ref[span, :].astype(F32)
    parts = []
    for h in range(queries):
        kv = h // groups
        do_h = head_window(do_rows, h)
        delta = jnp.sum(do_h * head_window(o_rows, h), axis=-1, keepdims=True)
        do_b = do_h.astype(BF16)
        query, key, value = heads[h, span, :], heads[queries + kv], heads[queries + pairs + kv]
        weights = jnp.exp(causal_scores(rows, rank, query, key) - lse_ref[span, h : h + 1])
        grad_w = lax.dot_general(do_b, value, (((1,), (1,)), ((), ())), preferred_element_type=F32)
        ds = (weights * (grad_w - delta) * HEAD_DIM ** (-0.5)).astype(BF16)
        dq = jnp.dot(ds, key, preferred_element_type=F32)
        parts.append(turn_window(dq, cos_ref[span, :], -sin_ref[span, :]))
        dkv[kv] += dot_tn(ds, query)
        dkv[pairs + kv] += dot_tn(weights.astype(BF16), do_b)
    joined = heads_joined(parts)
    dq_ref[span, pl.ds(0, joined.shape[1])] = joined.astype(BF16)


def close_keys(rows, dkv, cos_ref, sin_ref, dqkv_ref):
    pairs = KV_HEADS // RANKS
    first = HEADS // RANKS * HEAD_DIM

    @pl.loop(0, RANKS)
    def _(b):
        span = rows_of(b, rows)
        parts = [turn_window(dkv[i, span, :], cos_ref[span, :], -sin_ref[span, :]) for i in range(pairs)]
        parts += [dkv[pairs + i, span, :] for i in range(pairs)]
        joined = heads_joined(parts)
        dqkv_ref[span, pl.ds(first, joined.shape[1])] = joined.astype(BF16)


def put_blocks(target, value):
    *lead, rows, cols = target.shape
    if rows % 16 == 0:
        target.reshape(value.shape[0], cols)[...] = value.astype(BF16)
        return
    for block in range(value.shape[0] // rows):
        index, left = [], block
        for size in reversed(lead):
            index.append(left % size)
            left //= size
        target[tuple(reversed(index))] = value[block * rows : (block + 1) * rows].astype(BF16)


def start_kernel(count, n, ahead, n_down, *refs):
    refs = Refs(refs)
    (tokens,) = refs.take(1)
    pieces, later, downs = refs.take(n), refs.take(ahead), refs.take(n_down)
    (all_tokens,) = refs.take(1)
    full, blocks_later, downs_full = refs.take(n), refs.take(ahead), refs.take(n_down)
    (land,) = refs.take(1)
    blocks = refs.take(n)
    send, recv, local = refs.take(3)
    place = Place(count)
    net = Net(place, send, recv, local)
    shares = [Share(net, pieces[i], blocks[i]) for i in range(n)]
    shares_later = [Share(net, later[i], blocks_later[i]) for i in range(ahead)]
    gathers = [Gather(net, blocks[i], full[i]) for i in range(n)]
    gathers += [Gather(net, downs[i], downs_full[i], ranks=False) for i in range(n_down)]
    swap = Swap(net, tokens, land.at[place.zh * 2 + place.zl])
    place.greet(True, True)
    shares[0].start()
    swap.start()
    for share in shares[1:]:
        share.start()
    for i in range(2):
        shares[i].wait()
        gathers[i].begin()
    swap.wait()
    spreads = Spread(net, land)
    for i in range(2, len(gathers)):
        if i < n:
            shares[i].wait()
        gathers[i].begin()
    arrivals = spreads.arrivals()
    next(arrivals)
    for share in shares_later:
        share.start()
    gathers[0].middle()
    gathers[1].middle()
    for _ in arrivals:
        pass
    keep = net.here(land, all_tokens)
    gathers[0].final()
    for i in range(2, len(gathers)):
        gathers[i].middle()
        gathers[i - 1].final()
    gathers[-1].final()
    for gather in gathers:
        gather.done()
    for share in shares_later:
        share.wait()
    keep.wait()
    net.finish()


def body_kernel(count, rows, late, n_next, plan, *refs):
    refs = Refs(refs)
    n1_hbm, wq_hbm, cos_ref, sin_ref, h_ref, gain_ref, wo_hbm = refs.take(7)
    inner_hbm = refs.take(3)
    if n_next:
        (gain_next,) = refs.take(1)
        blocks = refs.take(n_next)
    else:
        (swap_src,) = refs.take(1)
    heads, o_ref, lse_ref, h1_ref, hn_ref, gate_ref, up_ref, u_ref, ng_hbm = refs.take(9)
    late_out = [refs.take(1)[0] if late[i] else None for i in range(3)]
    if n_next:
        (nn_hbm,) = refs.take(1)
        full = refs.take(n_next)
    else:
        (swap_dst,) = refs.take(1)
    n1, wq, wo = refs.take(3)
    inner = refs.take(3)
    out_a, land_a, land_n, out_b, land_b = refs.take(5)
    if n_next:
        (land_q,) = refs.take(1)
    send, recv, local = refs.take(3)

    place = Place(count)
    net = Net(place, send, recv, local)
    width = h_ref.shape[1]
    hidden = u_ref.shape[1]
    load_q = net.here(wq_hbm.at[:, pl.ds(0, wq.shape[1])], wq)
    load_n = net.here(n1_hbm, n1)
    load_out = net.here(wo_hbm, wo)
    jobs = {}
    loads, weights = [], []
    for i in range(3):
        if late[i]:
            jobs[("gate", "up", "down")[i]] = Gather(net, inner_hbm[i], inner[i], ranks=i < 2)
            loads.append(None)
        else:
            loads.append(net.here(inner_hbm[i], inner[i]))
        weights.append(inner[i].reshape((hidden, width) if i == 2 else (width, hidden)) if late[i] else inner[i])
    wg, wu, wd = weights
    for i in range(n_next):
        jobs[i] = Gather(net, blocks[i], full[i])
    if not n_next:
        jobs["swap"] = Swap(net, swap_src, swap_dst)
    peers = place.peers
    place.greet(True, not n_next)
    keeps = []

    def ready(i):
        if late[i]:
            jobs[("gate", "up", "down")[i]].done()
            keeps.append(net.here(inner[i], late_out[i]))
        else:
            loads[i].wait()

    tick = Ticks(plan(jobs))
    tick()

    load_q.wait()
    load_n.wait()
    project_heads(rows, n1, wq, cos_ref, sin_ref, heads)
    load_out.wait()
    sums = EvenSum(net, out_a, land_a)
    for i in (2, 0, 1):
        attend_rows(rows, peers[i][1], heads, o_ref, lse_ref)
        span = rows_of(peers[i][1], rows)

        def use(cols, y, i=i):
            out_a[i, :, cols] = y.astype(BF16)

        products(lambda: o_ref[span, :], wo, width, width, True, use)
        sums.ready(i)
    attend_rows(rows, place.rank, heads, o_ref, lse_ref)
    span = rows_of(place.rank, rows)

    def use_own(cols, y):
        h1_ref[:, cols] = h_ref[:, cols].astype(F32) + y

    products(lambda: o_ref[span, :], wo, width, width, True, use_own)
    sums.forward()
    tick()
    h1 = sums.result(h1_ref[...])
    h1_ref[...] = h1
    land_n[place.rank] = norm_rows(h1, gain_ref[...])
    gather = EvenSpread(net, land_n)
    tick()
    ready(0)
    ready(1)

    def inner_block(rank):
        span = rows_of(rank, rows)

        gate = jnp.dot(land_n[rank], wg[...], preferred_element_type=F32)
        up = jnp.dot(land_n[rank], wu[...], preferred_element_type=F32)
        gate_ref[span, :] = gate.astype(BF16)
        up_ref[span, :] = up.astype(BF16)
        u_ref[span, :] = (gate / (1.0 + jnp.exp(-gate)) * up).astype(BF16)

        return span

    inner_block(place.rank)
    tick()
    second = EvenSum(net, out_b, land_b)
    got_down = False
    for i, rank in gather.arrivals():
        span = inner_block(rank)
        if not got_down:
            tick()
            ready(2)
            got_down = True

        def use(cols, y, i=i):
            out_b[i, :, cols] = y.astype(BF16)

        products(lambda: u_ref[span, :], wd, width, width, False, use)
        second.ready(i)
        tick()
    keep = net.here(land_n, ng_hbm)
    span = rows_of(place.rank, rows)

    def use_down(cols, y):
        hn_ref[:, cols] = h1_ref[:, cols] + y

    products(lambda: u_ref[span, :], wd, width, width, False, use_down)
    second.forward()
    tick()
    hn = second.result(hn_ref[...])
    hn_ref[...] = hn
    if n_next:
        land_q[place.rank] = norm_rows(hn, gain_next[...])
        third = EvenSpread(net, land_q)
        tick()
        for _ in third.arrivals():
            tick()
        keep_next = net.here(land_q, nn_hbm)
        keep_next.wait()
    tick.rest()
    for i in range(n_next):
        jobs[i].done()
    if not n_next:
        jobs["swap"].wait()
    keep.wait()
    for copy in keeps:
        copy.wait()
    net.finish()


def plan_late(j):
    gate, down = j["gate"], j["down"]
    return [
        [gate.begin],
        [gate.middle, down.begin],
        [gate.final],
        [down.middle, j[0].begin, j[1].begin],
        [down.final],
        [],
        [],
        [j[0].middle],
        [j[0].final, j[1].middle],
        [j[2].begin, j[1].final],
        [],
        [],
        [j[2].middle],
        [j[2].final],
    ]


def plan_late_end(j):
    up, down = j["up"], j["down"]
    return [
        [up.begin],
        [up.middle, down.begin],
        [up.final],
        [down.middle],
        [down.final],
        [],
        [],
        [j["swap"].start],
    ]


def plan_early(j):
    return [
        [j[0].begin],
        [j[1].begin],
        [j[0].middle, j[1].middle, j[2].begin],
        [],
        [j[0].final],
        [j[1].final],
        [j[2].middle],
        [],
        [j[3].begin, j[2].final],
        [],
        [],
        [],
        [j[3].middle],
        [j[3].final],
    ]


def plan_end(j):
    down = j["down"]
    return [
        [down.begin],
        [],
        [down.middle],
        [],
        [down.final],
        [],
        [],
        [j["swap"].start],
    ]


class Back:
    def __init__(self, net, rows):
        self.net, self.place, self.rows = net, net.place, rows
        self.peers = net.place.peers

    def enter(self, r, tick):
        rows, place = self.rows, self.place
        width = r["gnew"].shape[1]
        total = EvenSum(self.net, r["out_a"], r["land_a"])
        for i in (2, 0, 1):
            span = rows_of(self.peers[i][1], rows)

            def use(cols, y, i=i):
                r["out_a"][i, :, cols] = y.astype(BF16)

            products(lambda: r["dqkv"][span, :], r["wq"], width, width, True, use)
            total.ready(i)
        tick()
        own = rows_of(place.rank, rows)

        def use_own(cols, y):
            r["gnew"][:, cols] = y

        products(lambda: r["dqkv"][own, :], r["wq"], width, width, True, use_own)
        total.forward()
        tick()
        dn = total.result(r["gnew"][...])
        back, ggain = norm_rows_back(r["hin"][...].astype(F32), r["gain_in"][...], dn)
        r["gnew"][...] = r["ghin"][...] + back
        return ggain

    def feed_forward(self, r, tick, ready, between):
        net, rows, place = self.net, self.rows, self.place
        land_g, dgu, out_b = r["land_g"], r["dgu"], r["out_b"]
        width = land_g.shape[2]
        hidden = r["gate"].shape[1]
        land_g[place.rank] = r["g"][...].astype(BF16)
        gather = EvenSpread(net, land_g)
        tick()
        ready()

        def inner_block(rank):
            span = rows_of(rank, rows)
            du = lax.dot_general(
                land_g[rank], r["wd"][...], (((1,), (1,)), ((), ())), preferred_element_type=F32
            )
            gate, up = r["gate"][span, :].astype(F32), r["up"][span, :].astype(F32)
            sg = 1.0 / (1.0 + jnp.exp(-gate))
            dgu[span, pl.ds(0, hidden)] = (du * up * sg * (1.0 + gate * (1.0 - sg))).astype(BF16)
            dgu[span, pl.ds(hidden, hidden)] = (du * gate * sg).astype(BF16)
            return span

        span = inner_block(place.rank)

        def use_mid(cols, y):
            r["gh"][:, cols] = y

        products(lambda: dgu[span, :], r["wgu"], width, width, True, use_mid)
        tick()
        second = EvenSum(net, out_b, r["land_b"])
        for i, rank in gather.arrivals():
            span = inner_block(rank)

            def use(cols, y, i=i):
                out_b[i, :, cols] = y.astype(BF16)

            products(lambda: dgu[span, :], r["wgu"], width, width, True, use)
            second.ready(i)
            tick()
        second.forward()
        tick()
        between()
        tick()
        dn = second.result(r["gh"][...])
        back, ggain = norm_rows_back(r["h1"][...], r["gain"][...], dn)
        r["gh"][...] = r["g"][...].astype(F32) + back
        r["gg"][...] = ggain

    def weight_grads(self, r, down_made):
        net = self.net
        buffers, copies = r["buffers"], []
        tile = buffers.shape[1]
        tall, hidden = r["u"].shape
        width = r["land_g"].shape[2]
        g_all = r["land_g"][...].reshape(tall, width)

        def emit(lhs, rhs, outs, m):
            slot = len(copies) % 2
            if len(copies) >= 2:
                for copy in copies[-2]:
                    copy.wait()
            buffers[slot, :, pl.ds(0, rhs.shape[1])] = dot_tn(lhs, rhs).astype(BF16)
            cols = rhs.shape[1] // len(outs)
            copies.append([
                net.here(buffers.at[slot, :, pl.ds(k * cols, cols)], out.at[pl.ds(m * tile, tile)])
                for k, out in enumerate(outs)
            ])

        for k, part in enumerate((r["part_da"], r["part_db"])):
            cols = part.shape[-1]
            made = dot_tn(r["u"][...], g_all[:, k * cols : (k + 1) * cols])
            part.reshape(hidden, cols)[...] = made.astype(BF16)
        down_made()
        for m in range(width // tile):
            emit(r["n2"][:, m * tile : (m + 1) * tile], r["dgu"][...], [r["g_gate"], r["g_up"]], m)
        return copies[-2] + copies[-1]

    def attention(self, r, tick, ready):
        net, rows, place = self.net, self.rows, self.place
        land_h = r["land_h"]
        land_h[place.rank] = r["gh"][...].astype(BF16)
        gather = EvenSpread(net, land_h)
        tick()
        ready()
        r["dkv"][...] = jnp.zeros(r["dkv"].shape, F32)

        def block(rank):
            do_rows = jnp.dot(land_h[rank], r["wo"][...], preferred_element_type=F32)
            do_rows = do_rows.astype(BF16).astype(F32)
            attend_rows_back(
                rows, rank, do_rows, r["heads"], r["o"], r["lse"], r["cos"], r["sin"], r["dqkv"], r["dkv"]
            )

        block(place.rank)
        tick()
        for _, rank in gather.arrivals():
            block(rank)
            tick()
        close_keys(rows, r["dkv"], r["cos"], r["sin"], r["dqkv"])


ATTEND = ("wo", "heads", "o", "lse", "cos", "sin")


def back_kernel(count, rows, names, out_names, scratch_names, n_parts, kinds, plan, *refs):
    refs = Refs(refs)
    r = dict(zip(names, refs.take(len(names))))
    parts = refs.take(n_parts)
    r.update(zip(out_names, refs.take(len(out_names))))
    red_out = refs.take(len(kinds))
    r.update(zip(scratch_names, refs.take(len(scratch_names))))
    red_scratch = [refs.take(5 if ranks else 4) for ranks in kinds]
    gains_scratch = refs.take(5) if "gains_out" in r else None
    send, recv, local = refs.take(3)

    place = Place(count)
    net = Net(place, send, recv, local)
    back = Back(net, rows)
    entering, inner, attention = "hin" in r, "h1" in r, "heads_hbm" in r
    last = "gains_out" in r
    waits = {}

    def load(name, source, target):
        waits[name] = net.here(source, target)

    parts = parts + ([r["part_o"], r["part_q"]] if last else [r["part_da"], r["part_db"]])
    jobs = []
    for part, out, scratch, ranks in zip(parts, red_out, red_scratch, kinds):
        jobs.append(Reduce(net, part, out, *scratch, *([] if ranks else [None]), ranks=ranks))
    if entering:
        load("wq", r["wq_hbm"].at[:, pl.ds(0, r["wq"].shape[1])], r["wq"])
    if inner:
        hidden = r["wd"].shape[0]
        load("wd", r["wd_hbm"], r["wd"])
        load("wg", r["wgate_hbm"], r["wgu"].at[:, pl.ds(0, hidden)])
        load("wu", r["wup_hbm"], r["wgu"].at[:, pl.ds(hidden, hidden)])
        load("u", r["u_hbm"], r["u"])
        load("n2", r["n2_hbm"], r["n2"])
    if attention:
        for name in ("wo", "heads", "o", "lse", "n1"):
            load(name, r[name + "_hbm"], r[name])
    place.greet(len(jobs) > 0, "swap_src" in r or last)
    if "swap_src" in r:
        jobs.append(Swap(net, r["swap_src"], r["swap_dst"]))
    tick = Ticks(plan(jobs))
    tick()
    ends = []

    def ready_inner():
        for name in ("wd", "wg", "wu"):
            waits[name].wait()

    def between():
        waits["u"].wait()
        waits["n2"].wait()
        ends.extend(back.weight_grads(r, tick))

    def ready_attention():
        for name in ("wo", "heads", "o", "lse"):
            waits[name].wait()

    if entering and inner:
        waits["wq"].wait()
        r["ggin"][...] = back.enter(r, tick)
        r["g"] = r["gnew"]
    if inner:
        back.feed_forward(r, tick, ready_inner, between)
    if attention:
        back.attention(r, tick, ready_attention)
        waits["n1"].wait()
        width = r["land_h"].shape[2]
        tall = r["o"].shape[0]

        def grad_out():
            return dot_tn(r["land_h"][...].reshape(tall, width), r["o"][...])

        def grad_qkv():
            return dot_tn(r["n1"][...].reshape(tall, width), r["dqkv"][...])

        if not last:
            r["g_out"][...] = grad_out().astype(BF16)
            r["g_qkv"][...] = grad_qkv().astype(BF16)
        else:
            waits["wq"].wait()
            made = Ticks([
                [],
                [lambda: put_blocks(r["part_q"], grad_qkv()), lambda: put_blocks(r["part_o"], grad_out())],
            ])

            def both():
                made()
                tick()

            ggain = back.enter(r, both)
            finish_last(net, r, jobs, ggain, gains_scratch)
            for copy in ends:
                copy.wait()
            net.finish()
            return
    tick.rest()
    if "swap_src" in r:
        jobs[-1].wait()
    for copy in ends:
        copy.wait()
    net.finish()


def finish_last(net, r, jobs, ggain, scratch):
    r["gsend"][...] = r["gnew"][...].astype(BF16)
    swap = Swap(net, r["gsend"], r["swap_dst"])
    gains_all, gains_part = r["gains_all"], r["gains_part"]
    gains_all[...] = r["other_gains"][...]
    gains_all[0:1, :] = ggain
    gains_part[...] = jnp.zeros(gains_part.shape, BF16)
    count = gains_part.shape[0]
    piece = gains_all.shape[1] // (16 * count)
    for block in range(16 * count):
        index = (block // 16, block // 8 % 2, block // 4 % 2, block // 2 % 2, block % 2)
        gains_part[index + (slice(None), slice(0, piece))] = gains_all[
            :, block * piece : (block + 1) * piece
        ].astype(BF16)
    small = Reduce(net, gains_part, r["gains_out"], *scratch, added=True)
    small.begin()
    for step in plan_finish(jobs, small, swap):
        step()
    swap.wait()


def plan_finish(j, s, swap):
    return [
        s.along_a, j[2].along_a, j[3].along_a, j[1].along_zh, j[0].among_ranks, s.along_zh, j[2].along_zh,
        s.among_ranks, j[3].along_zh, swap.start, j[1].among_ranks, j[0].done, j[2].among_ranks, s.done, j[1].done,
        j[3].among_ranks, j[2].done, j[3].done,
    ]


def plan_first(j):
    da, db, swap = j
    return [
        [],
        [],
        [],
        [],
        [],
        [],
        [swap.start],
        [da.begin, db.begin],
        [da.along_a],
        [db.along_a],
        [],
        [da.along_zh],
        [db.along_zh],
        [],
        [da.among_ranks, db.among_ranks],
    ]


def plan_middle(j):
    gate, up, out, qkv, da, db = j
    return [
        [gate.begin, up.begin, out.begin, qkv.begin],
        [gate.along_a],
        [up.along_a],
        [],
        [out.along_a],
        [gate.along_zh],
        [qkv.along_a],
        [],
        [up.along_zh],
        [da.begin, db.begin],
        [gate.among_ranks, da.along_a],
        [out.along_zh, db.along_a, qkv.along_zh, up.among_ranks, out.among_ranks, gate.done, da.along_zh, up.done],
        [qkv.among_ranks, db.along_zh, out.done, qkv.done, da.among_ranks, db.among_ranks],
    ]


def plan_last(j):
    gate, up, out, qkv = j
    return [
        [gate.begin, up.begin],
        [gate.along_a],
        [],
        [up.along_a],
        [],
        [gate.along_zh],
        [],
        [out.begin, qkv.begin],
    ]


def pack_weights(w_qkv, w_out, w_gate_up, gains, count, layer):
    rows = w_qkv.shape[1]
    attn_cols = HEADS * HEAD_DIM
    kv_cols = KV_HEADS * HEAD_DIM
    qkv = w_qkv[layer]
    q = qkv[:, :attn_cols].reshape(rows, RANKS, -1)
    k = qkv[:, attn_cols : attn_cols + kv_cols].reshape(rows, RANKS, -1)
    v = qkv[:, attn_cols + kv_cols :].reshape(rows, RANKS, -1)
    columns = [q, k, v]
    if layer == 0:
        scales = jnp.pad(gains.reshape(2 * LAYERS, rows).T, ((0, 0), (0, GAIN_COLS - 2 * LAYERS)))
        columns.append(jnp.broadcast_to(scales[:, None], (rows, RANKS, GAIN_COLS)))
    head = jnp.concatenate(columns, axis=2).transpose(1, 0, 2)
    out = w_out[layer].T.reshape(rows, RANKS, -1).transpose(1, 0, 2)
    gu = w_gate_up[layer].reshape(rows, 2, count, 2, 2, 2, 2, -1)
    gu = gu.transpose(1, 3, 6, 0, 2, 4, 5, 7).reshape(2, RANKS, rows, -1)
    return head, out, gu[0], gu[1]


def unpack_grads(head, out, gate, up, count):
    rows = head.shape[1]
    q_cols = HEADS * HEAD_DIM // RANKS
    kv_cols = KV_HEADS * HEAD_DIM // RANKS
    wide = lambda part: part.transpose(1, 0, 2).reshape(rows, -1)
    qkv = jnp.concatenate(
        [
            wide(head[:, :, :q_cols]),
            wide(head[:, :, q_cols : q_cols + kv_cols]),
            wide(head[:, :, q_cols + kv_cols : q_cols + 2 * kv_cols]),
        ],
        axis=1,
    )
    order = lambda part: (
        part.reshape(2, 2, rows, count, 2, 2, -1).transpose(2, 3, 0, 4, 5, 1, 6).reshape(rows, -1)
    )
    return qkv, wide(out).T, jnp.stack([order(gate), order(up)], axis=1)


VM = pl.BlockSpec(memory_space=pltpu.VMEM)
AN = pl.BlockSpec(memory_space=pl.ANY)


def params(collective_id):
    return pltpu.CompilerParams(
        collective_id=collective_id, has_side_effects=True, vmem_limit_bytes=VMEM_BYTES
    )


def like(shape, dtype=BF16):
    return jax.ShapeDtypeStruct(tuple(shape), dtype)


def full_shape(count, tail):
    return (count, 2, 2, 2, 2) + tuple(tail)


def call_start(count, tokens, pieces, later, downs):
    rows, width = tokens.shape
    n, ahead, n_down = len(pieces), len(later), len(downs)
    outs = [like((RANKS, rows, width))]
    outs += [like(full_shape(count, p.shape[1:])) for p in pieces]
    outs += [like((2, 2) + p.shape[1:]) for p in later]
    outs += [like((count, 2, 2) + d.shape) for d in downs]
    got = pl.pallas_call(
        functools.partial(start_kernel, count, n, ahead, n_down),
        out_shape=outs,
        in_specs=[AN] * len(outs),
        out_specs=[AN] * len(outs),
        scratch_shapes=[pltpu.VMEM((RANKS, rows, width), BF16)]
        + [pltpu.VMEM((2, 2) + p.shape[1:], BF16) for p in pieces]
        + sems(count),
        compiler_params=params(1),
        name="start",
    )(tokens, *pieces, *later, *downs)
    cut = n + 1 + ahead
    return got[0], [flat(f) for f in got[1 : n + 1]], got[n + 1 : cut], [flat(d) for d in got[cut:]]


def flat(value):
    return value.reshape(-1, value.shape[-1])


def call_body(count, n1, wq, tables, h, gain, wo, inner, late, plan, gain_next=None, blocks=(), swap=None):
    rows, width = h.shape
    tall = RANKS * rows
    hidden = inner[0].shape[-1]
    n_next = len(blocks)
    heads = (HEADS + 2 * KV_HEADS) // RANKS
    cols = heads * HEAD_DIM
    o_cols = HEADS // RANKS * HEAD_DIM
    three = pltpu.VMEM((3, rows, width), BF16)
    four = pltpu.VMEM((RANKS, rows, width), BF16)
    shapes = []
    for i in range(3):
        shape = inner[i].shape
        if late[i]:
            shape = full_shape(count, shape[2:]) if i < 2 else (count, 2, 2) + shape
        shapes.append(shape)
    outs = [
        like((heads, tall, 128)),
        like((tall, o_cols)),
        like((tall, 128), F32),
        like((rows, width), F32),
        like((rows, width), F32),
        like((tall, hidden)),
        like((tall, hidden)),
        like((tall, hidden)),
        like((RANKS, rows, width)),
    ]
    n_state = len(outs)
    outs += [like(shapes[i]) for i in range(3) if late[i]]
    if n_next:
        outs += [like((RANKS, rows, width))] + [like(full_shape(count, b.shape[2:])) for b in blocks]
        extra = (gain_next, *blocks)
    else:
        outs += [like(swap.shape)]
        extra = (swap,)
    got = pl.pallas_call(
        functools.partial(body_kernel, count, rows, late, n_next, plan),
        out_shape=outs,
        in_specs=[AN, AN, VM, VM, VM, VM, AN, AN, AN, AN] + ([VM] + [AN] * n_next if n_next else [AN]),
        out_specs=[VM] * (n_state - 1) + [AN] * (len(outs) - n_state + 1),
        scratch_shapes=[
            four,
            pltpu.VMEM((width, cols), BF16),
            pltpu.VMEM(wo.shape, BF16),
        ]
        + [pltpu.VMEM(shape, BF16) for shape in shapes]
        + [three, three, four, three, three]
        + ([four] if n_next else [])
        + sems(count),
        compiler_params=params(2 if n_next else 3),
        name="body_more" if n_next else "body",
    )(n1, wq, *tables, h, gain, wo, *inner, *extra)
    got = list(got)
    state, rest = got[:n_state], got[n_state:]
    inner = [flat(rest.pop(0)) if late[i] else inner[i] for i in range(3)]
    return state, inner, rest[0], [flat(f) for f in rest[1:]]


def call_back(name, count, rows, inputs, outputs, scratch, parts, made, kinds, plan, collective_id):
    shapes = [p.shape for p in parts] + list(made)
    red_out = [like(((RANKS,) if ranks else ()) + shape[-2:]) for shape, ranks in zip(shapes, kinds)]
    scratch_shapes = [pltpu.VMEM(shape, dtype) for shape, dtype in scratch.values()]
    for shape, ranks in zip(shapes, kinds):
        scratch_shapes += Reduce.scratch(shape, ranks=ranks)
    if "gains_out" in outputs:
        scratch_shapes += Reduce.scratch(scratch["gains_part"][0])
    got = pl.pallas_call(
        functools.partial(
            back_kernel, count, rows, tuple(inputs), tuple(outputs), tuple(scratch), len(parts), kinds, plan
        ),
        out_shape=[shape for shape, _ in outputs.values()] + red_out,
        in_specs=[spec for _, spec in inputs.values()] + [AN] * len(parts),
        out_specs=[spec for _, spec in outputs.values()] + [VM] * len(red_out),
        scratch_shapes=scratch_shapes + sems(count),
        compiler_params=params(collective_id),
        name=name,
    )(*[value for value, _ in inputs.values()], *parts)
    return dict(zip(outputs, got)), got[len(outputs) :]


def shards(dp_size, ctx_size, tokens, cotangent, w_qkv, w_out, w_gate_up, w_down, gains):
    count = dp_size // 4
    rows, width = tokens.shape
    length = RANKS * rows
    hidden = w_gate_up.shape[-1] // RANKS
    tall = lambda value: value.reshape(length, width)
    rank = lax.rem(lax.div(lax.axis_index("dp"), 2), 2) * 2 + lax.rem(lax.axis_index("ctx"), 2)

    swap = lambda value: lax.ppermute(value, ("dp", "ctx"), swap_pairs(dp_size, ctx_size))
    tie = lax.optimization_barrier

    tables = wide_tables(length)
    windows = window_tables(length)

    packed = [pack_weights(w_qkv, w_out, w_gate_up, gains, count, layer) for layer in range(LAYERS)]
    whole_rows = w_qkv.shape[1] % 16 == 0
    if whole_rows:
        head, out, gate, up = packed[0]
        now, later, downs = (head, out, up), (gate, *packed[1]), ()
    else:
        now, later, downs = packed[0], packed[1], (w_down[0],)
    all_tokens, full, blocks, downs = call_start(count, tokens, now, later, downs)
    gain_rows = full[0][:, -GAIN_COLS:][:, : 2 * LAYERS].astype(F32).T
    gain = lambda layer, which: gain_rows[2 * layer + which][None]
    h = lax.dynamic_index_in_dim(all_tokens, rank, 0, keepdims=False)
    n1 = norm_rows(all_tokens.astype(F32), gain(0, 0))
    if whole_rows:
        inner, late, plan = (blocks[0], full[2], w_down[0]), (True, False, True), plan_late
        *blocks, last_up = blocks[1:]
    else:
        inner, late, plan = (*full[2:], *downs), (False, False, False), plan_early

    records = []
    for layer in range(LAYERS):
        wq, wo = full[:2]
        if layer + 1 < LAYERS:
            state, inner, n1_next, full = call_body(
                count, n1, wq, tables, h, gain(layer, 1), wo, inner, late, plan, gain(layer + 1, 0), blocks
            )
            if whole_rows:
                late, plan = (False, True, True), plan_late_end
                next_inner = (full[2], last_up, w_down[layer + 1])
            else:
                late, plan = (False, False, True), plan_end
                next_inner = (*full[2:], w_down[layer + 1])
        else:
            state, inner, g, _ = call_body(
                count, n1, wq, tables, h, gain(layer, 1), wo, inner, late, plan,
                swap=cotangent.astype(BF16),
            )
            n1_next = None
        heads, mixed, lse, h1, h_next, gate, up, u, n2 = state
        records.append(dict(
            hin=h, n1=n1, heads=heads, o=mixed, lse=lse, h1=h1, n2=tall(n2), gate=gate, up=up, u=u,
            wq=wq, wo=wo, wgate=inner[0], wup=inner[1], wd=inner[2],
        ))
        h, n1, inner = h_next, n1_next, next_inner

    hidden = records[0]["u"].shape[1]
    heads = (HEADS + 2 * KV_HEADS) // RANKS
    cols = heads * HEAD_DIM
    o_cols = HEADS // RANKS * HEAD_DIM
    shape7 = lambda value: value.reshape(count, 2, 2, 2, 2, -1, value.shape[-1])
    three, four = ((3, rows, width), BF16), ((RANKS, rows, width), BF16)
    row_f32 = ((rows, width), F32)

    def inner_in(layer):
        rec = records[layer]
        names = dict(wd="wd", wgate="wgate", wup="wup", u="u", n2="n2")
        values = {key + "_hbm": (rec[name], AN) for key, name in names.items()}
        return dict(
            values, gate=(rec["gate"], VM), up=(rec["up"], VM), h1=(rec["h1"], VM), gain=(gain(layer, 1), VM)
        )

    inner_out = dict(
        gh=(like((rows, width), F32), VM),
        gg=(like((1, width), F32), VM),
        g_gate=(like((width, hidden)), AN),
        g_up=(like((width, hidden)), AN),
    )
    shape_d = (count, 2, 2, w_down.shape[1], width // 2)
    inner_scratch = dict(
        part_da=(shape_d, BF16),
        part_db=(shape_d, BF16),
        wd=((hidden, width), BF16),
        wgu=((width, 2 * hidden), BF16),
        u=((length, hidden), BF16),
        n2=((length, width), BF16),
        dgu=((length, 2 * hidden), BF16),
        buffers=((2, 256, 2 * hidden), BF16),
        land_g=four,
        out_b=three,
        land_b=three,
    )

    def attention_in(layer):
        rec = records[layer]
        values = {name + "_hbm": (rec[name], AN) for name in ("wo", "heads", "o", "lse", "n1")}
        return dict(values, cos=(windows[0], VM), sin=(windows[1], VM))

    attention_scratch = dict(
        wo=((width, o_cols), BF16),
        heads=((heads, length, 128), BF16),
        o=((length, o_cols), BF16),
        lse=((length, 128), F32),
        n1=four,
        dkv=((2 * KV_HEADS // RANKS, length, 128), F32),
        land_h=four,
    )

    def enter_in(layer):
        rec = records[layer]
        return dict(wq_hbm=(rec["wq"], AN), hin=(rec["hin"], VM), gain_in=(gain(layer, 0), VM))

    enter_scratch = dict(wq=((width, cols), BF16), out_a=three, land_a=three)

    first, down_1 = call_back(
        "back_first", count, rows,
        dict(g=(g, VM), swap_src=(h.astype(BF16), AN), **inner_in(1), **attention_in(1)),
        dict(
            inner_out,
            dqkv=(like((length, cols)), VM),
            g_out=(like((width, o_cols)), VM),
            g_qkv=(like((width, cols)), VM),
            swap_dst=(like((rows, width)), AN),
        ),
        dict(**inner_scratch, **attention_scratch), [], [shape_d] * 2, (False,) * 2, plan_first, 4,
    )
    parts_of = lambda got: [shape7(got["g_gate"]), shape7(got["g_up"])]
    middle, grads_1 = call_back(
        "back_mid", count, rows,
        dict(dqkv=(first["dqkv"], VM), ghin=(first["gh"], VM), **enter_in(1), **inner_in(0)),
        dict(ggin=(like((1, width), F32), VM), **inner_out),
        dict(gnew=row_f32, **enter_scratch, **inner_scratch),
        parts_of(first) + [shape7(first["g_out"]), shape7(first["g_qkv"])],
        [shape_d] * 2, (True,) * 4 + (False,) * 2, plan_middle, 5,
    )
    others = jnp.concatenate([jnp.zeros((1, width), F32), middle["gg"], middle["ggin"], first["gg"]], axis=0)
    others = jnp.pad(others, ((0, 16 - 2 * LAYERS), (0, 0)))
    shard_rows = w_qkv.shape[1]
    shape_o, shape_q = (full_shape(count, (shard_rows, c)) for c in (o_cols, cols))
    final, grads_0 = call_back(
        "back_last", count, rows,
        dict(gh=(middle["gh"], VM), ghin=(middle["gh"], VM), other_gains=(others, VM), **enter_in(0), **attention_in(0)),
        dict(swap_dst=(like((rows, width)), AN), gains_out=(like((16, GAIN_COLS), F32), VM)),
        dict(
            gnew=row_f32,
            gsend=((rows, width), BF16),
            gains_all=((16, width), F32),
            gains_part=(full_shape(count, (16, GAIN_COLS)), BF16),
            part_o=(shape_o, BF16),
            part_q=(shape_q, BF16),
            dqkv=((length, cols), BF16),
            **enter_scratch,
            **attention_scratch,
        ),
        parts_of(middle), [shape_o, shape_q], (True,) * 4, plan_last, 6,
    )
    out_act, grad_tokens, gains_sum = first["swap_dst"], final["swap_dst"], final["gains_out"]
    grads = (grads_0, grads_1[:4])
    downs = (grads_1[4:], down_1)
    piece = gains.shape[-1]
    grad_gains = gains_sum[: 2 * LAYERS, :piece].reshape(LAYERS, 2, piece)
    stacked = [unpack_grads(q, o, gate, up, count) for gate, up, o, q in grads]
    s_qkv, s_out, s_gu = (jnp.stack([s[i] for s in stacked]) for i in range(3))
    s_down = jnp.stack([jnp.concatenate(d, axis=1) for d in downs])
    wide = lambda value: value.astype(F32)
    return (wide(out_act), wide(grad_tokens), wide(s_qkv), wide(s_out), wide(s_gu), wide(s_down), grad_gains)


def solution(mesh):
    both = ("dp", "ctx")
    return jax.shard_map(
        functools.partial(shards, mesh.shape["dp"], mesh.shape["ctx"]),
        mesh=mesh,
        in_specs=(
            P(both, None),
            P(both, None),
            P(None, both, None),
            P(None, None, both),
            P(None, both, None, None),
            P(None, both, None),
            P(None, None, both),
        ),
        out_specs=(
            P(both, None),
            P(both, None),
            P(None, both, None),
            P(None, None, both),
            P(None, both, None, None),
            P(None, both, None),
            P(None, None, both),
        ),
        check_vma=False,
    )
```

```python
import functools

import jax
import jax.numpy as jnp
import numpy as np
from jax import lax
from jax.experimental import pallas as pl
from jax.experimental.pallas import tpu as pltpu
from jax.sharding import PartitionSpec as P

HEADS = 16
KV_HEADS = 8
HEAD_DIM = 96
LAYERS = 2
RANKS = 4
GAIN_COLS = 128

NORM_EPS = 1e-05
ROPE_BASE = 100000.0
MASKED = -1e30
MESH = pl.DeviceIdType.MESH
BF16 = jnp.bfloat16
F32 = jnp.float32
VMEM_BYTES = 62 * 1024 * 1024


class Place:
    def __init__(self, count):
        self.count = count
        self.dp = lax.axis_index("dp")
        self.ctx = lax.axis_index("ctx")
        self.core = lax.rem(self.dp, 2)
        self.x = lax.rem(lax.div(self.dp, 2), 2)
        self.a = lax.div(self.dp, 4)
        self.zh = lax.div(self.ctx, 2)
        self.zl = lax.rem(self.ctx, 2)
        self.rank = self.x * 2 + self.zl
        dpx = self.dp + 2 - 4 * self.x
        ctz = self.ctx + 1 - 2 * self.zl
        x2, z2 = 1 - self.x, 1 - self.zl
        self.peers = (
            ((dpx, self.ctx), x2 * 2 + self.zl),
            ((self.dp, ctz), self.x * 2 + z2),
            ((dpx, ctz), x2 * 2 + z2),
        )
        self.core_peer = (self.dp + 1 - 2 * self.core, self.ctx)
        self.zh_peer = (self.dp, self.ctx + 2 - 4 * self.zh)
        self.others = []
        for k in range(1, count):
            ahead = lax.rem(self.a + k, count)
            behind = lax.rem(self.a + count - k, count)
            self.others.append(((self.dp + (ahead - self.a) * 4, self.ctx), ahead, behind))
        self.moves = self.x != self.zh
        self.swap_peer = (self.dp + (self.zh - self.x) * 2, self.ctx + (self.x - self.zh) * 2)

    def greet(self, weights, swap):
        devices = [d for d, _ in self.peers]
        if weights:
            devices += [self.core_peer, self.zh_peer] + [o[0] for o in self.others]
        barrier = pltpu.get_barrier_semaphore()
        for device in devices:
            pl.semaphore_signal(barrier, inc=1, device_id=device, device_id_type=MESH)
        if swap:

            @pl.when(self.moves)
            def _():
                pl.semaphore_signal(barrier, inc=1, device_id=self.swap_peer, device_id_type=MESH)

        expected = len(devices)
        if swap:
            expected = expected + self.x + self.zh - 2 * self.x * self.zh
        pl.semaphore_wait(barrier, expected)


class Net:
    def __init__(self, place, send, recv, local):
        self.place, self.send, self.recv, self.local = place, send, recv, local
        self.n, self.m = 0, 0
        self.sends = []

    def remote(self, src, dst, device):
        copy = self.prepare(src, dst, device)
        copy.start()
        self.sends.append(copy)
        return copy

    def prepare(self, src, dst, device):
        i = self.n
        self.n += 1
        return pltpu.make_async_remote_copy(
            src_ref=src, dst_ref=dst, send_sem=self.send.at[i], recv_sem=self.recv.at[i],
            device_id=device, device_id_type=MESH,
        )

    def here(self, src, dst):
        i = self.m
        self.m += 1
        copy = pltpu.make_async_copy(src, dst, self.local.at[i])
        copy.start()
        return copy

    def finish(self):
        for copy in self.sends:
            copy.wait_send()


REMOTE_SEMS, LOCAL_SEMS = 128, 48


def sems(count=2):
    n = REMOTE_SEMS * max(1, count // 2)
    return [
        pltpu.SemaphoreType.DMA((n,)),
        pltpu.SemaphoreType.DMA((n,)),
        pltpu.SemaphoreType.DMA((LOCAL_SEMS,)),
    ]


class Swap:
    def __init__(self, net, src, dst):
        self.net, self.src, self.dst = net, src, dst

    def start(self):
        net, place = self.net, self.net.place
        self.copy = net.prepare(self.src, self.dst, place.swap_peer)
        self.stay = pltpu.make_async_copy(self.src, self.dst, net.local.at[net.m])
        net.m += 1

        @pl.when(place.moves)
        def _():
            self.copy.start()

        @pl.when(jnp.logical_not(place.moves))
        def _():
            self.stay.start()

    def wait(self):
        @pl.when(self.net.place.moves)
        def _():
            self.copy.wait_recv()
            self.copy.wait_send()

        @pl.when(jnp.logical_not(self.net.place.moves))
        def _():
            self.stay.wait()


class Share:
    def __init__(self, net, piece, block):
        self.net, self.piece, self.block = net, piece, block

    def start(self):
        net, place = self.net, self.net.place
        mine = self.block.at[place.x, place.zl]
        self.copies = [net.remote(self.piece.at[rank], mine, device) for device, rank in place.peers]
        self.own = net.here(self.piece.at[place.rank], mine)

    def wait(self):
        for copy in self.copies:
            copy.wait_recv()
        self.own.wait()


class Gather:
    def __init__(self, net, block, full, ranks=True, ahead=None):
        self.net, self.block, self.full, self.ranks, self.ahead = net, block, full, ranks, ahead

    def slot(self, a, core, zh):
        if self.ranks:
            return self.full.at[a, :, core, zh, :]
        return self.full.at[a, core, zh]

    def column(self, a, core):
        if self.ranks:
            return self.full.at[a, :, core, :, :]
        return self.full.at[a, core]

    def begin(self):
        net, p = self.net, self.net.place
        mine = self.slot(p.a, p.core, p.zh)
        self.own = [net.here(self.block, mine)]
        self.cores = [net.remote(self.block, mine, p.core_peer)]
        if self.ahead is None:
            self.across = net.remote(self.block, mine, p.zh_peer)
            self.near = [net.remote(self.block, mine, o[0]) for o in p.others]
            return
        got = self.slot(p.a, p.core, 1 - p.zh)
        self.far = [net.remote(self.ahead.at[0], got, o[0]) for o in p.others]
        self.cores.append(net.remote(self.ahead.at[0], got, p.core_peer))
        self.own.append(net.here(self.ahead.at[0], got))
        for k, other in enumerate(p.others):
            self.own.append(net.here(self.ahead.at[k + 1], self.slot(other[2], p.core, p.zh)))

    def middle(self):
        net, p = self.net, self.net.place
        self.across.wait_recv()
        got = self.slot(p.a, p.core, 1 - p.zh)
        self.far = [net.remote(got, got, o[0]) for o in p.others]
        self.cores.append(net.remote(got, got, p.core_peer))

    def final(self):
        net, p = self.net, self.net.place
        for copy in self.own:
            copy.wait()
        for k, other in enumerate(p.others):
            if self.ahead is None:
                self.near[k].wait_recv()
            self.far[k].wait_recv()
            got = self.column(other[2], p.core)
            self.cores.append(net.remote(got, got, p.core_peer))

    def done(self):
        for copy in self.cores:
            copy.wait_recv()


class Ahead:
    def __init__(self, net, block, got):
        self.net, self.block, self.got = net, block, got

    def begin(self):
        net, p = self.net, self.net.place
        self.copies = [net.remote(self.block, self.got.at[0], p.zh_peer)]
        self.copies += [net.remote(self.block, self.got.at[k + 1], o[0]) for k, o in enumerate(p.others)]

    def done(self):
        for copy in self.copies:
            copy.wait_recv()


class Reduce:
    def __init__(self, net, part, out, held, from_core, from_a, from_zh, from_rank, ranks=True, added=False):
        self.net, self.part, self.out = net, part, out
        self.held, self.from_core, self.from_a = held, from_core, from_a
        self.from_zh, self.from_rank = from_zh, from_rank
        self.ranks, self.added = ranks, added

    def half(self, core):
        return self.part.at[:, :, core] if self.ranks else self.part.at[:, core]

    def begin(self):
        net, p = self.net, self.net.place
        self.load = net.here(self.half(p.core), self.held)
        self.by_core = net.remote(self.half(1 - p.core), self.from_core, p.core_peer)

    def along_a(self):
        net, p = self.net, self.net.place
        self.load.wait()
        self.by_core.wait_recv()
        add_into(self.held, self.from_core)
        self.by_a = [
            net.remote(self.held.at[other[1]], self.from_a.at[k], other[0])
            for k, other in enumerate(p.others)
        ]

    def along_zh(self):
        net, p = self.net, self.net.place
        mine = self.held.at[p.a]
        for k, copy in enumerate(self.by_a):
            copy.wait_recv()
            add_into(mine, self.from_a.at[k])
        there = mine.at[:, 1 - p.zh] if self.ranks else mine.at[1 - p.zh]
        self.by_zh = net.remote(there, self.from_zh, p.zh_peer)

    def among_ranks(self):
        net, p = self.net, self.net.place
        self.by_zh.wait_recv()
        if not self.ranks:
            total = self.held[p.a, p.zh].astype(F32) + self.from_zh[...].astype(F32)
            self.out[...] = total.astype(self.out.dtype)
            return
        for x in range(2):
            for zl in range(2):
                add_into(self.held.at[p.a, x, p.zh, zl], self.from_zh.at[x, zl])
        self.by_rank = []
        for device, rank in p.peers:
            rank_x, rank_zl = lax.div(rank, 2), lax.rem(rank, 2)
            self.by_rank.append(
                net.remote(
                    self.held.at[p.a, rank_x, p.zh, rank_zl], self.from_rank.at[len(self.by_rank)], device
                )
            )

    def done(self):
        if not self.ranks:
            return
        p = self.net.place
        own = self.held[p.a, p.x, p.zh, p.zl].astype(F32)
        for copy in self.by_rank:
            copy.wait_recv()
        if self.added:
            for j in range(3):
                own = own + self.from_rank[j].astype(F32)
            self.out[...] = own
            return
        self.out[p.rank] = own.astype(self.out.dtype)
        for j, (_, rank) in enumerate(p.peers):
            self.out[rank] = self.from_rank[j].astype(self.out.dtype)

    @staticmethod
    def scratch(shape, ranks=True):
        tail = shape[-2:]
        count = shape[0]
        inner = ((2, 2, 2) if ranks else (2,)) + tail
        fewer = ((2, 2) if ranks else ()) + tail
        shapes = [(count,) + inner, (count,) + inner, (max(count - 1, 1),) + inner, fewer]
        if ranks:
            shapes.append((3,) + tail)
        return [pltpu.VMEM(s, BF16) for s in shapes]


def add_into(target, source):
    lead = target.shape[:-2]
    total = 1
    for size in lead:
        total *= size
    if total == 1 and not lead:
        target[...] = (target[...].astype(F32) + source[...].astype(F32)).astype(BF16)
        return

    @pl.loop(0, total)
    def _(j):
        index, left = [], j
        for size in reversed(lead):
            index.append(lax.rem(left, size))
            left = lax.div(left, size)
        index = tuple(reversed(index))
        target[index] = (target[index].astype(F32) + source[index].astype(F32)).astype(BF16)


class Spread:
    def __init__(self, net, land):
        self.net, self.land = net, land
        self.peers = net.place.peers
        mine = land.at[net.place.rank]
        self.along_x = net.remote(mine, mine, self.peers[0][0])
        self.along_zl = net.remote(mine, mine, self.peers[1][0])

    def arrivals(self):
        self.along_zl.wait_recv()
        got = self.land.at[self.peers[1][1]]
        relay = self.net.remote(got, got, self.peers[0][0])
        yield 1, self.peers[1][1]
        self.along_x.wait_recv()
        yield 0, self.peers[0][1]
        relay.wait_recv()
        yield 2, self.peers[2][1]

    def wait(self):
        for _ in self.arrivals():
            pass


class Sum:
    def __init__(self, net, out, land):
        self.net, self.out, self.land = net, out, land
        self.peers = net.place.peers

    def ready(self, i):
        if i == 2:
            self.diagonal = self.net.remote(self.out.at[2], self.land.at[0], self.peers[0][0])
        elif i == 0:
            self.along_x = self.net.remote(self.out.at[0], self.land.at[1], self.peers[0][0])

    def forward(self):
        self.diagonal.wait_recv()
        add_into(self.out.at[1], self.land.at[0])
        self.along_zl = self.net.remote(self.out.at[1], self.land.at[2], self.peers[1][0])

    def result(self, own):
        self.along_x.wait_recv()
        self.along_zl.wait_recv()
        return own + self.land[1].astype(F32) + self.land[2].astype(F32)


class EvenSpread:
    def __init__(self, net, land):
        self.net, self.land = net, land
        self.peers = net.place.peers
        self.half = land.shape[1] // 2
        me = net.place.rank
        self.x_high = self.go(me, 1, 0)
        self.z_low = self.go(me, 0, 1)
        self.x_low = self.go(me, 0, 0)
        self.z_high = self.go(me, 1, 1)

    def go(self, rank, part, i):
        rows = self.land.at[rank, pl.ds(part * self.half, self.half)]
        return self.net.remote(rows, rows, self.peers[i][0])

    def arrivals(self):
        self.x_high.wait_recv()
        on_z = self.go(self.peers[0][1], 1, 1)
        self.z_low.wait_recv()
        on_x = self.go(self.peers[1][1], 0, 0)
        self.x_low.wait_recv()
        yield 0, self.peers[0][1]
        self.z_high.wait_recv()
        yield 1, self.peers[1][1]
        on_z.wait_recv()
        on_x.wait_recv()
        yield 2, self.peers[2][1]

    def wait(self):
        for _ in self.arrivals():
            pass


class EvenSum:
    def __init__(self, net, out, land):
        self.net, self.out, self.land = net, out, land
        self.peers = net.place.peers
        self.half = out.shape[1] // 2

    def go(self, i, part, slot, peer):
        rows = pl.ds(part * self.half, self.half)
        return self.net.remote(self.out.at[i, rows], self.land.at[slot, rows], self.peers[peer][0])

    def ready(self, i):
        if i == 2:
            self.low, self.high = self.go(2, 0, 0, 0), self.go(2, 1, 0, 1)
        elif i == 0:
            self.x_low = self.go(0, 0, 1, 0)
        else:
            self.z_high = self.go(1, 1, 2, 1)

    def forward(self):
        low, high = pl.ds(0, self.half), pl.ds(self.half, self.half)
        self.high.wait_recv()
        add_into(self.out.at[0, high], self.land.at[0, high])
        self.x_high = self.go(0, 1, 1, 0)
        self.low.wait_recv()
        add_into(self.out.at[1, low], self.land.at[0, low])
        self.z_low = self.go(1, 0, 2, 1)

    def result(self, own):
        for copy in (self.x_low, self.x_high, self.z_low, self.z_high):
            copy.wait_recv()
        return own + self.land[1].astype(F32) + self.land[2].astype(F32)


def products(x, w_ref, count, tile, transposed, use):
    def part(cols):
        if transposed:
            w, dims = w_ref[cols, :], (((1,), (1,)), ((), ()))
        else:
            w, dims = w_ref[:, cols], (((1,), (0,)), ((), ()))
        use(cols, lax.dot_general(x(), w, dims, preferred_element_type=F32))

    for j in range(count // tile):
        part(pl.ds(j * tile, tile))


def norm_rows(h, gain):
    factor = lax.rsqrt(jnp.mean(h * h, axis=-1, keepdims=True) + NORM_EPS)
    return (h * factor * gain).astype(BF16)


def norm_rows_back(h, gain, grad):
    factor = lax.rsqrt(jnp.mean(h * h, axis=-1, keepdims=True) + NORM_EPS)
    z = grad * gain
    inner = jnp.sum(z * h, axis=-1, keepdims=True)
    back = factor * z - h * (factor * factor * factor * inner / h.shape[-1])
    return back, jnp.sum(grad * h * factor, axis=0, keepdims=True)


def rows_of(rank, rows):
    return pl.ds(pl.multiple_of(rank * rows, rows), rows)


class Refs:
    def __init__(self, refs):
        self.refs = list(refs)

    def take(self, n):
        got, self.refs = self.refs[:n], self.refs[n:]
        return got


class Ticks:
    def __init__(self, plan):
        self.plan = list(plan)

    def __call__(self):
        if self.plan:
            for step in self.plan.pop(0):
                step()

    def rest(self):
        while self.plan:
            self()


def np_tables(length):
    steps = np.arange(HEAD_DIM // 2, dtype=np.float32)
    inverse = np.exp(steps * np.float32(-2.0 * np.log(ROPE_BASE) / HEAD_DIM)).astype(np.float32)
    angles = np.arange(length, dtype=np.float32)[:, None] * inverse[None, :]
    return np.cos(angles), np.sin(angles)


def wide_tables(length):
    cosine, sine = np_tables(length)
    turned = (HEADS + KV_HEADS) // RANKS
    still = KV_HEADS // RANKS * HEAD_DIM
    cos_all = np.concatenate([cosine] * (2 * turned) + [np.ones((length, still))], axis=1)
    sin_all = np.concatenate([-sine, sine] * turned + [np.zeros((length, still))], axis=1)
    return jnp.asarray(cos_all, F32), jnp.asarray(sin_all, F32)


def turn(values, cosine, sine):
    cols = values.shape[1]
    half = HEAD_DIM // 2
    lane = lax.broadcasted_iota(jnp.int32, values.shape, 1)
    other = jnp.where(
        lax.rem(lane, HEAD_DIM) < half,
        pltpu.roll(values, cols - half, 1),
        pltpu.roll(values, half, 1),
    )
    return values * cosine + other * sine


def head_window(values, h):
    offset = HEAD_DIM * h
    start = offset // 128 * 128
    size = 128 if offset - start + HEAD_DIM <= 128 else 256
    window = values[:, start : start + size]
    if offset > start:
        window = pltpu.roll(window, size - (offset - start), 1)
    window = window[:, :128]
    lane = lax.broadcasted_iota(jnp.int32, window.shape, 1)
    return jnp.where(lane < HEAD_DIM, window, 0.0)


def heads_joined(parts):
    rows = parts[0].shape[0]
    columns = [jnp.zeros((rows, 128), F32) for _ in range(len(parts) * HEAD_DIM // 128 + 1)]
    for h, part in enumerate(parts):
        offset = HEAD_DIM * h
        first = offset // 128
        shift = offset - first * 128
        if shift == 0:
            columns[first] = columns[first] + part
            continue
        double = jnp.concatenate([part, jnp.zeros((rows, 128), F32)], axis=1)
        double = pltpu.roll(double, shift, 1)
        columns[first] = columns[first] + double[:, :128]
        columns[first + 1] = columns[first + 1] + double[:, 128:]
    return jnp.concatenate(columns[:-1], axis=1)


def project_heads(rows, n1, wq, cos_ref, sin_ref, heads):
    count = heads.shape[0]

    @pl.loop(0, RANKS)
    def _(b):
        span = rows_of(b, rows)
        y = jnp.dot(n1[b], wq[...], preferred_element_type=F32)
        y = turn(y, cos_ref[span, :], sin_ref[span, :])
        for h in range(count):
            heads[h, span, :] = head_window(y, h).astype(BF16)


def causal_scores(rows, rank, query, key):
    scores = lax.dot_general(query, key, (((1,), (1,)), ((), ())), preferred_element_type=F32)
    row = lax.broadcasted_iota(jnp.int32, scores.shape, 0) + rank * rows
    col = lax.broadcasted_iota(jnp.int32, scores.shape, 1)
    return jnp.where(col <= row, scores * HEAD_DIM ** (-0.5), MASKED)


def attend_rows(rows, rank, heads, o_ref, lse_ref):
    span = rows_of(rank, rows)
    queries = HEADS // RANKS
    pairs = KV_HEADS // RANKS
    groups = HEADS // KV_HEADS
    mixed = []
    lane = lax.broadcasted_iota(jnp.int32, (rows, 128), 1)
    lse_all = jnp.zeros((rows, 128), F32)
    for h in range(queries):
        kv = h // groups
        scores = causal_scores(rows, rank, heads[h, span, :], heads[queries + kv])
        highest = jnp.max(scores, axis=-1, keepdims=True)
        weights = jnp.exp(scores - highest)
        total = jnp.sum(weights, axis=-1, keepdims=True)
        lse = highest + jnp.log(total)
        lse_all = jnp.where(lane == h, lse, lse_all)
        weights = (weights * (1.0 / total)).astype(BF16)
        mixed.append(
            jnp.dot(weights, heads[queries + pairs + kv], preferred_element_type=F32)
        )
    lse_ref[span, :] = lse_all
    o_ref[span, :] = heads_joined(mixed).astype(BF16)


def window_tables(length):
    cosine, sine = np_tables(length)
    none = np.zeros((length, 128 - HEAD_DIM))
    cos_one = np.concatenate([cosine, cosine, none], axis=1)
    sin_one = np.concatenate([-sine, sine, none], axis=1)
    return jnp.asarray(cos_one, F32), jnp.asarray(sin_one, F32)


def turn_window(values, cosine, sine):
    half = HEAD_DIM // 2
    lane = lax.broadcasted_iota(jnp.int32, values.shape, 1)
    other = jnp.where(lane < half, pltpu.roll(values, 128 - half, 1), pltpu.roll(values, half, 1))
    return values * cosine + other * sine


def dot_tn(a, b):
    return lax.dot_general(a, b, (((0,), (0,)), ((), ())), preferred_element_type=F32)


def attend_rows_back(rows, rank, do_rows, heads, o_ref, lse_ref, cos_ref, sin_ref, dq_ref, dkv):
    span = rows_of(rank, rows)
    queries = HEADS // RANKS
    pairs = KV_HEADS // RANKS
    groups = HEADS // KV_HEADS
    o_rows = o_ref[span, :].astype(F32)
    parts = []
    for h in range(queries):
        kv = h // groups
        do_h = head_window(do_rows, h)
        delta = jnp.sum(do_h * head_window(o_rows, h), axis=-1, keepdims=True)
        do_b = do_h.astype(BF16)
        query, key, value = heads[h, span, :], heads[queries + kv], heads[queries + pairs + kv]
        weights = jnp.exp(causal_scores(rows, rank, query, key) - lse_ref[span, h : h + 1])
        grad_w = lax.dot_general(do_b, value, (((1,), (1,)), ((), ())), preferred_element_type=F32)
        ds = (weights * (grad_w - delta) * HEAD_DIM ** (-0.5)).astype(BF16)
        dq = jnp.dot(ds, key, preferred_element_type=F32)
        parts.append(turn_window(dq, cos_ref[span, :], -sin_ref[span, :]))
        dkv[kv] += dot_tn(ds, query)
        dkv[pairs + kv] += dot_tn(weights.astype(BF16), do_b)
    joined = heads_joined(parts)
    dq_ref[span, pl.ds(0, joined.shape[1])] = joined.astype(BF16)


def close_keys(rows, dkv, cos_ref, sin_ref, dqkv_ref):
    pairs = KV_HEADS // RANKS
    first = HEADS // RANKS * HEAD_DIM

    @pl.loop(0, RANKS)
    def _(b):
        span = rows_of(b, rows)
        parts = [turn_window(dkv[i, span, :], cos_ref[span, :], -sin_ref[span, :]) for i in range(pairs)]
        parts += [dkv[pairs + i, span, :] for i in range(pairs)]
        joined = heads_joined(parts)
        dqkv_ref[span, pl.ds(first, joined.shape[1])] = joined.astype(BF16)


def put_blocks(target, value):
    *lead, rows, cols = target.shape
    if rows % 16 == 0:
        target.reshape(value.shape[0], cols)[...] = value.astype(BF16)
        return
    for block in range(value.shape[0] // rows):
        index, left = [], block
        for size in reversed(lead):
            index.append(left % size)
            left //= size
        target[tuple(reversed(index))] = value[block * rows : (block + 1) * rows].astype(BF16)


def start_kernel(count, n, n_later, n_ahead, *refs):
    refs = Refs(refs)
    (tokens,) = refs.take(1)
    pieces, later = refs.take(n), refs.take(n_later)
    (all_tokens,) = refs.take(1)
    full, blocks_later, got_ahead = refs.take(n), refs.take(n_later), refs.take(n_ahead)
    (land,) = refs.take(1)
    blocks = refs.take(n)
    send, recv, local = refs.take(3)
    place = Place(count)
    net = Net(place, send, recv, local)
    shares = [Share(net, pieces[i], blocks[i]) for i in range(n)]
    shares_later = [Share(net, later[i], blocks_later[i]) for i in range(n_later)]
    gathers = [Gather(net, blocks[i], full[i]) for i in range(n)]
    aheads = [Ahead(net, blocks_later[i], got_ahead[i]) for i in range(n_ahead)]
    swap = Swap(net, tokens, land.at[place.zh * 2 + place.zl])
    place.greet(True, True)
    shares[0].start()
    swap.start()
    for share in shares[1:] + shares_later[:n_ahead]:
        share.start()
    for i in range(2):
        shares[i].wait()
        gathers[i].begin()
    swap.wait()
    spreads = Spread(net, land)
    for i in range(2, n):
        shares[i].wait()
        gathers[i].begin()
    for i in range(n_ahead):
        shares_later[i].wait()
        aheads[i].begin()
    arrivals = spreads.arrivals()
    next(arrivals)
    for share in shares_later[n_ahead:]:
        share.start()
    gathers[0].middle()
    gathers[1].middle()
    for _ in arrivals:
        pass
    keep = net.here(land, all_tokens)
    gathers[0].final()
    for i in range(2, n):
        gathers[i].middle()
        gathers[i - 1].final()
    gathers[-1].final()
    for gather in gathers + aheads:
        gather.done()
    for share in shares_later[n_ahead:]:
        share.wait()
    keep.wait()
    net.finish()


def body_kernel(count, rows, late, started, n_next, n_ahead, plan, *refs):
    refs = Refs(refs)
    n1_hbm, wq_hbm, cos_ref, sin_ref, h_ref, gain_ref, wo_hbm = refs.take(7)
    inner_hbm = refs.take(3)
    ahead_hbm = [refs.take(1)[0] if started[i] else None for i in range(3)]
    if n_next:
        (gain_next,) = refs.take(1)
        blocks = refs.take(n_next)
    else:
        (swap_src,) = refs.take(1)
    heads, o_ref, lse_ref, h1_ref, hn_ref, gate_ref, up_ref, u_ref, ng_hbm = refs.take(9)
    late_out = [refs.take(1)[0] if late[i] else None for i in range(3)]
    if n_next:
        (nn_hbm,) = refs.take(1)
        full = refs.take(n_next)
    else:
        (swap_dst,) = refs.take(1)
    n1, wq, wo = refs.take(3)
    inner = refs.take(3)
    out_a, land_a, land_n, out_b, land_b = refs.take(5)
    if n_next:
        (land_q,) = refs.take(1)
    send, recv, local = refs.take(3)

    place = Place(count)
    net = Net(place, send, recv, local)
    width = h_ref.shape[1]
    hidden = u_ref.shape[1]
    load_q = net.here(wq_hbm.at[:, pl.ds(0, wq.shape[1])], wq)
    load_n = net.here(n1_hbm, n1)
    load_out = net.here(wo_hbm, wo)
    jobs = {}
    loads, weights = [], []
    for i in range(3):
        if late[i]:
            jobs[("gate", "up", "down")[i]] = Gather(net, inner_hbm[i], inner[i], i < 2, ahead_hbm[i])
            loads.append(None)
        else:
            loads.append(net.here(inner_hbm[i], inner[i]))
        weights.append(inner[i].reshape((hidden, width) if i == 2 else (width, hidden)) if late[i] else inner[i])
    wg, wu, wd = weights
    for i in range(n_next):
        jobs[i] = (Ahead if i >= n_next - n_ahead else Gather)(net, blocks[i], full[i])
    if not n_next:
        jobs["swap"] = Swap(net, swap_src, swap_dst)
    peers = place.peers
    place.greet(True, not n_next)
    keeps = []

    def ready(i):
        if late[i]:
            jobs[("gate", "up", "down")[i]].done()
            keeps.append(net.here(inner[i], late_out[i]))
        else:
            loads[i].wait()

    tick = Ticks(plan(jobs))
    tick()

    load_q.wait()
    load_n.wait()
    project_heads(rows, n1, wq, cos_ref, sin_ref, heads)
    load_out.wait()
    sums = EvenSum(net, out_a, land_a)
    for i in (2, 0, 1):
        attend_rows(rows, peers[i][1], heads, o_ref, lse_ref)
        span = rows_of(peers[i][1], rows)

        def use(cols, y, i=i):
            out_a[i, :, cols] = y.astype(BF16)

        products(lambda: o_ref[span, :], wo, width, width, True, use)
        sums.ready(i)
    attend_rows(rows, place.rank, heads, o_ref, lse_ref)
    span = rows_of(place.rank, rows)

    def use_own(cols, y):
        h1_ref[:, cols] = h_ref[:, cols].astype(F32) + y

    products(lambda: o_ref[span, :], wo, width, width, True, use_own)
    sums.forward()
    tick()
    h1 = sums.result(h1_ref[...])
    h1_ref[...] = h1
    land_n[place.rank] = norm_rows(h1, gain_ref[...])
    gather = EvenSpread(net, land_n)
    tick()
    ready(0)
    ready(1)

    def inner_block(rank):
        span = rows_of(rank, rows)

        gate = jnp.dot(land_n[rank], wg[...], preferred_element_type=F32)
        up = jnp.dot(land_n[rank], wu[...], preferred_element_type=F32)
        gate_ref[span, :] = gate.astype(BF16)
        up_ref[span, :] = up.astype(BF16)
        u_ref[span, :] = (gate / (1.0 + jnp.exp(-gate)) * up).astype(BF16)

        return span

    inner_block(place.rank)
    tick()
    second = EvenSum(net, out_b, land_b)
    got_down = False
    for i, rank in gather.arrivals():
        span = inner_block(rank)
        if not got_down:
            tick()
            ready(2)
            got_down = True

        def use(cols, y, i=i):
            out_b[i, :, cols] = y.astype(BF16)

        products(lambda: u_ref[span, :], wd, width, width, False, use)
        second.ready(i)
        tick()
    keep = net.here(land_n, ng_hbm)
    span = rows_of(place.rank, rows)

    def use_down(cols, y):
        hn_ref[:, cols] = h1_ref[:, cols] + y

    products(lambda: u_ref[span, :], wd, width, width, False, use_down)
    second.forward()
    tick()
    hn = second.result(hn_ref[...])
    hn_ref[...] = hn
    if n_next:
        land_q[place.rank] = norm_rows(hn, gain_next[...])
        third = EvenSpread(net, land_q)
        tick()
        for _ in third.arrivals():
            tick()
        keep_next = net.here(land_q, nn_hbm)
        keep_next.wait()
    tick.rest()
    for i in range(n_next):
        jobs[i].done()
    if not n_next:
        jobs["swap"].wait()
    keep.wait()
    for copy in keeps:
        copy.wait()
    net.finish()


def plan_late(j):
    gate, up, down = j["gate"], j["up"], j["down"]
    return [
        [gate.begin, up.begin],
        [gate.middle, down.begin],
        [up.final, gate.final],
        [down.middle, j[0].begin, j[1].begin],
        [down.final],
        [],
        [],
        [j[0].middle],
        [j[0].final, j[1].middle],
        [j[2].begin, j[1].final],
    ]


def plan_late_end(j):
    gate, up, down = j["gate"], j["up"], j["down"]
    return [
        [up.begin, gate.begin],
        [up.middle, down.begin],
        [gate.final, up.final],
        [down.middle],
        [down.final],
        [],
        [],
        [j["swap"].start],
    ]


def plan_early(j):
    down = j["down"]
    return [
        [down.begin],
        [down.middle, j[0].begin],
        [],
        [down.final, j[1].begin, j[2].begin],
        [j[0].middle],
        [],
        [],
        [j[0].final],
        [j[1].middle, j[2].middle],
        [j[3].begin, j[1].final, j[2].final],
        [],
        [],
        [j[3].middle],
        [j[3].final],
    ]


def plan_end(j):
    down = j["down"]
    return [
        [down.begin],
        [],
        [down.middle],
        [],
        [down.final],
        [],
        [],
        [j["swap"].start],
    ]


class Back:
    def __init__(self, net, rows):
        self.net, self.place, self.rows = net, net.place, rows
        self.peers = net.place.peers

    def enter(self, r, tick):
        rows, place = self.rows, self.place
        width = r["gnew"].shape[1]
        total = EvenSum(self.net, r["out_a"], r["land_a"])
        for i in (2, 0, 1):
            span = rows_of(self.peers[i][1], rows)

            def use(cols, y, i=i):
                r["out_a"][i, :, cols] = y.astype(BF16)

            products(lambda: r["dqkv"][span, :], r["wq"], width, width, True, use)
            total.ready(i)
        tick()
        own = rows_of(place.rank, rows)

        def use_own(cols, y):
            r["gnew"][:, cols] = y

        products(lambda: r["dqkv"][own, :], r["wq"], width, width, True, use_own)
        total.forward()
        tick()
        dn = total.result(r["gnew"][...])
        back, ggain = norm_rows_back(r["hin"][...].astype(F32), r["gain_in"][...], dn)
        r["gnew"][...] = r["ghin"][...] + back
        return ggain

    def feed_forward(self, r, tick, ready, between):
        net, rows, place = self.net, self.rows, self.place
        land_g, dgu, out_b = r["land_g"], r["dgu"], r["out_b"]
        width = land_g.shape[2]
        hidden = r["gate"].shape[1]
        land_g[place.rank] = r["g"][...].astype(BF16)
        gather = EvenSpread(net, land_g)
        tick()
        ready()

        def inner_block(rank):
            span = rows_of(rank, rows)
            du = lax.dot_general(
                land_g[rank], r["wd"][...], (((1,), (1,)), ((), ())), preferred_element_type=F32
            )
            gate, up = r["gate"][span, :].astype(F32), r["up"][span, :].astype(F32)
            sg = 1.0 / (1.0 + jnp.exp(-gate))
            dgu[span, pl.ds(0, hidden)] = (du * up * sg * (1.0 + gate * (1.0 - sg))).astype(BF16)
            dgu[span, pl.ds(hidden, hidden)] = (du * gate * sg).astype(BF16)
            return span

        span = inner_block(place.rank)

        def use_mid(cols, y):
            r["gh"][:, cols] = y

        products(lambda: dgu[span, :], r["wgu"], width, width, True, use_mid)
        tick()
        second = EvenSum(net, out_b, r["land_b"])
        for i, rank in gather.arrivals():
            span = inner_block(rank)

            def use(cols, y, i=i):
                out_b[i, :, cols] = y.astype(BF16)

            products(lambda: dgu[span, :], r["wgu"], width, width, True, use)
            second.ready(i)
            tick()
        second.forward()
        tick()
        between()
        tick()
        dn = second.result(r["gh"][...])
        back, ggain = norm_rows_back(r["h1"][...], r["gain"][...], dn)
        r["gh"][...] = r["g"][...].astype(F32) + back
        r["gg"][...] = ggain

    def weight_grads(self, r, down_made):
        net = self.net
        buffers, copies = r["buffers"], []
        tile = buffers.shape[1]
        tall, hidden = r["u"].shape
        width = r["land_g"].shape[2]
        g_all = r["land_g"][...].reshape(tall, width)

        def emit(lhs, rhs, outs, m):
            slot = len(copies) % 2
            if len(copies) >= 2:
                for copy in copies[-2]:
                    copy.wait()
            buffers[slot, :, pl.ds(0, rhs.shape[1])] = dot_tn(lhs, rhs).astype(BF16)
            cols = rhs.shape[1] // len(outs)
            copies.append([
                net.here(buffers.at[slot, :, pl.ds(k * cols, cols)], out.at[pl.ds(m * tile, tile)])
                for k, out in enumerate(outs)
            ])

        for k, part in enumerate((r["part_da"], r["part_db"])):
            cols = part.shape[-1]
            made = dot_tn(r["u"][...], g_all[:, k * cols : (k + 1) * cols])
            part.reshape(hidden, cols)[...] = made.astype(BF16)
        down_made()
        for m in range(width // tile):
            emit(r["n2"][:, m * tile : (m + 1) * tile], r["dgu"][...], [r["g_gate"], r["g_up"]], m)
        return copies[-2] + copies[-1]

    def attention(self, r, tick, ready):
        net, rows, place = self.net, self.rows, self.place
        land_h = r["land_h"]
        land_h[place.rank] = r["gh"][...].astype(BF16)
        gather = EvenSpread(net, land_h)
        tick()
        ready()
        r["dkv"][...] = jnp.zeros(r["dkv"].shape, F32)

        def block(rank):
            do_rows = jnp.dot(land_h[rank], r["wo"][...], preferred_element_type=F32)
            do_rows = do_rows.astype(BF16).astype(F32)
            attend_rows_back(
                rows, rank, do_rows, r["heads"], r["o"], r["lse"], r["cos"], r["sin"], r["dqkv"], r["dkv"]
            )

        block(place.rank)
        tick()
        for _, rank in gather.arrivals():
            block(rank)
            tick()
        close_keys(rows, r["dkv"], r["cos"], r["sin"], r["dqkv"])


ATTEND = ("wo", "heads", "o", "lse", "cos", "sin")


def back_kernel(count, rows, names, out_names, scratch_names, n_parts, kinds, plan, *refs):
    refs = Refs(refs)
    r = dict(zip(names, refs.take(len(names))))
    parts = refs.take(n_parts)
    r.update(zip(out_names, refs.take(len(out_names))))
    red_out = refs.take(len(kinds))
    r.update(zip(scratch_names, refs.take(len(scratch_names))))
    red_scratch = [refs.take(5 if ranks else 4) for ranks in kinds]
    gains_scratch = refs.take(5) if "gains_out" in r else None
    send, recv, local = refs.take(3)

    place = Place(count)
    net = Net(place, send, recv, local)
    back = Back(net, rows)
    entering, inner, attention = "hin" in r, "h1" in r, "heads_hbm" in r
    last = "gains_out" in r
    waits = {}

    def load(name, source, target):
        waits[name] = net.here(source, target)

    parts = parts + ([r["part_o"], r["part_q"]] if last else [r["part_da"], r["part_db"]])
    jobs = []
    for part, out, scratch, ranks in zip(parts, red_out, red_scratch, kinds):
        jobs.append(Reduce(net, part, out, *scratch, *([] if ranks else [None]), ranks=ranks))
    if entering:
        load("wq", r["wq_hbm"].at[:, pl.ds(0, r["wq"].shape[1])], r["wq"])
    if inner:
        hidden = r["wd"].shape[0]
        load("wd", r["wd_hbm"], r["wd"])
        load("wg", r["wgate_hbm"], r["wgu"].at[:, pl.ds(0, hidden)])
        load("wu", r["wup_hbm"], r["wgu"].at[:, pl.ds(hidden, hidden)])
        load("u", r["u_hbm"], r["u"])
        load("n2", r["n2_hbm"], r["n2"])
    if attention:
        for name in ("wo", "heads", "o", "lse", "n1"):
            load(name, r[name + "_hbm"], r[name])
    place.greet(len(jobs) > 0, "swap_src" in r or last)
    if "swap_src" in r:
        jobs.append(Swap(net, r["swap_src"], r["swap_dst"]))
    tick = Ticks(plan(jobs))
    tick()
    ends = []

    def ready_inner():
        for name in ("wd", "wg", "wu"):
            waits[name].wait()

    def between():
        waits["u"].wait()
        waits["n2"].wait()
        ends.extend(back.weight_grads(r, tick))

    def ready_attention():
        for name in ("wo", "heads", "o", "lse"):
            waits[name].wait()

    if entering and inner:
        waits["wq"].wait()
        r["ggin"][...] = back.enter(r, tick)
        r["g"] = r["gnew"]
    if inner:
        back.feed_forward(r, tick, ready_inner, between)
    if attention:
        back.attention(r, tick, ready_attention)
        waits["n1"].wait()
        width = r["land_h"].shape[2]
        tall = r["o"].shape[0]

        def grad_out():
            return dot_tn(r["land_h"][...].reshape(tall, width), r["o"][...])

        def grad_qkv():
            return dot_tn(r["n1"][...].reshape(tall, width), r["dqkv"][...])

        if not last:
            r["g_out"][...] = grad_out().astype(BF16)
            r["g_qkv"][...] = grad_qkv().astype(BF16)
        else:
            waits["wq"].wait()
            made = Ticks([
                [],
                [lambda: put_blocks(r["part_q"], grad_qkv()), lambda: put_blocks(r["part_o"], grad_out())],
            ])

            def both():
                made()
                tick()

            ggain = back.enter(r, both)
            finish_last(net, r, jobs, ggain, gains_scratch)
            for copy in ends:
                copy.wait()
            net.finish()
            return
    tick.rest()
    if "swap_src" in r:
        jobs[-1].wait()
    for copy in ends:
        copy.wait()
    net.finish()


def finish_last(net, r, jobs, ggain, scratch):
    r["gsend"][...] = r["gnew"][...].astype(BF16)
    swap = Swap(net, r["gsend"], r["swap_dst"])
    gains_all, gains_part = r["gains_all"], r["gains_part"]
    gains_all[...] = r["other_gains"][...]
    gains_all[0:1, :] = ggain
    gains_part[...] = jnp.zeros(gains_part.shape, BF16)
    count = gains_part.shape[0]
    piece = gains_all.shape[1] // (16 * count)
    for block in range(16 * count):
        index = (block // 16, block // 8 % 2, block // 4 % 2, block // 2 % 2, block % 2)
        gains_part[index + (slice(None), slice(0, piece))] = gains_all[
            :, block * piece : (block + 1) * piece
        ].astype(BF16)
    small = Reduce(net, gains_part, r["gains_out"], *scratch, added=True)
    small.begin()
    for step in plan_finish(jobs, small, swap):
        step()
    swap.wait()


def plan_finish(j, s, swap):
    return [
        s.along_a, j[2].along_a, j[3].along_a, j[1].along_zh, j[0].among_ranks, s.along_zh, j[2].along_zh,
        s.among_ranks, j[3].along_zh, swap.start, j[1].among_ranks, j[0].done, j[2].among_ranks, s.done, j[1].done,
        j[3].among_ranks, j[2].done, j[3].done,
    ]


def plan_first(j):
    da, db, swap = j
    return [
        [],
        [],
        [],
        [],
        [],
        [],
        [swap.start],
        [da.begin, db.begin],
        [da.along_a],
        [db.along_a],
        [],
        [da.along_zh],
        [db.along_zh],
        [],
        [da.among_ranks, db.among_ranks],
    ]


def plan_middle(j):
    gate, up, out, qkv, da, db = j
    return [
        [gate.begin, up.begin, out.begin, qkv.begin],
        [gate.along_a],
        [up.along_a],
        [],
        [out.along_a],
        [gate.along_zh],
        [qkv.along_a],
        [],
        [up.along_zh],
        [da.begin, db.begin],
        [gate.among_ranks, da.along_a],
        [out.along_zh, db.along_a, qkv.along_zh, up.among_ranks, out.among_ranks, gate.done, da.along_zh, up.done],
        [qkv.among_ranks, db.along_zh, out.done, qkv.done, da.among_ranks, db.among_ranks],
    ]


def plan_last(j):
    gate, up, out, qkv = j
    return [
        [gate.begin, up.begin],
        [gate.along_a],
        [],
        [up.along_a],
        [],
        [gate.along_zh],
        [],
        [out.begin, qkv.begin],
    ]


def pack_weights(w_qkv, w_out, w_gate_up, gains, count, layer):
    rows = w_qkv.shape[1]
    attn_cols = HEADS * HEAD_DIM
    kv_cols = KV_HEADS * HEAD_DIM
    qkv = w_qkv[layer]
    q = qkv[:, :attn_cols].reshape(rows, RANKS, -1)
    k = qkv[:, attn_cols : attn_cols + kv_cols].reshape(rows, RANKS, -1)
    v = qkv[:, attn_cols + kv_cols :].reshape(rows, RANKS, -1)
    columns = [q, k, v]
    if layer == 0:
        scales = jnp.pad(gains.reshape(2 * LAYERS, rows).T, ((0, 0), (0, GAIN_COLS - 2 * LAYERS)))
        columns.append(jnp.broadcast_to(scales[:, None], (rows, RANKS, GAIN_COLS)))
    head = jnp.concatenate(columns, axis=2).transpose(1, 0, 2)
    out = w_out[layer].T.reshape(rows, RANKS, -1).transpose(1, 0, 2)
    gu = w_gate_up[layer].reshape(rows, 2, count, 2, 2, 2, 2, -1)
    gu = gu.transpose(1, 3, 6, 0, 2, 4, 5, 7).reshape(2, RANKS, rows, -1)
    return head, out, gu[0], gu[1]


def unpack_grads(head, out, gate, up, count):
    rows = head.shape[1]
    q_cols = HEADS * HEAD_DIM // RANKS
    kv_cols = KV_HEADS * HEAD_DIM // RANKS
    wide = lambda part: part.transpose(1, 0, 2).reshape(rows, -1)
    qkv = jnp.concatenate(
        [
            wide(head[:, :, :q_cols]),
            wide(head[:, :, q_cols : q_cols + kv_cols]),
            wide(head[:, :, q_cols + kv_cols : q_cols + 2 * kv_cols]),
        ],
        axis=1,
    )
    order = lambda part: (
        part.reshape(2, 2, rows, count, 2, 2, -1).transpose(2, 3, 0, 4, 5, 1, 6).reshape(rows, -1)
    )
    return qkv, wide(out).T, jnp.stack([order(gate), order(up)], axis=1)


VM = pl.BlockSpec(memory_space=pltpu.VMEM)
AN = pl.BlockSpec(memory_space=pl.ANY)


def params(collective_id):
    return pltpu.CompilerParams(
        collective_id=collective_id, has_side_effects=True, vmem_limit_bytes=VMEM_BYTES
    )


def like(shape, dtype=BF16):
    return jax.ShapeDtypeStruct(tuple(shape), dtype)


def full_shape(count, tail):
    return (count, 2, 2, 2, 2) + tuple(tail)


def call_start(count, tokens, pieces, later, n_ahead):
    rows, width = tokens.shape
    n, n_later = len(pieces), len(later)
    outs = [like((RANKS, rows, width))]
    outs += [like(full_shape(count, p.shape[1:])) for p in pieces]
    outs += [like((2, 2) + p.shape[1:]) for p in later]
    outs += [like((count, 2, 2) + p.shape[1:]) for p in later[:n_ahead]]
    got = pl.pallas_call(
        functools.partial(start_kernel, count, n, n_later, n_ahead),
        out_shape=outs,
        in_specs=[AN] * (1 + n + n_later),
        out_specs=[AN] * len(outs),
        scratch_shapes=[pltpu.VMEM((RANKS, rows, width), BF16)]
        + [pltpu.VMEM((2, 2) + p.shape[1:], BF16) for p in pieces]
        + sems(count),
        compiler_params=params(1),
        name="start",
    )(tokens, *pieces, *later)
    cut = n + 1 + n_later
    return got[0], [flat(f) for f in got[1 : n + 1]], got[n + 1 : cut], got[cut:]


def flat(value):
    return value.reshape(-1, value.shape[-1])


def call_body(
    count, n1, wq, tables, h, gain, wo, inner, late, ahead, plan, gain_next=None, blocks=(), n_ahead=0, swap=None
):
    started = tuple(value is not None for value in ahead)
    rows, width = h.shape
    tall = RANKS * rows
    hidden = inner[0].shape[-1]
    n_next = len(blocks)
    heads = (HEADS + 2 * KV_HEADS) // RANKS
    cols = heads * HEAD_DIM
    o_cols = HEADS // RANKS * HEAD_DIM
    three = pltpu.VMEM((3, rows, width), BF16)
    four = pltpu.VMEM((RANKS, rows, width), BF16)
    shapes = []
    for i in range(3):
        shape = inner[i].shape
        if late[i]:
            shape = full_shape(count, shape[2:]) if i < 2 else (count, 2, 2) + shape
        shapes.append(shape)
    outs = [
        like((heads, tall, 128)),
        like((tall, o_cols)),
        like((tall, 128), F32),
        like((rows, width), F32),
        like((rows, width), F32),
        like((tall, hidden)),
        like((tall, hidden)),
        like((tall, hidden)),
        like((RANKS, rows, width)),
    ]
    n_state = len(outs)
    outs += [like(shapes[i]) for i in range(3) if late[i]]
    if n_next:
        outs += [like((RANKS, rows, width))]
        outs += [like(full_shape(count, b.shape[2:])) for b in blocks[: n_next - n_ahead]]
        outs += [like((count,) + b.shape) for b in blocks[n_next - n_ahead :]]
        extra = (gain_next, *blocks)
    else:
        outs += [like(swap.shape)]
        extra = (swap,)
    got = pl.pallas_call(
        functools.partial(body_kernel, count, rows, late, started, n_next, n_ahead, plan),
        out_shape=outs,
        in_specs=[AN, AN, VM, VM, VM, VM, AN, AN, AN, AN]
        + [AN] * sum(started)
        + ([VM] + [AN] * n_next if n_next else [AN]),
        out_specs=[VM] * (n_state - 1) + [AN] * (len(outs) - n_state + 1),
        scratch_shapes=[
            four,
            pltpu.VMEM((width, cols), BF16),
            pltpu.VMEM(wo.shape, BF16),
        ]
        + [pltpu.VMEM(shape, BF16) for shape in shapes]
        + [three, three, four, three, three]
        + ([four] if n_next else [])
        + sems(count),
        compiler_params=params(2 if n_next else 3),
        name="body_more" if n_next else "body",
    )(n1, wq, *tables, h, gain, wo, *inner, *[value for value in ahead if value is not None], *extra)
    got = list(got)
    state, rest = got[:n_state], got[n_state:]
    inner = [flat(rest.pop(0)) if late[i] else inner[i] for i in range(3)]
    rest, last = rest[: len(rest) - n_ahead], rest[len(rest) - n_ahead :]
    return state, inner, rest[0], [flat(f) for f in rest[1:]], last


def call_back(name, count, rows, inputs, outputs, scratch, parts, made, kinds, plan, collective_id):
    shapes = [p.shape for p in parts] + list(made)
    red_out = [like(((RANKS,) if ranks else ()) + shape[-2:]) for shape, ranks in zip(shapes, kinds)]
    scratch_shapes = [pltpu.VMEM(shape, dtype) for shape, dtype in scratch.values()]
    for shape, ranks in zip(shapes, kinds):
        scratch_shapes += Reduce.scratch(shape, ranks=ranks)
    if "gains_out" in outputs:
        scratch_shapes += Reduce.scratch(scratch["gains_part"][0])
    got = pl.pallas_call(
        functools.partial(
            back_kernel, count, rows, tuple(inputs), tuple(outputs), tuple(scratch), len(parts), kinds, plan
        ),
        out_shape=[shape for shape, _ in outputs.values()] + red_out,
        in_specs=[spec for _, spec in inputs.values()] + [AN] * len(parts),
        out_specs=[spec for _, spec in outputs.values()] + [VM] * len(red_out),
        scratch_shapes=scratch_shapes + sems(count),
        compiler_params=params(collective_id),
        name=name,
    )(*[value for value, _ in inputs.values()], *parts)
    return dict(zip(outputs, got)), got[len(outputs) :]


def shards(dp_size, ctx_size, tokens, cotangent, w_qkv, w_out, w_gate_up, w_down, gains):
    count = dp_size // 4
    rows, width = tokens.shape
    length = RANKS * rows
    hidden = w_gate_up.shape[-1] // RANKS
    tall = lambda value: value.reshape(length, width)
    rank = lax.rem(lax.div(lax.axis_index("dp"), 2), 2) * 2 + lax.rem(lax.axis_index("ctx"), 2)

    swap = lambda value: lax.ppermute(value, ("dp", "ctx"), swap_pairs(dp_size, ctx_size))
    tie = lax.optimization_barrier

    tables = wide_tables(length)
    windows = window_tables(length)

    packed = [pack_weights(w_qkv, w_out, w_gate_up, gains, count, layer) for layer in range(LAYERS)]
    whole_rows = w_qkv.shape[1] % 16 == 0
    none = (None, None, None)
    if whole_rows:
        head, out, gate, up = packed[0]
        now, later, n_ahead = (head, out), (up, gate, *packed[1]), 1
    else:
        now, later, n_ahead = packed[0], packed[1], 0
    all_tokens, full, blocks, ahead = call_start(count, tokens, now, later, n_ahead)
    gain_rows = full[0][:, -GAIN_COLS:][:, : 2 * LAYERS].astype(F32).T
    gain = lambda layer, which: gain_rows[2 * layer + which][None]
    h = lax.dynamic_index_in_dim(all_tokens, rank, 0, keepdims=False)
    n1 = norm_rows(all_tokens.astype(F32), gain(0, 0))
    if whole_rows:
        up, gate, *blocks, last_up = blocks
        inner, late, ahead, plan = (gate, up, w_down[0]), (True, True, True), (None, ahead[0], None), plan_late
    else:
        inner, late, ahead, plan = (*full[2:], w_down[0]), (False, False, True), none, plan_early

    records = []
    for layer in range(LAYERS):
        wq, wo = full[:2]
        if layer + 1 < LAYERS:
            state, inner, n1_next, full, last_got = call_body(
                count, n1, wq, tables, h, gain(layer, 1), wo, inner, late, ahead, plan,
                gain(layer + 1, 0), blocks, n_ahead,
            )
            if whole_rows:
                late, ahead, plan = (True, True, True), (last_got[0], None, None), plan_late_end
                next_inner = (blocks[-1], last_up, w_down[layer + 1])
            else:
                late, plan = (False, False, True), plan_end
                next_inner = (*full[2:], w_down[layer + 1])
        else:
            state, inner, g, _, _ = call_body(
                count, n1, wq, tables, h, gain(layer, 1), wo, inner, late, ahead, plan,
                swap=cotangent.astype(BF16),
            )
            n1_next = None
        heads, mixed, lse, h1, h_next, gate, up, u, n2 = state
        records.append(dict(
            hin=h, n1=n1, heads=heads, o=mixed, lse=lse, h1=h1, n2=tall(n2), gate=gate, up=up, u=u,
            wq=wq, wo=wo, wgate=inner[0], wup=inner[1], wd=inner[2],
        ))
        h, n1, inner = h_next, n1_next, next_inner

    hidden = records[0]["u"].shape[1]
    heads = (HEADS + 2 * KV_HEADS) // RANKS
    cols = heads * HEAD_DIM
    o_cols = HEADS // RANKS * HEAD_DIM
    shape7 = lambda value: value.reshape(count, 2, 2, 2, 2, -1, value.shape[-1])
    three, four = ((3, rows, width), BF16), ((RANKS, rows, width), BF16)
    row_f32 = ((rows, width), F32)

    def inner_in(layer):
        rec = records[layer]
        names = dict(wd="wd", wgate="wgate", wup="wup", u="u", n2="n2")
        values = {key + "_hbm": (rec[name], AN) for key, name in names.items()}
        return dict(
            values, gate=(rec["gate"], VM), up=(rec["up"], VM), h1=(rec["h1"], VM), gain=(gain(layer, 1), VM)
        )

    inner_out = dict(
        gh=(like((rows, width), F32), VM),
        gg=(like((1, width), F32), VM),
        g_gate=(like((width, hidden)), AN),
        g_up=(like((width, hidden)), AN),
    )
    shape_d = (count, 2, 2, w_down.shape[1], width // 2)
    inner_scratch = dict(
        part_da=(shape_d, BF16),
        part_db=(shape_d, BF16),
        wd=((hidden, width), BF16),
        wgu=((width, 2 * hidden), BF16),
        u=((length, hidden), BF16),
        n2=((length, width), BF16),
        dgu=((length, 2 * hidden), BF16),
        buffers=((2, 256, 2 * hidden), BF16),
        land_g=four,
        out_b=three,
        land_b=three,
    )

    def attention_in(layer):
        rec = records[layer]
        values = {name + "_hbm": (rec[name], AN) for name in ("wo", "heads", "o", "lse", "n1")}
        return dict(values, cos=(windows[0], VM), sin=(windows[1], VM))

    attention_scratch = dict(
        wo=((width, o_cols), BF16),
        heads=((heads, length, 128), BF16),
        o=((length, o_cols), BF16),
        lse=((length, 128), F32),
        n1=four,
        dkv=((2 * KV_HEADS // RANKS, length, 128), F32),
        land_h=four,
    )

    def enter_in(layer):
        rec = records[layer]
        return dict(wq_hbm=(rec["wq"], AN), hin=(rec["hin"], VM), gain_in=(gain(layer, 0), VM))

    enter_scratch = dict(wq=((width, cols), BF16), out_a=three, land_a=three)

    first, down_1 = call_back(
        "back_first", count, rows,
        dict(g=(g, VM), swap_src=(h.astype(BF16), AN), **inner_in(1), **attention_in(1)),
        dict(
            inner_out,
            dqkv=(like((length, cols)), VM),
            g_out=(like((width, o_cols)), VM),
            g_qkv=(like((width, cols)), VM),
            swap_dst=(like((rows, width)), AN),
        ),
        dict(**inner_scratch, **attention_scratch), [], [shape_d] * 2, (False,) * 2, plan_first, 4,
    )
    parts_of = lambda got: [shape7(got["g_gate"]), shape7(got["g_up"])]
    middle, grads_1 = call_back(
        "back_mid", count, rows,
        dict(dqkv=(first["dqkv"], VM), ghin=(first["gh"], VM), **enter_in(1), **inner_in(0)),
        dict(ggin=(like((1, width), F32), VM), **inner_out),
        dict(gnew=row_f32, **enter_scratch, **inner_scratch),
        parts_of(first) + [shape7(first["g_out"]), shape7(first["g_qkv"])],
        [shape_d] * 2, (True,) * 4 + (False,) * 2, plan_middle, 5,
    )
    others = jnp.concatenate([jnp.zeros((1, width), F32), middle["gg"], middle["ggin"], first["gg"]], axis=0)
    others = jnp.pad(others, ((0, 16 - 2 * LAYERS), (0, 0)))
    shard_rows = w_qkv.shape[1]
    shape_o, shape_q = (full_shape(count, (shard_rows, c)) for c in (o_cols, cols))
    final, grads_0 = call_back(
        "back_last", count, rows,
        dict(gh=(middle["gh"], VM), ghin=(middle["gh"], VM), other_gains=(others, VM), **enter_in(0), **attention_in(0)),
        dict(swap_dst=(like((rows, width)), AN), gains_out=(like((16, GAIN_COLS), F32), VM)),
        dict(
            gnew=row_f32,
            gsend=((rows, width), BF16),
            gains_all=((16, width), F32),
            gains_part=(full_shape(count, (16, GAIN_COLS)), BF16),
            part_o=(shape_o, BF16),
            part_q=(shape_q, BF16),
            dqkv=((length, cols), BF16),
            **enter_scratch,
            **attention_scratch,
        ),
        parts_of(middle), [shape_o, shape_q], (True,) * 4, plan_last, 6,
    )
    out_act, grad_tokens, gains_sum = first["swap_dst"], final["swap_dst"], final["gains_out"]
    grads = (grads_0, grads_1[:4])
    downs = (grads_1[4:], down_1)
    piece = gains.shape[-1]
    grad_gains = gains_sum[: 2 * LAYERS, :piece].reshape(LAYERS, 2, piece)
    stacked = [unpack_grads(q, o, gate, up, count) for gate, up, o, q in grads]
    s_qkv, s_out, s_gu = (jnp.stack([s[i] for s in stacked]) for i in range(3))
    s_down = jnp.stack([jnp.concatenate(d, axis=1) for d in downs])
    wide = lambda value: value.astype(F32)
    return (wide(out_act), wide(grad_tokens), wide(s_qkv), wide(s_out), wide(s_gu), wide(s_down), grad_gains)


def solution(mesh):
    both = ("dp", "ctx")
    return jax.shard_map(
        functools.partial(shards, mesh.shape["dp"], mesh.shape["ctx"]),
        mesh=mesh,
        in_specs=(
            P(both, None),
            P(both, None),
            P(None, both, None),
            P(None, None, both),
            P(None, both, None, None),
            P(None, both, None),
            P(None, None, both),
        ),
        out_specs=(
            P(both, None),
            P(both, None),
            P(None, both, None),
            P(None, None, both),
            P(None, both, None, None),
            P(None, both, None),
            P(None, None, both),
        ),
        check_vma=False,
    )
```

```python
import functools

import jax
import jax.numpy as jnp
import numpy as np
from jax import lax
from jax.experimental import pallas as pl
from jax.experimental.pallas import tpu as pltpu
from jax.sharding import PartitionSpec as P

HEADS = 16
KV_HEADS = 8
HEAD_DIM = 96
LAYERS = 2
RANKS = 4
GAIN_COLS = 128

NORM_EPS = 1e-05
ROPE_BASE = 100000.0
MASKED = -1e30
MESH = pl.DeviceIdType.MESH
BF16 = jnp.bfloat16
F32 = jnp.float32
VMEM_BYTES = 62 * 1024 * 1024


class Place:
    def __init__(self, count):
        self.count = count
        self.dp = lax.axis_index("dp")
        self.ctx = lax.axis_index("ctx")
        self.core = lax.rem(self.dp, 2)
        self.x = lax.rem(lax.div(self.dp, 2), 2)
        self.a = lax.div(self.dp, 4)
        self.zh = lax.div(self.ctx, 2)
        self.zl = lax.rem(self.ctx, 2)
        self.rank = self.x * 2 + self.zl
        dpx = self.dp + 2 - 4 * self.x
        ctz = self.ctx + 1 - 2 * self.zl
        x2, z2 = 1 - self.x, 1 - self.zl
        self.peers = (
            ((dpx, self.ctx), x2 * 2 + self.zl),
            ((self.dp, ctz), self.x * 2 + z2),
            ((dpx, ctz), x2 * 2 + z2),
        )
        self.core_peer = (self.dp + 1 - 2 * self.core, self.ctx)
        self.zh_peer = (self.dp, self.ctx + 2 - 4 * self.zh)
        self.others = []
        for k in range(1, count):
            ahead = lax.rem(self.a + k, count)
            behind = lax.rem(self.a + count - k, count)
            self.others.append(((self.dp + (ahead - self.a) * 4, self.ctx), ahead, behind))
        self.moves = self.x != self.zh
        self.swap_peer = (self.dp + (self.zh - self.x) * 2, self.ctx + (self.x - self.zh) * 2)

    def greet(self, weights, swap):
        devices = [d for d, _ in self.peers]
        if weights:
            devices += [self.core_peer, self.zh_peer] + [o[0] for o in self.others]
        barrier = pltpu.get_barrier_semaphore()
        for device in devices:
            pl.semaphore_signal(barrier, inc=1, device_id=device, device_id_type=MESH)
        if swap:

            @pl.when(self.moves)
            def _():
                pl.semaphore_signal(barrier, inc=1, device_id=self.swap_peer, device_id_type=MESH)

        expected = len(devices)
        if swap:
            expected = expected + self.x + self.zh - 2 * self.x * self.zh
        pl.semaphore_wait(barrier, expected)


class Net:
    def __init__(self, place, send, recv, local):
        self.place, self.send, self.recv, self.local = place, send, recv, local
        self.n, self.m = 0, 0
        self.sends = []

    def remote(self, src, dst, device):
        copy = self.prepare(src, dst, device)
        copy.start()
        self.sends.append(copy)
        return copy

    def prepare(self, src, dst, device):
        i = self.n
        self.n += 1
        return pltpu.make_async_remote_copy(
            src_ref=src, dst_ref=dst, send_sem=self.send.at[i], recv_sem=self.recv.at[i],
            device_id=device, device_id_type=MESH,
        )

    def here(self, src, dst):
        i = self.m
        self.m += 1
        copy = pltpu.make_async_copy(src, dst, self.local.at[i])
        copy.start()
        return copy

    def finish(self):
        for copy in self.sends:
            copy.wait_send()


REMOTE_SEMS, LOCAL_SEMS = 128, 64


def sems(count=2):
    n = REMOTE_SEMS * max(1, count // 2)
    return [
        pltpu.SemaphoreType.DMA((n,)),
        pltpu.SemaphoreType.DMA((n,)),
        pltpu.SemaphoreType.DMA((LOCAL_SEMS,)),
    ]


class Swap:
    def __init__(self, net, src, dst):
        self.net, self.src, self.dst = net, src, dst

    def start(self):
        net, place = self.net, self.net.place
        self.copy = net.prepare(self.src, self.dst, place.swap_peer)
        self.stay = pltpu.make_async_copy(self.src, self.dst, net.local.at[net.m])
        net.m += 1

        @pl.when(place.moves)
        def _():
            self.copy.start()

        @pl.when(jnp.logical_not(place.moves))
        def _():
            self.stay.start()

    def wait(self):
        @pl.when(self.net.place.moves)
        def _():
            self.copy.wait_recv()
            self.copy.wait_send()

        @pl.when(jnp.logical_not(self.net.place.moves))
        def _():
            self.stay.wait()


class Share:
    def __init__(self, net, piece, block):
        self.net, self.piece, self.block = net, piece, block

    def start(self):
        net, place = self.net, self.net.place
        mine = self.block.at[place.x, place.zl]
        self.copies = [net.remote(self.piece.at[rank], mine, device) for device, rank in place.peers]
        self.own = net.here(self.piece.at[place.rank], mine)

    def wait(self):
        for copy in self.copies:
            copy.wait_recv()
        self.own.wait()


class Gather:
    def __init__(self, net, block, full, ranks=True, ahead=None):
        self.net, self.block, self.full, self.ranks, self.ahead = net, block, full, ranks, ahead

    def slot(self, a, core, zh):
        if self.ranks:
            return self.full.at[a, :, core, zh, :]
        return self.full.at[a, core, zh]

    def column(self, a, core):
        if self.ranks:
            return self.full.at[a, :, core, :, :]
        return self.full.at[a, core]

    def begin(self):
        net, p = self.net, self.net.place
        mine = self.slot(p.a, p.core, p.zh)
        self.own = [net.here(self.block, mine)]
        self.cores = [net.remote(self.block, mine, p.core_peer)]
        if self.ahead is None:
            self.across = net.remote(self.block, mine, p.zh_peer)
            self.near = [net.remote(self.block, mine, o[0]) for o in p.others]
            return
        got = self.slot(p.a, p.core, 1 - p.zh)
        self.far = [net.remote(self.ahead.at[0], got, o[0]) for o in p.others]
        self.cores.append(net.remote(self.ahead.at[0], got, p.core_peer))
        self.own.append(net.here(self.ahead.at[0], got))
        for k, other in enumerate(p.others):
            self.own.append(net.here(self.ahead.at[k + 1], self.slot(other[2], p.core, p.zh)))

    def middle(self):
        net, p = self.net, self.net.place
        self.across.wait_recv()
        got = self.slot(p.a, p.core, 1 - p.zh)
        self.far = [net.remote(got, got, o[0]) for o in p.others]
        self.cores.append(net.remote(got, got, p.core_peer))

    def final(self):
        net, p = self.net, self.net.place
        for copy in self.own:
            copy.wait()
        for k, other in enumerate(p.others):
            if self.ahead is None:
                self.near[k].wait_recv()
            self.far[k].wait_recv()
            got = self.column(other[2], p.core)
            self.cores.append(net.remote(got, got, p.core_peer))

    def done(self):
        for copy in self.cores:
            copy.wait_recv()


class Ahead:
    def __init__(self, net, block, got):
        self.net, self.block, self.got = net, block, got

    def begin(self):
        net, p = self.net, self.net.place
        self.copies = [net.remote(self.block, self.got.at[0], p.zh_peer)]
        self.copies += [net.remote(self.block, self.got.at[k + 1], o[0]) for k, o in enumerate(p.others)]

    def done(self):
        for copy in self.copies:
            copy.wait_recv()


class Reduce:
    def __init__(self, net, part, out, held, from_core, from_a, from_zh, from_rank, ranks=True, added=False):
        self.net, self.part, self.out = net, part, out
        self.held, self.from_core, self.from_a = held, from_core, from_a
        self.from_zh, self.from_rank = from_zh, from_rank
        self.ranks, self.added = ranks, added

    def half(self, core):
        return self.part.at[:, :, core] if self.ranks else self.part.at[:, core]

    def begin(self):
        net, p = self.net, self.net.place
        self.load = net.here(self.half(p.core), self.held)
        self.by_core = net.remote(self.half(1 - p.core), self.from_core, p.core_peer)

    def along_a(self):
        net, p = self.net, self.net.place
        self.load.wait()
        self.by_core.wait_recv()
        add_into(self.held, self.from_core)
        self.by_a = [
            net.remote(self.held.at[other[1]], self.from_a.at[k], other[0])
            for k, other in enumerate(p.others)
        ]

    def along_zh(self):
        net, p = self.net, self.net.place
        mine = self.held.at[p.a]
        for k, copy in enumerate(self.by_a):
            copy.wait_recv()
            add_into(mine, self.from_a.at[k])
        there = mine.at[:, 1 - p.zh] if self.ranks else mine.at[1 - p.zh]
        self.by_zh = net.remote(there, self.from_zh, p.zh_peer)

    def among_ranks(self):
        net, p = self.net, self.net.place
        self.by_zh.wait_recv()
        if not self.ranks:
            total = self.held[p.a, p.zh].astype(F32) + self.from_zh[...].astype(F32)
            self.out[...] = total.astype(self.out.dtype)
            return
        for x in range(2):
            for zl in range(2):
                add_into(self.held.at[p.a, x, p.zh, zl], self.from_zh.at[x, zl])
        self.by_rank = []
        for device, rank in p.peers:
            rank_x, rank_zl = lax.div(rank, 2), lax.rem(rank, 2)
            self.by_rank.append(
                net.remote(
                    self.held.at[p.a, rank_x, p.zh, rank_zl], self.from_rank.at[len(self.by_rank)], device
                )
            )

    def done(self):
        if not self.ranks:
            return
        p = self.net.place
        own = self.held[p.a, p.x, p.zh, p.zl].astype(F32)
        for copy in self.by_rank:
            copy.wait_recv()
        if self.added:
            for j in range(3):
                own = own + self.from_rank[j].astype(F32)
            self.out[...] = own
            return
        self.out[p.rank] = own.astype(self.out.dtype)
        for j, (_, rank) in enumerate(p.peers):
            self.out[rank] = self.from_rank[j].astype(self.out.dtype)

    @staticmethod
    def scratch(shape, ranks=True):
        tail = shape[-2:]
        count = shape[0]
        inner = ((2, 2, 2) if ranks else (2,)) + tail
        fewer = ((2, 2) if ranks else ()) + tail
        shapes = [(count,) + inner, (count,) + inner, (max(count - 1, 1),) + inner, fewer]
        if ranks:
            shapes.append((3,) + tail)
        return [pltpu.VMEM(s, BF16) for s in shapes]


def add_into(target, source):
    lead = target.shape[:-2]
    total = 1
    for size in lead:
        total *= size
    if total == 1 and not lead:
        target[...] = (target[...].astype(F32) + source[...].astype(F32)).astype(BF16)
        return

    @pl.loop(0, total)
    def _(j):
        index, left = [], j
        for size in reversed(lead):
            index.append(lax.rem(left, size))
            left = lax.div(left, size)
        index = tuple(reversed(index))
        target[index] = (target[index].astype(F32) + source[index].astype(F32)).astype(BF16)


class Spread:
    def __init__(self, net, land):
        self.net, self.land = net, land
        self.peers = net.place.peers
        mine = land.at[net.place.rank]
        self.along_x = net.remote(mine, mine, self.peers[0][0])
        self.along_zl = net.remote(mine, mine, self.peers[1][0])

    def arrivals(self):
        self.along_zl.wait_recv()
        got = self.land.at[self.peers[1][1]]
        relay = self.net.remote(got, got, self.peers[0][0])
        yield 1, self.peers[1][1]
        self.along_x.wait_recv()
        yield 0, self.peers[0][1]
        relay.wait_recv()
        yield 2, self.peers[2][1]

    def wait(self):
        for _ in self.arrivals():
            pass


class Sum:
    def __init__(self, net, out, land):
        self.net, self.out, self.land = net, out, land
        self.peers = net.place.peers

    def ready(self, i):
        if i == 2:
            self.diagonal = self.net.remote(self.out.at[2], self.land.at[0], self.peers[0][0])
        elif i == 0:
            self.along_x = self.net.remote(self.out.at[0], self.land.at[1], self.peers[0][0])

    def forward(self):
        self.diagonal.wait_recv()
        add_into(self.out.at[1], self.land.at[0])
        self.along_zl = self.net.remote(self.out.at[1], self.land.at[2], self.peers[1][0])

    def result(self, own):
        self.along_x.wait_recv()
        self.along_zl.wait_recv()
        return own + self.land[1].astype(F32) + self.land[2].astype(F32)


class EvenSpread:
    def __init__(self, net, land):
        self.net, self.land = net, land
        self.peers = net.place.peers
        self.half = land.shape[1] // 2
        me = net.place.rank
        self.x_high = self.go(me, 1, 0)
        self.z_low = self.go(me, 0, 1)
        self.x_low = self.go(me, 0, 0)
        self.z_high = self.go(me, 1, 1)

    def go(self, rank, part, i):
        rows = self.land.at[rank, pl.ds(part * self.half, self.half)]
        return self.net.remote(rows, rows, self.peers[i][0])

    def arrivals(self):
        self.x_high.wait_recv()
        on_z = self.go(self.peers[0][1], 1, 1)
        self.z_low.wait_recv()
        on_x = self.go(self.peers[1][1], 0, 0)
        self.x_low.wait_recv()
        yield 0, self.peers[0][1]
        self.z_high.wait_recv()
        yield 1, self.peers[1][1]
        on_z.wait_recv()
        on_x.wait_recv()
        yield 2, self.peers[2][1]

    def wait(self):
        for _ in self.arrivals():
            pass


class EvenSum:
    def __init__(self, net, out, land):
        self.net, self.out, self.land = net, out, land
        self.peers = net.place.peers
        self.half = out.shape[1] // 2

    def go(self, i, part, slot, peer):
        rows = pl.ds(part * self.half, self.half)
        return self.net.remote(self.out.at[i, rows], self.land.at[slot, rows], self.peers[peer][0])

    def ready(self, i):
        if i == 2:
            self.low, self.high = self.go(2, 0, 0, 0), self.go(2, 1, 0, 1)
        elif i == 0:
            self.x_low = self.go(0, 0, 1, 0)
        else:
            self.z_high = self.go(1, 1, 2, 1)

    def forward(self):
        low, high = pl.ds(0, self.half), pl.ds(self.half, self.half)
        self.high.wait_recv()
        add_into(self.out.at[0, high], self.land.at[0, high])
        self.x_high = self.go(0, 1, 1, 0)
        self.low.wait_recv()
        add_into(self.out.at[1, low], self.land.at[0, low])
        self.z_low = self.go(1, 0, 2, 1)

    def result(self, own):
        for copy in (self.x_low, self.x_high, self.z_low, self.z_high):
            copy.wait_recv()
        return own + self.land[1].astype(F32) + self.land[2].astype(F32)


def products(x, w_ref, count, tile, transposed, use):
    def part(cols):
        if transposed:
            w, dims = w_ref[cols, :], (((1,), (1,)), ((), ()))
        else:
            w, dims = w_ref[:, cols], (((1,), (0,)), ((), ()))
        use(cols, lax.dot_general(x(), w, dims, preferred_element_type=F32))

    for j in range(count // tile):
        part(pl.ds(j * tile, tile))


def norm_rows(h, gain):
    factor = lax.rsqrt(jnp.mean(h * h, axis=-1, keepdims=True) + NORM_EPS)
    return (h * factor * gain).astype(BF16)


def norm_rows_back(h, gain, grad):
    factor = lax.rsqrt(jnp.mean(h * h, axis=-1, keepdims=True) + NORM_EPS)
    z = grad * gain
    inner = jnp.sum(z * h, axis=-1, keepdims=True)
    back = factor * z - h * (factor * factor * factor * inner / h.shape[-1])
    return back, jnp.sum(grad * h * factor, axis=0, keepdims=True)


def rows_of(rank, rows):
    return pl.ds(pl.multiple_of(rank * rows, rows), rows)


class Refs:
    def __init__(self, refs):
        self.refs = list(refs)

    def take(self, n):
        got, self.refs = self.refs[:n], self.refs[n:]
        return got


class Ticks:
    def __init__(self, plan):
        self.plan = list(plan)

    def __call__(self):
        if self.plan:
            for step in self.plan.pop(0):
                step()

    def rest(self):
        while self.plan:
            self()


def np_tables(length):
    steps = np.arange(HEAD_DIM // 2, dtype=np.float32)
    inverse = np.exp(steps * np.float32(-2.0 * np.log(ROPE_BASE) / HEAD_DIM)).astype(np.float32)
    angles = np.arange(length, dtype=np.float32)[:, None] * inverse[None, :]
    return np.cos(angles), np.sin(angles)


def wide_tables(length):
    cosine, sine = np_tables(length)
    turned = (HEADS + KV_HEADS) // RANKS
    still = KV_HEADS // RANKS * HEAD_DIM
    cos_all = np.concatenate([cosine] * (2 * turned) + [np.ones((length, still))], axis=1)
    sin_all = np.concatenate([-sine, sine] * turned + [np.zeros((length, still))], axis=1)
    return jnp.asarray(cos_all, F32), jnp.asarray(sin_all, F32)


def turn(values, cosine, sine):
    cols = values.shape[1]
    half = HEAD_DIM // 2
    lane = lax.broadcasted_iota(jnp.int32, values.shape, 1)
    other = jnp.where(
        lax.rem(lane, HEAD_DIM) < half,
        pltpu.roll(values, cols - half, 1),
        pltpu.roll(values, half, 1),
    )
    return values * cosine + other * sine


def head_window(values, h):
    offset = HEAD_DIM * h
    start = offset // 128 * 128
    size = 128 if offset - start + HEAD_DIM <= 128 else 256
    window = values[:, start : start + size]
    if offset > start:
        window = pltpu.roll(window, size - (offset - start), 1)
    window = window[:, :128]
    lane = lax.broadcasted_iota(jnp.int32, window.shape, 1)
    return jnp.where(lane < HEAD_DIM, window, 0.0)


def heads_joined(parts):
    rows = parts[0].shape[0]
    columns = [jnp.zeros((rows, 128), F32) for _ in range(len(parts) * HEAD_DIM // 128 + 1)]
    for h, part in enumerate(parts):
        offset = HEAD_DIM * h
        first = offset // 128
        shift = offset - first * 128
        if shift == 0:
            columns[first] = columns[first] + part
            continue
        double = jnp.concatenate([part, jnp.zeros((rows, 128), F32)], axis=1)
        double = pltpu.roll(double, shift, 1)
        columns[first] = columns[first] + double[:, :128]
        columns[first + 1] = columns[first + 1] + double[:, 128:]
    return jnp.concatenate(columns[:-1], axis=1)


def project_heads(rows, n1, wq, cos_ref, sin_ref, heads):
    count = heads.shape[0]

    @pl.loop(0, RANKS)
    def _(b):
        span = rows_of(b, rows)
        y = jnp.dot(n1[b], wq[...], preferred_element_type=F32)
        y = turn(y, cos_ref[span, :], sin_ref[span, :])
        for h in range(count):
            heads[h, span, :] = head_window(y, h).astype(BF16)


def causal_scores(rows, rank, query, key):
    scores = lax.dot_general(query, key, (((1,), (1,)), ((), ())), preferred_element_type=F32)
    row = lax.broadcasted_iota(jnp.int32, scores.shape, 0) + rank * rows
    col = lax.broadcasted_iota(jnp.int32, scores.shape, 1)
    return jnp.where(col <= row, scores * HEAD_DIM ** (-0.5), MASKED)


def attend_rows(rows, rank, heads, o_ref, lse_ref):
    span = rows_of(rank, rows)
    queries = HEADS // RANKS
    pairs = KV_HEADS // RANKS
    groups = HEADS // KV_HEADS
    mixed = []
    lane = lax.broadcasted_iota(jnp.int32, (rows, 128), 1)
    lse_all = jnp.zeros((rows, 128), F32)
    for h in range(queries):
        kv = h // groups
        scores = causal_scores(rows, rank, heads[h, span, :], heads[queries + kv])
        highest = jnp.max(scores, axis=-1, keepdims=True)
        weights = jnp.exp(scores - highest)
        total = jnp.sum(weights, axis=-1, keepdims=True)
        lse = highest + jnp.log(total)
        lse_all = jnp.where(lane == h, lse, lse_all)
        weights = (weights * (1.0 / total)).astype(BF16)
        mixed.append(
            jnp.dot(weights, heads[queries + pairs + kv], preferred_element_type=F32)
        )
    lse_ref[span, :] = lse_all
    o_ref[span, :] = heads_joined(mixed).astype(BF16)


def window_tables(length):
    cosine, sine = np_tables(length)
    none = np.zeros((length, 128 - HEAD_DIM))
    cos_one = np.concatenate([cosine, cosine, none], axis=1)
    sin_one = np.concatenate([-sine, sine, none], axis=1)
    return jnp.asarray(cos_one, F32), jnp.asarray(sin_one, F32)


def turn_window(values, cosine, sine):
    half = HEAD_DIM // 2
    lane = lax.broadcasted_iota(jnp.int32, values.shape, 1)
    other = jnp.where(lane < half, pltpu.roll(values, 128 - half, 1), pltpu.roll(values, half, 1))
    return values * cosine + other * sine


def dot_tn(a, b):
    return lax.dot_general(a, b, (((0,), (0,)), ((), ())), preferred_element_type=F32)


def attend_rows_back(rows, rank, do_rows, heads, o_ref, lse_ref, cos_ref, sin_ref, dq_ref, dkv):
    span = rows_of(rank, rows)
    queries = HEADS // RANKS
    pairs = KV_HEADS // RANKS
    groups = HEADS // KV_HEADS
    o_rows = o_ref[span, :].astype(F32)
    parts = []
    for h in range(queries):
        kv = h // groups
        do_h = head_window(do_rows, h)
        delta = jnp.sum(do_h * head_window(o_rows, h), axis=-1, keepdims=True)
        do_b = do_h.astype(BF16)
        query, key, value = heads[h, span, :], heads[queries + kv], heads[queries + pairs + kv]
        weights = jnp.exp(causal_scores(rows, rank, query, key) - lse_ref[span, h : h + 1])
        grad_w = lax.dot_general(do_b, value, (((1,), (1,)), ((), ())), preferred_element_type=F32)
        ds = (weights * (grad_w - delta) * HEAD_DIM ** (-0.5)).astype(BF16)
        dq = jnp.dot(ds, key, preferred_element_type=F32)
        parts.append(turn_window(dq, cos_ref[span, :], -sin_ref[span, :]))
        dkv[kv] += dot_tn(ds, query)
        dkv[pairs + kv] += dot_tn(weights.astype(BF16), do_b)
    joined = heads_joined(parts)
    dq_ref[span, pl.ds(0, joined.shape[1])] = joined.astype(BF16)


def close_keys(rows, dkv, cos_ref, sin_ref, dqkv_ref):
    pairs = KV_HEADS // RANKS
    first = HEADS // RANKS * HEAD_DIM

    @pl.loop(0, RANKS)
    def _(b):
        span = rows_of(b, rows)
        parts = [turn_window(dkv[i, span, :], cos_ref[span, :], -sin_ref[span, :]) for i in range(pairs)]
        parts += [dkv[pairs + i, span, :] for i in range(pairs)]
        joined = heads_joined(parts)
        dqkv_ref[span, pl.ds(first, joined.shape[1])] = joined.astype(BF16)


def put_blocks(target, value):
    *lead, rows, cols = target.shape
    if rows % 16 == 0:
        target.reshape(value.shape[0], cols)[...] = value.astype(BF16)
        return
    for block in range(value.shape[0] // rows):
        index, left = [], block
        for size in reversed(lead):
            index.append(left % size)
            left //= size
        target[tuple(reversed(index))] = value[block * rows : (block + 1) * rows].astype(BF16)


def start_kernel(count, n, n_later, n_ahead, *refs):
    refs = Refs(refs)
    (tokens,) = refs.take(1)
    pieces, later = refs.take(n), refs.take(n_later)
    (all_tokens,) = refs.take(1)
    full, blocks_later, got_ahead = refs.take(n), refs.take(n_later), refs.take(n_ahead)
    own_tokens, land = refs.take(2)
    blocks = refs.take(n)
    send, recv, local = refs.take(3)
    place = Place(count)
    net = Net(place, send, recv, local)
    shares = [Share(net, pieces[i], blocks[i]) for i in range(n)]
    shares_later = [Share(net, later[i], blocks_later[i]) for i in range(n_later)]
    gathers = [Gather(net, blocks[i], full[i]) for i in range(n)]
    aheads = [Ahead(net, blocks_later[i], got_ahead[i]) for i in range(n_ahead)]
    swap = Swap(net, tokens, land.at[place.zh * 2 + place.zl])
    place.greet(True, True)
    shares[0].start()
    swap.start()
    for share in shares[1:] + shares_later[:n_ahead]:
        share.start()
    for i in range(2):
        shares[i].wait()
        gathers[i].begin()
    swap.wait()
    spreads = Spread(net, land)
    keep_own = net.here(land.at[place.rank], own_tokens)
    for i in range(2, n):
        shares[i].wait()
        gathers[i].begin()
    for i in range(n_ahead):
        shares_later[i].wait()
        aheads[i].begin()
    arrivals = spreads.arrivals()
    next(arrivals)
    for share in shares_later[n_ahead:]:
        share.start()
    gathers[0].middle()
    gathers[1].middle()
    for _ in arrivals:
        pass
    keep = net.here(land, all_tokens)
    gathers[0].final()
    for i in range(2, n):
        gathers[i].middle()
        gathers[i - 1].final()
    gathers[-1].final()
    for gather in gathers + aheads:
        gather.done()
    for share in shares_later[n_ahead:]:
        share.wait()
    keep_own.wait()
    keep.wait()
    net.finish()


def body_kernel(count, rows, late, started, n_next, n_ahead, plan, *refs):
    refs = Refs(refs)
    n1_hbm, wq_hbm, cos_ref, sin_ref, h_ref, gain_ref, wo_hbm = refs.take(7)
    inner_hbm = refs.take(3)
    ahead_hbm = [refs.take(1)[0] if started[i] else None for i in range(3)]
    if n_next:
        (gain_next,) = refs.take(1)
        blocks = refs.take(n_next)
    else:
        (swap_src,) = refs.take(1)
    heads, o_ref, lse_ref, h1_ref, hn_ref, hb_ref, gate_ref, up_ref, u_ref, ng_hbm = refs.take(10)
    late_out = [refs.take(1)[0] if late[i] else None for i in range(3)]
    if n_next:
        (nn_hbm,) = refs.take(1)
        full = refs.take(n_next)
    else:
        (swap_dst,) = refs.take(1)
    n1, wq, wo = refs.take(3)
    inner = refs.take(3)
    out_a, land_a, land_n, out_b, land_b = refs.take(5)
    if n_next:
        (land_q,) = refs.take(1)
    send, recv, local = refs.take(3)

    place = Place(count)
    net = Net(place, send, recv, local)
    width = h_ref.shape[1]
    hidden = u_ref.shape[1]
    load_q = net.here(wq_hbm.at[:, pl.ds(0, wq.shape[1])], wq)
    load_n = net.here(n1_hbm, n1)
    load_out = net.here(wo_hbm, wo)
    jobs = {}
    loads, weights = [], []
    for i in range(3):
        if late[i]:
            jobs[("gate", "up", "down")[i]] = Gather(net, inner_hbm[i], inner[i], i < 2, ahead_hbm[i])
            loads.append(None)
        else:
            loads.append(net.here(inner_hbm[i], inner[i]))
        weights.append(inner[i].reshape((hidden, width) if i == 2 else (width, hidden)) if late[i] else inner[i])
    wg, wu, wd = weights
    for i in range(n_next):
        jobs[i] = (Ahead if i >= n_next - n_ahead else Gather)(net, blocks[i], full[i])
    if not n_next:
        jobs["swap"] = Swap(net, swap_src, swap_dst)
    peers = place.peers
    place.greet(True, not n_next)
    keeps = []

    def ready(i):
        if late[i]:
            jobs[("gate", "up", "down")[i]].done()
            keeps.append(net.here(inner[i], late_out[i]))
        else:
            loads[i].wait()

    tick = Ticks(plan(jobs))
    tick()

    load_q.wait()
    load_n.wait()
    project_heads(rows, n1, wq, cos_ref, sin_ref, heads)
    load_out.wait()
    sums = EvenSum(net, out_a, land_a)
    for i in (2, 0, 1):
        attend_rows(rows, peers[i][1], heads, o_ref, lse_ref)
        span = rows_of(peers[i][1], rows)

        def use(cols, y, i=i):
            out_a[i, :, cols] = y.astype(BF16)

        products(lambda: o_ref[span, :], wo, width, width, True, use)
        sums.ready(i)
    attend_rows(rows, place.rank, heads, o_ref, lse_ref)
    span = rows_of(place.rank, rows)

    def use_own(cols, y):
        h1_ref[:, cols] = h_ref[:, cols].astype(F32) + y

    products(lambda: o_ref[span, :], wo, width, width, True, use_own)
    sums.forward()
    tick()
    h1 = sums.result(h1_ref[...])
    h1_ref[...] = h1
    land_n[place.rank] = norm_rows(h1, gain_ref[...])
    gather = EvenSpread(net, land_n)
    tick()
    ready(0)
    ready(1)

    def inner_block(rank):
        span = rows_of(rank, rows)

        gate = jnp.dot(land_n[rank], wg[...], preferred_element_type=F32)
        up = jnp.dot(land_n[rank], wu[...], preferred_element_type=F32)
        gate_ref[span, :] = gate.astype(BF16)
        up_ref[span, :] = up.astype(BF16)
        u_ref[span, :] = (gate / (1.0 + jnp.exp(-gate)) * up).astype(BF16)

        return span

    inner_block(place.rank)
    tick()
    second = EvenSum(net, out_b, land_b)
    got_down = False
    for i, rank in gather.arrivals():
        span = inner_block(rank)
        if not got_down:
            tick()
            ready(2)
            got_down = True

        def use(cols, y, i=i):
            out_b[i, :, cols] = y.astype(BF16)

        products(lambda: u_ref[span, :], wd, width, width, False, use)
        second.ready(i)
        tick()
    keep = net.here(land_n, ng_hbm)
    span = rows_of(place.rank, rows)

    def use_down(cols, y):
        hn_ref[:, cols] = h1_ref[:, cols] + y

    products(lambda: u_ref[span, :], wd, width, width, False, use_down)
    second.forward()
    tick()
    hn = second.result(hn_ref[...])
    hn_ref[...] = hn
    hb_ref[...] = hn.astype(BF16)
    if n_next:
        land_q[place.rank] = norm_rows(hn, gain_next[...])
        third = EvenSpread(net, land_q)
        tick()
        for _ in third.arrivals():
            tick()
        keep_next = net.here(land_q, nn_hbm)
        keep_next.wait()
    tick.rest()
    for i in range(n_next):
        jobs[i].done()
    if not n_next:
        jobs["swap"].wait()
    keep.wait()
    for copy in keeps:
        copy.wait()
    net.finish()


def plan_late(j):
    gate, up, down = j["gate"], j["up"], j["down"]
    return [
        [gate.begin, up.begin],
        [gate.middle, down.begin],
        [up.final, gate.final],
        [down.middle, j[0].begin, j[1].begin],
        [down.final],
        [],
        [],
        [j[0].middle],
        [j[0].final, j[1].middle],
        [j[2].begin, j[1].final],
    ]


def plan_late_end(j):
    gate, up, down = j["gate"], j["up"], j["down"]
    return [
        [up.begin, gate.begin],
        [up.middle, down.begin],
        [gate.final, up.final],
        [down.middle],
        [down.final],
        [],
        [],
        [j["swap"].start],
    ]


def plan_early(j):
    down = j["down"]
    return [
        [down.begin],
        [down.middle, j[0].begin],
        [],
        [down.final, j[1].begin, j[2].begin],
        [j[0].middle],
        [],
        [],
        [j[0].final],
        [j[1].middle, j[2].middle],
        [j[3].begin, j[1].final, j[2].final],
        [],
        [],
        [j[3].middle],
        [j[3].final],
    ]


def plan_end(j):
    down = j["down"]
    return [
        [down.begin],
        [],
        [down.middle],
        [],
        [down.final],
        [],
        [],
        [j["swap"].start],
    ]


class Back:
    def __init__(self, net, rows):
        self.net, self.place, self.rows = net, net.place, rows
        self.peers = net.place.peers

    def enter(self, r, tick):
        rows, place = self.rows, self.place
        width = r["gnew"].shape[1]
        total = EvenSum(self.net, r["out_a"], r["land_a"])
        for i in (2, 0, 1):
            span = rows_of(self.peers[i][1], rows)

            def use(cols, y, i=i):
                r["out_a"][i, :, cols] = y.astype(BF16)

            products(lambda: r["dqkv"][span, :], r["wq"], width, width, True, use)
            total.ready(i)
        tick()
        own = rows_of(place.rank, rows)

        def use_own(cols, y):
            r["gnew"][:, cols] = y

        products(lambda: r["dqkv"][own, :], r["wq"], width, width, True, use_own)
        total.forward()
        tick()
        dn = total.result(r["gnew"][...])
        back, ggain = norm_rows_back(r["hin"][...].astype(F32), r["gain_in"][...], dn)
        r["gnew"][...] = r["ghin"][...] + back
        return ggain

    def feed_forward(self, r, tick, ready, between):
        net, rows, place = self.net, self.rows, self.place
        land_g, dgu, out_b = r["land_g"], r["dgu"], r["out_b"]
        width = land_g.shape[2]
        hidden = r["gate"].shape[1]
        land_g[place.rank] = r["g"][...].astype(BF16)
        gather = EvenSpread(net, land_g)
        tick()
        ready()

        def inner_block(rank):
            span = rows_of(rank, rows)
            du = lax.dot_general(
                land_g[rank], r["wd"][...], (((1,), (1,)), ((), ())), preferred_element_type=F32
            )
            gate, up = r["gate"][span, :].astype(F32), r["up"][span, :].astype(F32)
            sg = 1.0 / (1.0 + jnp.exp(-gate))
            dgu[span, pl.ds(0, hidden)] = (du * up * sg * (1.0 + gate * (1.0 - sg))).astype(BF16)
            dgu[span, pl.ds(hidden, hidden)] = (du * gate * sg).astype(BF16)
            return span

        span = inner_block(place.rank)

        def use_mid(cols, y):
            r["gh"][:, cols] = y

        products(lambda: dgu[span, :], r["wgu"], width, width, True, use_mid)
        tick()
        second = EvenSum(net, out_b, r["land_b"])
        for i, rank in gather.arrivals():
            span = inner_block(rank)

            def use(cols, y, i=i):
                out_b[i, :, cols] = y.astype(BF16)

            products(lambda: dgu[span, :], r["wgu"], width, width, True, use)
            second.ready(i)
            tick()
        second.forward()
        tick()
        between()
        tick()
        dn = second.result(r["gh"][...])
        back, ggain = norm_rows_back(r["h1"][...], r["gain"][...], dn)
        r["gh"][...] = r["g"][...].astype(F32) + back
        r["gg"][...] = ggain

    def weight_grads(self, r, down_made):
        net = self.net
        buffers, copies = r["buffers"], []
        tile = buffers.shape[1]
        tall, hidden = r["u"].shape
        width = r["land_g"].shape[2]
        g_all = r["land_g"][...].reshape(tall, width)

        def emit(lhs, rhs, outs, m):
            slot = len(copies) % 2
            if len(copies) >= 2:
                for copy in copies[-2]:
                    copy.wait()
            buffers[slot, :, pl.ds(0, rhs.shape[1])] = dot_tn(lhs, rhs).astype(BF16)
            cols = rhs.shape[1] // len(outs)
            copies.append([
                net.here(buffers.at[slot, :, pl.ds(k * cols, cols)], out.at[pl.ds(m * tile, tile)])
                for k, out in enumerate(outs)
            ])

        for k, part in enumerate((r["part_da"], r["part_db"])):
            cols = part.shape[-1]
            made = dot_tn(r["u"][...], g_all[:, k * cols : (k + 1) * cols])
            part.reshape(hidden, cols)[...] = made.astype(BF16)
        down_made()
        for m in range(width // tile):
            emit(r["n2"][:, m * tile : (m + 1) * tile], r["dgu"][...], [r[name] for name in INNER_GRADS], m)
        return copies[-2] + copies[-1]

    def attention(self, r, tick, ready):
        net, rows, place = self.net, self.rows, self.place
        land_h = r["land_h"]
        land_h[place.rank] = r["gh"][...].astype(BF16)
        gather = EvenSpread(net, land_h)
        tick()
        ready()
        r["dkv"][...] = jnp.zeros(r["dkv"].shape, F32)

        def block(rank):
            do_rows = jnp.dot(land_h[rank], r["wo"][...], preferred_element_type=F32)
            do_rows = do_rows.astype(BF16).astype(F32)
            attend_rows_back(
                rows, rank, do_rows, r["heads"], r["o"], r["lse"], r["cos"], r["sin"], r["dqkv"], r["dkv"]
            )

        block(place.rank)
        tick()
        for _, rank in gather.arrivals():
            block(rank)
            tick()
        close_keys(rows, r["dkv"], r["cos"], r["sin"], r["dqkv"])


INNER_GRADS = ("g_gate_a", "g_gate_b", "g_up_a", "g_up_b")


def back_kernel(count, rows, names, out_names, scratch_names, n_parts, kinds, plan, *refs):
    refs = Refs(refs)
    r = dict(zip(names, refs.take(len(names))))
    parts = refs.take(n_parts)
    r.update(zip(out_names, refs.take(len(out_names))))
    red_out = refs.take(len(kinds))
    r.update(zip(scratch_names, refs.take(len(scratch_names))))
    red_scratch = [refs.take(5 if ranks else 4) for ranks in kinds]
    gains_scratch = refs.take(5) if "gains_out" in r else None
    send, recv, local = refs.take(3)

    place = Place(count)
    net = Net(place, send, recv, local)
    back = Back(net, rows)
    entering, inner, attention = "hin" in r, "h1" in r, "heads_hbm" in r
    last = "gains_out" in r
    waits = {}

    def load(name, source, target):
        waits[name] = net.here(source, target)

    parts = parts + ([r["part_o"], r["part_q"]] if last else [r["part_da"], r["part_db"]])
    jobs = []
    for part, out, scratch, ranks in zip(parts, red_out, red_scratch, kinds):
        jobs.append(Reduce(net, part, out, *scratch, *([] if ranks else [None]), ranks=ranks))
    if entering:
        load("wq", r["wq_hbm"].at[:, pl.ds(0, r["wq"].shape[1])], r["wq"])
    if inner:
        hidden = r["wd"].shape[0]
        load("wd", r["wd_hbm"], r["wd"])
        load("wg", r["wgate_hbm"], r["wgu"].at[:, pl.ds(0, hidden)])
        load("wu", r["wup_hbm"], r["wgu"].at[:, pl.ds(hidden, hidden)])
        load("u", r["u_hbm"], r["u"])
        load("n2", r["n2_hbm"], r["n2"])
    if attention:
        for name in ("wo", "heads", "o", "lse", "n1"):
            load(name, r[name + "_hbm"], r[name])
    place.greet(len(jobs) > 0, "swap_src" in r or last)
    if "swap_src" in r:
        jobs.append(Swap(net, r["swap_src"], r["swap_dst"]))
    tick = Ticks(plan(jobs))
    tick()
    ends = []

    def ready_inner():
        for name in ("wd", "wg", "wu"):
            waits[name].wait()

    def between():
        waits["u"].wait()
        waits["n2"].wait()
        ends.extend(back.weight_grads(r, tick))

    def ready_attention():
        for name in ("wo", "heads", "o", "lse"):
            waits[name].wait()

    if entering and inner:
        waits["wq"].wait()
        r["ggin"][...] = back.enter(r, tick)
        r["g"] = r["gnew"]
    if inner:
        back.feed_forward(r, tick, ready_inner, between)
    if attention:
        back.attention(r, tick, ready_attention)
        waits["n1"].wait()
        width = r["land_h"].shape[2]
        tall = r["o"].shape[0]

        def grad_out():
            return dot_tn(r["land_h"][...].reshape(tall, width), r["o"][...])

        def grad_qkv():
            return dot_tn(r["n1"][...].reshape(tall, width), r["dqkv"][...])

        if not last:
            r["g_out"][...] = grad_out().astype(BF16)
            r["g_qkv"][...] = grad_qkv().astype(BF16)
        else:
            waits["wq"].wait()
            made = Ticks([
                [],
                [lambda: put_blocks(r["part_q"], grad_qkv()), lambda: put_blocks(r["part_o"], grad_out())],
            ])

            def both():
                made()
                tick()

            ggain = back.enter(r, both)
            finish_last(net, r, jobs, ggain, gains_scratch)
            for copy in ends:
                copy.wait()
            net.finish()
            return
    tick.rest()
    if "swap_src" in r:
        jobs[-1].wait()
    for copy in ends:
        copy.wait()
    net.finish()


def finish_last(net, r, jobs, ggain, scratch):
    r["gsend"][...] = r["gnew"][...].astype(BF16)
    swap = Swap(net, r["gsend"], r["swap_dst"])
    gains_all, gains_part = r["gains_all"], r["gains_part"]
    gains_all[...] = r["other_gains"][...]
    gains_all[0:1, :] = ggain
    gains_part[...] = jnp.zeros(gains_part.shape, BF16)
    count = gains_part.shape[0]
    piece = gains_all.shape[1] // (16 * count)
    for block in range(16 * count):
        index = (block // 16, block // 8 % 2, block // 4 % 2, block // 2 % 2, block % 2)
        gains_part[index + (slice(None), slice(0, piece))] = gains_all[
            :, block * piece : (block + 1) * piece
        ].astype(BF16)
    small = Reduce(net, gains_part, r["gains_out"], *scratch, added=True)
    small.begin()
    for step in plan_finish(jobs, small, swap):
        step()
    swap.wait()


def plan_finish(j, s, swap):
    ga, gb, ua, ub, out, qkv = j
    return [
        s.along_a, ub.along_zh, out.along_a, qkv.along_a, ga.among_ranks, s.along_zh, out.along_zh, gb.among_ranks,
        s.among_ranks, ua.among_ranks, swap.start, ub.among_ranks, ga.done, qkv.along_zh, gb.done, out.among_ranks,
        s.done, ua.done, ub.done, out.done, qkv.among_ranks, qkv.done,
    ]


def plan_first(j):
    da, db, swap = j
    return [
        [],
        [],
        [],
        [],
        [],
        [],
        [swap.start],
        [da.begin, db.begin],
        [da.along_a],
        [db.along_a],
        [],
        [da.along_zh],
        [db.along_zh],
        [],
        [da.among_ranks, db.among_ranks],
    ]


def plan_middle(j):
    ga, gb, ua, ub, out, qkv, da, db = j
    return [
        [ga.begin, gb.begin, ua.begin, ub.begin, out.begin, qkv.begin],
        [ga.along_a],
        [gb.along_a, ga.along_zh],
        [ua.along_a],
        [gb.along_zh],
        [ub.along_a, ua.along_zh],
        [out.along_a],
        [ga.among_ranks],
        [ub.along_zh, qkv.along_a],
        [da.begin, db.begin, gb.among_ranks],
        [out.along_zh, ua.among_ranks, da.along_a],
        [db.along_a, ub.among_ranks, qkv.along_zh, out.among_ranks, ga.done, gb.done, da.along_zh, ua.done, ub.done],
        [qkv.among_ranks, db.along_zh, out.done, qkv.done, da.among_ranks, db.among_ranks],
    ]


def plan_last(j):
    ga, gb, ua, ub, out, qkv = j
    return [
        [ga.begin, gb.begin, ua.begin, ub.begin],
        [ga.along_a],
        [gb.along_a],
        [ga.along_zh, ua.along_a],
        [],
        [gb.along_zh, ub.along_a],
        [],
        [out.begin, qkv.begin, ua.along_zh],
    ]


def pack_weights(w_qkv, w_out, w_gate_up, gains, count, layer):
    rows = w_qkv.shape[1]
    attn_cols = HEADS * HEAD_DIM
    kv_cols = KV_HEADS * HEAD_DIM
    qkv = w_qkv[layer]
    q = qkv[:, :attn_cols].reshape(rows, RANKS, -1)
    k = qkv[:, attn_cols : attn_cols + kv_cols].reshape(rows, RANKS, -1)
    v = qkv[:, attn_cols + kv_cols :].reshape(rows, RANKS, -1)
    columns = [q, k, v]
    if layer == 0:
        scales = jnp.pad(gains.reshape(2 * LAYERS, rows).T, ((0, 0), (0, GAIN_COLS - 2 * LAYERS)))
        columns.append(jnp.broadcast_to(scales[:, None], (rows, RANKS, GAIN_COLS)))
    head = jnp.concatenate(columns, axis=2).transpose(1, 0, 2)
    out = w_out[layer].T.reshape(rows, RANKS, -1).transpose(1, 0, 2)
    gu = w_gate_up[layer].reshape(rows, 2, count, 2, 2, 2, 2, -1)
    gu = gu.transpose(1, 3, 6, 0, 2, 4, 5, 7).reshape(2, RANKS, rows, -1)
    return head, out, gu[0], gu[1]


def unpack_grads(head, out, gate, up, count):
    rows = head.shape[1]
    q_cols = HEADS * HEAD_DIM // RANKS
    kv_cols = KV_HEADS * HEAD_DIM // RANKS
    wide = lambda part: part.transpose(1, 0, 2).reshape(rows, -1)
    qkv = jnp.concatenate(
        [
            wide(head[:, :, :q_cols]),
            wide(head[:, :, q_cols : q_cols + kv_cols]),
            wide(head[:, :, q_cols + kv_cols : q_cols + 2 * kv_cols]),
        ],
        axis=1,
    )
    order = lambda part: (
        part.reshape(2, 2, rows, count, 2, 2, -1).transpose(2, 3, 0, 4, 5, 1, 6).reshape(rows, -1)
    )
    return qkv, wide(out).T, jnp.stack([order(gate), order(up)], axis=1)


VM = pl.BlockSpec(memory_space=pltpu.VMEM)
AN = pl.BlockSpec(memory_space=pl.ANY)


def params(collective_id):
    return pltpu.CompilerParams(
        collective_id=collective_id, has_side_effects=True, vmem_limit_bytes=VMEM_BYTES
    )


def like(shape, dtype=BF16):
    return jax.ShapeDtypeStruct(tuple(shape), dtype)


def full_shape(count, tail):
    return (count, 2, 2, 2, 2) + tuple(tail)


def call_start(count, tokens, pieces, later, n_ahead):
    rows, width = tokens.shape
    n, n_later = len(pieces), len(later)
    outs = [like((RANKS, rows, width))]
    outs += [like(full_shape(count, p.shape[1:])) for p in pieces]
    outs += [like((2, 2) + p.shape[1:]) for p in later]
    outs += [like((count, 2, 2) + p.shape[1:]) for p in later[:n_ahead]]
    outs += [like((rows, width))]
    got = pl.pallas_call(
        functools.partial(start_kernel, count, n, n_later, n_ahead),
        out_shape=outs,
        in_specs=[AN] * (1 + n + n_later),
        out_specs=[AN] * len(outs),
        scratch_shapes=[pltpu.VMEM((RANKS, rows, width), BF16)]
        + [pltpu.VMEM((2, 2) + p.shape[1:], BF16) for p in pieces]
        + sems(count),
        compiler_params=params(1),
        name="start",
    )(tokens, *pieces, *later)
    cut = n + 1 + n_later
    return got[0], got[-1], [flat(f) for f in got[1 : n + 1]], got[n + 1 : cut], got[cut:-1]


def flat(value):
    return value.reshape(-1, value.shape[-1])


def call_body(
    count, n1, wq, tables, h, gain, wo, inner, late, ahead, plan, gain_next=None, blocks=(), n_ahead=0, swap=None
):
    started = tuple(value is not None for value in ahead)
    rows, width = h.shape
    tall = RANKS * rows
    hidden = inner[0].shape[-1]
    n_next = len(blocks)
    heads = (HEADS + 2 * KV_HEADS) // RANKS
    cols = heads * HEAD_DIM
    o_cols = HEADS // RANKS * HEAD_DIM
    three = pltpu.VMEM((3, rows, width), BF16)
    four = pltpu.VMEM((RANKS, rows, width), BF16)
    shapes = []
    for i in range(3):
        shape = inner[i].shape
        if late[i]:
            shape = full_shape(count, shape[2:]) if i < 2 else (count, 2, 2) + shape
        shapes.append(shape)
    outs = [
        like((heads, tall, 128)),
        like((tall, o_cols)),
        like((tall, 128), F32),
        like((rows, width), F32),
        like((rows, width), F32),
        like((rows, width)),
        like((tall, hidden)),
        like((tall, hidden)),
        like((tall, hidden)),
        like((RANKS, rows, width)),
    ]
    n_state = len(outs)
    outs += [like(shapes[i]) for i in range(3) if late[i]]
    if n_next:
        outs += [like((RANKS, rows, width))]
        outs += [like(full_shape(count, b.shape[2:])) for b in blocks[: n_next - n_ahead]]
        outs += [like((count,) + b.shape) for b in blocks[n_next - n_ahead :]]
        extra = (gain_next, *blocks)
    else:
        outs += [like(swap.shape)]
        extra = (swap,)
    got = pl.pallas_call(
        functools.partial(body_kernel, count, rows, late, started, n_next, n_ahead, plan),
        out_shape=outs,
        in_specs=[AN, AN, VM, VM, VM, VM, AN, AN, AN, AN]
        + [AN] * sum(started)
        + ([VM] + [AN] * n_next if n_next else [AN]),
        out_specs=[VM] * (n_state - 1) + [AN] * (len(outs) - n_state + 1),
        scratch_shapes=[
            four,
            pltpu.VMEM((width, cols), BF16),
            pltpu.VMEM(wo.shape, BF16),
        ]
        + [pltpu.VMEM(shape, BF16) for shape in shapes]
        + [three, three, four, three, three]
        + ([four] if n_next else [])
        + sems(count),
        compiler_params=params(2 if n_next else 3),
        name="body_more" if n_next else "body",
    )(n1, wq, *tables, h, gain, wo, *inner, *[value for value in ahead if value is not None], *extra)
    got = list(got)
    state, rest = got[:n_state], got[n_state:]
    inner = [flat(rest.pop(0)) if late[i] else inner[i] for i in range(3)]
    rest, last = rest[: len(rest) - n_ahead], rest[len(rest) - n_ahead :]
    return state, inner, rest[0], [flat(f) for f in rest[1:]], last


def call_back(name, count, rows, inputs, outputs, scratch, parts, made, kinds, plan, collective_id):
    shapes = [p.shape for p in parts] + list(made)
    red_out = [like(((RANKS,) if ranks else ()) + shape[-2:]) for shape, ranks in zip(shapes, kinds)]
    scratch_shapes = [pltpu.VMEM(shape, dtype) for shape, dtype in scratch.values()]
    for shape, ranks in zip(shapes, kinds):
        scratch_shapes += Reduce.scratch(shape, ranks=ranks)
    if "gains_out" in outputs:
        scratch_shapes += Reduce.scratch(scratch["gains_part"][0])
    got = pl.pallas_call(
        functools.partial(
            back_kernel, count, rows, tuple(inputs), tuple(outputs), tuple(scratch), len(parts), kinds, plan
        ),
        out_shape=[shape for shape, _ in outputs.values()] + red_out,
        in_specs=[spec for _, spec in inputs.values()] + [AN] * len(parts),
        out_specs=[spec for _, spec in outputs.values()] + [VM] * len(red_out),
        scratch_shapes=scratch_shapes + sems(count),
        compiler_params=params(collective_id),
        name=name,
    )(*[value for value, _ in inputs.values()], *parts)
    return dict(zip(outputs, got)), got[len(outputs) :]


def shards(dp_size, ctx_size, tokens, cotangent, w_qkv, w_out, w_gate_up, w_down, gains):
    count = dp_size // 4
    rows, width = tokens.shape
    length = RANKS * rows
    hidden = w_gate_up.shape[-1] // RANKS
    tall = lambda value: value.reshape(length, width)

    swap = lambda value: lax.ppermute(value, ("dp", "ctx"), swap_pairs(dp_size, ctx_size))
    tie = lax.optimization_barrier

    tables = wide_tables(length)
    windows = window_tables(length)

    packed = [pack_weights(w_qkv, w_out, w_gate_up, gains, count, layer) for layer in range(LAYERS)]
    whole_rows = w_qkv.shape[1] % 16 == 0
    none = (None, None, None)
    if whole_rows:
        head, out, gate, up = packed[0]
        now, later, n_ahead = (head, out), (up, gate, *packed[1]), 1
    else:
        now, later, n_ahead = packed[0], packed[1], 0
    all_tokens, h, full, blocks, ahead = call_start(count, tokens, now, later, n_ahead)
    gain_rows = full[0][:, -GAIN_COLS:][:, : 2 * LAYERS].astype(F32).T
    gain = lambda layer, which: gain_rows[2 * layer + which][None]
    n1 = norm_rows(all_tokens.astype(F32), gain(0, 0))
    if whole_rows:
        up, gate, *blocks, last_up = blocks
        inner, late, ahead, plan = (gate, up, w_down[0]), (True, True, True), (None, ahead[0], None), plan_late
    else:
        inner, late, ahead, plan = (*full[2:], w_down[0]), (False, False, True), none, plan_early

    records = []
    for layer in range(LAYERS):
        wq, wo = full[:2]
        if layer + 1 < LAYERS:
            state, inner, n1_next, full, last_got = call_body(
                count, n1, wq, tables, h, gain(layer, 1), wo, inner, late, ahead, plan,
                gain(layer + 1, 0), blocks, n_ahead,
            )
            if whole_rows:
                late, ahead, plan = (True, True, True), (last_got[0], None, None), plan_late_end
                next_inner = (blocks[-1], last_up, w_down[layer + 1])
            else:
                late, plan = (False, False, True), plan_end
                next_inner = (*full[2:], w_down[layer + 1])
        else:
            state, inner, g, _, _ = call_body(
                count, n1, wq, tables, h, gain(layer, 1), wo, inner, late, ahead, plan,
                swap=cotangent.astype(BF16),
            )
            n1_next = None
        heads, mixed, lse, h1, h_next, h_round, gate, up, u, n2 = state
        records.append(dict(
            hin=h, n1=n1, heads=heads, o=mixed, lse=lse, h1=h1, n2=tall(n2), gate=gate, up=up, u=u,
            wq=wq, wo=wo, wgate=inner[0], wup=inner[1], wd=inner[2],
        ))
        h, n1, inner = h_next, n1_next, next_inner

    hidden = records[0]["u"].shape[1]
    heads = (HEADS + 2 * KV_HEADS) // RANKS
    cols = heads * HEAD_DIM
    o_cols = HEADS // RANKS * HEAD_DIM
    shape7 = lambda value: value.reshape(count, 2, 2, 2, 2, -1, value.shape[-1])
    three, four = ((3, rows, width), BF16), ((RANKS, rows, width), BF16)
    row_f32 = ((rows, width), F32)

    def inner_in(layer):
        rec = records[layer]
        names = dict(wd="wd", wgate="wgate", wup="wup", u="u", n2="n2")
        values = {key + "_hbm": (rec[name], AN) for key, name in names.items()}
        return dict(
            values, gate=(rec["gate"], VM), up=(rec["up"], VM), h1=(rec["h1"], VM), gain=(gain(layer, 1), VM)
        )

    inner_out = dict(
        gh=(like((rows, width), F32), VM),
        gg=(like((1, width), F32), VM),
        **{name: (like((width, hidden // 2)), AN) for name in INNER_GRADS},
    )
    shape_d = (count, 2, 2, w_down.shape[1], width // 2)
    inner_scratch = dict(
        part_da=(shape_d, BF16),
        part_db=(shape_d, BF16),
        wd=((hidden, width), BF16),
        wgu=((width, 2 * hidden), BF16),
        u=((length, hidden), BF16),
        n2=((length, width), BF16),
        dgu=((length, 2 * hidden), BF16),
        buffers=((2, 256, 2 * hidden), BF16),
        land_g=four,
        out_b=three,
        land_b=three,
    )

    def attention_in(layer):
        rec = records[layer]
        values = {name + "_hbm": (rec[name], AN) for name in ("wo", "heads", "o", "lse", "n1")}
        return dict(values, cos=(windows[0], VM), sin=(windows[1], VM))

    attention_scratch = dict(
        wo=((width, o_cols), BF16),
        heads=((heads, length, 128), BF16),
        o=((length, o_cols), BF16),
        lse=((length, 128), F32),
        n1=four,
        dkv=((2 * KV_HEADS // RANKS, length, 128), F32),
        land_h=four,
    )

    def enter_in(layer):
        rec = records[layer]
        return dict(wq_hbm=(rec["wq"], AN), hin=(rec["hin"], VM), gain_in=(gain(layer, 0), VM))

    enter_scratch = dict(wq=((width, cols), BF16), out_a=three, land_a=three)

    first, down_1 = call_back(
        "back_first", count, rows,
        dict(g=(g, VM), swap_src=(h_round, AN), **inner_in(1), **attention_in(1)),
        dict(
            inner_out,
            dqkv=(like((length, cols)), VM),
            g_out=(like((width, o_cols)), VM),
            g_qkv=(like((width, cols)), VM),
            swap_dst=(like((rows, width)), AN),
        ),
        dict(**inner_scratch, **attention_scratch), [], [shape_d] * 2, (False,) * 2, plan_first, 4,
    )
    parts_of = lambda got: [shape7(got[name]) for name in INNER_GRADS]
    middle, grads_1 = call_back(
        "back_mid", count, rows,
        dict(dqkv=(first["dqkv"], VM), ghin=(first["gh"], VM), **enter_in(1), **inner_in(0)),
        dict(ggin=(like((1, width), F32), VM), **inner_out),
        dict(gnew=row_f32, **enter_scratch, **inner_scratch),
        parts_of(first) + [shape7(first["g_out"]), shape7(first["g_qkv"])],
        [shape_d] * 2, (True,) * 6 + (False,) * 2, plan_middle, 5,
    )
    others = jnp.concatenate([jnp.zeros((1, width), F32), middle["gg"], middle["ggin"], first["gg"]], axis=0)
    others = jnp.pad(others, ((0, 16 - 2 * LAYERS), (0, 0)))
    shard_rows = w_qkv.shape[1]
    shape_o, shape_q = (full_shape(count, (shard_rows, c)) for c in (o_cols, cols))
    final, grads_0 = call_back(
        "back_last", count, rows,
        dict(gh=(middle["gh"], VM), ghin=(middle["gh"], VM), other_gains=(others, VM), **enter_in(0), **attention_in(0)),
        dict(swap_dst=(like((rows, width)), AN), gains_out=(like((16, GAIN_COLS), F32), VM)),
        dict(
            gnew=row_f32,
            gsend=((rows, width), BF16),
            gains_all=((16, width), F32),
            gains_part=(full_shape(count, (16, GAIN_COLS)), BF16),
            part_o=(shape_o, BF16),
            part_q=(shape_q, BF16),
            dqkv=((length, cols), BF16),
            **enter_scratch,
            **attention_scratch,
        ),
        parts_of(middle), [shape_o, shape_q], (True,) * 6, plan_last, 6,
    )
    out_act, grad_tokens, gains_sum = first["swap_dst"], final["swap_dst"], final["gains_out"]
    grads = (grads_0, grads_1[:6])
    downs = (grads_1[6:], down_1)
    piece = gains.shape[-1]
    grad_gains = gains_sum[: 2 * LAYERS, :piece].reshape(LAYERS, 2, piece)
    beside = lambda *halves: jnp.concatenate(halves, axis=2)
    stacked = [unpack_grads(q, o, beside(ga, gb), beside(ua, ub), count) for ga, gb, ua, ub, o, q in grads]
    s_qkv, s_out, s_gu = (jnp.stack([s[i] for s in stacked]) for i in range(3))
    s_down = jnp.stack([jnp.concatenate(d, axis=1) for d in downs])
    wide = lambda value: value.astype(F32)
    return (wide(out_act), wide(grad_tokens), wide(s_qkv), wide(s_out), wide(s_gu), wide(s_down), grad_gains)


def solution(mesh):
    both = ("dp", "ctx")
    return jax.shard_map(
        functools.partial(shards, mesh.shape["dp"], mesh.shape["ctx"]),
        mesh=mesh,
        in_specs=(
            P(both, None),
            P(both, None),
            P(None, both, None),
            P(None, None, both),
            P(None, both, None, None),
            P(None, both, None),
            P(None, None, both),
        ),
        out_specs=(
            P(both, None),
            P(both, None),
            P(None, both, None),
            P(None, None, both),
            P(None, both, None, None),
            P(None, both, None),
            P(None, None, both),
        ),
        check_vma=False,
    )
```

```python
import functools

import jax
import jax.numpy as jnp
import numpy as np
from jax import lax
from jax.experimental import pallas as pl
from jax.experimental.pallas import tpu as pltpu
from jax.sharding import PartitionSpec as P

HEADS = 16
KV_HEADS = 8
HEAD_DIM = 96
LAYERS = 2
RANKS = 4
GAIN_COLS = 128

NORM_EPS = 1e-05
ROPE_BASE = 100000.0
MASKED = -1e30
MESH = pl.DeviceIdType.MESH
BF16 = jnp.bfloat16
F32 = jnp.float32
VMEM_BYTES = 62 * 1024 * 1024


class Place:
    def __init__(self, count):
        self.count = count
        self.dp = lax.axis_index("dp")
        self.ctx = lax.axis_index("ctx")
        self.core = lax.rem(self.dp, 2)
        self.x = lax.rem(lax.div(self.dp, 2), 2)
        self.a = lax.div(self.dp, 4)
        self.zh = lax.div(self.ctx, 2)
        self.zl = lax.rem(self.ctx, 2)
        self.rank = self.x * 2 + self.zl
        dpx = self.dp + 2 - 4 * self.x
        ctz = self.ctx + 1 - 2 * self.zl
        x2, z2 = 1 - self.x, 1 - self.zl
        self.peers = (
            ((dpx, self.ctx), x2 * 2 + self.zl),
            ((self.dp, ctz), self.x * 2 + z2),
            ((dpx, ctz), x2 * 2 + z2),
        )
        self.core_peer = (self.dp + 1 - 2 * self.core, self.ctx)
        self.zh_peer = (self.dp, self.ctx + 2 - 4 * self.zh)
        self.others = []
        for k in range(1, count):
            ahead = lax.rem(self.a + k, count)
            behind = lax.rem(self.a + count - k, count)
            self.others.append(((self.dp + (ahead - self.a) * 4, self.ctx), ahead, behind))
        self.moves = self.x != self.zh
        self.swap_peer = (self.dp + (self.zh - self.x) * 2, self.ctx + (self.x - self.zh) * 2)

    def greet(self, weights, swap):
        devices = [d for d, _ in self.peers]
        if weights:
            devices += [self.core_peer, self.zh_peer] + [o[0] for o in self.others]
        barrier = pltpu.get_barrier_semaphore()
        for device in devices:
            pl.semaphore_signal(barrier, inc=1, device_id=device, device_id_type=MESH)
        if swap:

            @pl.when(self.moves)
            def _():
                pl.semaphore_signal(barrier, inc=1, device_id=self.swap_peer, device_id_type=MESH)

        expected = len(devices)
        if swap:
            expected = expected + self.x + self.zh - 2 * self.x * self.zh
        pl.semaphore_wait(barrier, expected)


class Net:
    def __init__(self, place, send, recv, local):
        self.place, self.send, self.recv, self.local = place, send, recv, local
        self.n, self.m = 0, 0
        self.sends = []

    def remote(self, src, dst, device):
        copy = self.prepare(src, dst, device)
        copy.start()
        self.sends.append(copy)
        return copy

    def prepare(self, src, dst, device):
        i = self.n
        self.n += 1
        return pltpu.make_async_remote_copy(
            src_ref=src, dst_ref=dst, send_sem=self.send.at[i], recv_sem=self.recv.at[i],
            device_id=device, device_id_type=MESH,
        )

    def here(self, src, dst):
        i = self.m
        self.m += 1
        copy = pltpu.make_async_copy(src, dst, self.local.at[i])
        copy.start()
        return copy

    def finish(self):
        for copy in self.sends:
            copy.wait_send()


REMOTE_SEMS, LOCAL_SEMS = 128, 64


def sems(count=2):
    n = REMOTE_SEMS * max(1, count // 2)
    return [
        pltpu.SemaphoreType.DMA((n,)),
        pltpu.SemaphoreType.DMA((n,)),
        pltpu.SemaphoreType.DMA((LOCAL_SEMS,)),
    ]


class Swap:
    def __init__(self, net, src, dst):
        self.net, self.src, self.dst = net, src, dst

    def start(self):
        net, place = self.net, self.net.place
        self.copy = net.prepare(self.src, self.dst, place.swap_peer)
        self.stay = pltpu.make_async_copy(self.src, self.dst, net.local.at[net.m])
        net.m += 1

        @pl.when(place.moves)
        def _():
            self.copy.start()

        @pl.when(jnp.logical_not(place.moves))
        def _():
            self.stay.start()

    def wait(self):
        @pl.when(self.net.place.moves)
        def _():
            self.copy.wait_recv()
            self.copy.wait_send()

        @pl.when(jnp.logical_not(self.net.place.moves))
        def _():
            self.stay.wait()


class Share:
    def __init__(self, net, piece, block):
        self.net, self.piece, self.block = net, piece, block

    def start(self):
        net, place = self.net, self.net.place
        mine = self.block.at[place.x, place.zl]
        self.copies = [net.remote(self.piece.at[rank], mine, device) for device, rank in place.peers]
        self.own = net.here(self.piece.at[place.rank], mine)

    def wait(self):
        for copy in self.copies:
            copy.wait_recv()
        self.own.wait()


class Gather:
    def __init__(self, net, block, full, ranks=True, ahead=None):
        self.net, self.block, self.full, self.ranks, self.ahead = net, block, full, ranks, ahead

    def slot(self, a, core, zh):
        if self.ranks:
            return self.full.at[a, :, core, zh, :]
        return self.full.at[a, core, zh]

    def column(self, a, core):
        if self.ranks:
            return self.full.at[a, :, core, :, :]
        return self.full.at[a, core]

    def begin(self):
        net, p = self.net, self.net.place
        mine = self.slot(p.a, p.core, p.zh)
        self.own = [net.here(self.block, mine)]
        self.cores = [net.remote(self.block, mine, p.core_peer)]
        if self.ahead is None:
            self.across = net.remote(self.block, mine, p.zh_peer)
            self.near = [net.remote(self.block, mine, o[0]) for o in p.others]
            return
        got = self.slot(p.a, p.core, 1 - p.zh)
        self.far = [net.remote(self.ahead.at[0], got, o[0]) for o in p.others]
        self.cores.append(net.remote(self.ahead.at[0], got, p.core_peer))
        self.own.append(net.here(self.ahead.at[0], got))
        for k, other in enumerate(p.others):
            self.own.append(net.here(self.ahead.at[k + 1], self.slot(other[2], p.core, p.zh)))

    def middle(self):
        net, p = self.net, self.net.place
        self.across.wait_recv()
        got = self.slot(p.a, p.core, 1 - p.zh)
        self.far = [net.remote(got, got, o[0]) for o in p.others]
        self.cores.append(net.remote(got, got, p.core_peer))

    def final(self):
        net, p = self.net, self.net.place
        for copy in self.own:
            copy.wait()
        for k, other in enumerate(p.others):
            if self.ahead is None:
                self.near[k].wait_recv()
            self.far[k].wait_recv()
            got = self.column(other[2], p.core)
            self.cores.append(net.remote(got, got, p.core_peer))

    def done(self):
        for copy in self.cores:
            copy.wait_recv()


class Ahead:
    def __init__(self, net, block, got):
        self.net, self.block, self.got = net, block, got

    def begin(self):
        net, p = self.net, self.net.place
        self.copies = [net.remote(self.block, self.got.at[0], p.zh_peer)]
        self.copies += [net.remote(self.block, self.got.at[k + 1], o[0]) for k, o in enumerate(p.others)]

    def done(self):
        for copy in self.copies:
            copy.wait_recv()


class Reduce:
    def __init__(self, net, part, out, held, from_core, from_a, from_zh, from_rank, ranks=True, added=False):
        self.net, self.part, self.out = net, part, out
        self.held, self.from_core, self.from_a = held, from_core, from_a
        self.from_zh, self.from_rank = from_zh, from_rank
        self.ranks, self.added = ranks, added

    def half(self, core):
        return self.part.at[:, :, core] if self.ranks else self.part.at[:, core]

    def begin(self):
        net, p = self.net, self.net.place
        self.load = net.here(self.half(p.core), self.held)
        self.by_core = net.remote(self.half(1 - p.core), self.from_core, p.core_peer)

    def along_a(self):
        net, p = self.net, self.net.place
        self.load.wait()
        self.by_core.wait_recv()
        add_into(self.held, self.from_core)
        self.by_a = [
            net.remote(self.held.at[other[1]], self.from_a.at[k], other[0])
            for k, other in enumerate(p.others)
        ]

    def along_zh(self):
        net, p = self.net, self.net.place
        mine = self.held.at[p.a]
        for k, copy in enumerate(self.by_a):
            copy.wait_recv()
            add_into(mine, self.from_a.at[k])
        there = mine.at[:, 1 - p.zh] if self.ranks else mine.at[1 - p.zh]
        self.by_zh = net.remote(there, self.from_zh, p.zh_peer)

    def among_ranks(self):
        net, p = self.net, self.net.place
        self.by_zh.wait_recv()
        if not self.ranks:
            total = self.held[p.a, p.zh].astype(F32) + self.from_zh[...].astype(F32)
            self.out[...] = total.astype(self.out.dtype)
            return
        for x in range(2):
            for zl in range(2):
                add_into(self.held.at[p.a, x, p.zh, zl], self.from_zh.at[x, zl])
        self.by_rank = []
        for device, rank in p.peers:
            rank_x, rank_zl = lax.div(rank, 2), lax.rem(rank, 2)
            self.by_rank.append(
                net.remote(
                    self.held.at[p.a, rank_x, p.zh, rank_zl], self.from_rank.at[len(self.by_rank)], device
                )
            )

    def done(self):
        if not self.ranks:
            return
        p = self.net.place
        own = self.held[p.a, p.x, p.zh, p.zl].astype(F32)
        for copy in self.by_rank:
            copy.wait_recv()
        if self.added:
            for j in range(3):
                own = own + self.from_rank[j].astype(F32)
            self.out[...] = own
            return
        self.out[p.rank] = own.astype(self.out.dtype)
        for j, (_, rank) in enumerate(p.peers):
            self.out[rank] = self.from_rank[j].astype(self.out.dtype)

    @staticmethod
    def scratch(shape, ranks=True):
        tail = shape[-2:]
        count = shape[0]
        inner = ((2, 2, 2) if ranks else (2,)) + tail
        fewer = ((2, 2) if ranks else ()) + tail
        shapes = [(count,) + inner, (count,) + inner, (max(count - 1, 1),) + inner, fewer]
        if ranks:
            shapes.append((3,) + tail)
        return [pltpu.VMEM(s, BF16) for s in shapes]


def add_into(target, source):
    lead = target.shape[:-2]
    total = 1
    for size in lead:
        total *= size
    if total == 1 and not lead:
        target[...] = (target[...].astype(F32) + source[...].astype(F32)).astype(BF16)
        return

    @pl.loop(0, total)
    def _(j):
        index, left = [], j
        for size in reversed(lead):
            index.append(lax.rem(left, size))
            left = lax.div(left, size)
        index = tuple(reversed(index))
        target[index] = (target[index].astype(F32) + source[index].astype(F32)).astype(BF16)


class Spread:
    def __init__(self, net, land):
        self.net, self.land = net, land
        self.peers = net.place.peers
        mine = land.at[net.place.rank]
        self.along_x = net.remote(mine, mine, self.peers[0][0])
        self.along_zl = net.remote(mine, mine, self.peers[1][0])

    def arrivals(self):
        self.along_zl.wait_recv()
        got = self.land.at[self.peers[1][1]]
        relay = self.net.remote(got, got, self.peers[0][0])
        yield 1, self.peers[1][1]
        self.along_x.wait_recv()
        yield 0, self.peers[0][1]
        relay.wait_recv()
        yield 2, self.peers[2][1]

    def wait(self):
        for _ in self.arrivals():
            pass


class Sum:
    def __init__(self, net, out, land):
        self.net, self.out, self.land = net, out, land
        self.peers = net.place.peers

    def ready(self, i):
        if i == 2:
            self.diagonal = self.net.remote(self.out.at[2], self.land.at[0], self.peers[0][0])
        elif i == 0:
            self.along_x = self.net.remote(self.out.at[0], self.land.at[1], self.peers[0][0])

    def forward(self):
        self.diagonal.wait_recv()
        add_into(self.out.at[1], self.land.at[0])
        self.along_zl = self.net.remote(self.out.at[1], self.land.at[2], self.peers[1][0])

    def result(self, own):
        self.along_x.wait_recv()
        self.along_zl.wait_recv()
        return own + self.land[1].astype(F32) + self.land[2].astype(F32)


class EvenSpread:
    def __init__(self, net, land):
        self.net, self.land = net, land
        self.peers = net.place.peers
        self.half = land.shape[1] // 2
        me = net.place.rank
        self.x_high = self.go(me, 1, 0)
        self.z_low = self.go(me, 0, 1)
        self.x_low = self.go(me, 0, 0)
        self.z_high = self.go(me, 1, 1)

    def go(self, rank, part, i):
        rows = self.land.at[rank, pl.ds(part * self.half, self.half)]
        return self.net.remote(rows, rows, self.peers[i][0])

    def arrivals(self):
        self.x_high.wait_recv()
        on_z = self.go(self.peers[0][1], 1, 1)
        self.z_low.wait_recv()
        on_x = self.go(self.peers[1][1], 0, 0)
        self.x_low.wait_recv()
        yield 0, self.peers[0][1]
        self.z_high.wait_recv()
        yield 1, self.peers[1][1]
        on_z.wait_recv()
        on_x.wait_recv()
        yield 2, self.peers[2][1]

    def wait(self):
        for _ in self.arrivals():
            pass


class EvenSum:
    def __init__(self, net, out, land):
        self.net, self.out, self.land = net, out, land
        self.peers = net.place.peers
        self.half = out.shape[1] // 2

    def go(self, i, part, slot, peer):
        rows = pl.ds(part * self.half, self.half)
        return self.net.remote(self.out.at[i, rows], self.land.at[slot, rows], self.peers[peer][0])

    def ready(self, i):
        if i == 2:
            self.low, self.high = self.go(2, 0, 0, 0), self.go(2, 1, 0, 1)
        elif i == 0:
            self.x_low = self.go(0, 0, 1, 0)
        else:
            self.z_high = self.go(1, 1, 2, 1)

    def forward(self):
        low, high = pl.ds(0, self.half), pl.ds(self.half, self.half)
        self.high.wait_recv()
        add_into(self.out.at[0, high], self.land.at[0, high])
        self.x_high = self.go(0, 1, 1, 0)
        self.low.wait_recv()
        add_into(self.out.at[1, low], self.land.at[0, low])
        self.z_low = self.go(1, 0, 2, 1)

    def result(self, own):
        for copy in (self.x_low, self.x_high, self.z_low, self.z_high):
            copy.wait_recv()
        return own + self.land[1].astype(F32) + self.land[2].astype(F32)


def products(x, w_ref, count, tile, transposed, use):
    def part(cols):
        if transposed:
            w, dims = w_ref[cols, :], (((1,), (1,)), ((), ()))
        else:
            w, dims = w_ref[:, cols], (((1,), (0,)), ((), ()))
        use(cols, lax.dot_general(x(), w, dims, preferred_element_type=F32))

    for j in range(count // tile):
        part(pl.ds(j * tile, tile))


def norm_rows(h, gain):
    factor = lax.rsqrt(jnp.mean(h * h, axis=-1, keepdims=True) + NORM_EPS)
    return (h * factor * gain).astype(BF16)


def norm_rows_back(h, gain, grad):
    factor = lax.rsqrt(jnp.mean(h * h, axis=-1, keepdims=True) + NORM_EPS)
    z = grad * gain
    inner = jnp.sum(z * h, axis=-1, keepdims=True)
    back = factor * z - h * (factor * factor * factor * inner / h.shape[-1])
    return back, jnp.sum(grad * h * factor, axis=0, keepdims=True)


def rows_of(rank, rows):
    return pl.ds(pl.multiple_of(rank * rows, rows), rows)


class Refs:
    def __init__(self, refs):
        self.refs = list(refs)

    def take(self, n):
        got, self.refs = self.refs[:n], self.refs[n:]
        return got


class Ticks:
    def __init__(self, plan):
        self.plan = list(plan)

    def __call__(self):
        if self.plan:
            for step in self.plan.pop(0):
                step()

    def rest(self):
        while self.plan:
            self()


def np_tables(length):
    steps = np.arange(HEAD_DIM // 2, dtype=np.float32)
    inverse = np.exp(steps * np.float32(-2.0 * np.log(ROPE_BASE) / HEAD_DIM)).astype(np.float32)
    angles = np.arange(length, dtype=np.float32)[:, None] * inverse[None, :]
    return np.cos(angles), np.sin(angles)


def wide_tables(length):
    cosine, sine = np_tables(length)
    turned = (HEADS + KV_HEADS) // RANKS
    still = KV_HEADS // RANKS * HEAD_DIM
    cos_all = np.concatenate([cosine] * (2 * turned) + [np.ones((length, still))], axis=1)
    sin_all = np.concatenate([-sine, sine] * turned + [np.zeros((length, still))], axis=1)
    return jnp.asarray(cos_all, F32), jnp.asarray(sin_all, F32)


def turn(values, cosine, sine):
    cols = values.shape[1]
    half = HEAD_DIM // 2
    lane = lax.broadcasted_iota(jnp.int32, values.shape, 1)
    other = jnp.where(
        lax.rem(lane, HEAD_DIM) < half,
        pltpu.roll(values, cols - half, 1),
        pltpu.roll(values, half, 1),
    )
    return values * cosine + other * sine


def head_window(values, h):
    offset = HEAD_DIM * h
    start = offset // 128 * 128
    size = 128 if offset - start + HEAD_DIM <= 128 else 256
    window = values[:, start : start + size]
    if offset > start:
        window = pltpu.roll(window, size - (offset - start), 1)
    window = window[:, :128]
    lane = lax.broadcasted_iota(jnp.int32, window.shape, 1)
    return jnp.where(lane < HEAD_DIM, window, 0.0)


def heads_joined(parts):
    rows = parts[0].shape[0]
    columns = [jnp.zeros((rows, 128), F32) for _ in range(len(parts) * HEAD_DIM // 128 + 1)]
    for h, part in enumerate(parts):
        offset = HEAD_DIM * h
        first = offset // 128
        shift = offset - first * 128
        if shift == 0:
            columns[first] = columns[first] + part
            continue
        double = jnp.concatenate([part, jnp.zeros((rows, 128), F32)], axis=1)
        double = pltpu.roll(double, shift, 1)
        columns[first] = columns[first] + double[:, :128]
        columns[first + 1] = columns[first + 1] + double[:, 128:]
    return jnp.concatenate(columns[:-1], axis=1)


def project_heads(rows, n1, wq, cos_ref, sin_ref, heads):
    count = heads.shape[0]

    @pl.loop(0, RANKS)
    def _(b):
        span = rows_of(b, rows)
        y = jnp.dot(n1[b], wq[...], preferred_element_type=F32)
        y = turn(y, cos_ref[span, :], sin_ref[span, :])
        for h in range(count):
            heads[h, span, :] = head_window(y, h).astype(BF16)


def causal_scores(rows, rank, query, key):
    scores = lax.dot_general(query, key, (((1,), (1,)), ((), ())), preferred_element_type=F32)
    row = lax.broadcasted_iota(jnp.int32, scores.shape, 0) + rank * rows
    col = lax.broadcasted_iota(jnp.int32, scores.shape, 1)
    return jnp.where(col <= row, scores * HEAD_DIM ** (-0.5), MASKED)


def attend_rows(rows, rank, heads, o_ref, lse_ref):
    span = rows_of(rank, rows)
    queries = HEADS // RANKS
    pairs = KV_HEADS // RANKS
    groups = HEADS // KV_HEADS
    mixed = []
    lane = lax.broadcasted_iota(jnp.int32, (rows, 128), 1)
    lse_all = jnp.zeros((rows, 128), F32)
    for h in range(queries):
        kv = h // groups
        scores = causal_scores(rows, rank, heads[h, span, :], heads[queries + kv])
        highest = jnp.max(scores, axis=-1, keepdims=True)
        weights = jnp.exp(scores - highest)
        total = jnp.sum(weights, axis=-1, keepdims=True)
        lse = highest + jnp.log(total)
        lse_all = jnp.where(lane == h, lse, lse_all)
        weights = (weights * (1.0 / total)).astype(BF16)
        mixed.append(
            jnp.dot(weights, heads[queries + pairs + kv], preferred_element_type=F32)
        )
    lse_ref[span, :] = lse_all
    o_ref[span, :] = heads_joined(mixed).astype(BF16)


def window_tables(length):
    cosine, sine = np_tables(length)
    none = np.zeros((length, 128 - HEAD_DIM))
    cos_one = np.concatenate([cosine, cosine, none], axis=1)
    sin_one = np.concatenate([-sine, sine, none], axis=1)
    return jnp.asarray(cos_one, F32), jnp.asarray(sin_one, F32)


def turn_window(values, cosine, sine):
    half = HEAD_DIM // 2
    lane = lax.broadcasted_iota(jnp.int32, values.shape, 1)
    other = jnp.where(lane < half, pltpu.roll(values, 128 - half, 1), pltpu.roll(values, half, 1))
    return values * cosine + other * sine


def dot_tn(a, b):
    return lax.dot_general(a, b, (((0,), (0,)), ((), ())), preferred_element_type=F32)


def attend_rows_back(rows, rank, do_rows, heads, o_ref, lse_ref, cos_ref, sin_ref, dq_ref, dkv):
    span = rows_of(rank, rows)
    queries = HEADS // RANKS
    pairs = KV_HEADS // RANKS
    groups = HEADS // KV_HEADS
    o_rows = o_ref[span, :].astype(F32)
    parts = []
    for h in range(queries):
        kv = h // groups
        do_h = head_window(do_rows, h)
        delta = jnp.sum(do_h * head_window(o_rows, h), axis=-1, keepdims=True)
        do_b = do_h.astype(BF16)
        query, key, value = heads[h, span, :], heads[queries + kv], heads[queries + pairs + kv]
        weights = jnp.exp(causal_scores(rows, rank, query, key) - lse_ref[span, h : h + 1])
        grad_w = lax.dot_general(do_b, value, (((1,), (1,)), ((), ())), preferred_element_type=F32)
        ds = (weights * (grad_w - delta) * HEAD_DIM ** (-0.5)).astype(BF16)
        dq = jnp.dot(ds, key, preferred_element_type=F32)
        parts.append(turn_window(dq, cos_ref[span, :], -sin_ref[span, :]))
        dkv[kv] += dot_tn(ds, query)
        dkv[pairs + kv] += dot_tn(weights.astype(BF16), do_b)
    joined = heads_joined(parts)
    dq_ref[span, pl.ds(0, joined.shape[1])] = joined.astype(BF16)


def close_keys(rows, dkv, cos_ref, sin_ref, dqkv_ref):
    pairs = KV_HEADS // RANKS
    first = HEADS // RANKS * HEAD_DIM

    @pl.loop(0, RANKS)
    def _(b):
        span = rows_of(b, rows)
        parts = [turn_window(dkv[i, span, :], cos_ref[span, :], -sin_ref[span, :]) for i in range(pairs)]
        parts += [dkv[pairs + i, span, :] for i in range(pairs)]
        joined = heads_joined(parts)
        dqkv_ref[span, pl.ds(first, joined.shape[1])] = joined.astype(BF16)


def put_blocks(target, value):
    *lead, rows, cols = target.shape
    if rows % 16 == 0:
        target.reshape(value.shape[0], cols)[...] = value.astype(BF16)
        return
    for block in range(value.shape[0] // rows):
        index, left = [], block
        for size in reversed(lead):
            index.append(left % size)
            left //= size
        target[tuple(reversed(index))] = value[block * rows : (block + 1) * rows].astype(BF16)


def start_kernel(count, n, n_later, n_ahead, *refs):
    refs = Refs(refs)
    (tokens,) = refs.take(1)
    pieces, later = refs.take(n), refs.take(n_later)
    (all_tokens,) = refs.take(1)
    full, blocks_later, got_ahead = refs.take(n), refs.take(n_later), refs.take(n_ahead)
    own_tokens, land = refs.take(2)
    blocks = refs.take(n)
    send, recv, local = refs.take(3)
    place = Place(count)
    net = Net(place, send, recv, local)
    shares = [Share(net, pieces[i], blocks[i]) for i in range(n)]
    shares_later = [Share(net, later[i], blocks_later[i]) for i in range(n_later)]
    gathers = [Gather(net, blocks[i], full[i]) for i in range(n)]
    aheads = [Ahead(net, blocks_later[i], got_ahead[i]) for i in range(n_ahead)]
    swap = Swap(net, tokens, land.at[place.zh * 2 + place.zl])
    place.greet(True, True)
    shares[0].start()
    swap.start()
    for share in shares[1:] + shares_later[:n_ahead]:
        share.start()
    for i in range(2):
        shares[i].wait()
        gathers[i].begin()
    swap.wait()
    spreads = Spread(net, land)
    keep_own = net.here(land.at[place.rank], own_tokens)
    for i in range(2, n):
        shares[i].wait()
        gathers[i].begin()
    for i in range(n_ahead):
        shares_later[i].wait()
        aheads[i].begin()
    arrivals = spreads.arrivals()
    next(arrivals)
    for share in shares_later[n_ahead:]:
        share.start()
    gathers[0].middle()
    gathers[1].middle()
    for _ in arrivals:
        pass
    keep = net.here(land, all_tokens)
    gathers[0].final()
    for i in range(2, n):
        gathers[i].middle()
        gathers[i - 1].final()
    gathers[-1].final()
    for gather in gathers + aheads:
        gather.done()
    for share in shares_later[n_ahead:]:
        share.wait()
    keep_own.wait()
    keep.wait()
    net.finish()


def body_kernel(count, rows, late, started, n_next, n_ahead, plan, *refs):
    refs = Refs(refs)
    n1_hbm, wq_hbm, cos_ref, sin_ref, h_ref, gain_ref, wo_hbm = refs.take(7)
    inner_hbm = refs.take(3)
    ahead_hbm = [refs.take(1)[0] if started[i] else None for i in range(3)]
    if n_next:
        (gain_next,) = refs.take(1)
        blocks = refs.take(n_next)
    else:
        (swap_src,) = refs.take(1)
    early_out = refs.take(6)
    h1_ref, hn_ref, hb_ref, ng_hbm = refs.take(4)
    late_out = [refs.take(1)[0] if late[i] else None for i in range(3)]
    if n_next:
        (nn_hbm,) = refs.take(1)
        full = refs.take(n_next)
    else:
        (swap_dst,) = refs.take(1)
    early = refs.take(6)
    heads, o_ref, lse_ref, gate_ref, up_ref, u_ref = early
    n1, wq, wo = refs.take(3)
    inner = refs.take(3)
    out_a, land_a, land_n, out_b, land_b = refs.take(5)
    if n_next:
        (land_q,) = refs.take(1)
    send, recv, local = refs.take(3)

    place = Place(count)
    net = Net(place, send, recv, local)
    width = h_ref.shape[1]
    hidden = u_ref.shape[1]
    load_q = net.here(wq_hbm.at[:, pl.ds(0, wq.shape[1])], wq)
    load_n = net.here(n1_hbm, n1)
    load_out = net.here(wo_hbm, wo)
    jobs = {}
    loads, weights = [], []
    for i in range(3):
        if late[i]:
            jobs[("gate", "up", "down")[i]] = Gather(net, inner_hbm[i], inner[i], i < 2, ahead_hbm[i])
            loads.append(None)
        else:
            loads.append(net.here(inner_hbm[i], inner[i]))
        weights.append(inner[i].reshape((hidden, width) if i == 2 else (width, hidden)) if late[i] else inner[i])
    wg, wu, wd = weights
    for i in range(n_next):
        jobs[i] = (Ahead if i >= n_next - n_ahead else Gather)(net, blocks[i], full[i])
    if not n_next:
        jobs["swap"] = Swap(net, swap_src, swap_dst)
    peers = place.peers
    place.greet(True, not n_next)
    keeps = []

    def ready(i):
        if late[i]:
            jobs[("gate", "up", "down")[i]].done()
            keeps.append(net.here(inner[i], late_out[i]))
        else:
            loads[i].wait()

    tick = Ticks(plan(jobs))
    tick()

    load_q.wait()
    load_n.wait()
    project_heads(rows, n1, wq, cos_ref, sin_ref, heads)
    load_out.wait()
    sums = EvenSum(net, out_a, land_a)
    for i in (2, 0, 1):
        attend_rows(rows, peers[i][1], heads, o_ref, lse_ref)
        span = rows_of(peers[i][1], rows)

        def use(cols, y, i=i):
            out_a[i, :, cols] = y.astype(BF16)

        products(lambda: o_ref[span, :], wo, width, width, True, use)
        sums.ready(i)
    attend_rows(rows, place.rank, heads, o_ref, lse_ref)
    span = rows_of(place.rank, rows)

    def use_own(cols, y):
        h1_ref[:, cols] = h_ref[:, cols].astype(F32) + y

    products(lambda: o_ref[span, :], wo, width, width, True, use_own)
    sums.forward()
    tick()
    h1 = sums.result(h1_ref[...])
    h1_ref[...] = h1
    land_n[place.rank] = norm_rows(h1, gain_ref[...])
    gather = EvenSpread(net, land_n)
    tick()
    ready(0)
    ready(1)

    def inner_block(rank):
        span = rows_of(rank, rows)

        gate = jnp.dot(land_n[rank], wg[...], preferred_element_type=F32)
        up = jnp.dot(land_n[rank], wu[...], preferred_element_type=F32)
        gate_ref[span, :] = gate.astype(BF16)
        up_ref[span, :] = up.astype(BF16)
        u_ref[span, :] = (gate / (1.0 + jnp.exp(-gate)) * up).astype(BF16)

        return span

    inner_block(place.rank)
    tick()
    second = EvenSum(net, out_b, land_b)
    got_down = False
    for i, rank in gather.arrivals():
        span = inner_block(rank)
        if not got_down:
            tick()
            ready(2)
            got_down = True

        def use(cols, y, i=i):
            out_b[i, :, cols] = y.astype(BF16)

        products(lambda: u_ref[span, :], wd, width, width, False, use)
        second.ready(i)
        tick()
    keep = net.here(land_n, ng_hbm)
    for ref, out in zip(early, early_out):
        keeps.append(net.here(ref, out))
    span = rows_of(place.rank, rows)

    def use_down(cols, y):
        hn_ref[:, cols] = h1_ref[:, cols] + y

    products(lambda: u_ref[span, :], wd, width, width, False, use_down)
    second.forward()
    tick()
    hn = second.result(hn_ref[...])
    hn_ref[...] = hn
    hb_ref[...] = hn.astype(BF16)
    if n_next:
        land_q[place.rank] = norm_rows(hn, gain_next[...])
        third = EvenSpread(net, land_q)
        tick()
        for _ in third.arrivals():
            tick()
        keep_next = net.here(land_q, nn_hbm)
        keep_next.wait()
    tick.rest()
    for i in range(n_next):
        jobs[i].done()
    if not n_next:
        jobs["swap"].wait()
    keep.wait()
    for copy in keeps:
        copy.wait()
    net.finish()


def plan_late(j):
    gate, up, down = j["gate"], j["up"], j["down"]
    return [
        [gate.begin, up.begin],
        [gate.middle, down.begin],
        [up.final, gate.final],
        [down.middle, j[0].begin, j[1].begin],
        [down.final],
        [],
        [],
        [j[0].middle],
        [j[0].final, j[1].middle],
        [j[2].begin, j[1].final],
    ]


def plan_late_end(j):
    gate, up, down = j["gate"], j["up"], j["down"]
    return [
        [up.begin, gate.begin],
        [up.middle, down.begin],
        [gate.final, up.final],
        [down.middle],
        [down.final],
        [],
        [],
        [j["swap"].start],
    ]


def plan_early(j):
    down = j["down"]
    return [
        [down.begin],
        [down.middle, j[0].begin],
        [],
        [down.final, j[1].begin, j[2].begin],
        [j[0].middle],
        [],
        [],
        [j[0].final],
        [j[1].middle, j[2].middle],
        [j[3].begin, j[1].final, j[2].final],
        [],
        [],
        [j[3].middle],
        [j[3].final],
    ]


def plan_end(j):
    down = j["down"]
    return [
        [down.begin],
        [],
        [down.middle],
        [],
        [down.final],
        [],
        [],
        [j["swap"].start],
    ]


class Back:
    def __init__(self, net, rows):
        self.net, self.place, self.rows = net, net.place, rows
        self.peers = net.place.peers

    def enter(self, r, tick):
        rows, place = self.rows, self.place
        width = r["gnew"].shape[1]
        total = EvenSum(self.net, r["out_a"], r["land_a"])
        for i in (2, 0, 1):
            span = rows_of(self.peers[i][1], rows)

            def use(cols, y, i=i):
                r["out_a"][i, :, cols] = y.astype(BF16)

            products(lambda: r["dqkv"][span, :], r["wq"], width, width, True, use)
            total.ready(i)
        tick()
        own = rows_of(place.rank, rows)

        def use_own(cols, y):
            r["gnew"][:, cols] = y

        products(lambda: r["dqkv"][own, :], r["wq"], width, width, True, use_own)
        total.forward()
        tick()
        dn = total.result(r["gnew"][...])
        back, ggain = norm_rows_back(r["hin"][...].astype(F32), r["gain_in"][...], dn)
        r["gnew"][...] = r["ghin"][...] + back
        return ggain

    def feed_forward(self, r, tick, ready, between):
        net, rows, place = self.net, self.rows, self.place
        land_g, dgu, out_b = r["land_g"], r["dgu"], r["out_b"]
        width = land_g.shape[2]
        hidden = r["gate"].shape[1]
        land_g[place.rank] = r["g"][...].astype(BF16)
        gather = EvenSpread(net, land_g)
        tick()
        ready()

        def inner_block(rank):
            span = rows_of(rank, rows)
            du = lax.dot_general(
                land_g[rank], r["wd"][...], (((1,), (1,)), ((), ())), preferred_element_type=F32
            )
            gate, up = r["gate"][span, :].astype(F32), r["up"][span, :].astype(F32)
            sg = 1.0 / (1.0 + jnp.exp(-gate))
            dgu[span, pl.ds(0, hidden)] = (du * up * sg * (1.0 + gate * (1.0 - sg))).astype(BF16)
            dgu[span, pl.ds(hidden, hidden)] = (du * gate * sg).astype(BF16)
            return span

        span = inner_block(place.rank)

        def use_mid(cols, y):
            r["gh"][:, cols] = y

        products(lambda: dgu[span, :], r["wgu"], width, width, True, use_mid)
        tick()
        second = EvenSum(net, out_b, r["land_b"])
        for i, rank in gather.arrivals():
            span = inner_block(rank)

            def use(cols, y, i=i):
                out_b[i, :, cols] = y.astype(BF16)

            products(lambda: dgu[span, :], r["wgu"], width, width, True, use)
            second.ready(i)
            tick()
        second.forward()
        tick()
        between()
        tick()
        dn = second.result(r["gh"][...])
        back, ggain = norm_rows_back(r["h1"][...], r["gain"][...], dn)
        r["gh"][...] = r["g"][...].astype(F32) + back
        r["gg"][...] = ggain

    def weight_grads(self, r, down_made):
        net = self.net
        buffers, copies = r["buffers"], []
        tile = buffers.shape[1]
        tall, hidden = r["u"].shape
        width = r["land_g"].shape[2]
        g_all = r["land_g"][...].reshape(tall, width)

        def emit(lhs, rhs, outs, m):
            slot = len(copies) % 2
            if len(copies) >= 2:
                for copy in copies[-2]:
                    copy.wait()
            buffers[slot, :, pl.ds(0, rhs.shape[1])] = dot_tn(lhs, rhs).astype(BF16)
            cols = rhs.shape[1] // len(outs)
            copies.append([
                net.here(buffers.at[slot, :, pl.ds(k * cols, cols)], out.at[pl.ds(m * tile, tile)])
                for k, out in enumerate(outs)
            ])

        for k, part in enumerate((r["part_da"], r["part_db"])):
            cols = part.shape[-1]
            made = dot_tn(r["u"][...], g_all[:, k * cols : (k + 1) * cols])
            part.reshape(hidden, cols)[...] = made.astype(BF16)
        down_made()
        for m in range(width // tile):
            emit(r["n2"][:, m * tile : (m + 1) * tile], r["dgu"][...], [r[name] for name in INNER_GRADS], m)
        return copies[-2] + copies[-1]

    def attention(self, r, tick, ready):
        net, rows, place = self.net, self.rows, self.place
        land_h = r["land_h"]
        land_h[place.rank] = r["gh"][...].astype(BF16)
        gather = EvenSpread(net, land_h)
        tick()
        ready()
        r["dkv"][...] = jnp.zeros(r["dkv"].shape, F32)

        def block(rank):
            do_rows = jnp.dot(land_h[rank], r["wo"][...], preferred_element_type=F32)
            do_rows = do_rows.astype(BF16).astype(F32)
            attend_rows_back(
                rows, rank, do_rows, r["heads"], r["o"], r["lse"], r["cos"], r["sin"], r["dqkv"], r["dkv"]
            )

        block(place.rank)
        tick()
        for _, rank in gather.arrivals():
            block(rank)
            tick()
        close_keys(rows, r["dkv"], r["cos"], r["sin"], r["dqkv"])


INNER_GRADS = ("g_gate_a", "g_gate_b", "g_up_a", "g_up_b")


def back_kernel(count, rows, names, out_names, scratch_names, n_parts, kinds, plan, *refs):
    refs = Refs(refs)
    r = dict(zip(names, refs.take(len(names))))
    parts = refs.take(n_parts)
    r.update(zip(out_names, refs.take(len(out_names))))
    red_out = refs.take(len(kinds))
    r.update(zip(scratch_names, refs.take(len(scratch_names))))
    red_scratch = [refs.take(5 if ranks else 4) for ranks in kinds]
    gains_scratch = refs.take(5) if "gains_out" in r else None
    send, recv, local = refs.take(3)

    place = Place(count)
    net = Net(place, send, recv, local)
    back = Back(net, rows)
    entering, inner, attention = "hin" in r, "h1" in r, "heads_hbm" in r
    last = "gains_out" in r
    waits = {}

    def load(name, source, target):
        waits[name] = net.here(source, target)

    parts = parts + ([r["part_o"], r["part_q"]] if last else [r["part_da"], r["part_db"]])
    jobs = []
    for part, out, scratch, ranks in zip(parts, red_out, red_scratch, kinds):
        jobs.append(Reduce(net, part, out, *scratch, *([] if ranks else [None]), ranks=ranks))
    if entering:
        load("wq", r["wq_hbm"].at[:, pl.ds(0, r["wq"].shape[1])], r["wq"])
    if inner:
        hidden = r["wd"].shape[0]
        load("wd", r["wd_hbm"], r["wd"])
        load("wg", r["wgate_hbm"], r["wgu"].at[:, pl.ds(0, hidden)])
        load("wu", r["wup_hbm"], r["wgu"].at[:, pl.ds(hidden, hidden)])
        load("u", r["u_hbm"], r["u"])
        load("n2", r["n2_hbm"], r["n2"])
    if attention:
        for name in ("wo", "heads", "o", "lse", "n1"):
            load(name, r[name + "_hbm"], r[name])
    place.greet(len(jobs) > 0, "swap_src" in r or last)
    if "swap_src" in r:
        jobs.append(Swap(net, r["swap_src"], r["swap_dst"]))
    tick = Ticks(plan(jobs))
    tick()
    ends = []

    def ready_inner():
        for name in ("wd", "wg", "wu"):
            waits[name].wait()

    def between():
        waits["u"].wait()
        waits["n2"].wait()
        ends.extend(back.weight_grads(r, tick))

    def ready_attention():
        for name in ("wo", "heads", "o", "lse"):
            waits[name].wait()

    if entering and inner:
        waits["wq"].wait()
        r["ggin"][...] = back.enter(r, tick)
        r["g"] = r["gnew"]
    if inner:
        back.feed_forward(r, tick, ready_inner, between)
    if attention:
        back.attention(r, tick, ready_attention)
        waits["n1"].wait()
        width = r["land_h"].shape[2]
        tall = r["o"].shape[0]

        def grad_out():
            return dot_tn(r["land_h"][...].reshape(tall, width), r["o"][...])

        def grad_qkv():
            return dot_tn(r["n1"][...].reshape(tall, width), r["dqkv"][...])

        if not last:
            r["g_out"][...] = grad_out().astype(BF16)
            r["g_qkv"][...] = grad_qkv().astype(BF16)
        else:
            waits["wq"].wait()
            made = Ticks([
                [],
                [lambda: put_blocks(r["part_q"], grad_qkv()), lambda: put_blocks(r["part_o"], grad_out())],
            ])

            def both():
                made()
                tick()

            ggain = back.enter(r, both)
            finish_last(net, r, jobs, ggain, gains_scratch)
            for copy in ends:
                copy.wait()
            net.finish()
            return
    tick.rest()
    if "swap_src" in r:
        jobs[-1].wait()
    for copy in ends:
        copy.wait()
    net.finish()


def finish_last(net, r, jobs, ggain, scratch):
    r["gsend"][...] = r["gnew"][...].astype(BF16)
    swap = Swap(net, r["gsend"], r["swap_dst"])
    gains_all, gains_part = r["gains_all"], r["gains_part"]
    gains_all[...] = r["other_gains"][...]
    gains_all[0:1, :] = ggain
    gains_part[...] = jnp.zeros(gains_part.shape, BF16)
    count = gains_part.shape[0]
    piece = gains_all.shape[1] // (16 * count)
    for block in range(16 * count):
        index = (block // 16, block // 8 % 2, block // 4 % 2, block // 2 % 2, block % 2)
        gains_part[index + (slice(None), slice(0, piece))] = gains_all[
            :, block * piece : (block + 1) * piece
        ].astype(BF16)
    small = Reduce(net, gains_part, r["gains_out"], *scratch, added=True)
    small.begin()
    for step in plan_finish(jobs, small, swap):
        step()
    swap.wait()


def plan_finish(j, s, swap):
    ga, gb, ua, ub, out, qkv = j
    return [
        s.along_a, ub.along_zh, out.along_a, qkv.along_a, ga.among_ranks, s.along_zh, out.along_zh, gb.among_ranks,
        s.among_ranks, ua.among_ranks, swap.start, ub.among_ranks, ga.done, qkv.along_zh, gb.done, out.among_ranks,
        s.done, ua.done, ub.done, out.done, qkv.among_ranks, qkv.done,
    ]


def plan_first(j):
    da, db, swap = j
    return [
        [],
        [],
        [],
        [],
        [],
        [],
        [swap.start],
        [da.begin, db.begin],
        [da.along_a],
        [db.along_a],
        [],
        [da.along_zh],
        [db.along_zh],
        [],
        [da.among_ranks, db.among_ranks],
    ]


def plan_middle(j):
    ga, gb, ua, ub, out, qkv, da, db = j
    return [
        [ga.begin, gb.begin, ua.begin, ub.begin, out.begin, qkv.begin],
        [ga.along_a],
        [gb.along_a, ga.along_zh],
        [ua.along_a],
        [gb.along_zh],
        [ub.along_a, ua.along_zh],
        [out.along_a],
        [ga.among_ranks],
        [ub.along_zh, qkv.along_a],
        [da.begin, db.begin, gb.among_ranks],
        [out.along_zh, ua.among_ranks, da.along_a],
        [db.along_a, ub.among_ranks, qkv.along_zh, out.among_ranks, ga.done, gb.done, da.along_zh, ua.done, ub.done],
        [qkv.among_ranks, db.along_zh, out.done, qkv.done, da.among_ranks, db.among_ranks],
    ]


def plan_last(j):
    ga, gb, ua, ub, out, qkv = j
    return [
        [ga.begin, gb.begin, ua.begin, ub.begin],
        [ga.along_a],
        [gb.along_a],
        [ga.along_zh, ua.along_a],
        [],
        [gb.along_zh, ub.along_a],
        [],
        [out.begin, qkv.begin, ua.along_zh],
    ]


def pack_weights(w_qkv, w_out, w_gate_up, gains, count, layer):
    rows = w_qkv.shape[1]
    attn_cols = HEADS * HEAD_DIM
    kv_cols = KV_HEADS * HEAD_DIM
    qkv = w_qkv[layer]
    q = qkv[:, :attn_cols].reshape(rows, RANKS, -1)
    k = qkv[:, attn_cols : attn_cols + kv_cols].reshape(rows, RANKS, -1)
    v = qkv[:, attn_cols + kv_cols :].reshape(rows, RANKS, -1)
    columns = [q, k, v]
    if layer == 0:
        scales = jnp.pad(gains.reshape(2 * LAYERS, rows).T, ((0, 0), (0, GAIN_COLS - 2 * LAYERS)))
        columns.append(jnp.broadcast_to(scales[:, None], (rows, RANKS, GAIN_COLS)))
    head = jnp.concatenate(columns, axis=2).transpose(1, 0, 2)
    out = w_out[layer].T.reshape(rows, RANKS, -1).transpose(1, 0, 2)
    gu = w_gate_up[layer].reshape(rows, 2, count, 2, 2, 2, 2, -1)
    gu = gu.transpose(1, 3, 6, 0, 2, 4, 5, 7).reshape(2, RANKS, rows, -1)
    return head, out, gu[0], gu[1]


def unpack_grads(head, out, gate, up, count):
    rows = head.shape[1]
    q_cols = HEADS * HEAD_DIM // RANKS
    kv_cols = KV_HEADS * HEAD_DIM // RANKS
    wide = lambda part: part.transpose(1, 0, 2).reshape(rows, -1)
    qkv = jnp.concatenate(
        [
            wide(head[:, :, :q_cols]),
            wide(head[:, :, q_cols : q_cols + kv_cols]),
            wide(head[:, :, q_cols + kv_cols : q_cols + 2 * kv_cols]),
        ],
        axis=1,
    )
    order = lambda part: (
        part.reshape(2, 2, rows, count, 2, 2, -1).transpose(2, 3, 0, 4, 5, 1, 6).reshape(rows, -1)
    )
    return qkv, wide(out).T, jnp.stack([order(gate), order(up)], axis=1)


VM = pl.BlockSpec(memory_space=pltpu.VMEM)
AN = pl.BlockSpec(memory_space=pl.ANY)


def params(collective_id):
    return pltpu.CompilerParams(
        collective_id=collective_id, has_side_effects=True, vmem_limit_bytes=VMEM_BYTES
    )


def like(shape, dtype=BF16):
    return jax.ShapeDtypeStruct(tuple(shape), dtype)


def full_shape(count, tail):
    return (count, 2, 2, 2, 2) + tuple(tail)


def call_start(count, tokens, pieces, later, n_ahead):
    rows, width = tokens.shape
    n, n_later = len(pieces), len(later)
    outs = [like((RANKS, rows, width))]
    outs += [like(full_shape(count, p.shape[1:])) for p in pieces]
    outs += [like((2, 2) + p.shape[1:]) for p in later]
    outs += [like((count, 2, 2) + p.shape[1:]) for p in later[:n_ahead]]
    outs += [like((rows, width))]
    got = pl.pallas_call(
        functools.partial(start_kernel, count, n, n_later, n_ahead),
        out_shape=outs,
        in_specs=[AN] * (1 + n + n_later),
        out_specs=[AN] * len(outs),
        scratch_shapes=[pltpu.VMEM((RANKS, rows, width), BF16)]
        + [pltpu.VMEM((2, 2) + p.shape[1:], BF16) for p in pieces]
        + sems(count),
        compiler_params=params(1),
        name="start",
    )(tokens, *pieces, *later)
    cut = n + 1 + n_later
    return got[0], got[-1], [flat(f) for f in got[1 : n + 1]], got[n + 1 : cut], got[cut:-1]


def flat(value):
    return value.reshape(-1, value.shape[-1])


def call_body(
    count, n1, wq, tables, h, gain, wo, inner, late, ahead, plan, gain_next=None, blocks=(), n_ahead=0, swap=None
):
    started = tuple(value is not None for value in ahead)
    rows, width = h.shape
    tall = RANKS * rows
    hidden = inner[0].shape[-1]
    n_next = len(blocks)
    heads = (HEADS + 2 * KV_HEADS) // RANKS
    cols = heads * HEAD_DIM
    o_cols = HEADS // RANKS * HEAD_DIM
    three = pltpu.VMEM((3, rows, width), BF16)
    four = pltpu.VMEM((RANKS, rows, width), BF16)
    shapes = []
    for i in range(3):
        shape = inner[i].shape
        if late[i]:
            shape = full_shape(count, shape[2:]) if i < 2 else (count, 2, 2) + shape
        shapes.append(shape)
    outs = [
        like((heads, tall, 128)),
        like((tall, o_cols)),
        like((tall, 128), F32),
        like((tall, hidden)),
        like((tall, hidden)),
        like((tall, hidden)),
        like((rows, width), F32),
        like((rows, width), F32),
        like((rows, width)),
        like((RANKS, rows, width)),
    ]
    n_state = len(outs)
    outs += [like(shapes[i]) for i in range(3) if late[i]]
    if n_next:
        outs += [like((RANKS, rows, width))]
        outs += [like(full_shape(count, b.shape[2:])) for b in blocks[: n_next - n_ahead]]
        outs += [like((count,) + b.shape) for b in blocks[n_next - n_ahead :]]
        extra = (gain_next, *blocks)
    else:
        outs += [like(swap.shape)]
        extra = (swap,)
    got = pl.pallas_call(
        functools.partial(body_kernel, count, rows, late, started, n_next, n_ahead, plan),
        out_shape=outs,
        in_specs=[AN, AN, VM, VM, VM, VM, AN, AN, AN, AN]
        + [AN] * sum(started)
        + ([VM] + [AN] * n_next if n_next else [AN]),
        out_specs=[AN] * 6 + [VM] * 3 + [AN] * (len(outs) - n_state + 1),
        scratch_shapes=[pltpu.VMEM(out.shape, out.dtype) for out in outs[:6]]
        + [
            four,
            pltpu.VMEM((width, cols), BF16),
            pltpu.VMEM(wo.shape, BF16),
        ]
        + [pltpu.VMEM(shape, BF16) for shape in shapes]
        + [three, three, four, three, three]
        + ([four] if n_next else [])
        + sems(count),
        compiler_params=params(2 if n_next else 3),
        name="body_more" if n_next else "body",
    )(n1, wq, *tables, h, gain, wo, *inner, *[value for value in ahead if value is not None], *extra)
    got = list(got)
    state, rest = got[:n_state], got[n_state:]
    inner = [flat(rest.pop(0)) if late[i] else inner[i] for i in range(3)]
    rest, last = rest[: len(rest) - n_ahead], rest[len(rest) - n_ahead :]
    return state, inner, rest[0], [flat(f) for f in rest[1:]], last


def call_back(name, count, rows, inputs, outputs, scratch, parts, made, kinds, plan, collective_id):
    shapes = [p.shape for p in parts] + list(made)
    red_out = [like(((RANKS,) if ranks else ()) + shape[-2:]) for shape, ranks in zip(shapes, kinds)]
    scratch_shapes = [pltpu.VMEM(shape, dtype) for shape, dtype in scratch.values()]
    for shape, ranks in zip(shapes, kinds):
        scratch_shapes += Reduce.scratch(shape, ranks=ranks)
    if "gains_out" in outputs:
        scratch_shapes += Reduce.scratch(scratch["gains_part"][0])
    got = pl.pallas_call(
        functools.partial(
            back_kernel, count, rows, tuple(inputs), tuple(outputs), tuple(scratch), len(parts), kinds, plan
        ),
        out_shape=[shape for shape, _ in outputs.values()] + red_out,
        in_specs=[spec for _, spec in inputs.values()] + [AN] * len(parts),
        out_specs=[spec for _, spec in outputs.values()] + [VM] * len(red_out),
        scratch_shapes=scratch_shapes + sems(count),
        compiler_params=params(collective_id),
        name=name,
    )(*[value for value, _ in inputs.values()], *parts)
    return dict(zip(outputs, got)), got[len(outputs) :]


def shards(dp_size, ctx_size, tokens, cotangent, w_qkv, w_out, w_gate_up, w_down, gains):
    count = dp_size // 4
    rows, width = tokens.shape
    length = RANKS * rows
    hidden = w_gate_up.shape[-1] // RANKS
    tall = lambda value: value.reshape(length, width)

    swap = lambda value: lax.ppermute(value, ("dp", "ctx"), swap_pairs(dp_size, ctx_size))
    tie = lax.optimization_barrier

    tables = wide_tables(length)
    windows = window_tables(length)

    packed = [pack_weights(w_qkv, w_out, w_gate_up, gains, count, layer) for layer in range(LAYERS)]
    whole_rows = w_qkv.shape[1] % 16 == 0
    none = (None, None, None)
    if whole_rows:
        head, out, gate, up = packed[0]
        now, later, n_ahead = (head, out), (up, gate, *packed[1]), 1
    else:
        now, later, n_ahead = packed[0], packed[1], 0
    all_tokens, h, full, blocks, ahead = call_start(count, tokens, now, later, n_ahead)
    gain_rows = full[0][:, -GAIN_COLS:][:, : 2 * LAYERS].astype(F32).T
    gain = lambda layer, which: gain_rows[2 * layer + which][None]
    n1 = norm_rows(all_tokens.astype(F32), gain(0, 0))
    if whole_rows:
        up, gate, *blocks, last_up = blocks
        inner, late, ahead, plan = (gate, up, w_down[0]), (True, True, True), (None, ahead[0], None), plan_late
    else:
        inner, late, ahead, plan = (*full[2:], w_down[0]), (False, False, True), none, plan_early

    records = []
    for layer in range(LAYERS):
        wq, wo = full[:2]
        if layer + 1 < LAYERS:
            state, inner, n1_next, full, last_got = call_body(
                count, n1, wq, tables, h, gain(layer, 1), wo, inner, late, ahead, plan,
                gain(layer + 1, 0), blocks, n_ahead,
            )
            if whole_rows:
                late, ahead, plan = (True, True, True), (last_got[0], None, None), plan_late_end
                next_inner = (blocks[-1], last_up, w_down[layer + 1])
            else:
                late, plan = (False, False, True), plan_end
                next_inner = (*full[2:], w_down[layer + 1])
        else:
            state, inner, g, _, _ = call_body(
                count, n1, wq, tables, h, gain(layer, 1), wo, inner, late, ahead, plan,
                swap=cotangent.astype(BF16),
            )
            n1_next = None
        heads, mixed, lse, gate, up, u, h1, h_next, h_round, n2 = state
        records.append(dict(
            hin=h, n1=n1, heads=heads, o=mixed, lse=lse, h1=h1, n2=tall(n2), gate=gate, up=up, u=u,
            wq=wq, wo=wo, wgate=inner[0], wup=inner[1], wd=inner[2],
        ))
        h, n1, inner = h_next, n1_next, next_inner

    hidden = records[0]["u"].shape[1]
    heads = (HEADS + 2 * KV_HEADS) // RANKS
    cols = heads * HEAD_DIM
    o_cols = HEADS // RANKS * HEAD_DIM
    shape7 = lambda value: value.reshape(count, 2, 2, 2, 2, -1, value.shape[-1])
    three, four = ((3, rows, width), BF16), ((RANKS, rows, width), BF16)
    row_f32 = ((rows, width), F32)

    def inner_in(layer):
        rec = records[layer]
        names = dict(wd="wd", wgate="wgate", wup="wup", u="u", n2="n2")
        values = {key + "_hbm": (rec[name], AN) for key, name in names.items()}
        return dict(
            values, gate=(rec["gate"], VM), up=(rec["up"], VM), h1=(rec["h1"], VM), gain=(gain(layer, 1), VM)
        )

    inner_out = dict(
        gh=(like((rows, width), F32), VM),
        gg=(like((1, width), F32), VM),
        **{name: (like((width, hidden // 2)), AN) for name in INNER_GRADS},
    )
    shape_d = (count, 2, 2, w_down.shape[1], width // 2)
    inner_scratch = dict(
        part_da=(shape_d, BF16),
        part_db=(shape_d, BF16),
        wd=((hidden, width), BF16),
        wgu=((width, 2 * hidden), BF16),
        u=((length, hidden), BF16),
        n2=((length, width), BF16),
        dgu=((length, 2 * hidden), BF16),
        buffers=((2, 256, 2 * hidden), BF16),
        land_g=four,
        out_b=three,
        land_b=three,
    )

    def attention_in(layer):
        rec = records[layer]
        values = {name + "_hbm": (rec[name], AN) for name in ("wo", "heads", "o", "lse", "n1")}
        return dict(values, cos=(windows[0], VM), sin=(windows[1], VM))

    attention_scratch = dict(
        wo=((width, o_cols), BF16),
        heads=((heads, length, 128), BF16),
        o=((length, o_cols), BF16),
        lse=((length, 128), F32),
        n1=four,
        dkv=((2 * KV_HEADS // RANKS, length, 128), F32),
        land_h=four,
    )

    def enter_in(layer):
        rec = records[layer]
        return dict(wq_hbm=(rec["wq"], AN), hin=(rec["hin"], VM), gain_in=(gain(layer, 0), VM))

    enter_scratch = dict(wq=((width, cols), BF16), out_a=three, land_a=three)

    first, down_1 = call_back(
        "back_first", count, rows,
        dict(g=(g, VM), swap_src=(h_round, AN), **inner_in(1), **attention_in(1)),
        dict(
            inner_out,
            dqkv=(like((length, cols)), VM),
            g_out=(like((width, o_cols)), VM),
            g_qkv=(like((width, cols)), VM),
            swap_dst=(like((rows, width)), AN),
        ),
        dict(**inner_scratch, **attention_scratch), [], [shape_d] * 2, (False,) * 2, plan_first, 4,
    )
    parts_of = lambda got: [shape7(got[name]) for name in INNER_GRADS]
    middle, grads_1 = call_back(
        "back_mid", count, rows,
        dict(dqkv=(first["dqkv"], VM), ghin=(first["gh"], VM), **enter_in(1), **inner_in(0)),
        dict(ggin=(like((1, width), F32), VM), **inner_out),
        dict(gnew=row_f32, **enter_scratch, **inner_scratch),
        parts_of(first) + [shape7(first["g_out"]), shape7(first["g_qkv"])],
        [shape_d] * 2, (True,) * 6 + (False,) * 2, plan_middle, 5,
    )
    others = jnp.concatenate([jnp.zeros((1, width), F32), middle["gg"], middle["ggin"], first["gg"]], axis=0)
    others = jnp.pad(others, ((0, 16 - 2 * LAYERS), (0, 0)))
    shard_rows = w_qkv.shape[1]
    shape_o, shape_q = (full_shape(count, (shard_rows, c)) for c in (o_cols, cols))
    final, grads_0 = call_back(
        "back_last", count, rows,
        dict(gh=(middle["gh"], VM), ghin=(middle["gh"], VM), other_gains=(others, VM), **enter_in(0), **attention_in(0)),
        dict(swap_dst=(like((rows, width)), AN), gains_out=(like((16, GAIN_COLS), F32), VM)),
        dict(
            gnew=row_f32,
            gsend=((rows, width), BF16),
            gains_all=((16, width), F32),
            gains_part=(full_shape(count, (16, GAIN_COLS)), BF16),
            part_o=(shape_o, BF16),
            part_q=(shape_q, BF16),
            dqkv=((length, cols), BF16),
            **enter_scratch,
            **attention_scratch,
        ),
        parts_of(middle), [shape_o, shape_q], (True,) * 6, plan_last, 6,
    )
    out_act, grad_tokens, gains_sum = first["swap_dst"], final["swap_dst"], final["gains_out"]
    grads = (grads_0, grads_1[:6])
    downs = (grads_1[6:], down_1)
    piece = gains.shape[-1]
    grad_gains = gains_sum[: 2 * LAYERS, :piece].reshape(LAYERS, 2, piece)
    beside = lambda *halves: jnp.concatenate(halves, axis=2)
    stacked = [unpack_grads(q, o, beside(ga, gb), beside(ua, ub), count) for ga, gb, ua, ub, o, q in grads]
    s_qkv, s_out, s_gu = (jnp.stack([s[i] for s in stacked]) for i in range(3))
    s_down = jnp.stack([jnp.concatenate(d, axis=1) for d in downs])
    wide = lambda value: value.astype(F32)
    return (wide(out_act), wide(grad_tokens), wide(s_qkv), wide(s_out), wide(s_gu), wide(s_down), grad_gains)


def solution(mesh):
    both = ("dp", "ctx")
    return jax.shard_map(
        functools.partial(shards, mesh.shape["dp"], mesh.shape["ctx"]),
        mesh=mesh,
        in_specs=(
            P(both, None),
            P(both, None),
            P(None, both, None),
            P(None, None, both),
            P(None, both, None, None),
            P(None, both, None),
            P(None, None, both),
        ),
        out_specs=(
            P(both, None),
            P(both, None),
            P(None, both, None),
            P(None, None, both),
            P(None, both, None, None),
            P(None, both, None),
            P(None, None, both),
        ),
        check_vma=False,
    )
```

```python
import functools

import jax
import jax.numpy as jnp
import numpy as np
from jax import lax
from jax.experimental import pallas as pl
from jax.experimental.pallas import tpu as pltpu
from jax.sharding import PartitionSpec as P

HEADS = 16
KV_HEADS = 8
HEAD_DIM = 96
LAYERS = 2
RANKS = 4
GAIN_COLS = 128

NORM_EPS = 1e-05
ROPE_BASE = 100000.0
MASKED = -1e30
MESH = pl.DeviceIdType.MESH
BF16 = jnp.bfloat16
F32 = jnp.float32
VMEM_BYTES = 62 * 1024 * 1024


class Place:
    def __init__(self, count):
        self.count = count
        self.dp = lax.axis_index("dp")
        self.ctx = lax.axis_index("ctx")
        self.core = lax.rem(self.dp, 2)
        self.x = lax.rem(lax.div(self.dp, 2), 2)
        self.a = lax.div(self.dp, 4)
        self.zh = lax.div(self.ctx, 2)
        self.zl = lax.rem(self.ctx, 2)
        self.rank = self.x * 2 + self.zl
        dpx = self.dp + 2 - 4 * self.x
        ctz = self.ctx + 1 - 2 * self.zl
        x2, z2 = 1 - self.x, 1 - self.zl
        self.peers = (
            ((dpx, self.ctx), x2 * 2 + self.zl),
            ((self.dp, ctz), self.x * 2 + z2),
            ((dpx, ctz), x2 * 2 + z2),
        )
        self.core_peer = (self.dp + 1 - 2 * self.core, self.ctx)
        self.zh_peer = (self.dp, self.ctx + 2 - 4 * self.zh)
        self.others = []
        for k in range(1, count):
            ahead = lax.rem(self.a + k, count)
            behind = lax.rem(self.a + count - k, count)
            self.others.append(((self.dp + (ahead - self.a) * 4, self.ctx), ahead, behind))
        self.moves = self.x != self.zh
        self.swap_peer = (self.dp + (self.zh - self.x) * 2, self.ctx + (self.x - self.zh) * 2)

    def greet(self, weights, swap):
        devices = [d for d, _ in self.peers]
        if weights:
            devices += [self.core_peer, self.zh_peer] + [o[0] for o in self.others]
        barrier = pltpu.get_barrier_semaphore()
        for device in devices:
            pl.semaphore_signal(barrier, inc=1, device_id=device, device_id_type=MESH)
        if swap:

            @pl.when(self.moves)
            def _():
                pl.semaphore_signal(barrier, inc=1, device_id=self.swap_peer, device_id_type=MESH)

        expected = len(devices)
        if swap:
            expected = expected + self.x + self.zh - 2 * self.x * self.zh
        pl.semaphore_wait(barrier, expected)


class Net:
    def __init__(self, place, send, recv, local):
        self.place, self.send, self.recv, self.local = place, send, recv, local
        self.n, self.m = 0, 0
        self.sends = []

    def remote(self, src, dst, device):
        copy = self.prepare(src, dst, device)
        copy.start()
        self.sends.append(copy)
        return copy

    def prepare(self, src, dst, device):
        i = self.n
        self.n += 1
        return pltpu.make_async_remote_copy(
            src_ref=src, dst_ref=dst, send_sem=self.send.at[i], recv_sem=self.recv.at[i],
            device_id=device, device_id_type=MESH,
        )

    def here(self, src, dst):
        i = self.m
        self.m += 1
        copy = pltpu.make_async_copy(src, dst, self.local.at[i])
        copy.start()
        return copy

    def finish(self):
        for copy in self.sends:
            copy.wait_send()


REMOTE_SEMS, LOCAL_SEMS = 128, 64


def sems(count=2):
    n = REMOTE_SEMS * max(1, count // 2)
    return [
        pltpu.SemaphoreType.DMA((n,)),
        pltpu.SemaphoreType.DMA((n,)),
        pltpu.SemaphoreType.DMA((LOCAL_SEMS,)),
    ]


class Swap:
    def __init__(self, net, src, dst):
        self.net, self.src, self.dst = net, src, dst

    def start(self):
        net, place = self.net, self.net.place
        self.copy = net.prepare(self.src, self.dst, place.swap_peer)
        self.stay = pltpu.make_async_copy(self.src, self.dst, net.local.at[net.m])
        net.m += 1

        @pl.when(place.moves)
        def _():
            self.copy.start()

        @pl.when(jnp.logical_not(place.moves))
        def _():
            self.stay.start()

    def wait(self):
        @pl.when(self.net.place.moves)
        def _():
            self.copy.wait_recv()
            self.copy.wait_send()

        @pl.when(jnp.logical_not(self.net.place.moves))
        def _():
            self.stay.wait()


class Share:
    def __init__(self, net, piece, block):
        self.net, self.piece, self.block = net, piece, block

    def start(self):
        net, place = self.net, self.net.place
        mine = self.block.at[place.x, place.zl]
        self.copies = [net.remote(self.piece.at[rank], mine, device) for device, rank in place.peers]
        self.own = net.here(self.piece.at[place.rank], mine)

    def wait(self):
        for copy in self.copies:
            copy.wait_recv()
        self.own.wait()


class Gather:
    def __init__(self, net, block, full, ranks=True, ahead=None):
        self.net, self.block, self.full, self.ranks, self.ahead = net, block, full, ranks, ahead

    def slot(self, a, core, zh):
        if self.ranks:
            return self.full.at[a, :, core, zh, :]
        return self.full.at[a, core, zh]

    def column(self, a, core):
        if self.ranks:
            return self.full.at[a, :, core, :, :]
        return self.full.at[a, core]

    def begin(self):
        net, p = self.net, self.net.place
        mine = self.slot(p.a, p.core, p.zh)
        self.own = [net.here(self.block, mine)]
        self.cores = [net.remote(self.block, mine, p.core_peer)]
        if self.ahead is None:
            self.across = net.remote(self.block, mine, p.zh_peer)
            self.near = [net.remote(self.block, mine, o[0]) for o in p.others]
            return
        got = self.slot(p.a, p.core, 1 - p.zh)
        self.far = [net.remote(self.ahead.at[0], got, o[0]) for o in p.others]
        self.cores.append(net.remote(self.ahead.at[0], got, p.core_peer))
        self.own.append(net.here(self.ahead.at[0], got))
        for k, other in enumerate(p.others):
            self.own.append(net.here(self.ahead.at[k + 1], self.slot(other[2], p.core, p.zh)))

    def middle(self):
        net, p = self.net, self.net.place
        self.across.wait_recv()
        got = self.slot(p.a, p.core, 1 - p.zh)
        self.far = [net.remote(got, got, o[0]) for o in p.others]
        self.cores.append(net.remote(got, got, p.core_peer))

    def final(self):
        net, p = self.net, self.net.place
        for copy in self.own:
            copy.wait()
        for k, other in enumerate(p.others):
            if self.ahead is None:
                self.near[k].wait_recv()
            self.far[k].wait_recv()
            got = self.column(other[2], p.core)
            self.cores.append(net.remote(got, got, p.core_peer))

    def done(self):
        for copy in self.cores:
            copy.wait_recv()


class Ahead:
    def __init__(self, net, block, got):
        self.net, self.block, self.got = net, block, got

    def begin(self):
        net, p = self.net, self.net.place
        self.copies = [net.remote(self.block, self.got.at[0], p.zh_peer)]
        self.copies += [net.remote(self.block, self.got.at[k + 1], o[0]) for k, o in enumerate(p.others)]

    def done(self):
        for copy in self.copies:
            copy.wait_recv()


class Reduce:
    def __init__(self, net, part, out, held, from_core, from_a, from_zh, from_rank, ranks=True, added=False):
        self.net, self.part, self.out = net, part, out
        self.held, self.from_core, self.from_a = held, from_core, from_a
        self.from_zh, self.from_rank = from_zh, from_rank
        self.ranks, self.added = ranks, added

    def half(self, core):
        return self.part.at[:, :, core] if self.ranks else self.part.at[:, core]

    def begin(self):
        net, p = self.net, self.net.place
        self.load = net.here(self.half(p.core), self.held)
        self.by_core = net.remote(self.half(1 - p.core), self.from_core, p.core_peer)

    def along_a(self):
        net, p = self.net, self.net.place
        self.load.wait()
        self.by_core.wait_recv()
        add_into(self.held, self.from_core)
        self.by_a = [
            net.remote(self.held.at[other[1]], self.from_a.at[k], other[0])
            for k, other in enumerate(p.others)
        ]

    def along_zh(self):
        net, p = self.net, self.net.place
        mine = self.held.at[p.a]
        for k, copy in enumerate(self.by_a):
            copy.wait_recv()
            add_into(mine, self.from_a.at[k])
        there = mine.at[:, 1 - p.zh] if self.ranks else mine.at[1 - p.zh]
        self.by_zh = net.remote(there, self.from_zh, p.zh_peer)

    def among_ranks(self):
        net, p = self.net, self.net.place
        self.by_zh.wait_recv()
        if not self.ranks:
            total = self.held[p.a, p.zh].astype(F32) + self.from_zh[...].astype(F32)
            self.out[...] = total.astype(self.out.dtype)
            return
        for x in range(2):
            for zl in range(2):
                add_into(self.held.at[p.a, x, p.zh, zl], self.from_zh.at[x, zl])
        self.by_rank = []
        for device, rank in p.peers:
            rank_x, rank_zl = lax.div(rank, 2), lax.rem(rank, 2)
            self.by_rank.append(
                net.remote(
                    self.held.at[p.a, rank_x, p.zh, rank_zl], self.from_rank.at[len(self.by_rank)], device
                )
            )

    def done(self):
        if not self.ranks:
            return
        p = self.net.place
        own = self.held[p.a, p.x, p.zh, p.zl].astype(F32)
        for copy in self.by_rank:
            copy.wait_recv()
        if self.added:
            for j in range(3):
                own = own + self.from_rank[j].astype(F32)
            self.out[...] = own
            return
        self.out[p.rank] = own.astype(self.out.dtype)
        for j, (_, rank) in enumerate(p.peers):
            self.out[rank] = self.from_rank[j].astype(self.out.dtype)

    @staticmethod
    def scratch(shape, ranks=True):
        tail = shape[-2:]
        count = shape[0]
        inner = ((2, 2, 2) if ranks else (2,)) + tail
        fewer = ((2, 2) if ranks else ()) + tail
        shapes = [(count,) + inner, (count,) + inner, (max(count - 1, 1),) + inner, fewer]
        if ranks:
            shapes.append((3,) + tail)
        return [pltpu.VMEM(s, BF16) for s in shapes]


def add_into(target, source):
    lead = target.shape[:-2]
    total = 1
    for size in lead:
        total *= size
    if total == 1 and not lead:
        target[...] = (target[...].astype(F32) + source[...].astype(F32)).astype(BF16)
        return

    @pl.loop(0, total)
    def _(j):
        index, left = [], j
        for size in reversed(lead):
            index.append(lax.rem(left, size))
            left = lax.div(left, size)
        index = tuple(reversed(index))
        target[index] = (target[index].astype(F32) + source[index].astype(F32)).astype(BF16)


class Spread:
    def __init__(self, net, land):
        self.net, self.land = net, land
        self.peers = net.place.peers
        mine = land.at[net.place.rank]
        self.along_x = net.remote(mine, mine, self.peers[0][0])
        self.along_zl = net.remote(mine, mine, self.peers[1][0])

    def arrivals(self):
        self.along_zl.wait_recv()
        got = self.land.at[self.peers[1][1]]
        relay = self.net.remote(got, got, self.peers[0][0])
        yield 1, self.peers[1][1]
        self.along_x.wait_recv()
        yield 0, self.peers[0][1]
        relay.wait_recv()
        yield 2, self.peers[2][1]

    def wait(self):
        for _ in self.arrivals():
            pass


class Sum:
    def __init__(self, net, out, land):
        self.net, self.out, self.land = net, out, land
        self.peers = net.place.peers

    def ready(self, i):
        if i == 2:
            self.diagonal = self.net.remote(self.out.at[2], self.land.at[0], self.peers[0][0])
        elif i == 0:
            self.along_x = self.net.remote(self.out.at[0], self.land.at[1], self.peers[0][0])

    def forward(self):
        self.diagonal.wait_recv()
        add_into(self.out.at[1], self.land.at[0])
        self.along_zl = self.net.remote(self.out.at[1], self.land.at[2], self.peers[1][0])

    def result(self, own):
        self.along_x.wait_recv()
        self.along_zl.wait_recv()
        return own + self.land[1].astype(F32) + self.land[2].astype(F32)


class EvenSpread:
    def __init__(self, net, land):
        self.net, self.land = net, land
        self.peers = net.place.peers
        self.half = land.shape[1] // 2
        me = net.place.rank
        self.x_high = self.go(me, 1, 0)
        self.z_low = self.go(me, 0, 1)
        self.x_low = self.go(me, 0, 0)
        self.z_high = self.go(me, 1, 1)

    def go(self, rank, part, i):
        rows = self.land.at[rank, pl.ds(part * self.half, self.half)]
        return self.net.remote(rows, rows, self.peers[i][0])

    def arrivals(self):
        self.x_high.wait_recv()
        on_z = self.go(self.peers[0][1], 1, 1)
        self.z_low.wait_recv()
        on_x = self.go(self.peers[1][1], 0, 0)
        self.x_low.wait_recv()
        yield 0, self.peers[0][1]
        self.z_high.wait_recv()
        yield 1, self.peers[1][1]
        on_z.wait_recv()
        on_x.wait_recv()
        yield 2, self.peers[2][1]

    def wait(self):
        for _ in self.arrivals():
            pass


class EvenSum:
    def __init__(self, net, out, land):
        self.net, self.out, self.land = net, out, land
        self.peers = net.place.peers
        self.half = out.shape[1] // 2

    def go(self, i, part, slot, peer):
        rows = pl.ds(part * self.half, self.half)
        return self.net.remote(self.out.at[i, rows], self.land.at[slot, rows], self.peers[peer][0])

    def ready(self, i):
        if i == 2:
            self.low, self.high = self.go(2, 0, 0, 0), self.go(2, 1, 0, 1)
        elif i == 0:
            self.x_low = self.go(0, 0, 1, 0)
        else:
            self.z_high = self.go(1, 1, 2, 1)

    def forward(self):
        low, high = pl.ds(0, self.half), pl.ds(self.half, self.half)
        self.high.wait_recv()
        add_into(self.out.at[0, high], self.land.at[0, high])
        self.x_high = self.go(0, 1, 1, 0)
        self.low.wait_recv()
        add_into(self.out.at[1, low], self.land.at[0, low])
        self.z_low = self.go(1, 0, 2, 1)

    def result(self, own):
        for copy in (self.x_low, self.x_high, self.z_low, self.z_high):
            copy.wait_recv()
        return own + self.land[1].astype(F32) + self.land[2].astype(F32)


def products(x, w_ref, count, tile, transposed, use):
    def part(cols):
        if transposed:
            w, dims = w_ref[cols, :], (((1,), (1,)), ((), ()))
        else:
            w, dims = w_ref[:, cols], (((1,), (0,)), ((), ()))
        use(cols, lax.dot_general(x(), w, dims, preferred_element_type=F32))

    for j in range(count // tile):
        part(pl.ds(j * tile, tile))


def norm_rows(h, gain):
    factor = lax.rsqrt(jnp.mean(h * h, axis=-1, keepdims=True) + NORM_EPS)
    return (h * factor * gain).astype(BF16)


def norm_rows_back(h, gain, grad):
    factor = lax.rsqrt(jnp.mean(h * h, axis=-1, keepdims=True) + NORM_EPS)
    z = grad * gain
    inner = jnp.sum(z * h, axis=-1, keepdims=True)
    back = factor * z - h * (factor * factor * factor * inner / h.shape[-1])
    return back, jnp.sum(grad * h * factor, axis=0, keepdims=True)


def rows_of(rank, rows):
    return pl.ds(pl.multiple_of(rank * rows, rows), rows)


class Refs:
    def __init__(self, refs):
        self.refs = list(refs)

    def take(self, n):
        got, self.refs = self.refs[:n], self.refs[n:]
        return got


class Ticks:
    def __init__(self, plan):
        self.plan = list(plan)

    def __call__(self):
        if self.plan:
            for step in self.plan.pop(0):
                step()

    def rest(self):
        while self.plan:
            self()


def np_tables(length):
    steps = np.arange(HEAD_DIM // 2, dtype=np.float32)
    inverse = np.exp(steps * np.float32(-2.0 * np.log(ROPE_BASE) / HEAD_DIM)).astype(np.float32)
    angles = np.arange(length, dtype=np.float32)[:, None] * inverse[None, :]
    return np.cos(angles), np.sin(angles)


def wide_tables(length):
    cosine, sine = np_tables(length)
    turned = (HEADS + KV_HEADS) // RANKS
    still = KV_HEADS // RANKS * HEAD_DIM
    cos_all = np.concatenate([cosine] * (2 * turned) + [np.ones((length, still))], axis=1)
    sin_all = np.concatenate([-sine, sine] * turned + [np.zeros((length, still))], axis=1)
    return jnp.asarray(cos_all, F32), jnp.asarray(sin_all, F32)


def turn(values, cosine, sine):
    cols = values.shape[1]
    half = HEAD_DIM // 2
    lane = lax.broadcasted_iota(jnp.int32, values.shape, 1)
    other = jnp.where(
        lax.rem(lane, HEAD_DIM) < half,
        pltpu.roll(values, cols - half, 1),
        pltpu.roll(values, half, 1),
    )
    return values * cosine + other * sine


def head_window(values, h):
    offset = HEAD_DIM * h
    start = offset // 128 * 128
    size = 128 if offset - start + HEAD_DIM <= 128 else 256
    window = values[:, start : start + size]
    if offset > start:
        window = pltpu.roll(window, size - (offset - start), 1)
    window = window[:, :128]
    lane = lax.broadcasted_iota(jnp.int32, window.shape, 1)
    return jnp.where(lane < HEAD_DIM, window, 0.0)


def heads_joined(parts):
    rows = parts[0].shape[0]
    columns = [jnp.zeros((rows, 128), F32) for _ in range(len(parts) * HEAD_DIM // 128 + 1)]
    for h, part in enumerate(parts):
        offset = HEAD_DIM * h
        first = offset // 128
        shift = offset - first * 128
        if shift == 0:
            columns[first] = columns[first] + part
            continue
        double = jnp.concatenate([part, jnp.zeros((rows, 128), F32)], axis=1)
        double = pltpu.roll(double, shift, 1)
        columns[first] = columns[first] + double[:, :128]
        columns[first + 1] = columns[first + 1] + double[:, 128:]
    return jnp.concatenate(columns[:-1], axis=1)


def project_heads(rows, n1, wq, cos_ref, sin_ref, heads):
    count = heads.shape[0]

    @pl.loop(0, RANKS)
    def _(b):
        span = rows_of(b, rows)
        y = jnp.dot(n1[b], wq[...], preferred_element_type=F32)
        y = turn(y, cos_ref[span, :], sin_ref[span, :])
        for h in range(count):
            heads[h, span, :] = head_window(y, h).astype(BF16)


def causal_scores(rows, rank, query, key):
    scores = lax.dot_general(query, key, (((1,), (1,)), ((), ())), preferred_element_type=F32)
    row = lax.broadcasted_iota(jnp.int32, scores.shape, 0) + rank * rows
    col = lax.broadcasted_iota(jnp.int32, scores.shape, 1)
    return jnp.where(col <= row, scores * HEAD_DIM ** (-0.5), MASKED)


def attend_rows(rows, rank, heads, o_ref, lse_ref):
    span = rows_of(rank, rows)
    queries = HEADS // RANKS
    pairs = KV_HEADS // RANKS
    groups = HEADS // KV_HEADS
    mixed = []
    lane = lax.broadcasted_iota(jnp.int32, (rows, 128), 1)
    lse_all = jnp.zeros((rows, 128), F32)
    for h in range(queries):
        kv = h // groups
        scores = causal_scores(rows, rank, heads[h, span, :], heads[queries + kv])
        highest = jnp.max(scores, axis=-1, keepdims=True)
        weights = jnp.exp(scores - highest)
        total = jnp.sum(weights, axis=-1, keepdims=True)
        lse = highest + jnp.log(total)
        lse_all = jnp.where(lane == h, lse, lse_all)
        weights = (weights * (1.0 / total)).astype(BF16)
        mixed.append(
            jnp.dot(weights, heads[queries + pairs + kv], preferred_element_type=F32)
        )
    lse_ref[span, :] = lse_all
    o_ref[span, :] = heads_joined(mixed).astype(BF16)


def window_tables(length):
    cosine, sine = np_tables(length)
    none = np.zeros((length, 128 - HEAD_DIM))
    cos_one = np.concatenate([cosine, cosine, none], axis=1)
    sin_one = np.concatenate([-sine, sine, none], axis=1)
    return jnp.asarray(cos_one, F32), jnp.asarray(sin_one, F32)


def turn_window(values, cosine, sine):
    half = HEAD_DIM // 2
    lane = lax.broadcasted_iota(jnp.int32, values.shape, 1)
    other = jnp.where(lane < half, pltpu.roll(values, 128 - half, 1), pltpu.roll(values, half, 1))
    return values * cosine + other * sine


def dot_tn(a, b):
    return lax.dot_general(a, b, (((0,), (0,)), ((), ())), preferred_element_type=F32)


def attend_rows_back(rows, rank, do_rows, heads, o_ref, lse_ref, cos_ref, sin_ref, dq_ref, dkv):
    span = rows_of(rank, rows)
    queries = HEADS // RANKS
    pairs = KV_HEADS // RANKS
    groups = HEADS // KV_HEADS
    o_rows = o_ref[span, :].astype(F32)
    parts = []
    for h in range(queries):
        kv = h // groups
        do_h = head_window(do_rows, h)
        delta = jnp.sum(do_h * head_window(o_rows, h), axis=-1, keepdims=True)
        do_b = do_h.astype(BF16)
        query, key, value = heads[h, span, :], heads[queries + kv], heads[queries + pairs + kv]
        weights = jnp.exp(causal_scores(rows, rank, query, key) - lse_ref[span, h : h + 1])
        grad_w = lax.dot_general(do_b, value, (((1,), (1,)), ((), ())), preferred_element_type=F32)
        ds = (weights * (grad_w - delta) * HEAD_DIM ** (-0.5)).astype(BF16)
        dq = jnp.dot(ds, key, preferred_element_type=F32)
        parts.append(turn_window(dq, cos_ref[span, :], -sin_ref[span, :]))
        dkv[kv] += dot_tn(ds, query)
        dkv[pairs + kv] += dot_tn(weights.astype(BF16), do_b)
    joined = heads_joined(parts)
    dq_ref[span, pl.ds(0, joined.shape[1])] = joined.astype(BF16)


def close_keys(rows, dkv, cos_ref, sin_ref, dqkv_ref):
    pairs = KV_HEADS // RANKS
    first = HEADS // RANKS * HEAD_DIM

    @pl.loop(0, RANKS)
    def _(b):
        span = rows_of(b, rows)
        parts = [turn_window(dkv[i, span, :], cos_ref[span, :], -sin_ref[span, :]) for i in range(pairs)]
        parts += [dkv[pairs + i, span, :] for i in range(pairs)]
        joined = heads_joined(parts)
        dqkv_ref[span, pl.ds(first, joined.shape[1])] = joined.astype(BF16)


def put_blocks(target, value):
    *lead, rows, cols = target.shape
    if rows % 16 == 0:
        target.reshape(value.shape[0], cols)[...] = value.astype(BF16)
        return
    for block in range(value.shape[0] // rows):
        index, left = [], block
        for size in reversed(lead):
            index.append(left % size)
            left //= size
        target[tuple(reversed(index))] = value[block * rows : (block + 1) * rows].astype(BF16)


def start_kernel(count, n, n_later, n_ahead, *refs):
    refs = Refs(refs)
    (tokens,) = refs.take(1)
    pieces, later = refs.take(n), refs.take(n_later)
    (all_tokens,) = refs.take(1)
    full, blocks_later, got_ahead = refs.take(n), refs.take(n_later), refs.take(n_ahead)
    own_tokens, land = refs.take(2)
    blocks = refs.take(n)
    send, recv, local = refs.take(3)
    place = Place(count)
    net = Net(place, send, recv, local)
    shares = [Share(net, pieces[i], blocks[i]) for i in range(n)]
    shares_later = [Share(net, later[i], blocks_later[i]) for i in range(n_later)]
    gathers = [Gather(net, blocks[i], full[i]) for i in range(n)]
    aheads = [Ahead(net, blocks_later[i], got_ahead[i]) for i in range(n_ahead)]
    swap = Swap(net, tokens, land.at[place.zh * 2 + place.zl])
    place.greet(True, True)
    shares[0].start()
    swap.start()
    for share in shares[1:] + shares_later[:n_ahead]:
        share.start()
    for i in range(2):
        shares[i].wait()
        gathers[i].begin()
    swap.wait()
    spreads = Spread(net, land)
    keep_own = net.here(land.at[place.rank], own_tokens)
    for i in range(2, n):
        shares[i].wait()
        gathers[i].begin()
    for i in range(n_ahead):
        shares_later[i].wait()
        aheads[i].begin()
    arrivals = spreads.arrivals()
    next(arrivals)
    for share in shares_later[n_ahead:]:
        share.start()
    gathers[0].middle()
    gathers[1].middle()
    for _ in arrivals:
        pass
    keep = net.here(land, all_tokens)
    gathers[0].final()
    for i in range(2, n):
        gathers[i].middle()
        gathers[i - 1].final()
    gathers[-1].final()
    for gather in gathers + aheads:
        gather.done()
    for share in shares_later[n_ahead:]:
        share.wait()
    keep_own.wait()
    keep.wait()
    net.finish()


def body_kernel(count, rows, late, started, n_next, n_ahead, plan, *refs):
    refs = Refs(refs)
    n1_hbm, wq_hbm, cos_ref, sin_ref, h_ref, gain_ref, wo_hbm = refs.take(7)
    inner_hbm = refs.take(3)
    ahead_hbm = [refs.take(1)[0] if started[i] else None for i in range(3)]
    if n_next:
        (gain_next,) = refs.take(1)
        blocks = refs.take(n_next)
    else:
        (swap_src,) = refs.take(1)
    early_out = refs.take(6)
    h1_ref, hn_ref, hb_ref, ng_hbm = refs.take(4)
    late_out = [refs.take(1)[0] if late[i] else None for i in range(3)]
    if n_next:
        (nn_hbm,) = refs.take(1)
        full = refs.take(n_next)
    else:
        (swap_dst,) = refs.take(1)
    early = refs.take(6)
    heads, o_ref, lse_ref, gate_ref, up_ref, u_ref = early
    n1, wq, wo = refs.take(3)
    inner = refs.take(3)
    out_a, land_a, land_n, out_b, land_b = refs.take(5)
    if n_next:
        (land_q,) = refs.take(1)
    send, recv, local = refs.take(3)

    place = Place(count)
    net = Net(place, send, recv, local)
    width = h_ref.shape[1]
    hidden = u_ref.shape[1]
    load_q = net.here(wq_hbm.at[:, pl.ds(0, wq.shape[1])], wq)
    load_n = net.here(n1_hbm, n1)
    load_out = net.here(wo_hbm, wo)
    jobs = {}
    loads, weights = [], []
    for i in range(3):
        if late[i]:
            jobs[("gate", "up", "down")[i]] = Gather(net, inner_hbm[i], inner[i], i < 2, ahead_hbm[i])
            loads.append(None)
        else:
            loads.append(net.here(inner_hbm[i], inner[i]))
        weights.append(inner[i].reshape((hidden, width) if i == 2 else (width, hidden)) if late[i] else inner[i])
    wg, wu, wd = weights
    for i in range(n_next):
        jobs[i] = (Ahead if i >= n_next - n_ahead else Gather)(net, blocks[i], full[i])
    if not n_next:
        jobs["swap"] = Swap(net, swap_src, swap_dst)
    peers = place.peers
    place.greet(True, not n_next)
    keeps = []

    def ready(i):
        if late[i]:
            jobs[("gate", "up", "down")[i]].done()
            keeps.append(net.here(inner[i], late_out[i]))
        else:
            loads[i].wait()

    tick = Ticks(plan(jobs))
    tick()

    load_q.wait()
    load_n.wait()
    project_heads(rows, n1, wq, cos_ref, sin_ref, heads)
    load_out.wait()
    sums = EvenSum(net, out_a, land_a)
    for i in (2, 0, 1):
        attend_rows(rows, peers[i][1], heads, o_ref, lse_ref)
        span = rows_of(peers[i][1], rows)

        def use(cols, y, i=i):
            out_a[i, :, cols] = y.astype(BF16)

        products(lambda: o_ref[span, :], wo, width, width, True, use)
        sums.ready(i)
    attend_rows(rows, place.rank, heads, o_ref, lse_ref)
    span = rows_of(place.rank, rows)

    def use_own(cols, y):
        h1_ref[:, cols] = h_ref[:, cols].astype(F32) + y

    products(lambda: o_ref[span, :], wo, width, width, True, use_own)
    sums.forward()
    tick()
    h1 = sums.result(h1_ref[...])
    h1_ref[...] = h1
    land_n[place.rank] = norm_rows(h1, gain_ref[...])
    gather = EvenSpread(net, land_n)
    tick()
    ready(0)
    ready(1)

    def inner_block(rank):
        span = rows_of(rank, rows)

        gate = jnp.dot(land_n[rank], wg[...], preferred_element_type=F32)
        up = jnp.dot(land_n[rank], wu[...], preferred_element_type=F32)
        gate_ref[span, :] = gate.astype(BF16)
        up_ref[span, :] = up.astype(BF16)
        u_ref[span, :] = (gate / (1.0 + jnp.exp(-gate)) * up).astype(BF16)

        return span

    inner_block(place.rank)
    tick()
    second = EvenSum(net, out_b, land_b)
    got_down = False
    for i, rank in gather.arrivals():
        span = inner_block(rank)
        if not got_down:
            tick()
            ready(2)
            got_down = True

        def use(cols, y, i=i):
            out_b[i, :, cols] = y.astype(BF16)

        products(lambda: u_ref[span, :], wd, width, width, False, use)
        second.ready(i)
        tick()
    keep = net.here(land_n, ng_hbm)
    for ref, out in zip(early, early_out):
        keeps.append(net.here(ref, out))
    span = rows_of(place.rank, rows)

    def use_down(cols, y):
        hn_ref[:, cols] = h1_ref[:, cols] + y

    products(lambda: u_ref[span, :], wd, width, width, False, use_down)
    second.forward()
    tick()
    hn = second.result(hn_ref[...])
    hn_ref[...] = hn
    hb_ref[...] = hn.astype(BF16)
    if n_next:
        land_q[place.rank] = norm_rows(hn, gain_next[...])
        third = EvenSpread(net, land_q)
        tick()
        for _ in third.arrivals():
            tick()
        keep_next = net.here(land_q, nn_hbm)
        keep_next.wait()
    tick.rest()
    for i in range(n_next):
        jobs[i].done()
    if not n_next:
        jobs["swap"].wait()
    keep.wait()
    for copy in keeps:
        copy.wait()
    net.finish()


def plan_late(j):
    gate, up, down = j["gate"], j["up"], j["down"]
    return [
        [gate.begin, up.begin],
        [gate.middle, down.begin],
        [up.final, gate.final],
        [down.middle, j[0].begin, j[1].begin],
        [down.final],
        [],
        [],
        [j[0].middle],
        [j[0].final, j[1].middle],
        [j[2].begin, j[1].final],
    ]


def plan_late_end(j):
    gate, up, down = j["gate"], j["up"], j["down"]
    return [
        [up.begin, gate.begin],
        [up.middle, down.begin],
        [gate.final, up.final],
        [down.middle],
        [down.final],
        [],
        [],
        [j["swap"].start],
    ]


def plan_early(j):
    down = j["down"]
    return [
        [down.begin],
        [down.middle, j[0].begin],
        [],
        [down.final, j[1].begin, j[2].begin],
        [j[0].middle],
        [],
        [],
        [j[0].final],
        [j[1].middle, j[2].middle],
        [j[3].begin, j[1].final, j[2].final],
        [],
        [],
        [j[3].middle],
        [j[3].final],
    ]


def plan_end(j):
    down = j["down"]
    return [
        [down.begin],
        [],
        [down.middle],
        [],
        [down.final],
        [],
        [],
        [j["swap"].start],
    ]


class Back:
    def __init__(self, net, rows):
        self.net, self.place, self.rows = net, net.place, rows
        self.peers = net.place.peers

    def enter(self, r, tick):
        rows, place = self.rows, self.place
        width = r["gnew"].shape[1]
        total = EvenSum(self.net, r["out_a"], r["land_a"])
        for i in (2, 0, 1):
            span = rows_of(self.peers[i][1], rows)

            def use(cols, y, i=i):
                r["out_a"][i, :, cols] = y.astype(BF16)

            products(lambda: r["dqkv"][span, :], r["wq"], width, width, True, use)
            total.ready(i)
        tick()
        own = rows_of(place.rank, rows)

        def use_own(cols, y):
            r["gnew"][:, cols] = y

        products(lambda: r["dqkv"][own, :], r["wq"], width, width, True, use_own)
        total.forward()
        tick()
        dn = total.result(r["gnew"][...])
        back, ggain = norm_rows_back(r["hin"][...].astype(F32), r["gain_in"][...], dn)
        r["gnew"][...] = r["ghin"][...] + back
        return ggain

    def feed_forward(self, r, tick, ready, between):
        net, rows, place = self.net, self.rows, self.place
        land_g, dgu, out_b = r["land_g"], r["dgu"], r["out_b"]
        width = land_g.shape[2]
        hidden = r["gate"].shape[1]
        land_g[place.rank] = r["g"][...].astype(BF16)
        gather = EvenSpread(net, land_g)
        tick()
        ready()

        def inner_block(rank):
            span = rows_of(rank, rows)
            du = lax.dot_general(
                land_g[rank], r["wd"][...], (((1,), (1,)), ((), ())), preferred_element_type=F32
            )
            gate, up = r["gate"][span, :].astype(F32), r["up"][span, :].astype(F32)
            sg = 1.0 / (1.0 + jnp.exp(-gate))
            dgu[span, pl.ds(0, hidden)] = (du * up * sg * (1.0 + gate * (1.0 - sg))).astype(BF16)
            dgu[span, pl.ds(hidden, hidden)] = (du * gate * sg).astype(BF16)
            return span

        span = inner_block(place.rank)

        def use_mid(cols, y):
            r["gh"][:, cols] = y

        products(lambda: dgu[span, :], r["wgu"], width, width, True, use_mid)
        tick()
        second = EvenSum(net, out_b, r["land_b"])
        for i, rank in gather.arrivals():
            span = inner_block(rank)

            def use(cols, y, i=i):
                out_b[i, :, cols] = y.astype(BF16)

            products(lambda: dgu[span, :], r["wgu"], width, width, True, use)
            second.ready(i)
            tick()
        second.forward()
        tick()
        between()
        tick()
        dn = second.result(r["gh"][...])
        back, ggain = norm_rows_back(r["h1"][...], r["gain"][...], dn)
        r["gh"][...] = r["g"][...].astype(F32) + back
        r["gg"][...] = ggain

    def weight_grads(self, r, down_made):
        net = self.net
        buffers, copies = r["buffers"], []
        tile = buffers.shape[1]
        tall, hidden = r["u"].shape
        width = r["land_g"].shape[2]
        g_all = r["land_g"][...].reshape(tall, width)

        def emit(lhs, rhs, outs, m):
            slot = len(copies) % 2
            if len(copies) >= 2:
                for copy in copies[-2]:
                    copy.wait()
            buffers[slot, :, pl.ds(0, rhs.shape[1])] = dot_tn(lhs, rhs).astype(BF16)
            cols = rhs.shape[1] // len(outs)
            copies.append([
                net.here(buffers.at[slot, :, pl.ds(k * cols, cols)], out.at[pl.ds(m * tile, tile)])
                for k, out in enumerate(outs)
            ])

        for k, part in enumerate((r["part_da"], r["part_db"])):
            cols = part.shape[-1]
            made = dot_tn(r["u"][...], g_all[:, k * cols : (k + 1) * cols])
            part.reshape(hidden, cols)[...] = made.astype(BF16)
        down_made()
        for m in range(width // tile):
            emit(r["n2"][:, m * tile : (m + 1) * tile], r["dgu"][...], [r[name] for name in INNER_GRADS], m)
        return copies[-2] + copies[-1]

    def attention(self, r, tick, ready):
        net, rows, place = self.net, self.rows, self.place
        land_h = r["land_h"]
        land_h[place.rank] = r["gh"][...].astype(BF16)
        gather = EvenSpread(net, land_h)
        tick()
        ready()
        r["dkv"][...] = jnp.zeros(r["dkv"].shape, F32)

        def block(rank):
            do_rows = jnp.dot(land_h[rank], r["wo"][...], preferred_element_type=F32)
            do_rows = do_rows.astype(BF16).astype(F32)
            attend_rows_back(
                rows, rank, do_rows, r["heads"], r["o"], r["lse"], r["cos"], r["sin"], r["dqkv"], r["dkv"]
            )

        block(place.rank)
        tick()
        for _, rank in gather.arrivals():
            block(rank)
            tick()
        close_keys(rows, r["dkv"], r["cos"], r["sin"], r["dqkv"])


INNER_GRADS = ("g_gate_a", "g_gate_b", "g_up_a", "g_up_b")


def back_kernel(count, rows, names, out_names, scratch_names, n_parts, kinds, plan, *refs):
    refs = Refs(refs)
    r = dict(zip(names, refs.take(len(names))))
    parts = refs.take(n_parts)
    r.update(zip(out_names, refs.take(len(out_names))))
    red_out = refs.take(len(kinds))
    r.update(zip(scratch_names, refs.take(len(scratch_names))))
    red_scratch = [refs.take(5 if ranks else 4) for ranks in kinds]
    gains_scratch = refs.take(5) if "gains_out" in r else None
    send, recv, local = refs.take(3)

    place = Place(count)
    net = Net(place, send, recv, local)
    back = Back(net, rows)
    entering, inner, attention = "hin" in r, "h1" in r, "heads_hbm" in r
    last = "gains_out" in r
    waits = {}

    def load(name, source, target):
        waits[name] = net.here(source, target)

    parts = parts + ([r["part_o"], r["part_q"]] if last else [r["part_da"], r["part_db"]])
    jobs = []
    for part, out, scratch, ranks in zip(parts, red_out, red_scratch, kinds):
        jobs.append(Reduce(net, part, out, *scratch, *([] if ranks else [None]), ranks=ranks))
    if entering:
        load("wq", r["wq_hbm"].at[:, pl.ds(0, r["wq"].shape[1])], r["wq"])
    if inner:
        hidden = r["wd"].shape[0]
        load("wd", r["wd_hbm"], r["wd"])
        load("wg", r["wgate_hbm"], r["wgu"].at[:, pl.ds(0, hidden)])
        load("wu", r["wup_hbm"], r["wgu"].at[:, pl.ds(hidden, hidden)])
        load("gate", r["gate_hbm"], r["gate"])
        load("up", r["up_hbm"], r["up"])
        load("u", r["u_hbm"], r["u"])
        load("n2", r["n2_hbm"], r["n2"])
    if attention:
        for name in ("wo", "heads", "o", "lse", "n1"):
            load(name, r[name + "_hbm"], r[name])
    place.greet(len(jobs) > 0, "swap_src" in r or last)
    if "swap_src" in r:
        jobs.append(Swap(net, r["swap_src"], r["swap_dst"]))
    tick = Ticks(plan(jobs))
    tick()
    ends = []

    def ready_inner():
        for name in ("wd", "wg", "wu", "gate", "up"):
            waits[name].wait()

    def between():
        waits["u"].wait()
        waits["n2"].wait()
        ends.extend(back.weight_grads(r, tick))

    def ready_attention():
        for name in ("wo", "heads", "o", "lse"):
            waits[name].wait()

    if entering and inner:
        waits["wq"].wait()
        r["ggin"][...] = back.enter(r, tick)
        r["g"] = r["gnew"]
    if inner:
        back.feed_forward(r, tick, ready_inner, between)
    if attention:
        back.attention(r, tick, ready_attention)
        waits["n1"].wait()
        width = r["land_h"].shape[2]
        tall = r["o"].shape[0]

        def grad_out():
            return dot_tn(r["land_h"][...].reshape(tall, width), r["o"][...])

        def grad_qkv():
            return dot_tn(r["n1"][...].reshape(tall, width), r["dqkv"][...])

        if not last:
            r["g_out"][...] = grad_out().astype(BF16)
            r["g_qkv"][...] = grad_qkv().astype(BF16)
        else:
            waits["wq"].wait()
            made = Ticks([
                [],
                [lambda: put_blocks(r["part_q"], grad_qkv()), lambda: put_blocks(r["part_o"], grad_out())],
            ])

            def both():
                made()
                tick()

            ggain = back.enter(r, both)
            finish_last(net, r, jobs, ggain, gains_scratch)
            for copy in ends:
                copy.wait()
            net.finish()
            return
    tick.rest()
    if "swap_src" in r:
        jobs[-1].wait()
    for copy in ends:
        copy.wait()
    net.finish()


def finish_last(net, r, jobs, ggain, scratch):
    r["gsend"][...] = r["gnew"][...].astype(BF16)
    swap = Swap(net, r["gsend"], r["swap_dst"])
    gains_all, gains_part = r["gains_all"], r["gains_part"]
    gains_all[...] = r["other_gains"][...]
    gains_all[0:1, :] = ggain
    gains_part[...] = jnp.zeros(gains_part.shape, BF16)
    count = gains_part.shape[0]
    piece = gains_all.shape[1] // (16 * count)
    for block in range(16 * count):
        index = (block // 16, block // 8 % 2, block // 4 % 2, block // 2 % 2, block % 2)
        gains_part[index + (slice(None), slice(0, piece))] = gains_all[
            :, block * piece : (block + 1) * piece
        ].astype(BF16)
    small = Reduce(net, gains_part, r["gains_out"], *scratch, added=True)
    small.begin()
    for step in plan_finish(jobs, small, swap):
        step()
    swap.wait()


def plan_finish(j, s, swap):
    ga, gb, ua, ub, out, qkv = j
    return [
        s.along_a, ub.along_zh, out.along_a, qkv.along_a, ga.among_ranks, s.along_zh, out.along_zh, gb.among_ranks,
        s.among_ranks, ua.among_ranks, swap.start, ub.among_ranks, ga.done, qkv.along_zh, gb.done, out.among_ranks,
        s.done, ua.done, ub.done, out.done, qkv.among_ranks, qkv.done,
    ]


def plan_first(j):
    da, db, swap = j
    return [
        [],
        [],
        [],
        [],
        [],
        [],
        [swap.start],
        [da.begin, db.begin],
        [da.along_a],
        [db.along_a],
        [],
        [da.along_zh],
        [db.along_zh],
        [],
        [da.among_ranks, db.among_ranks],
    ]


def plan_middle(j):
    ga, gb, ua, ub, out, qkv, da, db = j
    return [
        [ga.begin, gb.begin, ua.begin, ub.begin, out.begin, qkv.begin],
        [ga.along_a],
        [gb.along_a, ga.along_zh],
        [ua.along_a],
        [gb.along_zh],
        [ub.along_a, ua.along_zh],
        [out.along_a],
        [ga.among_ranks],
        [ub.along_zh, qkv.along_a],
        [da.begin, db.begin, gb.among_ranks],
        [out.along_zh, ua.among_ranks, da.along_a],
        [db.along_a, ub.among_ranks, qkv.along_zh, out.among_ranks, ga.done, gb.done, da.along_zh, ua.done, ub.done],
        [qkv.among_ranks, db.along_zh, out.done, qkv.done, da.among_ranks, db.among_ranks],
    ]


def plan_last(j):
    ga, gb, ua, ub, out, qkv = j
    return [
        [ga.begin, gb.begin, ua.begin, ub.begin],
        [ga.along_a],
        [gb.along_a],
        [ga.along_zh, ua.along_a],
        [],
        [gb.along_zh, ub.along_a],
        [],
        [out.begin, qkv.begin, ua.along_zh],
    ]


def pack_weights(w_qkv, w_out, w_gate_up, gains, count, layer):
    rows = w_qkv.shape[1]
    attn_cols = HEADS * HEAD_DIM
    kv_cols = KV_HEADS * HEAD_DIM
    qkv = w_qkv[layer]
    q = qkv[:, :attn_cols].reshape(rows, RANKS, -1)
    k = qkv[:, attn_cols : attn_cols + kv_cols].reshape(rows, RANKS, -1)
    v = qkv[:, attn_cols + kv_cols :].reshape(rows, RANKS, -1)
    columns = [q, k, v]
    if layer == 0:
        scales = jnp.pad(gains.reshape(2 * LAYERS, rows).T, ((0, 0), (0, GAIN_COLS - 2 * LAYERS)))
        columns.append(jnp.broadcast_to(scales[:, None], (rows, RANKS, GAIN_COLS)))
    head = jnp.concatenate(columns, axis=2).transpose(1, 0, 2)
    out = w_out[layer].T.reshape(rows, RANKS, -1).transpose(1, 0, 2)
    gu = w_gate_up[layer].reshape(rows, 2, count, 2, 2, 2, 2, -1)
    gu = gu.transpose(1, 3, 6, 0, 2, 4, 5, 7).reshape(2, RANKS, rows, -1)
    return head, out, gu[0], gu[1]


def unpack_grads(head, out, gate, up, count):
    rows = head.shape[1]
    q_cols = HEADS * HEAD_DIM // RANKS
    kv_cols = KV_HEADS * HEAD_DIM // RANKS
    wide = lambda part: part.transpose(1, 0, 2).reshape(rows, -1)
    qkv = jnp.concatenate(
        [
            wide(head[:, :, :q_cols]),
            wide(head[:, :, q_cols : q_cols + kv_cols]),
            wide(head[:, :, q_cols + kv_cols : q_cols + 2 * kv_cols]),
        ],
        axis=1,
    )
    order = lambda part: (
        part.reshape(2, 2, rows, count, 2, 2, -1).transpose(2, 3, 0, 4, 5, 1, 6).reshape(rows, -1)
    )
    return qkv, wide(out).T, jnp.stack([order(gate), order(up)], axis=1)


VM = pl.BlockSpec(memory_space=pltpu.VMEM)
AN = pl.BlockSpec(memory_space=pl.ANY)


def params(collective_id):
    return pltpu.CompilerParams(
        collective_id=collective_id, has_side_effects=True, vmem_limit_bytes=VMEM_BYTES
    )


def like(shape, dtype=BF16):
    return jax.ShapeDtypeStruct(tuple(shape), dtype)


def full_shape(count, tail):
    return (count, 2, 2, 2, 2) + tuple(tail)


def call_start(count, tokens, pieces, later, n_ahead):
    rows, width = tokens.shape
    n, n_later = len(pieces), len(later)
    outs = [like((RANKS, rows, width))]
    outs += [like(full_shape(count, p.shape[1:])) for p in pieces]
    outs += [like((2, 2) + p.shape[1:]) for p in later]
    outs += [like((count, 2, 2) + p.shape[1:]) for p in later[:n_ahead]]
    outs += [like((rows, width))]
    got = pl.pallas_call(
        functools.partial(start_kernel, count, n, n_later, n_ahead),
        out_shape=outs,
        in_specs=[AN] * (1 + n + n_later),
        out_specs=[AN] * len(outs),
        scratch_shapes=[pltpu.VMEM((RANKS, rows, width), BF16)]
        + [pltpu.VMEM((2, 2) + p.shape[1:], BF16) for p in pieces]
        + sems(count),
        compiler_params=params(1),
        name="start",
    )(tokens, *pieces, *later)
    cut = n + 1 + n_later
    return got[0], got[-1], [flat(f) for f in got[1 : n + 1]], got[n + 1 : cut], got[cut:-1]


def flat(value):
    return value.reshape(-1, value.shape[-1])


def call_body(
    count, n1, wq, tables, h, gain, wo, inner, late, ahead, plan, gain_next=None, blocks=(), n_ahead=0, swap=None
):
    started = tuple(value is not None for value in ahead)
    rows, width = h.shape
    tall = RANKS * rows
    hidden = inner[0].shape[-1]
    n_next = len(blocks)
    heads = (HEADS + 2 * KV_HEADS) // RANKS
    cols = heads * HEAD_DIM
    o_cols = HEADS // RANKS * HEAD_DIM
    three = pltpu.VMEM((3, rows, width), BF16)
    four = pltpu.VMEM((RANKS, rows, width), BF16)
    shapes = []
    for i in range(3):
        shape = inner[i].shape
        if late[i]:
            shape = full_shape(count, shape[2:]) if i < 2 else (count, 2, 2) + shape
        shapes.append(shape)
    outs = [
        like((heads, tall, 128)),
        like((tall, o_cols)),
        like((tall, 128), F32),
        like((tall, hidden)),
        like((tall, hidden)),
        like((tall, hidden)),
        like((rows, width), F32),
        like((rows, width), F32),
        like((rows, width)),
        like((RANKS, rows, width)),
    ]
    n_state = len(outs)
    outs += [like(shapes[i]) for i in range(3) if late[i]]
    if n_next:
        outs += [like((RANKS, rows, width))]
        outs += [like(full_shape(count, b.shape[2:])) for b in blocks[: n_next - n_ahead]]
        outs += [like((count,) + b.shape) for b in blocks[n_next - n_ahead :]]
        extra = (gain_next, *blocks)
    else:
        outs += [like(swap.shape)]
        extra = (swap,)
    got = pl.pallas_call(
        functools.partial(body_kernel, count, rows, late, started, n_next, n_ahead, plan),
        out_shape=outs,
        in_specs=[AN, AN, VM, VM, VM, VM, AN, AN, AN, AN]
        + [AN] * sum(started)
        + ([VM] + [AN] * n_next if n_next else [AN]),
        out_specs=[AN] * 6 + [VM] * 3 + [AN] * (len(outs) - n_state + 1),
        scratch_shapes=[pltpu.VMEM(out.shape, out.dtype) for out in outs[:6]]
        + [
            four,
            pltpu.VMEM((width, cols), BF16),
            pltpu.VMEM(wo.shape, BF16),
        ]
        + [pltpu.VMEM(shape, BF16) for shape in shapes]
        + [three, three, four, three, three]
        + ([four] if n_next else [])
        + sems(count),
        compiler_params=params(2 if n_next else 3),
        name="body_more" if n_next else "body",
    )(n1, wq, *tables, h, gain, wo, *inner, *[value for value in ahead if value is not None], *extra)
    got = list(got)
    state, rest = got[:n_state], got[n_state:]
    inner = [flat(rest.pop(0)) if late[i] else inner[i] for i in range(3)]
    rest, last = rest[: len(rest) - n_ahead], rest[len(rest) - n_ahead :]
    return state, inner, rest[0], [flat(f) for f in rest[1:]], last


def call_back(name, count, rows, inputs, outputs, scratch, parts, made, kinds, plan, collective_id):
    shapes = [p.shape for p in parts] + list(made)
    red_out = [like(((RANKS,) if ranks else ()) + shape[-2:]) for shape, ranks in zip(shapes, kinds)]
    scratch_shapes = [pltpu.VMEM(shape, dtype) for shape, dtype in scratch.values()]
    for shape, ranks in zip(shapes, kinds):
        scratch_shapes += Reduce.scratch(shape, ranks=ranks)
    if "gains_out" in outputs:
        scratch_shapes += Reduce.scratch(scratch["gains_part"][0])
    got = pl.pallas_call(
        functools.partial(
            back_kernel, count, rows, tuple(inputs), tuple(outputs), tuple(scratch), len(parts), kinds, plan
        ),
        out_shape=[shape for shape, _ in outputs.values()] + red_out,
        in_specs=[spec for _, spec in inputs.values()] + [AN] * len(parts),
        out_specs=[spec for _, spec in outputs.values()] + [VM] * len(red_out),
        scratch_shapes=scratch_shapes + sems(count),
        compiler_params=params(collective_id),
        name=name,
    )(*[value for value, _ in inputs.values()], *parts)
    return dict(zip(outputs, got)), got[len(outputs) :]


def shards(dp_size, ctx_size, tokens, cotangent, w_qkv, w_out, w_gate_up, w_down, gains):
    count = dp_size // 4
    rows, width = tokens.shape
    length = RANKS * rows
    hidden = w_gate_up.shape[-1] // RANKS
    tall = lambda value: value.reshape(length, width)

    swap = lambda value: lax.ppermute(value, ("dp", "ctx"), swap_pairs(dp_size, ctx_size))
    tie = lax.optimization_barrier

    tables = wide_tables(length)
    windows = window_tables(length)

    packed = [pack_weights(w_qkv, w_out, w_gate_up, gains, count, layer) for layer in range(LAYERS)]
    whole_rows = w_qkv.shape[1] % 16 == 0
    none = (None, None, None)
    if whole_rows:
        head, out, gate, up = packed[0]
        now, later, n_ahead = (head, out), (up, gate, *packed[1]), 1
    else:
        now, later, n_ahead = packed[0], packed[1], 0
    all_tokens, h, full, blocks, ahead = call_start(count, tokens, now, later, n_ahead)
    gain_rows = full[0][:, -GAIN_COLS:][:, : 2 * LAYERS].astype(F32).T
    gain = lambda layer, which: gain_rows[2 * layer + which][None]
    n1 = norm_rows(all_tokens.astype(F32), gain(0, 0))
    if whole_rows:
        up, gate, *blocks, last_up = blocks
        inner, late, ahead, plan = (gate, up, w_down[0]), (True, True, True), (None, ahead[0], None), plan_late
    else:
        inner, late, ahead, plan = (*full[2:], w_down[0]), (False, False, True), none, plan_early

    records = []
    for layer in range(LAYERS):
        wq, wo = full[:2]
        if layer + 1 < LAYERS:
            state, inner, n1_next, full, last_got = call_body(
                count, n1, wq, tables, h, gain(layer, 1), wo, inner, late, ahead, plan,
                gain(layer + 1, 0), blocks, n_ahead,
            )
            if whole_rows:
                late, ahead, plan = (True, True, True), (last_got[0], None, None), plan_late_end
                next_inner = (blocks[-1], last_up, w_down[layer + 1])
            else:
                late, plan = (False, False, True), plan_end
                next_inner = (*full[2:], w_down[layer + 1])
        else:
            state, inner, g, _, _ = call_body(
                count, n1, wq, tables, h, gain(layer, 1), wo, inner, late, ahead, plan,
                swap=cotangent.astype(BF16),
            )
            n1_next = None
        heads, mixed, lse, gate, up, u, h1, h_next, h_round, n2 = state
        records.append(dict(
            hin=h, n1=n1, heads=heads, o=mixed, lse=lse, h1=h1, n2=tall(n2), gate=gate, up=up, u=u,
            wq=wq, wo=wo, wgate=inner[0], wup=inner[1], wd=inner[2],
        ))
        h, n1, inner = h_next, n1_next, next_inner

    hidden = records[0]["u"].shape[1]
    heads = (HEADS + 2 * KV_HEADS) // RANKS
    cols = heads * HEAD_DIM
    o_cols = HEADS // RANKS * HEAD_DIM
    shape7 = lambda value: value.reshape(count, 2, 2, 2, 2, -1, value.shape[-1])
    three, four = ((3, rows, width), BF16), ((RANKS, rows, width), BF16)
    row_f32 = ((rows, width), F32)

    def inner_in(layer):
        rec = records[layer]
        names = dict(wd="wd", wgate="wgate", wup="wup", u="u", n2="n2", gate="gate", up="up")
        values = {key + "_hbm": (rec[name], AN) for key, name in names.items()}
        return dict(
            values, h1=(rec["h1"], VM), gain=(gain(layer, 1), VM)
        )

    inner_out = dict(
        gh=(like((rows, width), F32), VM),
        gg=(like((1, width), F32), VM),
        **{name: (like((width, hidden // 2)), AN) for name in INNER_GRADS},
    )
    shape_d = (count, 2, 2, w_down.shape[1], width // 2)
    inner_scratch = dict(
        part_da=(shape_d, BF16),
        part_db=(shape_d, BF16),
        wd=((hidden, width), BF16),
        wgu=((width, 2 * hidden), BF16),
        u=((length, hidden), BF16),
        gate=((length, hidden), BF16),
        up=((length, hidden), BF16),
        n2=((length, width), BF16),
        dgu=((length, 2 * hidden), BF16),
        buffers=((2, 256, 2 * hidden), BF16),
        land_g=four,
        out_b=three,
        land_b=three,
    )

    def attention_in(layer):
        rec = records[layer]
        values = {name + "_hbm": (rec[name], AN) for name in ("wo", "heads", "o", "lse", "n1")}
        return dict(values, cos=(windows[0], VM), sin=(windows[1], VM))

    attention_scratch = dict(
        wo=((width, o_cols), BF16),
        heads=((heads, length, 128), BF16),
        o=((length, o_cols), BF16),
        lse=((length, 128), F32),
        n1=four,
        dkv=((2 * KV_HEADS // RANKS, length, 128), F32),
        land_h=four,
    )

    def enter_in(layer):
        rec = records[layer]
        return dict(wq_hbm=(rec["wq"], AN), hin=(rec["hin"], VM), gain_in=(gain(layer, 0), VM))

    enter_scratch = dict(wq=((width, cols), BF16), out_a=three, land_a=three)

    first, down_1 = call_back(
        "back_first", count, rows,
        dict(g=(g, VM), swap_src=(h_round, AN), **inner_in(1), **attention_in(1)),
        dict(
            inner_out,
            dqkv=(like((length, cols)), VM),
            g_out=(like((width, o_cols)), VM),
            g_qkv=(like((width, cols)), VM),
            swap_dst=(like((rows, width)), AN),
        ),
        dict(**inner_scratch, **attention_scratch), [], [shape_d] * 2, (False,) * 2, plan_first, 4,
    )
    parts_of = lambda got: [shape7(got[name]) for name in INNER_GRADS]
    middle, grads_1 = call_back(
        "back_mid", count, rows,
        dict(dqkv=(first["dqkv"], VM), ghin=(first["gh"], VM), **enter_in(1), **inner_in(0)),
        dict(ggin=(like((1, width), F32), VM), **inner_out),
        dict(gnew=row_f32, **enter_scratch, **inner_scratch),
        parts_of(first) + [shape7(first["g_out"]), shape7(first["g_qkv"])],
        [shape_d] * 2, (True,) * 6 + (False,) * 2, plan_middle, 5,
    )
    others = jnp.concatenate([jnp.zeros((1, width), F32), middle["gg"], middle["ggin"], first["gg"]], axis=0)
    others = jnp.pad(others, ((0, 16 - 2 * LAYERS), (0, 0)))
    shard_rows = w_qkv.shape[1]
    shape_o, shape_q = (full_shape(count, (shard_rows, c)) for c in (o_cols, cols))
    final, grads_0 = call_back(
        "back_last", count, rows,
        dict(gh=(middle["gh"], VM), ghin=(middle["gh"], VM), other_gains=(others, VM), **enter_in(0), **attention_in(0)),
        dict(swap_dst=(like((rows, width)), AN), gains_out=(like((16, GAIN_COLS), F32), VM)),
        dict(
            gnew=row_f32,
            gsend=((rows, width), BF16),
            gains_all=((16, width), F32),
            gains_part=(full_shape(count, (16, GAIN_COLS)), BF16),
            part_o=(shape_o, BF16),
            part_q=(shape_q, BF16),
            dqkv=((length, cols), BF16),
            **enter_scratch,
            **attention_scratch,
        ),
        parts_of(middle), [shape_o, shape_q], (True,) * 6, plan_last, 6,
    )
    out_act, grad_tokens, gains_sum = first["swap_dst"], final["swap_dst"], final["gains_out"]
    grads = (grads_0, grads_1[:6])
    downs = (grads_1[6:], down_1)
    piece = gains.shape[-1]
    grad_gains = gains_sum[: 2 * LAYERS, :piece].reshape(LAYERS, 2, piece)
    beside = lambda *halves: jnp.concatenate(halves, axis=2)
    stacked = [unpack_grads(q, o, beside(ga, gb), beside(ua, ub), count) for ga, gb, ua, ub, o, q in grads]
    s_qkv, s_out, s_gu = (jnp.stack([s[i] for s in stacked]) for i in range(3))
    s_down = jnp.stack([jnp.concatenate(d, axis=1) for d in downs])
    wide = lambda value: value.astype(F32)
    return (wide(out_act), wide(grad_tokens), wide(s_qkv), wide(s_out), wide(s_gu), wide(s_down), grad_gains)


def solution(mesh):
    both = ("dp", "ctx")
    return jax.shard_map(
        functools.partial(shards, mesh.shape["dp"], mesh.shape["ctx"]),
        mesh=mesh,
        in_specs=(
            P(both, None),
            P(both, None),
            P(None, both, None),
            P(None, None, both),
            P(None, both, None, None),
            P(None, both, None),
            P(None, None, both),
        ),
        out_specs=(
            P(both, None),
            P(both, None),
            P(None, both, None),
            P(None, None, both),
            P(None, both, None, None),
            P(None, both, None),
            P(None, None, both),
        ),
        check_vma=False,
    )
```
